32 devices in a mesh: dp: 16 (over z, y, x), tensor: 2 (over core).
Axes of the slice: x: 2, y: 2, z: 4, core: 2. Of those that a mesh axis runs over, the one named last changes fastest.
Arguments:
- tokens: bfloat16 [8192, 768], P('dp'), may hold values from -6 to 6
- segment_ids: int32 [16, 512], P('dp'), may hold values from 0 to 7, never falling along the last dimension, each value on 1 to 256 neighbouring positions
- expert_ids: int32 [8192, 2], P('dp'), may hold values from 0 to 3, all different within a row
- slot_order: int32 [16, 1024], P('dp'), may hold values from 0 to 1023, each once within a row
- gain_attn: bfloat16 [768], P('dp'), may hold values from 0.5 to 1.5
- qkv_weight: bfloat16 [768, 3, 768], P('dp', None, 'tensor'), may hold values from -0.21875 to 0.21875
- out_weight: bfloat16 [768, 768], P('tensor', 'dp'), may hold values from -0.625 to 0.625
- gain_ffn: bfloat16 [768], P('dp'), may hold values from 0.5 to 1.5
- router_weight: bfloat16 [768, 4], P('dp'), may hold values from -0.15625 to 0.15625
- gate_up: bfloat16 [4, 768, 2, 2048], P(None, 'dp', None, 'tensor'), may hold values from -0.21875 to 0.21875
- down_weight: bfloat16 [4, 2048, 768], P(None, 'tensor', 'dp'), may hold values from -0.25 to 0.25
- shared_gate_up: bfloat16 [768, 2, 2048], P('dp', None, 'tensor'), may hold values from -0.21875 to 0.21875
- shared_down: bfloat16 [2048, 768], P('tensor', 'dp'), may hold values from -0.1875 to 0.1875
- cotangent: bfloat16 [8192, 768], P('dp'), may hold values from -6 to 6
Outputs:
- output: bfloat16 [8192, 768], P('dp')
- grad_tokens: float32 [8192, 768], P('dp')
- grad_gain_attn: float32 [768], P('dp')
- grad_qkv: float32 [768, 3, 768], P('dp', None, 'tensor')
- grad_out: float32 [768, 768], P('tensor', 'dp')
- grad_gain_ffn: float32 [768], P('dp')
- grad_router: float32 [768, 4], P('dp')
- grad_gate_up: float32 [4, 768, 2, 2048], P(None, 'dp', None, 'tensor')
- grad_down: float32 [4, 2048, 768], P(None, 'tensor', 'dp')
- grad_shared_gate_up: float32 [768, 2, 2048], P('dp', None, 'tensor')
- grad_shared_down: float32 [2048, 768], P('tensor', 'dp')
The draws below stay inside these ranges and needn't reach their ends.
Inputs may be any that keep to these rules, and one draw needn't show every extreme that they name: `segment_ids`: in each row segment numbers never fall; each document has 1 to 256 tokens and one has exactly that many. `expert_ids`: each row names 2 different experts. Each row is a permutation of the 1024 pairs' ranks; pair t * 2 + r of the sequence has rank slot_order[t * 2 + r].
All inputs are finite; a program needn't handle non-finite values.
Results may differ from the reference program's by a relative error of at most 0.015.
Values may be sent and summed in bfloat16 or wider, within the bound.
A program may use at most 192 MiB of HBM per device.

```python
import math
import jax
import jax.numpy as jnp
import numpy as np
from jax import lax

D = 768
HEADS = 12
HD = 64
FF = 2048
SF = 2048
EXPERTS = 4
TOP = 2
TOK_DEV = 512
PAIRS = 1024
CAP = 256
TOKENS = 8192
N_DP = 16


def shard_levels(stream_key, dims, pieces, smallest, high):
    def one(dim, parts):
        steps = jax.random.uniform(jax.random.fold_in(jax.random.fold_in(stream_key, 6), dim), (parts,), jnp.float32, smallest / len(pieces), high / len(pieces))
        return jnp.repeat(jnp.exp(steps), dims[dim] // parts).reshape((-1,) + (1,) * (len(dims) - dim - 1))

    level = one(*pieces[0])
    for cut in pieces[1:]:
        level = level * one(*cut)
    return level


def different_ones(key, rows, number_of, top, lift):
    sequence = jax.random.permutation(jax.random.fold_in(key, 1), number_of)
    boost = sequence
    for power in range(3):
        boost = boost * boost // number_of
    boost = boost * lift // number_of
    lots = jax.random.randint(jax.random.fold_in(key, 2), (rows, number_of), 0, 4096) + boost
    fixed_rows = jax.random.permutation(jax.random.fold_in(key, 3), rows)[jnp.arange(number_of) % rows]
    lots = jnp.where(jnp.arange(rows)[:, None] == fixed_rows[None, :], 1 << 14, lots)
    priority = lots * number_of + jnp.arange(number_of)
    return lax.top_k(priority.astype(jnp.int32), top)[1].astype(jnp.int32)


def length_profile(number_of, total, reach, slope):
    loads = [(1 << 20) // math.isqrt(grade ** slope) + 1 for grade in range(2, number_of + 1)]
    spare, given = total - reach - (number_of - 1), [1] * (number_of - 1)
    while spare > 0:
        movable = [i for i in range(number_of - 1) if given[i] < reach]
        whole, remaining = sum([loads[i] for i in movable]), spare
        for i in movable:
            extra = min(reach - given[i], max(1, remaining * loads[i] // whole), spare)
            given[i] = given[i] + extra
            spare = spare - extra
    return np.array([reach] + given)


def uneven_parts(key, amount, total, limit, skew):
    if amount == 2:
        one = jax.random.randint(key, (), max(1, total - limit), min(limit, total - 1) + 1)
        return jnp.stack([one, total - one])
    tallies = jnp.asarray(length_profile(amount, total, limit, skew), jnp.int32)
    pairs = (amount - 1) // 2
    giver, sink = tallies[1:1 + 2 * pairs:2], tallies[2:2 + 2 * pairs:2]
    margin = jnp.minimum(giver - 1, limit - sink)
    shifted = jax.random.randint(jax.random.fold_in(key, 1), (pairs,), 0, 1 << 20) % (margin + 1)
    tallies = tallies.at[1:1 + 2 * pairs:2].set(giver - shifted).at[2:2 + 2 * pairs:2].set(sink + shifted)
    return tallies[jax.random.permutation(jax.random.fold_in(key, 2), amount)]


def bell_draw(rng, dims, width, bound, split=(), kind=jnp.bfloat16):
    drawn = width * jax.random.normal(rng, dims, jnp.float32)
    if split:
        drawn = drawn * shard_levels(rng, dims, split, -0.22, 0.18)
    return jnp.clip(drawn, -bound, bound).astype(kind)


def setup_inputs(seed: int = 0) -> dict:
    keys = jax.random.split(jax.random.key(seed), 15)
    return {
        "tokens": bell_draw(keys[0], (TOKENS, D), 1.0, 6.0, ((0, 16),)),
        "segment_ids": jax.vmap(lambda own: jnp.searchsorted(jnp.cumsum(uneven_parts(own, max(3, TOK_DEV // 64), TOK_DEV, TOK_DEV // 2, 2)), jnp.arange(TOK_DEV), side="right"))(jax.random.split(keys[1], N_DP)).reshape((N_DP, TOK_DEV)).astype(jnp.int32),
        "expert_ids": different_ones(keys[2], TOKENS, EXPERTS, TOP, 4096),
        "slot_order": jax.vmap(lambda own: jax.random.permutation(own, PAIRS))(jax.random.split(keys[3], N_DP)).reshape((N_DP, PAIRS)).astype(jnp.int32),
        "gain_attn": jnp.clip(1.0 + 0.1 * jax.random.normal(keys[4], (D,), jnp.float32), 0.5, 1.5).astype(jnp.bfloat16),
        "qkv_weight": bell_draw(keys[5], (D, 3, HEADS * HD), D ** -0.5, 0.21875, ((0, 16), (2, 2))),
        "out_weight": bell_draw(keys[6], (HEADS * HD, D), (HEADS * HD // 8) ** -0.5, 0.625, ((0, 2), (1, 16))),
        "gain_ffn": jnp.clip(1.0 + 0.1 * jax.random.normal(keys[7], (D,), jnp.float32), 0.5, 1.5).astype(jnp.bfloat16),
        "router_weight": bell_draw(keys[8], (D, EXPERTS), (2 * D) ** -0.5, 0.15625, ((0, 16),)),
        "gate_up": bell_draw(keys[9], (EXPERTS, D, 2, FF), D ** -0.5, 0.21875, ((1, 16), (3, 2))),
        "down_weight": bell_draw(keys[10], (EXPERTS, FF, D), (FF // 4) ** -0.5, 0.25, ((1, 2), (2, 16))),
        "shared_gate_up": bell_draw(keys[11], (D, 2, SF), D ** -0.5, 0.21875, ((0, 16), (2, 2))),
        "shared_down": bell_draw(keys[12], (SF, D), (SF // 2) ** -0.5, 0.1875, ((0, 2), (1, 16))),
        "cotangent": bell_draw(keys[13], (TOKENS, D), 1.0, 6.0, ((0, 16),)),
    }


@jax.custom_vjp
def low(v):
    return lax.optimization_barrier(v.astype(jnp.bfloat16)).astype(jnp.float32)

@jax.custom_vjp
def low_back(v):
    return v

def low_keep(v):
    return (low(v), None)

def low_pass(kept, grad):
    return (grad,)

def back_keep(v):
    return (v, None)

def back_low(kept, grad):
    return (low(grad),)
low.defvjp(low_keep, low_pass)
low_back.defvjp(back_keep, back_low)
epsilon = 1e-06
highest = lax.Precision.HIGHEST

def rms_scale(values):
    return lax.rsqrt(lax.optimization_barrier(jnp.mean(values * values, axis=-1, keepdims=True)) + epsilon)

def rotary(length, head_dim):
    half_dim = head_dim // 2
    position = jnp.arange(length).astype(jnp.float32)[:, None]
    inverse = jnp.exp(jnp.arange(half_dim).astype(jnp.float32) * (-2.0 * math.log(10000.0) / head_dim))
    angles = position * inverse[None, :]
    return (jnp.cos(angles)[:, None, :], jnp.sin(angles)[:, None, :])

def rotate(values, cosine, sine):
    half_dim = values.shape[-1] // 2
    first_half = values[..., :half_dim]
    second_half = values[..., half_dim:]
    return jnp.concatenate([first_half * cosine - second_half * sine, second_half * cosine + first_half * sine], axis=-1)

def route_slots(pair_ids, rank_order, capacity, experts):
    length = pair_ids.shape[0]
    top_count = pair_ids.shape[1]
    pair_expert = pair_ids.reshape(-1)
    pair_count = pair_expert.shape[0]
    ordered = jnp.zeros((pair_count,), jnp.int32).at[rank_order].set(pair_expert)
    onehot = (ordered[:, None] == jnp.arange(experts, dtype=jnp.int32)[None, :]).astype(jnp.int32)
    running = jnp.cumsum(onehot, axis=0)
    ranked_slot = lax.optimization_barrier(jnp.sum(running * onehot, axis=1)) - 1
    position = ranked_slot[rank_order]
    kept_pair = position < capacity
    slot_index = jnp.where(kept_pair, pair_expert * capacity + position, experts * capacity).astype(jnp.int32)
    token_of_pair = (jnp.arange(pair_count, dtype=jnp.int32) // top_count).astype(jnp.int32)
    slot_token = jnp.full((experts * capacity,), length, jnp.int32).at[slot_index].set(token_of_pair, mode='drop')
    return (slot_token, slot_index.reshape(length, top_count), kept_pair.reshape(length, top_count))

def attention(queries, keys_all, values_all, segment, scale):
    length, head_count, head_dim = queries.shape
    block = min(512, length)
    count_blocks = length // block
    positions = jnp.arange(length)

    def one_block(inputs):
        query_block, query_pos, query_seg = inputs
        scores = jnp.einsum('qhd,khd->hqk', query_block, keys_all, precision=highest) * scale
        scores = low_back(scores)
        allowed = (positions[None, :] <= query_pos[:, None]) & (segment[None, :] == query_seg[:, None])
        scores = jnp.where(allowed[None], scores, -1e+30)
        probs = low(jax.nn.softmax(scores, axis=-1))
        return jnp.einsum('hqk,khd->qhd', probs, values_all, precision=highest)
    blocks = (queries.reshape(count_blocks, block, head_count, head_dim), positions.reshape(count_blocks, block), segment.reshape(count_blocks, block))
    mixed_out = lax.map(jax.checkpoint(one_block), blocks)
    return mixed_out.reshape(length, head_count * head_dim)

def forward(xfull, params, segment, pair_ids, routing):
    gain_attn, qkv_weight, out_weight, gain_ffn, router_weight, gate_up, down_weight, shared_gate_up, shared_down = params
    slot_token, slot_index, kept_pair = routing
    length = xfull.shape[0]
    xn_one = low(xfull * rms_scale(xfull) * gain_attn)
    projected = jnp.einsum('td,dch->tch', xn_one, qkv_weight, precision=highest)
    cosine, sine = rotary(length, HD)
    query_proj = low_back(projected[:, 0]).reshape(length, HEADS, HD)
    key_proj = low_back(projected[:, 1]).reshape(length, HEADS, HD)
    value_all = low(low_back(projected[:, 2])).reshape(length, HEADS, HD)
    queries = low(rotate(query_proj, cosine, sine))
    keys_all = low(rotate(key_proj, cosine, sine))
    mixed = low(low_back(attention(queries, keys_all, value_all, segment, HD ** (-0.5))))
    attn = low_back(jnp.dot(mixed, out_weight, precision=highest))
    hidden_state = xfull + attn
    xn_two = low(hidden_state * rms_scale(hidden_state) * gain_ffn)
    logits = low_back(jnp.dot(xn_two, router_weight, precision=highest))
    probs = jax.nn.softmax(logits, axis=-1)
    gates = jnp.take_along_axis(probs, pair_ids, axis=1) * kept_pair.astype(jnp.float32)
    valid = slot_token < length
    dispatched = jnp.where(valid[:, None], xn_two[jnp.minimum(slot_token, length - 1)], 0.0).reshape(EXPERTS, CAP, D)
    both_parts = low_back(jnp.einsum('ecd,edjf->ecjf', dispatched, gate_up, precision=highest))
    expert_hidden = low(jax.nn.silu(both_parts[:, :, 0]) * both_parts[:, :, 1])
    expert_out = low_back(jnp.einsum('ecf,efd->ecd', expert_hidden, down_weight, precision=highest)).reshape(EXPERTS * CAP, D)
    picked = expert_out[jnp.minimum(slot_index, EXPERTS * CAP - 1)]
    moe = lax.optimization_barrier(jnp.sum(gates[:, :, None] * picked, axis=1))
    shared_both = low_back(jnp.einsum('td,djf->tjf', xn_two, shared_gate_up, precision=highest))
    shared_hidden = low(jax.nn.silu(shared_both[:, 0]) * shared_both[:, 1])
    shared_out = jnp.dot(shared_hidden, shared_down, precision=highest)
    return hidden_state + moe + shared_out

def add_pair(first, second):
    return first + second

def reference(tokens, segment_ids, expert_ids, slot_order, gain_attn, qkv_weight, out_weight, gain_ffn, router_weight, gate_up, down_weight, shared_gate_up, shared_down, cotangent):
    params = tuple((weight.astype(jnp.float32) for weight in (gain_attn, qkv_weight, out_weight, gain_ffn, router_weight, gate_up, down_weight, shared_gate_up, shared_down)))
    sequences = (tokens.reshape(N_DP, TOK_DEV, D), segment_ids, expert_ids.reshape(N_DP, TOK_DEV, TOP), slot_order, cotangent.reshape(N_DP, TOK_DEV, D))

    def one_sequence(totals, inputs):
        x_seq, segment, pair_ids, rank_order, cot_seq = inputs
        routing = route_slots(pair_ids, rank_order, CAP, EXPERTS)

        def layer_run(xfull, weights):
            return forward(xfull, weights, segment, pair_ids, routing)
        result, pullback = jax.vjp(layer_run, x_seq.astype(jnp.float32), params)
        dx_seq, dweights = pullback(cot_seq.astype(jnp.float32))
        totals = jax.tree.map(add_pair, totals, dweights)
        return (totals, (result.astype(jnp.bfloat16), dx_seq))
    zero_grads = tuple((jnp.zeros_like(weight) for weight in params))
    totals, (outputs, dx_all) = lax.scan(one_sequence, zero_grads, sequences)
    return (outputs.reshape(TOKENS, D), dx_all.reshape(TOKENS, D), totals[0], totals[1], totals[2], totals[3], totals[4], totals[5], totals[6], totals[7], totals[8])
```

```python
import functools
import math

import jax
import jax.numpy as jnp
from jax import lax
from jax.experimental import pallas as pl
from jax.experimental.pallas import tpu as pltpu
from jax.sharding import PartitionSpec as P

HD = 64
GROUP = 4
MESH = pl.DeviceIdType.MESH


epsilon = 1e-06


def rms_scale(values):
    return lax.rsqrt(jnp.mean(values * values, axis=-1, keepdims=True) + epsilon)


def rotary(length, head_dim):
    half_dim = head_dim // 2
    position = jnp.arange(length).astype(jnp.float32)[:, None]
    inverse = jnp.exp(
        jnp.arange(half_dim).astype(jnp.float32) * (-2.0 * math.log(10000.0) / head_dim)
    )
    angles = position * inverse[None, :]
    return (jnp.cos(angles)[:, None, :], jnp.sin(angles)[:, None, :])


def rotate(values, cosine, sine):
    half_dim = values.shape[-1] // 2
    first_half = values[..., :half_dim]
    second_half = values[..., half_dim:]
    return jnp.concatenate(
        [first_half * cosine - second_half * sine, second_half * cosine + first_half * sine],
        axis=-1,
    )


def route_slots(pair_ids, rank_order, capacity, experts):
    length = pair_ids.shape[0]
    top_count = pair_ids.shape[1]
    pair_expert = pair_ids.reshape(-1)
    pair_count = pair_expert.shape[0]
    ordered = jnp.zeros((pair_count,), jnp.int32).at[rank_order].set(pair_expert)
    onehot = (ordered[:, None] == jnp.arange(experts, dtype=jnp.int32)[None, :]).astype(jnp.int32)
    running = jnp.cumsum(onehot, axis=0)
    ranked_slot = jnp.sum(running * onehot, axis=1) - 1
    position = ranked_slot[rank_order]
    kept_pair = position < capacity
    slot_index = jnp.where(kept_pair, pair_expert * capacity + position, experts * capacity)
    token_of_pair = jnp.arange(pair_count, dtype=jnp.int32) // top_count
    slot_token = (
        jnp.full((experts * capacity,), length, jnp.int32)
        .at[slot_index]
        .set(token_of_pair, mode="drop")
    )
    return (slot_token, slot_index.reshape(length, top_count), kept_pair.reshape(length, top_count))


def silu_back(both_parts, grad_hidden):
    gate_part = both_parts[..., 0, :]
    up_part = both_parts[..., 1, :]
    sigma = jax.nn.sigmoid(gate_part)
    slope = sigma * (1.0 + gate_part * (1.0 - sigma))
    return jnp.stack(
        [grad_hidden * up_part * slope, grad_hidden * gate_part * sigma], axis=-2
    ).astype(jnp.bfloat16)


def silu_forward(both_parts):
    return (jax.nn.silu(both_parts[..., 0, :]) * both_parts[..., 1, :]).astype(jnp.bfloat16)


def norm_back(grad_norm, values, scale_rows, gain):
    grad_gain = jnp.sum(grad_norm * values * scale_rows, axis=0)
    inner = grad_norm * gain
    grad_values = scale_rows * inner - values * scale_rows**3 * jnp.mean(
        inner * values, axis=-1, keepdims=True
    )
    return (grad_values, grad_gain)


def split_blocks(length):
    block = min(512, length)
    return (block, length // block)


def masked_scores(query_block, keys_all, query_pos, query_seg, segment, scale):
    positions = jnp.arange(keys_all.shape[0])
    scores = (
        jnp.einsum("qhd,khd->hqk", query_block, keys_all, preferred_element_type=jnp.float32)
        * scale
    )
    allowed = (positions[None, :] <= query_pos[:, None]) & (segment[None, :] == query_seg[:, None])
    return jnp.where(allowed[None], scores, -1e30)


def attend_forward(queries, keys_all, values_all, segment, scale):
    length, head_count, head_dim = queries.shape
    block, count_blocks = split_blocks(length)
    positions = jnp.arange(length)

    def one_block(inputs):
        query_block, query_pos, query_seg = inputs
        scores = masked_scores(query_block, keys_all, query_pos, query_seg, segment, scale)
        largest = jnp.max(scores, axis=-1, keepdims=True)
        expo = jnp.exp(scores - largest)
        total = jnp.sum(expo, axis=-1, keepdims=True)
        probs = (expo / total).astype(jnp.bfloat16)
        mixed = jnp.einsum("hqk,khd->qhd", probs, values_all, preferred_element_type=jnp.float32)
        return (mixed.astype(jnp.bfloat16), (largest + jnp.log(total))[..., 0])

    blocks = (
        queries.reshape(count_blocks, block, head_count, head_dim),
        positions.reshape(count_blocks, block),
        segment.reshape(count_blocks, block),
    )
    mixed_all, log_totals = lax.map(one_block, blocks)
    return (mixed_all.reshape(length, head_count * head_dim), log_totals)


def attend_backward(queries, keys_all, values_all, segment, scale, grad_mixed, log_totals):
    length, head_count, head_dim = queries.shape
    block, count_blocks = split_blocks(length)
    positions = jnp.arange(length)

    def one_block(carry, inputs):
        grad_keys, grad_values = carry
        query_block, query_pos, query_seg, grad_block, log_block = inputs
        scores = masked_scores(query_block, keys_all, query_pos, query_seg, segment, scale)
        probs = jnp.exp(scores - log_block[:, :, None])
        grad_probs = jnp.einsum(
            "qhd,khd->hqk", grad_block, values_all, preferred_element_type=jnp.float32
        )
        inner = jnp.sum(probs * grad_probs, axis=-1, keepdims=True)
        grad_scores = (probs * (grad_probs - inner)).astype(jnp.bfloat16)
        grad_query = (
            jnp.einsum("hqk,khd->qhd", grad_scores, keys_all, preferred_element_type=jnp.float32)
            * scale
        )
        grad_keys = (
            grad_keys
            + jnp.einsum(
                "hqk,qhd->khd", grad_scores, query_block, preferred_element_type=jnp.float32
            )
            * scale
        )
        grad_values = grad_values + jnp.einsum(
            "hqk,qhd->khd",
            probs.astype(jnp.bfloat16),
            grad_block,
            preferred_element_type=jnp.float32,
        )
        return ((grad_keys, grad_values), grad_query)

    zeros_kv = jnp.zeros((length, head_count, head_dim), jnp.float32)
    blocks = (
        queries.reshape(count_blocks, block, head_count, head_dim),
        positions.reshape(count_blocks, block),
        segment.reshape(count_blocks, block),
        grad_mixed.reshape(count_blocks, block, head_count, head_dim),
        log_totals,
    )
    (grad_keys, grad_values), grad_queries = lax.scan(one_block, (zeros_kv, zeros_kv), blocks)
    return (grad_queries.reshape(length, head_count, head_dim), grad_keys, grad_values)


def sum_rows(grad, axis, scatter_dimension, tiled):
    part = lax.psum_scatter(
        grad.astype(jnp.bfloat16), axis, scatter_dimension=scatter_dimension, tiled=tiled
    )
    return part.astype(jnp.float32)


def local_plain(
    tokens,
    segment_ids,
    expert_ids,
    slot_order,
    gain_attn,
    qkv_weight,
    out_weight,
    gain_ffn,
    router_weight,
    gate_up,
    down_weight,
    shared_gate_up,
    shared_down,
    cotangent,
):
    g_one, w_qkv, w_out, g_two, w_router, w_gate_up, w_down, s_gate_up, s_down = (
        lax.all_gather(gain_attn, "dp", axis=0, tiled=True),
        lax.all_gather(qkv_weight, "dp", axis=0, tiled=True),
        lax.all_gather(out_weight, "dp", axis=1, tiled=True),
        lax.all_gather(gain_ffn, "dp", axis=0, tiled=True),
        lax.all_gather(router_weight, "dp", axis=0, tiled=True),
        lax.all_gather(gate_up, "dp", axis=1, tiled=True),
        lax.all_gather(down_weight, "dp", axis=2, tiled=True),
        lax.all_gather(shared_gate_up, "dp", axis=0, tiled=True),
        lax.all_gather(shared_down, "dp", axis=1, tiled=True),
    )
    length = tokens.shape[0]
    width = tokens.shape[1]
    experts_count = w_router.shape[1]
    top_count = expert_ids.shape[1]
    capacity = length * top_count // experts_count
    head_dim = HD
    local_heads = w_qkv.shape[2] // head_dim
    scale = head_dim ** (-0.5)
    segment = segment_ids[0]
    slot_token, slot_index, kept_pair = route_slots(
        expert_ids, slot_order[0], capacity, experts_count
    )
    kept_float = kept_pair.astype(jnp.float32)
    slot_valid = slot_token < length
    slot_rows = jnp.minimum(slot_token, length - 1)
    pair_slots = jnp.minimum(slot_index, experts_count * capacity - 1)
    xfull = tokens.astype(jnp.float32)
    rms_one = rms_scale(xfull)
    xn_one = (xfull * rms_one * g_one.astype(jnp.float32)).astype(jnp.bfloat16)
    projected = jnp.einsum("td,dch->tch", xn_one, w_qkv, preferred_element_type=jnp.float32)
    cosine, sine = rotary(length, head_dim)
    queries = rotate(projected[:, 0].reshape(length, local_heads, head_dim), cosine, sine).astype(
        jnp.bfloat16
    )
    keys_all = rotate(projected[:, 1].reshape(length, local_heads, head_dim), cosine, sine).astype(
        jnp.bfloat16
    )
    values_all = projected[:, 2].reshape(length, local_heads, head_dim).astype(jnp.bfloat16)
    mixed, log_totals = attend_forward(queries, keys_all, values_all, segment, scale)
    attn_share = lax.psum_scatter(
        jnp.dot(mixed, w_out, preferred_element_type=jnp.float32),
        "tensor",
        scatter_dimension=1,
        tiled=True,
    )
    attn = lax.all_gather(attn_share, "tensor", axis=1, tiled=True)
    hidden_state = xfull + attn
    rms_two = rms_scale(hidden_state)
    xn_two = (hidden_state * rms_two * g_two.astype(jnp.float32)).astype(jnp.bfloat16)
    logits = jnp.dot(xn_two, w_router, preferred_element_type=jnp.float32)
    probs = jax.nn.softmax(logits, axis=-1)
    gates = jnp.take_along_axis(probs, expert_ids, axis=1) * kept_float
    dispatched = (xn_two[slot_rows] * slot_valid[:, None].astype(jnp.bfloat16)).reshape(
        experts_count, capacity, width
    )
    both_parts = jnp.einsum(
        "ecd,edjf->ecjf", dispatched, w_gate_up, preferred_element_type=jnp.float32
    )
    expert_hidden = silu_forward(both_parts)
    expert_out = jnp.einsum(
        "ecf,efd->ecd", expert_hidden, w_down, preferred_element_type=jnp.float32
    ).reshape(experts_count * capacity, width)
    picked = expert_out[pair_slots]
    moe = jnp.sum(gates[:, :, None] * picked, axis=1)
    shared_both = jnp.einsum("td,djf->tjf", xn_two, s_gate_up, preferred_element_type=jnp.float32)
    shared_hidden = silu_forward(shared_both)
    shared_out = jnp.dot(shared_hidden, s_down, preferred_element_type=jnp.float32)
    ffn_share = lax.psum_scatter(
        (moe + shared_out).astype(jnp.bfloat16), "tensor", scatter_dimension=1, tiled=True
    ).astype(jnp.float32)
    ffn = lax.all_gather(ffn_share.astype(jnp.bfloat16), "tensor", axis=1, tiled=True).astype(
        ffn_share.dtype
    )
    output = (hidden_state + ffn).astype(jnp.bfloat16)
    grad_y = cotangent.astype(jnp.float32)
    grad_shared_hidden = jnp.einsum(
        "td,fd->tf", cotangent, s_down, preferred_element_type=jnp.float32
    )
    grad_s_down = jnp.einsum(
        "tf,td->fd", shared_hidden, cotangent, preferred_element_type=jnp.float32
    )
    grad_shared_both = silu_back(shared_both, grad_shared_hidden)
    grad_s_gate_up = jnp.einsum(
        "td,tjf->djf", xn_two, grad_shared_both, preferred_element_type=jnp.float32
    )
    grad_xn_shared = jnp.einsum(
        "tjf,djf->td", grad_shared_both, s_gate_up, preferred_element_type=jnp.float32
    )
    slot_gate = (
        jnp.zeros((experts_count * capacity,), jnp.float32)
        .at[slot_index.reshape(-1)]
        .set(gates.reshape(-1), mode="drop")
    )
    grad_expert_out = (
        (slot_gate[:, None] * grad_y[slot_rows])
        .astype(jnp.bfloat16)
        .reshape(experts_count, capacity, width)
    )
    grad_gates_part = kept_float * jnp.sum(grad_y[:, None, :] * picked, axis=-1)
    grad_expert_hidden = jnp.einsum(
        "ecd,efd->ecf", grad_expert_out, w_down, preferred_element_type=jnp.float32
    )
    grad_w_down = jnp.einsum(
        "ecf,ecd->efd", expert_hidden, grad_expert_out, preferred_element_type=jnp.float32
    )
    grad_both = silu_back(both_parts, grad_expert_hidden)
    grad_w_gate_up = jnp.einsum(
        "ecd,ecjf->edjf", dispatched, grad_both, preferred_element_type=jnp.float32
    )
    grad_dispatched = jnp.einsum(
        "ecjf,edjf->ecd", grad_both, w_gate_up, preferred_element_type=jnp.float32
    ).reshape(experts_count * capacity, width)
    grad_xn_moe = jnp.sum(kept_float[:, :, None] * grad_dispatched[pair_slots], axis=1)
    grad_xn_part, grad_gates_share = (
        lax.psum_scatter(grad_xn_shared + grad_xn_moe, "tensor", scatter_dimension=1, tiled=True),
        lax.psum_scatter(grad_gates_part, "tensor", scatter_dimension=1, tiled=True),
    )
    grad_xn_sum, grad_gates = (
        lax.all_gather(grad_xn_part, "tensor", axis=1, tiled=True),
        lax.all_gather(grad_gates_share, "tensor", axis=1, tiled=True),
    )
    expert_match = (
        expert_ids[:, :, None] == jnp.arange(experts_count, dtype=jnp.int32)[None, None, :]
    ).astype(jnp.float32)
    grad_probs = jnp.sum(expert_match * grad_gates[:, :, None], axis=1)
    grad_logits = (
        probs * (grad_probs - jnp.sum(probs * grad_probs, axis=-1, keepdims=True))
    ).astype(jnp.bfloat16)
    grad_w_router = jnp.einsum("td,te->de", xn_two, grad_logits, preferred_element_type=jnp.float32)
    grad_xn_two = grad_xn_sum + jnp.einsum(
        "te,de->td", grad_logits, w_router, preferred_element_type=jnp.float32
    )
    grad_norm_two, grad_g_two = norm_back(
        grad_xn_two, hidden_state, rms_two, g_two.astype(jnp.float32)
    )
    grad_hidden = grad_y + grad_norm_two
    grad_attn = grad_hidden.astype(jnp.bfloat16)
    grad_w_out = jnp.einsum("th,td->hd", mixed, grad_attn, preferred_element_type=jnp.float32)
    grad_mixed = jnp.einsum(
        "td,hd->th", grad_attn, w_out, preferred_element_type=jnp.float32
    ).astype(jnp.bfloat16)
    grad_queries, grad_keys, grad_values = attend_backward(
        queries, keys_all, values_all, segment, scale, grad_mixed, log_totals
    )
    grad_projected = (
        jnp.stack(
            [rotate(grad_queries, cosine, -sine), rotate(grad_keys, cosine, -sine), grad_values],
            axis=1,
        )
        .astype(jnp.bfloat16)
        .reshape(length, 3, local_heads * head_dim)
    )
    grad_w_qkv = jnp.einsum(
        "td,tch->dch", xn_one, grad_projected, preferred_element_type=jnp.float32
    )
    grad_xn_share = lax.psum_scatter(
        jnp.einsum("tch,dch->td", grad_projected, w_qkv, preferred_element_type=jnp.float32).astype(
            jnp.bfloat16
        ),
        "tensor",
        scatter_dimension=1,
        tiled=True,
    ).astype(jnp.float32)
    grad_xn_one = lax.all_gather(
        grad_xn_share.astype(jnp.bfloat16), "tensor", axis=1, tiled=True
    ).astype(grad_xn_share.dtype)
    grad_norm_one, grad_g_one = norm_back(grad_xn_one, xfull, rms_one, g_one.astype(jnp.float32))
    grad_tokens = grad_hidden + grad_norm_one
    (
        grad_g_one,
        grad_w_qkv,
        grad_w_out,
        grad_g_two,
        grad_w_router,
        grad_w_gate_up,
        grad_w_down,
        grad_s_gate_up,
        grad_s_down,
    ) = (
        lax.psum_scatter(grad_g_one, "dp", scatter_dimension=0, tiled=True),
        sum_rows(grad_w_qkv, "dp", scatter_dimension=0, tiled=True),
        sum_rows(grad_w_out, "dp", scatter_dimension=1, tiled=True),
        lax.psum_scatter(grad_g_two, "dp", scatter_dimension=0, tiled=True),
        lax.psum_scatter(grad_w_router, "dp", scatter_dimension=0, tiled=True),
        sum_rows(grad_w_gate_up, "dp", scatter_dimension=1, tiled=True),
        sum_rows(grad_w_down, "dp", scatter_dimension=2, tiled=True),
        sum_rows(grad_s_gate_up, "dp", scatter_dimension=0, tiled=True),
        sum_rows(grad_s_down, "dp", scatter_dimension=1, tiled=True),
    )
    return (
        output,
        grad_tokens,
        grad_g_one,
        grad_w_qkv,
        grad_w_out,
        grad_g_two,
        grad_w_router,
        grad_w_gate_up,
        grad_w_down,
        grad_s_gate_up,
        grad_s_down,
    )


class Place:
    def __init__(self, planes):
        d = lax.axis_index("dp")
        self.planes = planes
        self.d, self.c = d, lax.axis_index("tensor")
        self.z, self.p = d // GROUP, lax.rem(d, GROUP)
        bit0, bit1 = lax.rem(self.p, 2), self.p // 2
        flip0, flip1 = 1 - bit0, 1 - bit1
        self.member = [
            self.p,
            flip0 + 2 * bit1,
            bit0 + 2 * flip1,
            flip0 + 2 * flip1,
        ]

    def near(self, j):
        return (self.z * GROUP + self.member[j], self.c)

    def up(self):
        return (self.d + GROUP, self.c)

    def down(self):
        return (self.d - GROUP, self.c)

    def when(self, condition, action):
        pl.when(condition)(action)

    def has_up(self, k=1):
        return self.z + k < self.planes

    def has_down(self, k=1):
        return self.z - k >= 0

    def greet(self):
        barrier = pltpu.get_barrier_semaphore()

        def hello(device):
            pl.semaphore_signal(barrier, inc=1, device_id=device, device_id_type=MESH)

        for j in range(1, GROUP):
            hello(self.near(j))
        self.when(self.has_up(), lambda: hello(self.up()))
        self.when(self.has_down(), lambda: hello(self.down()))
        line = self.has_up().astype(jnp.int32) + self.has_down().astype(jnp.int32)
        pl.semaphore_wait(barrier, GROUP - 1 + line)


def send(source, target, send_sem, recv_sem, device):
    return pltpu.make_async_remote_copy(
        src_ref=source,
        dst_ref=target,
        send_sem=send_sem,
        recv_sem=recv_sem,
        device_id=device,
        device_id_type=MESH,
    )


def gather_kernel(planes, s_ref, e_ref, s_all, e_all, local_sem, s_recv, e_recv, s_send, e_send):
    at = Place(planes)
    own = at.d

    def s_copy(block, source, way, device):
        return send(source, s_all.at[block], s_send.at[way, block], s_recv.at[block], device)

    def e_copy(block, source, way, device):
        return send(source, e_all.at[block], e_send.at[way, block], e_recv.at[block], device)

    def s_landed(block):
        s_copy(block, s_ref, 0, at.near(1)).wait_recv()

    def e_landed(block):
        e_copy(block, e_ref.at[0], 0, at.near(1)).wait_recv()

    at.greet()
    keep_s = pltpu.make_async_copy(s_ref, s_all.at[own], local_sem.at[0])
    keep_e = pltpu.make_async_copy(e_ref.at[at.p], e_all.at[own], local_sem.at[1])
    keep_s.start()
    keep_e.start()
    for j in range(1, GROUP):
        send(
            e_ref.at[at.member[j]],
            e_all.at[own],
            e_send.at[1 + j, own],
            e_recv.at[own],
            at.near(j),
        ).start()
    at.when(at.has_up(), lambda: s_copy(own, s_ref, 0, at.up()).start())
    at.when(at.has_down(), lambda: s_copy(own, s_ref, 1, at.down()).start())
    s_copy(own, s_ref, 2, at.near(1)).start()
    s_copy(own, s_ref, 3, at.near(2)).start()
    at.when(at.has_up(), lambda: e_copy(own, e_ref.at[at.p], 0, at.up()).start())
    at.when(at.has_down(), lambda: e_copy(own, e_ref.at[at.p], 1, at.down()).start())

    for j in range(1, GROUP):
        block = at.z * GROUP + at.member[j]
        e_landed(block)
        at.when(at.has_up(), lambda: e_copy(block, e_all.at[block], 0, at.up()).start())
        at.when(at.has_down(), lambda: e_copy(block, e_all.at[block], 1, at.down()).start())

    def cross(plane):
        first = plane * GROUP + at.member[1]
        second = plane * GROUP + at.member[2]
        even = lax.rem(plane, 2) == 0
        s_landed(first)
        at.when(even, lambda: s_copy(first, s_all.at[first], 3, at.near(2)).start())
        s_landed(second)
        at.when(
            jnp.logical_not(even),
            lambda: s_copy(second, s_all.at[second], 2, at.near(1)).start(),
        )

    def spread(plane, onward, device_of):
        block = plane * GROUP + at.p
        s_landed(block)
        at.when(onward[0], lambda: s_copy(block, s_all.at[block], onward[1], device_of()).start())
        s_copy(block, s_all.at[block], 2, at.near(1)).start()
        s_copy(block, s_all.at[block], 3, at.near(2)).start()

    def pass_on(plane, onward, device_of):
        for j in range(GROUP):
            block = plane * GROUP + at.member[j]
            e_landed(block)
            at.when(
                onward[0], lambda: e_copy(block, e_all.at[block], onward[1], device_of()).start()
            )

    cross(at.z)
    for k in range(1, planes):
        below, above = at.z - k, at.z + k
        at.when(at.has_down(k), lambda: spread(below, (at.has_up(), 0), at.up))
        at.when(at.has_up(k), lambda: spread(above, (at.has_down(), 1), at.down))
        at.when(at.has_down(k), lambda: pass_on(below, (at.has_up(), 0), at.up))
        at.when(at.has_up(k), lambda: pass_on(above, (at.has_down(), 1), at.down))
        at.when(at.has_down(k), lambda: cross(below))
        at.when(at.has_up(k), lambda: cross(above))

    keep_s.wait()
    keep_e.wait()
    for j in range(1, GROUP):
        send(
            e_ref.at[at.member[j]],
            e_all.at[own],
            e_send.at[1 + j, own],
            e_recv.at[own],
            at.near(j),
        ).wait_send()
    for plane in range(planes):
        s_landed(plane * GROUP + at.member[3])
        block = plane * GROUP + at.p
        s_copy(block, s_ref, 2, at.near(1)).wait_send()
        s_copy(block, s_ref, 3, at.near(2)).wait_send()
        if plane % 2 == 0:
            s_copy(plane * GROUP + at.member[1], s_ref, 3, at.near(2)).wait_send()
        else:
            s_copy(plane * GROUP + at.member[2], s_ref, 2, at.near(1)).wait_send()

        def sent(way, device_of):
            s_copy(block, s_ref, way, device_of()).wait_send()
            for q in range(GROUP):
                e_copy(plane * GROUP + q, e_ref.at[0], way, device_of()).wait_send()

        at.when((at.z >= plane) & at.has_up(), lambda: sent(0, at.up))
        at.when((at.z <= plane) & at.has_down(), lambda: sent(1, at.down))


def gather_weights(planes, shared, expert):
    n = planes * GROUP
    anywhere = pl.BlockSpec(memory_space=pl.ANY)
    return pl.pallas_call(
        functools.partial(gather_kernel, planes),
        out_shape=(
            jax.ShapeDtypeStruct((n,) + shared.shape, shared.dtype),
            jax.ShapeDtypeStruct((n,) + expert.shape[1:], expert.dtype),
        ),
        in_specs=[anywhere, anywhere],
        out_specs=(anywhere, anywhere),
        scratch_shapes=[
            pltpu.SemaphoreType.DMA((2,)),
            pltpu.SemaphoreType.DMA((n,)),
            pltpu.SemaphoreType.DMA((n,)),
            pltpu.SemaphoreType.DMA((4, n)),
            pltpu.SemaphoreType.DMA((1 + GROUP, n)),
        ],
        compiler_params=pltpu.CompilerParams(collective_id=0, has_side_effects=True),
    )(shared, expert)


def reduce_kernel(
    planes,
    s_ref,
    e_ref,
    s_out,
    e_out,
    s_one,
    s_two,
    s_below,
    s_above,
    e_below,
    e_above,
    e_last,
    one_send,
    one_recv,
    two_send,
    two_recv,
    s_send,
    s_recv,
    e_send,
    e_recv,
    last_send,
    last_recv,
):
    at = Place(planes)
    f32 = jnp.float32

    def one_copy(plane, i, even):
        j = 1 if even else 2
        target = at.member[3] if i else at.member[j]
        return send(
            s_ref.at[plane * GROUP + target],
            s_one.at[plane, i],
            one_send.at[plane, i],
            one_recv.at[plane, i],
            at.near(j),
        )

    def two_copy(plane, even):
        j = 2 if even else 1
        return send(
            s_one.at[plane, 1],
            s_two.at[plane],
            two_send.at[plane],
            two_recv.at[plane],
            at.near(j),
        )

    def by_parity(plane, action):
        even = lax.rem(plane, 2) == 0
        at.when(even, lambda: action(True))
        at.when(jnp.logical_not(even), lambda: action(False))

    def s_line(source, plane, way):
        target, device = (s_below, at.up()) if way == 0 else (s_above, at.down())
        return send(source, target.at[plane], s_send.at[way, plane], s_recv.at[way, plane], device)

    def e_line(source, block, way):
        target, device = (e_below, at.up()) if way == 0 else (e_above, at.down())
        return send(source, target.at[block], e_send.at[way, block], e_recv.at[way, block], device)

    def last_copy(j):
        return send(
            e_ref.at[0],
            e_last.at[j],
            last_send.at[j],
            last_recv.at[j],
            at.near(j),
        )

    at.greet()

    def e_step(plane, way):
        behind = at.has_down() if way == 0 else at.has_up()
        held = e_below if way == 0 else e_above
        for j in range(GROUP):
            block = plane * GROUP + at.member[j]

            def add():
                e_line(e_ref.at[block], block, way).wait_recv()
                held[block] = (held[block].astype(f32) + e_ref[block].astype(f32)).astype(
                    held.dtype
                )
                e_line(held.at[block], block, way).start()

            at.when(behind, add)
            at.when(jnp.logical_not(behind), lambda: e_line(e_ref.at[block], block, way).start())

    def plane_sum(plane):
        def stage(even):
            mine = plane * GROUP + at.p
            other = plane * GROUP + (at.member[2] if even else at.member[1])
            one_copy(plane, 1, even).wait_recv()
            s_one[plane, 1] = (s_one[plane, 1].astype(f32) + s_ref[other].astype(f32)).astype(
                s_one.dtype
            )
            two_copy(plane, even).start()
            one_copy(plane, 0, even).wait_recv()
            two_copy(plane, even).wait_recv()
            s_two[plane] = (
                s_two[plane].astype(f32) + s_one[plane, 0].astype(f32) + s_ref[mine].astype(f32)
            ).astype(s_two.dtype)

        by_parity(plane, stage)

    def s_step(plane, way):
        plane_sum(plane)
        behind = at.has_down() if way == 0 else at.has_up()
        held = s_below if way == 0 else s_above

        def add():
            s_line(s_two.at[plane], plane, way).wait_recv()
            held[plane] = (held[plane].astype(f32) + s_two[plane].astype(f32)).astype(held.dtype)
            s_line(held.at[plane], plane, way).start()

        at.when(behind, add)
        at.when(jnp.logical_not(behind), lambda: s_line(s_two.at[plane], plane, way).start())

    def both_ways(action, k):
        at.when(at.has_up(k), lambda: action(at.z + k, 0))
        at.when(at.has_down(k), lambda: action(at.z - k, 1))

    def start_one(plane, way):
        def go(even):
            one_copy(plane, 1, even).start()
            one_copy(plane, 0, even).start()

        by_parity(plane, go)

    for k in range(planes - 1, 0, -1):
        both_ways(start_one, k)
    start_one(at.z, 0)
    for k in range(planes - 1, 0, -1):
        both_ways(e_step, k)
        both_ways(s_step, k)

    for j in range(GROUP):
        block = at.z * GROUP + at.member[j]
        at.when(at.has_down(), lambda: e_line(e_ref.at[block], block, 0).wait_recv())
        at.when(at.has_up(), lambda: e_line(e_ref.at[block], block, 1).wait_recv())
        low = jnp.where(at.has_down(), e_below[block].astype(f32), 0.0)
        high = jnp.where(at.has_up(), e_above[block].astype(f32), 0.0)
        total = e_ref[block].astype(f32) + low + high
        if j == 0:
            e_out[at.p] = total
        else:
            e_below[block] = total.astype(e_below.dtype)
            send(
                e_below.at[block],
                e_last.at[j],
                last_send.at[j],
                last_recv.at[j],
                at.near(j),
            ).start()
    plane_sum(at.z)
    at.when(at.has_down(), lambda: s_line(s_two.at[at.z], at.z, 0).wait_recv())
    at.when(at.has_up(), lambda: s_line(s_two.at[at.z], at.z, 1).wait_recv())
    low = jnp.where(at.has_down(), s_below[at.z].astype(f32), 0.0)
    high = jnp.where(at.has_up(), s_above[at.z].astype(f32), 0.0)
    s_out[...] = s_two[at.z].astype(f32) + low + high
    for j in range(1, GROUP):
        last_copy(j).wait_recv()
        e_out[at.member[j]] = e_last[j].astype(f32)

    for j in range(1, GROUP):
        last_copy(j).wait_send()
    for plane in range(planes):
        even = plane % 2 == 0
        one_copy(plane, 0, even).wait_send()
        one_copy(plane, 1, even).wait_send()
        two_copy(plane, even).wait_send()

        def sent(way):
            s_line(s_two.at[plane], plane, way).wait_send()
            for q in range(GROUP):
                block = plane * GROUP + q
                e_line(e_ref.at[block], block, way).wait_send()

        at.when(at.z < plane, lambda: sent(0))
        at.when(at.z > plane, lambda: sent(1))


def reduce_grads(planes, shared, expert):
    n, rows, s_width = shared.shape
    e_width = expert.shape[2]
    vmem = pl.BlockSpec(memory_space=pltpu.VMEM)
    bf16, dma = jnp.bfloat16, pltpu.SemaphoreType.DMA
    return pl.pallas_call(
        functools.partial(reduce_kernel, planes),
        out_shape=(
            jax.ShapeDtypeStruct((rows, s_width), jnp.float32),
            jax.ShapeDtypeStruct((GROUP, rows, e_width), jnp.float32),
        ),
        in_specs=[vmem, vmem],
        out_specs=(vmem, vmem),
        scratch_shapes=[
            pltpu.VMEM((planes, 2, rows, s_width), bf16),
            pltpu.VMEM((planes, rows, s_width), bf16),
            pltpu.VMEM((planes, rows, s_width), bf16),
            pltpu.VMEM((planes, rows, s_width), bf16),
            pltpu.VMEM((n, rows, e_width), bf16),
            pltpu.VMEM((n, rows, e_width), bf16),
            pltpu.VMEM((GROUP, rows, e_width), bf16),
            dma((planes, 2)),
            dma((planes, 2)),
            dma((planes,)),
            dma((planes,)),
            dma((2, planes)),
            dma((2, planes)),
            dma((2, n)),
            dma((2, n)),
            dma((GROUP,)),
            dma((GROUP,)),
        ],
        compiler_params=pltpu.CompilerParams(
            collective_id=1, has_side_effects=True, vmem_limit_bytes=60 << 20
        ),
    )(shared, expert)


def other_core(values):
    return lax.ppermute(values, "tensor", [(0, 1), (1, 0)])


def add_cores(values):
    return values + other_core(values)


def to_members(planes, blocks):
    out = [blocks[0]]
    for j in range(1, GROUP):
        order = [(d, (d // GROUP) * GROUP + ((d % GROUP) ^ j)) for d in range(planes * GROUP)]
        out.append(lax.ppermute(blocks[j], "dp", order))
    return jnp.stack(out)


def local_grouped(
    planes,
    tokens,
    segment_ids,
    expert_ids,
    slot_order,
    gain_attn,
    qkv_weight,
    out_weight,
    gain_ffn,
    router_weight,
    gate_up,
    down_weight,
    shared_gate_up,
    shared_down,
    cotangent,
):
    bf16, f32 = jnp.bfloat16, jnp.float32
    rows, heads_width = qkv_weight.shape[0], qkv_weight.shape[2]
    experts, hidden = down_weight.shape[0], down_weight.shape[1]
    s_hidden = shared_down.shape[0]
    length, width = tokens.shape
    top = expert_ids.shape[1]
    capacity = length * top // experts
    heads = heads_width // HD
    scale = HD ** (-0.5)
    n = planes * GROUP
    cuts = [2 * s_hidden, s_hidden, 3 * heads_width, heads_width, 128]
    edges = [sum(cuts[:i]) for i in range(len(cuts) + 1)]

    def part(array, i):
        return array[..., edges[i] : edges[i + 1]]

    small = jnp.concatenate([gain_attn[:, None], gain_ffn[:, None], router_weight], axis=1)
    small = jnp.pad(small, ((0, 0), (0, 128 - small.shape[1])))
    packed = jnp.concatenate(
        [
            shared_gate_up.reshape(rows, 2 * s_hidden),
            shared_down.T,
            qkv_weight.reshape(rows, 3 * heads_width),
            out_weight.T,
            small,
        ],
        axis=1,
    )
    expert_packed = jnp.concatenate(
        [gate_up.reshape(experts, rows, 2 * hidden), down_weight.transpose(0, 2, 1)], axis=2
    )
    all_packed, all_expert = gather_weights(planes, packed, expert_packed)
    all_packed = all_packed.reshape(width, -1)
    all_expert = all_expert.reshape(width, -1)
    s_gate_up, s_down_t, w_qkv, w_out_t = (part(all_packed, i) for i in range(4))
    small_all = part(all_packed, 4)
    g_one, g_two = small_all[:, 0].astype(f32), small_all[:, 1].astype(f32)
    w_router = small_all[:, 2 : 2 + experts]
    w_gate_up, w_down_t = all_expert[:, : 2 * hidden], all_expert[:, 2 * hidden :]

    def mm(spec, a, b):
        return jnp.einsum(spec, a, b, preferred_element_type=f32)

    member = lax.rem(lax.axis_index("dp"), GROUP)
    pair_expert = expert_ids.reshape(-1)
    order = slot_order[0]
    ahead = (pair_expert[None, :] == pair_expert[:, None]) & (order[None, :] < order[:, None])
    position = jnp.sum(ahead.astype(jnp.int32), axis=1)
    kept = (position < capacity).reshape(length, top)
    slot = jnp.where(
        kept, (jnp.bitwise_xor(pair_expert, member) * capacity + position).reshape(length, top), -1
    )
    kept_float = kept.astype(f32)
    slots = jnp.arange(experts * capacity, dtype=jnp.int32)
    pick = [(slot[:, r : r + 1] == slots[None, :]).astype(bf16) for r in range(top)]
    pick_any = sum(pick[1:], pick[0])

    segment = segment_ids[0]
    xfull = tokens.astype(f32)
    rms_one = rms_scale(xfull)
    xn_one = (xfull * rms_one * g_one).astype(bf16)
    projected = mm("td,dc->tc", xn_one, w_qkv).reshape(length, 3, heads, HD)
    cosine, sine = rotary(length, HD)
    queries = rotate(projected[:, 0], cosine, sine).astype(bf16)
    keys_all = rotate(projected[:, 1], cosine, sine).astype(bf16)
    values_all = projected[:, 2].astype(bf16)
    mixed, log_totals = attend_forward(queries, keys_all, values_all, segment, scale)
    hidden_state = xfull + add_cores(mm("th,dh->td", mixed, w_out_t))
    rms_two = rms_scale(hidden_state)
    xn_two = (hidden_state * rms_two * g_two).astype(bf16)
    logits = jnp.dot(xn_two, w_router, preferred_element_type=f32)
    probs = jax.nn.softmax(logits, axis=-1)
    match = (expert_ids[:, :, None] == jnp.arange(experts, dtype=jnp.int32)).astype(f32)
    gates = jnp.sum(match * probs[:, None, :], axis=2) * kept_float

    slot_gate = sum(
        jnp.sum(jnp.where(slot[:, r : r + 1] == slots[None, :], gates[:, r : r + 1], 0.0), axis=0)
        for r in range(top)
    )
    both = jnp.concatenate([xn_two, cotangent], axis=1)
    placed = mm("ts,td->sd", pick_any, both)
    placed = jnp.concatenate(
        [placed[:, :width], placed[:, width:] * slot_gate[:, None]], axis=1
    ).astype(bf16)
    arrived = to_members(planes, placed.reshape(experts, capacity, 2 * width))
    arrived = arrived.reshape(experts * capacity, 2 * width)
    xin, dye = arrived[:, :width], arrived[:, width:]

    shared_both = mm("td,df->tf", xn_two, s_gate_up).reshape(length, 2, s_hidden)
    shared_hidden = silu_forward(shared_both)
    shared_out = mm("tf,df->td", shared_hidden, s_down_t)
    grad_shared_hidden = mm("td,df->tf", cotangent, s_down_t)
    grad_s_down_t = mm("td,tf->df", cotangent, shared_hidden)
    grad_shared_both = silu_back(shared_both, grad_shared_hidden).reshape(length, -1)
    grad_s_gate_up = mm("td,tf->df", xn_two, grad_shared_both)
    grad_xn_shared = mm("tf,df->td", grad_shared_both, s_gate_up)

    both_parts = mm("sd,df->sf", xin, w_gate_up).reshape(-1, 2, hidden)
    expert_hidden = silu_forward(both_parts)
    expert_out = mm("sf,df->sd", expert_hidden, w_down_t).astype(bf16)
    grad_hidden_expert = mm("sd,df->sf", dye, w_down_t)
    grad_both = silu_back(both_parts, grad_hidden_expert).reshape(-1, 2 * hidden)
    grad_in = mm("sf,df->sd", grad_both, w_gate_up).astype(bf16)
    grad_down_t = mm("sd,sf->df", dye, expert_hidden)
    grad_gate_up = mm("sd,sf->df", xin, grad_both)
    back = jnp.concatenate([expert_out, grad_in], axis=1).reshape(experts, capacity, 2 * width)
    back = to_members(planes, back).reshape(experts * capacity, 2 * width)
    picked = [mm("ts,sd->td", pick[r], back[:, :width]) for r in range(top)]
    moe = sum(gates[:, r : r + 1] * picked[r] for r in range(top))
    grad_xn_moe = mm("ts,sd->td", pick_any, back[:, width:])
    grad_y = cotangent.astype(f32)
    grad_gates_part = kept_float * jnp.stack(
        [jnp.sum(grad_y * picked[r], axis=-1) for r in range(top)], axis=1
    )
    ffn_part = (moe + shared_out).astype(bf16)
    output = (
        hidden_state + (ffn_part.astype(f32) + other_core(ffn_part).astype(f32))
    ).astype(bf16)
    grad_xn_sum = add_cores(grad_xn_shared + grad_xn_moe)
    grad_gates = add_cores(grad_gates_part)

    grad_probs = jnp.sum(match * grad_gates[:, :, None], axis=1)
    grad_logits = (
        probs * (grad_probs - jnp.sum(probs * grad_probs, axis=-1, keepdims=True))
    ).astype(bf16)
    grad_w_router = mm("td,te->de", xn_two, grad_logits)
    grad_xn_two = grad_xn_sum + mm("te,de->td", grad_logits, w_router)
    grad_norm_two, grad_g_two = norm_back(grad_xn_two, hidden_state, rms_two, g_two)
    grad_hidden = grad_y + grad_norm_two
    grad_attn = grad_hidden.astype(bf16)
    grad_out_t = mm("td,th->dh", grad_attn, mixed)
    grad_mixed = mm("td,dh->th", grad_attn, w_out_t).astype(bf16)
    grad_queries, grad_keys, grad_values = attend_backward(
        queries, keys_all, values_all, segment, scale, grad_mixed, log_totals
    )
    grad_projected = (
        jnp.stack(
            [rotate(grad_queries, cosine, -sine), rotate(grad_keys, cosine, -sine), grad_values],
            axis=1,
        )
        .astype(bf16)
        .reshape(length, 3 * heads_width)
    )
    grad_w_qkv = mm("td,tc->dc", xn_one, grad_projected)
    xn_part = mm("tc,dc->td", grad_projected, w_qkv).astype(bf16)
    grad_xn_one = xn_part.astype(f32) + other_core(xn_part).astype(f32)
    grad_norm_one, grad_g_one = norm_back(grad_xn_one, xfull, rms_one, g_one)
    grad_tokens = grad_hidden + grad_norm_one

    small_grad = jnp.concatenate(
        [grad_g_one[:, None], grad_g_two[:, None], grad_w_router], axis=1
    )
    small_grad = jnp.pad(small_grad, ((0, 0), (0, 128 - small_grad.shape[1])))
    shared_grads = jnp.concatenate(
        [
            g.astype(bf16)
            for g in (grad_s_gate_up, grad_s_down_t, grad_w_qkv, grad_out_t, small_grad)
        ],
        axis=1,
    ).reshape(n, rows, -1)
    expert_grads = jnp.concatenate(
        [grad_gate_up.astype(bf16), grad_down_t.astype(bf16)], axis=1
    ).reshape(n, rows, -1)
    mine, mine_expert = reduce_grads(planes, shared_grads, expert_grads)
    small_mine = part(mine, 4)
    return (
        output,
        grad_tokens,
        small_mine[:, 0],
        part(mine, 2).reshape(rows, 3, heads_width),
        part(mine, 3).T,
        small_mine[:, 1],
        small_mine[:, 2 : 2 + experts],
        mine_expert[:, :, : 2 * hidden].reshape(experts, rows, 2, hidden),
        mine_expert[:, :, 2 * hidden :].transpose(0, 2, 1),
        part(mine, 0).reshape(rows, 2, s_hidden),
        part(mine, 1).T,
    )


def solution(mesh):
    def pick(*args):
        experts, rows = args[9].shape[0], args[5].shape[0]
        if experts == GROUP and mesh.shape["dp"] % GROUP == 0 and rows % 16 == 0:
            return local_grouped(mesh.shape["dp"] // GROUP, *args)
        return local_plain(*args)

    return jax.shard_map(
        pick,
        mesh=mesh,
        in_specs=(
            P("dp", None),
            P("dp", None),
            P("dp", None),
            P("dp", None),
            P("dp"),
            P("dp", None, "tensor"),
            P("tensor", "dp"),
            P("dp"),
            P("dp", None),
            P(None, "dp", None, "tensor"),
            P(None, "tensor", "dp"),
            P("dp", None, "tensor"),
            P("tensor", "dp"),
            P("dp", None),
        ),
        out_specs=(
            P("dp", None),
            P("dp", None),
            P("dp"),
            P("dp", None, "tensor"),
            P("tensor", "dp"),
            P("dp"),
            P("dp", None),
            P(None, "dp", None, "tensor"),
            P(None, "tensor", "dp"),
            P("dp", None, "tensor"),
            P("tensor", "dp"),
        ),
        check_vma=False,
    )
```

```python
import functools
import math

import jax
import jax.numpy as jnp
from jax import lax
from jax.experimental import pallas as pl
from jax.experimental.pallas import tpu as pltpu
from jax.sharding import PartitionSpec as P

HD = 64
GROUP = 4
MESH = pl.DeviceIdType.MESH


epsilon = 1e-06


def rms_scale(values):
    return lax.rsqrt(jnp.mean(values * values, axis=-1, keepdims=True) + epsilon)


def rotary(length, head_dim):
    half_dim = head_dim // 2
    position = jnp.arange(length).astype(jnp.float32)[:, None]
    inverse = jnp.exp(
        jnp.arange(half_dim).astype(jnp.float32) * (-2.0 * math.log(10000.0) / head_dim)
    )
    angles = position * inverse[None, :]
    return (jnp.cos(angles)[:, None, :], jnp.sin(angles)[:, None, :])


def rotate(values, cosine, sine):
    half_dim = values.shape[-1] // 2
    first_half = values[..., :half_dim]
    second_half = values[..., half_dim:]
    return jnp.concatenate(
        [first_half * cosine - second_half * sine, second_half * cosine + first_half * sine],
        axis=-1,
    )


def route_slots(pair_ids, rank_order, capacity, experts):
    length = pair_ids.shape[0]
    top_count = pair_ids.shape[1]
    pair_expert = pair_ids.reshape(-1)
    pair_count = pair_expert.shape[0]
    ordered = jnp.zeros((pair_count,), jnp.int32).at[rank_order].set(pair_expert)
    onehot = (ordered[:, None] == jnp.arange(experts, dtype=jnp.int32)[None, :]).astype(jnp.int32)
    running = jnp.cumsum(onehot, axis=0)
    ranked_slot = jnp.sum(running * onehot, axis=1) - 1
    position = ranked_slot[rank_order]
    kept_pair = position < capacity
    slot_index = jnp.where(kept_pair, pair_expert * capacity + position, experts * capacity)
    token_of_pair = jnp.arange(pair_count, dtype=jnp.int32) // top_count
    slot_token = (
        jnp.full((experts * capacity,), length, jnp.int32)
        .at[slot_index]
        .set(token_of_pair, mode="drop")
    )
    return (slot_token, slot_index.reshape(length, top_count), kept_pair.reshape(length, top_count))


def silu_back(both_parts, grad_hidden):
    gate_part = both_parts[..., 0, :]
    up_part = both_parts[..., 1, :]
    sigma = jax.nn.sigmoid(gate_part)
    slope = sigma * (1.0 + gate_part * (1.0 - sigma))
    return jnp.stack(
        [grad_hidden * up_part * slope, grad_hidden * gate_part * sigma], axis=-2
    ).astype(jnp.bfloat16)


def silu_forward(both_parts):
    return (jax.nn.silu(both_parts[..., 0, :]) * both_parts[..., 1, :]).astype(jnp.bfloat16)


def norm_back(grad_norm, values, scale_rows, gain):
    grad_gain = jnp.sum(grad_norm * values * scale_rows, axis=0)
    inner = grad_norm * gain
    grad_values = scale_rows * inner - values * scale_rows**3 * jnp.mean(
        inner * values, axis=-1, keepdims=True
    )
    return (grad_values, grad_gain)


def split_blocks(length):
    block = min(512, length)
    return (block, length // block)


def masked_scores(query_block, keys_all, query_pos, query_seg, segment, scale):
    positions = jnp.arange(keys_all.shape[0])
    scores = (
        jnp.einsum("qhd,khd->hqk", query_block, keys_all, preferred_element_type=jnp.float32)
        * scale
    )
    allowed = (positions[None, :] <= query_pos[:, None]) & (segment[None, :] == query_seg[:, None])
    return jnp.where(allowed[None], scores, -1e30)


def attend_forward(queries, keys_all, values_all, segment, scale):
    length, head_count, head_dim = queries.shape
    block, count_blocks = split_blocks(length)
    positions = jnp.arange(length)

    def one_block(inputs):
        query_block, query_pos, query_seg = inputs
        scores = masked_scores(query_block, keys_all, query_pos, query_seg, segment, scale)
        largest = jnp.max(scores, axis=-1, keepdims=True)
        expo = jnp.exp(scores - largest)
        total = jnp.sum(expo, axis=-1, keepdims=True)
        probs = (expo / total).astype(jnp.bfloat16)
        mixed = jnp.einsum("hqk,khd->qhd", probs, values_all, preferred_element_type=jnp.float32)
        return (mixed.astype(jnp.bfloat16), (largest + jnp.log(total))[..., 0])

    blocks = (
        queries.reshape(count_blocks, block, head_count, head_dim),
        positions.reshape(count_blocks, block),
        segment.reshape(count_blocks, block),
    )
    mixed_all, log_totals = lax.map(one_block, blocks)
    return (mixed_all.reshape(length, head_count * head_dim), log_totals)


def attend_backward(queries, keys_all, values_all, segment, scale, grad_mixed, log_totals):
    length, head_count, head_dim = queries.shape
    block, count_blocks = split_blocks(length)
    positions = jnp.arange(length)

    def one_block(carry, inputs):
        grad_keys, grad_values = carry
        query_block, query_pos, query_seg, grad_block, log_block = inputs
        scores = masked_scores(query_block, keys_all, query_pos, query_seg, segment, scale)
        probs = jnp.exp(scores - log_block[:, :, None])
        grad_probs = jnp.einsum(
            "qhd,khd->hqk", grad_block, values_all, preferred_element_type=jnp.float32
        )
        inner = jnp.sum(probs * grad_probs, axis=-1, keepdims=True)
        grad_scores = (probs * (grad_probs - inner)).astype(jnp.bfloat16)
        grad_query = (
            jnp.einsum("hqk,khd->qhd", grad_scores, keys_all, preferred_element_type=jnp.float32)
            * scale
        )
        grad_keys = (
            grad_keys
            + jnp.einsum(
                "hqk,qhd->khd", grad_scores, query_block, preferred_element_type=jnp.float32
            )
            * scale
        )
        grad_values = grad_values + jnp.einsum(
            "hqk,qhd->khd",
            probs.astype(jnp.bfloat16),
            grad_block,
            preferred_element_type=jnp.float32,
        )
        return ((grad_keys, grad_values), grad_query)

    zeros_kv = jnp.zeros((length, head_count, head_dim), jnp.float32)
    blocks = (
        queries.reshape(count_blocks, block, head_count, head_dim),
        positions.reshape(count_blocks, block),
        segment.reshape(count_blocks, block),
        grad_mixed.reshape(count_blocks, block, head_count, head_dim),
        log_totals,
    )
    (grad_keys, grad_values), grad_queries = lax.scan(one_block, (zeros_kv, zeros_kv), blocks)
    return (grad_queries.reshape(length, head_count, head_dim), grad_keys, grad_values)


def sum_rows(grad, axis, scatter_dimension, tiled):
    part = lax.psum_scatter(
        grad.astype(jnp.bfloat16), axis, scatter_dimension=scatter_dimension, tiled=tiled
    )
    return part.astype(jnp.float32)


def local_plain(
    tokens,
    segment_ids,
    expert_ids,
    slot_order,
    gain_attn,
    qkv_weight,
    out_weight,
    gain_ffn,
    router_weight,
    gate_up,
    down_weight,
    shared_gate_up,
    shared_down,
    cotangent,
):
    g_one, w_qkv, w_out, g_two, w_router, w_gate_up, w_down, s_gate_up, s_down = (
        lax.all_gather(gain_attn, "dp", axis=0, tiled=True),
        lax.all_gather(qkv_weight, "dp", axis=0, tiled=True),
        lax.all_gather(out_weight, "dp", axis=1, tiled=True),
        lax.all_gather(gain_ffn, "dp", axis=0, tiled=True),
        lax.all_gather(router_weight, "dp", axis=0, tiled=True),
        lax.all_gather(gate_up, "dp", axis=1, tiled=True),
        lax.all_gather(down_weight, "dp", axis=2, tiled=True),
        lax.all_gather(shared_gate_up, "dp", axis=0, tiled=True),
        lax.all_gather(shared_down, "dp", axis=1, tiled=True),
    )
    length = tokens.shape[0]
    width = tokens.shape[1]
    experts_count = w_router.shape[1]
    top_count = expert_ids.shape[1]
    capacity = length * top_count // experts_count
    head_dim = HD
    local_heads = w_qkv.shape[2] // head_dim
    scale = head_dim ** (-0.5)
    segment = segment_ids[0]
    slot_token, slot_index, kept_pair = route_slots(
        expert_ids, slot_order[0], capacity, experts_count
    )
    kept_float = kept_pair.astype(jnp.float32)
    slot_valid = slot_token < length
    slot_rows = jnp.minimum(slot_token, length - 1)
    pair_slots = jnp.minimum(slot_index, experts_count * capacity - 1)
    xfull = tokens.astype(jnp.float32)
    rms_one = rms_scale(xfull)
    xn_one = (xfull * rms_one * g_one.astype(jnp.float32)).astype(jnp.bfloat16)
    projected = jnp.einsum("td,dch->tch", xn_one, w_qkv, preferred_element_type=jnp.float32)
    cosine, sine = rotary(length, head_dim)
    queries = rotate(projected[:, 0].reshape(length, local_heads, head_dim), cosine, sine).astype(
        jnp.bfloat16
    )
    keys_all = rotate(projected[:, 1].reshape(length, local_heads, head_dim), cosine, sine).astype(
        jnp.bfloat16
    )
    values_all = projected[:, 2].reshape(length, local_heads, head_dim).astype(jnp.bfloat16)
    mixed, log_totals = attend_forward(queries, keys_all, values_all, segment, scale)
    attn_share = lax.psum_scatter(
        jnp.dot(mixed, w_out, preferred_element_type=jnp.float32),
        "tensor",
        scatter_dimension=1,
        tiled=True,
    )
    attn = lax.all_gather(attn_share, "tensor", axis=1, tiled=True)
    hidden_state = xfull + attn
    rms_two = rms_scale(hidden_state)
    xn_two = (hidden_state * rms_two * g_two.astype(jnp.float32)).astype(jnp.bfloat16)
    logits = jnp.dot(xn_two, w_router, preferred_element_type=jnp.float32)
    probs = jax.nn.softmax(logits, axis=-1)
    gates = jnp.take_along_axis(probs, expert_ids, axis=1) * kept_float
    dispatched = (xn_two[slot_rows] * slot_valid[:, None].astype(jnp.bfloat16)).reshape(
        experts_count, capacity, width
    )
    both_parts = jnp.einsum(
        "ecd,edjf->ecjf", dispatched, w_gate_up, preferred_element_type=jnp.float32
    )
    expert_hidden = silu_forward(both_parts)
    expert_out = jnp.einsum(
        "ecf,efd->ecd", expert_hidden, w_down, preferred_element_type=jnp.float32
    ).reshape(experts_count * capacity, width)
    picked = expert_out[pair_slots]
    moe = jnp.sum(gates[:, :, None] * picked, axis=1)
    shared_both = jnp.einsum("td,djf->tjf", xn_two, s_gate_up, preferred_element_type=jnp.float32)
    shared_hidden = silu_forward(shared_both)
    shared_out = jnp.dot(shared_hidden, s_down, preferred_element_type=jnp.float32)
    ffn_share = lax.psum_scatter(
        (moe + shared_out).astype(jnp.bfloat16), "tensor", scatter_dimension=1, tiled=True
    ).astype(jnp.float32)
    ffn = lax.all_gather(ffn_share.astype(jnp.bfloat16), "tensor", axis=1, tiled=True).astype(
        ffn_share.dtype
    )
    output = (hidden_state + ffn).astype(jnp.bfloat16)
    grad_y = cotangent.astype(jnp.float32)
    grad_shared_hidden = jnp.einsum(
        "td,fd->tf", cotangent, s_down, preferred_element_type=jnp.float32
    )
    grad_s_down = jnp.einsum(
        "tf,td->fd", shared_hidden, cotangent, preferred_element_type=jnp.float32
    )
    grad_shared_both = silu_back(shared_both, grad_shared_hidden)
    grad_s_gate_up = jnp.einsum(
        "td,tjf->djf", xn_two, grad_shared_both, preferred_element_type=jnp.float32
    )
    grad_xn_shared = jnp.einsum(
        "tjf,djf->td", grad_shared_both, s_gate_up, preferred_element_type=jnp.float32
    )
    slot_gate = (
        jnp.zeros((experts_count * capacity,), jnp.float32)
        .at[slot_index.reshape(-1)]
        .set(gates.reshape(-1), mode="drop")
    )
    grad_expert_out = (
        (slot_gate[:, None] * grad_y[slot_rows])
        .astype(jnp.bfloat16)
        .reshape(experts_count, capacity, width)
    )
    grad_gates_part = kept_float * jnp.sum(grad_y[:, None, :] * picked, axis=-1)
    grad_expert_hidden = jnp.einsum(
        "ecd,efd->ecf", grad_expert_out, w_down, preferred_element_type=jnp.float32
    )
    grad_w_down = jnp.einsum(
        "ecf,ecd->efd", expert_hidden, grad_expert_out, preferred_element_type=jnp.float32
    )
    grad_both = silu_back(both_parts, grad_expert_hidden)
    grad_w_gate_up = jnp.einsum(
        "ecd,ecjf->edjf", dispatched, grad_both, preferred_element_type=jnp.float32
    )
    grad_dispatched = jnp.einsum(
        "ecjf,edjf->ecd", grad_both, w_gate_up, preferred_element_type=jnp.float32
    ).reshape(experts_count * capacity, width)
    grad_xn_moe = jnp.sum(kept_float[:, :, None] * grad_dispatched[pair_slots], axis=1)
    grad_xn_part, grad_gates_share = (
        lax.psum_scatter(grad_xn_shared + grad_xn_moe, "tensor", scatter_dimension=1, tiled=True),
        lax.psum_scatter(grad_gates_part, "tensor", scatter_dimension=1, tiled=True),
    )
    grad_xn_sum, grad_gates = (
        lax.all_gather(grad_xn_part, "tensor", axis=1, tiled=True),
        lax.all_gather(grad_gates_share, "tensor", axis=1, tiled=True),
    )
    expert_match = (
        expert_ids[:, :, None] == jnp.arange(experts_count, dtype=jnp.int32)[None, None, :]
    ).astype(jnp.float32)
    grad_probs = jnp.sum(expert_match * grad_gates[:, :, None], axis=1)
    grad_logits = (
        probs * (grad_probs - jnp.sum(probs * grad_probs, axis=-1, keepdims=True))
    ).astype(jnp.bfloat16)
    grad_w_router = jnp.einsum("td,te->de", xn_two, grad_logits, preferred_element_type=jnp.float32)
    grad_xn_two = grad_xn_sum + jnp.einsum(
        "te,de->td", grad_logits, w_router, preferred_element_type=jnp.float32
    )
    grad_norm_two, grad_g_two = norm_back(
        grad_xn_two, hidden_state, rms_two, g_two.astype(jnp.float32)
    )
    grad_hidden = grad_y + grad_norm_two
    grad_attn = grad_hidden.astype(jnp.bfloat16)
    grad_w_out = jnp.einsum("th,td->hd", mixed, grad_attn, preferred_element_type=jnp.float32)
    grad_mixed = jnp.einsum(
        "td,hd->th", grad_attn, w_out, preferred_element_type=jnp.float32
    ).astype(jnp.bfloat16)
    grad_queries, grad_keys, grad_values = attend_backward(
        queries, keys_all, values_all, segment, scale, grad_mixed, log_totals
    )
    grad_projected = (
        jnp.stack(
            [rotate(grad_queries, cosine, -sine), rotate(grad_keys, cosine, -sine), grad_values],
            axis=1,
        )
        .astype(jnp.bfloat16)
        .reshape(length, 3, local_heads * head_dim)
    )
    grad_w_qkv = jnp.einsum(
        "td,tch->dch", xn_one, grad_projected, preferred_element_type=jnp.float32
    )
    grad_xn_share = lax.psum_scatter(
        jnp.einsum("tch,dch->td", grad_projected, w_qkv, preferred_element_type=jnp.float32).astype(
            jnp.bfloat16
        ),
        "tensor",
        scatter_dimension=1,
        tiled=True,
    ).astype(jnp.float32)
    grad_xn_one = lax.all_gather(
        grad_xn_share.astype(jnp.bfloat16), "tensor", axis=1, tiled=True
    ).astype(grad_xn_share.dtype)
    grad_norm_one, grad_g_one = norm_back(grad_xn_one, xfull, rms_one, g_one.astype(jnp.float32))
    grad_tokens = grad_hidden + grad_norm_one
    (
        grad_g_one,
        grad_w_qkv,
        grad_w_out,
        grad_g_two,
        grad_w_router,
        grad_w_gate_up,
        grad_w_down,
        grad_s_gate_up,
        grad_s_down,
    ) = (
        lax.psum_scatter(grad_g_one, "dp", scatter_dimension=0, tiled=True),
        sum_rows(grad_w_qkv, "dp", scatter_dimension=0, tiled=True),
        sum_rows(grad_w_out, "dp", scatter_dimension=1, tiled=True),
        lax.psum_scatter(grad_g_two, "dp", scatter_dimension=0, tiled=True),
        lax.psum_scatter(grad_w_router, "dp", scatter_dimension=0, tiled=True),
        sum_rows(grad_w_gate_up, "dp", scatter_dimension=1, tiled=True),
        sum_rows(grad_w_down, "dp", scatter_dimension=2, tiled=True),
        sum_rows(grad_s_gate_up, "dp", scatter_dimension=0, tiled=True),
        sum_rows(grad_s_down, "dp", scatter_dimension=1, tiled=True),
    )
    return (
        output,
        grad_tokens,
        grad_g_one,
        grad_w_qkv,
        grad_w_out,
        grad_g_two,
        grad_w_router,
        grad_w_gate_up,
        grad_w_down,
        grad_s_gate_up,
        grad_s_down,
    )


class Place:
    def __init__(self, planes):
        d = lax.axis_index("dp")
        self.planes = planes
        self.d, self.c = d, lax.axis_index("tensor")
        self.z, self.p = d // GROUP, lax.rem(d, GROUP)
        bit0, bit1 = lax.rem(self.p, 2), self.p // 2
        flip0, flip1 = 1 - bit0, 1 - bit1
        self.member = [
            self.p,
            flip0 + 2 * bit1,
            bit0 + 2 * flip1,
            flip0 + 2 * flip1,
        ]

    def near(self, j):
        return (self.z * GROUP + self.member[j], self.c)

    def up(self):
        return (self.d + GROUP, self.c)

    def down(self):
        return (self.d - GROUP, self.c)

    def twin(self):
        return (self.d, 1 - self.c)

    def when(self, condition, action):
        pl.when(condition)(action)

    def has_up(self, k=1):
        return self.z + k < self.planes

    def has_down(self, k=1):
        return self.z - k >= 0

    def greet(self):
        barrier = pltpu.get_barrier_semaphore()

        def hello(device):
            pl.semaphore_signal(barrier, inc=1, device_id=device, device_id_type=MESH)

        hello(self.twin())
        for j in range(1, GROUP):
            hello(self.near(j))
        self.when(self.has_up(), lambda: hello(self.up()))
        self.when(self.has_down(), lambda: hello(self.down()))
        line = self.has_up().astype(jnp.int32) + self.has_down().astype(jnp.int32)
        pl.semaphore_wait(barrier, GROUP + line)


def send(source, target, send_sem, recv_sem, device):
    return pltpu.make_async_remote_copy(
        src_ref=source,
        dst_ref=target,
        send_sem=send_sem,
        recv_sem=recv_sem,
        device_id=device,
        device_id_type=MESH,
    )


class Everywhere:
    def __init__(self, at, own, all_blocks, local_sem, recvs, sends):
        self.at, self.own, self.all = at, own, all_blocks
        self.local_sem, self.recvs, self.sends = local_sem, recvs, sends

    def copy(self, block, source, way, device):
        return send(source, self.all.at[block], self.sends.at[way, block], self.recvs.at[block], device)

    def keep(self):
        return pltpu.make_async_copy(self.own, self.all.at[self.at.d], self.local_sem)

    def landed(self, block):
        self.copy(block, self.own, 0, self.at.near(1)).wait_recv()

    def start_line(self):
        at = self.at
        at.when(at.has_up(), lambda: self.copy(at.d, self.own, 0, at.up()).start())
        at.when(at.has_down(), lambda: self.copy(at.d, self.own, 1, at.down()).start())

    def start_plane(self):
        at = self.at
        self.copy(at.d, self.own, 2, at.near(1)).start()
        self.copy(at.d, self.own, 3, at.near(2)).start()
        self.keep().start()

    def spread(self, k):
        at = self.at

        def go(plane, more, way, device_of):
            block = plane * GROUP + at.p
            source = self.all.at[block]
            self.landed(block)
            at.when(more, lambda: self.copy(block, source, way, device_of()).start())
            self.copy(block, source, 2, at.near(1)).start()
            self.copy(block, source, 3, at.near(2)).start()

        at.when(at.has_down(k), lambda: go(at.z - k, at.has_up(), 0, at.up))
        at.when(at.has_up(k), lambda: go(at.z + k, at.has_down(), 1, at.down))

    def cross(self, k):
        at = self.at

        def go(plane):
            first = plane * GROUP + at.member[1]
            second = plane * GROUP + at.member[2]
            even = lax.rem(plane, 2) == 0
            self.landed(first)
            at.when(even, lambda: self.copy(first, self.all.at[first], 3, at.near(2)).start())
            self.landed(second)
            at.when(
                jnp.logical_not(even),
                lambda: self.copy(second, self.all.at[second], 2, at.near(1)).start(),
            )

        if k == 0:
            go(at.z)
        else:
            at.when(at.has_down(k), lambda: go(at.z - k))
            at.when(at.has_up(k), lambda: go(at.z + k))

    def diagonal(self):
        for plane in range(self.at.planes):
            self.landed(plane * GROUP + self.at.member[3])
        self.keep().wait()

    def sent(self):
        at = self.at
        for plane in range(at.planes):
            block = plane * GROUP + at.p
            self.copy(block, self.own, 2, at.near(1)).wait_send()
            self.copy(block, self.own, 3, at.near(2)).wait_send()
            if plane % 2 == 0:
                self.copy(plane * GROUP + at.member[1], self.own, 3, at.near(2)).wait_send()
            else:
                self.copy(plane * GROUP + at.member[2], self.own, 2, at.near(1)).wait_send()

            def gone(way, device_of):
                self.copy(block, self.own, way, device_of()).wait_send()

            at.when((at.z >= plane) & at.has_up(), lambda: gone(0, at.up))
            at.when((at.z <= plane) & at.has_down(), lambda: gone(1, at.down))


class Experts:
    def __init__(self, at, own, all_blocks, local_sem, recvs, sends):
        self.at, self.own, self.all = at, own, all_blocks
        self.local_sem, self.recvs, self.sends = local_sem, recvs, sends

    def line(self, block, source, way, device):
        return send(source, self.all.at[block], self.sends.at[way, block], self.recvs.at[block], device)

    def across(self, j):
        at = self.at
        return send(
            self.own.at[at.member[j]],
            self.all.at[at.d],
            self.sends.at[1 + j, at.d],
            self.recvs.at[at.d],
            at.near(j),
        )

    def keep(self):
        return pltpu.make_async_copy(self.own.at[self.at.p], self.all.at[self.at.d], self.local_sem)

    def start_plane(self):
        for j in range(1, GROUP):
            self.across(j).start()
        self.keep().start()

    def start_line(self):
        at = self.at
        source = self.own.at[at.p]
        at.when(at.has_up(), lambda: self.line(at.d, source, 0, at.up()).start())
        at.when(at.has_down(), lambda: self.line(at.d, source, 1, at.down()).start())

    def landed(self, block):
        self.line(block, self.own.at[0], 0, self.at.near(1)).wait_recv()

    def plane_step(self, j):
        at = self.at
        block = at.z * GROUP + at.member[j]
        source = self.all.at[block]
        self.landed(block)
        at.when(at.has_up(), lambda: self.line(block, source, 0, at.up()).start())
        at.when(at.has_down(), lambda: self.line(block, source, 1, at.down()).start())

    def line_step(self, k, j):
        at = self.at

        def go(plane, more, way, device_of):
            block = plane * GROUP + at.member[j]
            self.landed(block)
            at.when(more, lambda: self.line(block, self.all.at[block], way, device_of()).start())

        at.when(at.has_down(k), lambda: go(at.z - k, at.has_up(), 0, at.up))
        at.when(at.has_up(k), lambda: go(at.z + k, at.has_down(), 1, at.down))

    def sent(self):
        at = self.at
        self.keep().wait()
        for j in range(1, GROUP):
            self.across(j).wait_send()
        for plane in range(at.planes):

            def gone(way, device_of):
                for q in range(GROUP):
                    self.line(plane * GROUP + q, self.own.at[0], way, device_of()).wait_send()

            at.when((at.z >= plane) & at.has_up(), lambda: gone(0, at.up))
            at.when((at.z <= plane) & at.has_down(), lambda: gone(1, at.down))


def dot_nn(a, b):
    return jnp.dot(a, b, preferred_element_type=jnp.float32)


def dot_nt(a, b):
    return lax.dot_general(a, b, (((1,), (1,)), ((), ())), preferred_element_type=jnp.float32)


def dot_tn(a, b):
    return lax.dot_general(a, b, (((0,), (0,)), ((), ())), preferred_element_type=jnp.float32)


def lanes(count=128):
    return lax.broadcasted_iota(jnp.int32, (1, count), 1)


def turn(values, cosine, sine):
    half = HD // 2
    other = jnp.where(
        lax.rem(lanes(), HD) < half,
        -pltpu.roll(values, 2 * HD - half, 1),
        pltpu.roll(values, half, 1),
    )
    return values * cosine + other * sine


def blocks_of(ref, start, stop):
    block = ref[:, :, start:stop]
    return block.reshape(block.shape[0] * block.shape[1], stop - start)


def attention_blocks(length):
    size = length // 2
    return [(i * size, (i + 1) * size) for i in range(2)]


def forward_kernel(
    planes,
    experts,
    x_ref,
    cot_ref,
    seg_col,
    seg_row,
    ids_ref,
    order_ref,
    ids_t_ref,
    order_t_ref,
    cos_ref,
    sin_ref,
    a_own,
    s_own,
    e_own,
    a_all,
    s_all,
    e_all,
    q_ref,
    k_ref,
    v_ref,
    o_ref,
    lse_ref,
    h_ref,
    xa_ref,
    xf_ref,
    probs_ref,
    pair_ref,
    placed_ref,
    arrived_ref,
    bias_ref,
    mine_ref,
    theirs_ref,
    local_sem,
    a_recv,
    a_send,
    s_recv,
    s_send,
    e_recv,
    e_send,
    twin_sem,
    token_recv,
    token_send,
):
    f32, bf16 = jnp.float32, jnp.bfloat16
    at = Place(planes)
    length, width = x_ref.shape
    heads_width = q_ref.shape[1]
    capacity = length * ids_ref.shape[1] // experts
    half = capacity // 2
    attn = Everywhere(at, a_own, a_all, local_sem.at[0], a_recv, a_send)
    shared = Everywhere(at, s_own, s_all, local_sem.at[1], s_recv, s_send)
    expert = Experts(at, e_own, e_all, local_sem.at[2], e_recv, e_send)

    at.greet()
    attn.start_line()
    attn.start_plane()
    expert.start_plane()
    shared.start_line()
    expert.start_line()

    todo = []
    for j in range(1, GROUP):
        todo.append(functools.partial(expert.plane_step, j))
    todo.append(shared.start_plane)
    for k in range(1, planes):
        todo.append(functools.partial(shared.spread, k))
        for j in range(GROUP):
            todo.append(functools.partial(expert.line_step, k, j))
        todo.append(functools.partial(shared.cross, k - 1))
    todo.append(functools.partial(shared.cross, planes - 1))
    todo.reverse()

    def tick(count=1):
        for _ in range(count):
            if todo:
                todo.pop()()

    for start, stop in attention_blocks(length):
        rows = lax.broadcasted_iota(jnp.int32, (stop - start, stop), 0) + start
        columns = lax.broadcasted_iota(jnp.int32, (stop - start, stop), 1)
        allowed = (columns <= rows) & (seg_col[start:stop, :] == seg_row[:, :stop])
        bias_ref[start:stop, :stop] = jnp.where(allowed, 0.0, -1e30)

    def slot_of(expert_id, position):
        which = position // half
        apart = which + at.c - 2 * which * at.c
        bit0, bit1 = lax.rem(expert_id, 2), expert_id // 2
        p0, p1 = lax.rem(at.p, 2), at.p // 2
        distance = (bit0 + p0 - 2 * bit0 * p0) + 2 * (bit1 + p1 - 2 * bit1 * p1)
        slot = apart * (experts * half) + distance * half + lax.rem(position, half)
        return jnp.where(position < capacity, slot, -1)

    slot_cols, slot_rows = [], []
    top = ids_ref.shape[1]
    for r in range(top):
        count_col = jnp.zeros((length, 1), jnp.int32)
        count_row = jnp.zeros((1, length), jnp.int32)
        for other in range(top):
            first = (ids_t_ref[other : other + 1, :] == ids_ref[:, r : r + 1]) & (
                order_t_ref[other : other + 1, :] < order_ref[:, r : r + 1]
            )
            count_col += jnp.sum(first.astype(jnp.int32), axis=1, keepdims=True)
            first = (ids_ref[:, other : other + 1] == ids_t_ref[r : r + 1, :]) & (
                order_ref[:, other : other + 1] < order_t_ref[r : r + 1, :]
            )
            count_row += jnp.sum(first.astype(jnp.int32), axis=0, keepdims=True)
        slot_cols.append(slot_of(ids_ref[:, r : r + 1], count_col))
        slot_rows.append(slot_of(ids_t_ref[r : r + 1, :], count_row))

    attn.spread(1)
    attn.cross(0)
    for k in range(2, planes):
        attn.spread(k)
        attn.cross(k - 1)
        tick()
    attn.cross(planes - 1)
    attn.diagonal()

    small = blocks_of(a_all, 4 * heads_width, 4 * heads_width + 128)
    small_rows = small.astype(f32).T
    g_one, g_two = small_rows[0:1, :], small_rows[1:2, :]
    x = x_ref[...].astype(f32)
    rms = lax.rsqrt(jnp.mean(x * x, axis=-1, keepdims=True) + epsilon)
    xa_ref[...] = (x * rms * g_one).astype(bf16)
    tick()
    cosine, sine = cos_ref[...], sin_ref[...]
    pairs = heads_width // 128
    for i, ref in enumerate((q_ref, k_ref)):
        part = dot_nn(xa_ref[...], blocks_of(a_all, i * heads_width, (i + 1) * heads_width))
        for g in range(pairs):
            columns = slice(128 * g, 128 * (g + 1))
            ref[:, columns] = turn(part[:, columns], cosine, sine).astype(bf16)
        tick()
    v_ref[...] = dot_nn(
        xa_ref[...], blocks_of(a_all, 2 * heads_width, 3 * heads_width)
    ).astype(bf16)
    tick()

    scale = HD ** (-0.5)
    for start, stop in attention_blocks(length):
        logs = jnp.zeros((stop - start, 128), f32)
        for g in range(pairs):
            columns = slice(128 * g, 128 * (g + 1))
            queries = q_ref[start:stop, columns]
            keys, values = k_ref[:stop, columns], v_ref[:stop, columns]
            mixed = []
            for i in range(2):
                one = jnp.where(lanes() // HD == i, queries, jnp.zeros_like(queries))
                scores = dot_nt(one, keys) * scale + bias_ref[start:stop, :stop]
                largest = jnp.max(scores, axis=-1, keepdims=True)
                expo = jnp.exp(scores - largest)
                total = jnp.sum(expo, axis=-1, keepdims=True)
                weights = (expo * (1.0 / total)).astype(bf16)
                mixed.append(dot_nn(weights, values))
                logs = jnp.where(lanes() == 2 * g + i, largest + jnp.log(total), logs)
            o_ref[start:stop, columns] = jnp.where(lanes() < HD, mixed[0], mixed[1]).astype(bf16)
            tick(2)
        lse_ref[start:stop, :] = logs

    mine_ref[...] = dot_nt(o_ref[...], blocks_of(a_all, 3 * heads_width, 4 * heads_width))
    swap = send(mine_ref, theirs_ref, twin_sem.at[0], twin_sem.at[1], at.twin())
    swap.start()
    tick(2)
    swap.wait_recv()
    h = x_ref[...].astype(f32) + (mine_ref[...] + theirs_ref[...])
    h_ref[...] = h
    rms = lax.rsqrt(jnp.mean(h * h, axis=-1, keepdims=True) + epsilon)
    xf_ref[...] = (h * rms * g_two).astype(bf16)

    is_expert = (lanes() >= 2) & (lanes() < 2 + experts)
    logits = jnp.where(is_expert, dot_nn(xf_ref[...], small), -1e30)
    expo = jnp.exp(logits - jnp.max(logits, axis=-1, keepdims=True))
    probs = expo / jnp.sum(expo, axis=-1, keepdims=True)
    probs_ref[...] = probs
    packed = jnp.zeros((length, 128), f32)
    for r in range(top):
        chosen = lanes() == ids_ref[:, r : r + 1] + 2
        gate = jnp.sum(jnp.where(chosen, probs, 0.0), axis=-1, keepdims=True)
        gate = jnp.where(slot_cols[r] >= 0, gate, 0.0)
        packed = jnp.where(lanes() == r, gate, packed)
        packed = jnp.where(lanes() == top + r, slot_cols[r].astype(f32), packed)
    pair_ref[...] = packed
    gate_rows = packed.T
    tick(2)

    def outgoing(j):
        return send(
            placed_ref.at[j], arrived_ref.at[0, j], token_send.at[j], token_recv.at[j], at.near(j)
        )

    for j in range(experts):
        index = lax.broadcasted_iota(jnp.int32, (half, 1), 0) + j * half
        pick = [slot_rows[r] == index for r in range(top)]
        slot_gate = sum(
            jnp.sum(jnp.where(pick[r], gate_rows[r : r + 1, :], 0.0), axis=1, keepdims=True)
            for r in range(top)
        )
        pick = sum(p.astype(f32) for p in pick).astype(bf16)
        target = arrived_ref.at[0, 0] if j == 0 else placed_ref.at[j]
        target[:, :width] = dot_nn(pick, xf_ref[...]).astype(bf16)
        target[:, width:] = (dot_nn(pick, cot_ref[...]) * slot_gate).astype(bf16)
        if j:
            outgoing(j).start()
        tick()
    for j in range(1, experts):
        outgoing(j).wait_recv()
        tick()
    across = send(arrived_ref.at[0], arrived_ref.at[1], twin_sem.at[2], twin_sem.at[3], at.twin())
    across.start()

    tick(len(todo))
    shared.diagonal()
    across.wait_recv()
    across.wait_send()
    swap.wait_send()
    for j in range(1, experts):
        outgoing(j).wait_send()
    attn.sent()
    shared.sent()
    expert.sent()


def forward_pass(planes, experts, inputs, own, heads_width):
    n = planes * GROUP
    bf16, f32, dma = jnp.bfloat16, jnp.float32, pltpu.SemaphoreType.DMA
    length, width = inputs[0].shape
    half = length * inputs[4].shape[1] // experts // 2
    vmem, anywhere = pl.BlockSpec(memory_space=pltpu.VMEM), pl.BlockSpec(memory_space=pl.ANY)
    shape = jax.ShapeDtypeStruct
    return pl.pallas_call(
        functools.partial(forward_kernel, planes, experts),
        out_shape=(
            shape((n,) + own[0].shape, bf16),
            shape((n,) + own[1].shape, bf16),
            shape((n,) + own[2].shape[1:], bf16),
            shape((length, heads_width), bf16),
            shape((length, heads_width), bf16),
            shape((length, heads_width), bf16),
            shape((length, heads_width), bf16),
            shape((length, 128), f32),
            shape((length, width), f32),
            shape((length, width), bf16),
            shape((length, width), bf16),
            shape((length, 128), f32),
            shape((length, 128), f32),
            shape((experts, half, 2 * width), bf16),
            shape((2, experts, half, 2 * width), bf16),
        ),
        in_specs=[vmem] * len(inputs) + [anywhere] * 3,
        out_specs=(vmem, anywhere, anywhere) + (vmem,) * 12,
        scratch_shapes=[
            pltpu.VMEM((length, length), f32),
            pltpu.VMEM((length, width), f32),
            pltpu.VMEM((length, width), f32),
            dma((3,)),
            dma((n,)),
            dma((4, n)),
            dma((n,)),
            dma((4, n)),
            dma((n,)),
            dma((1 + GROUP, n)),
            dma((4,)),
            dma((GROUP,)),
            dma((GROUP,)),
        ],
        compiler_params=pltpu.CompilerParams(
            collective_id=0, has_side_effects=True, vmem_limit_bytes=48 << 20
        ),
    )(*inputs, *own)


def reduce_kernel(
    planes,
    s_ref,
    e_ref,
    s_out,
    e_out,
    s_one,
    s_two,
    s_below,
    s_above,
    e_below,
    e_above,
    e_last,
    one_send,
    one_recv,
    two_send,
    two_recv,
    s_send,
    s_recv,
    e_send,
    e_recv,
    last_send,
    last_recv,
):
    at = Place(planes)
    f32 = jnp.float32

    def one_copy(plane, i, even):
        j = 1 if even else 2
        target = at.member[3] if i else at.member[j]
        return send(
            s_ref.at[plane * GROUP + target],
            s_one.at[plane, i],
            one_send.at[plane, i],
            one_recv.at[plane, i],
            at.near(j),
        )

    def two_copy(plane, even):
        j = 2 if even else 1
        return send(
            s_one.at[plane, 1],
            s_two.at[plane],
            two_send.at[plane],
            two_recv.at[plane],
            at.near(j),
        )

    def by_parity(plane, action):
        even = lax.rem(plane, 2) == 0
        at.when(even, lambda: action(True))
        at.when(jnp.logical_not(even), lambda: action(False))

    def s_line(source, plane, way):
        target, device = (s_below, at.up()) if way == 0 else (s_above, at.down())
        return send(source, target.at[plane], s_send.at[way, plane], s_recv.at[way, plane], device)

    def e_line(source, block, way):
        target, device = (e_below, at.up()) if way == 0 else (e_above, at.down())
        return send(source, target.at[block], e_send.at[way, block], e_recv.at[way, block], device)

    def last_copy(j):
        return send(
            e_ref.at[0],
            e_last.at[j],
            last_send.at[j],
            last_recv.at[j],
            at.near(j),
        )

    at.greet()

    def e_step(plane, way):
        behind = at.has_down() if way == 0 else at.has_up()
        held = e_below if way == 0 else e_above
        for j in range(GROUP):
            block = plane * GROUP + at.member[j]

            def add():
                e_line(e_ref.at[block], block, way).wait_recv()
                held[block] = (held[block].astype(f32) + e_ref[block].astype(f32)).astype(
                    held.dtype
                )
                e_line(held.at[block], block, way).start()

            at.when(behind, add)
            at.when(jnp.logical_not(behind), lambda: e_line(e_ref.at[block], block, way).start())

    def plane_sum(plane):
        def stage(even):
            mine = plane * GROUP + at.p
            other = plane * GROUP + (at.member[2] if even else at.member[1])
            one_copy(plane, 1, even).wait_recv()
            s_one[plane, 1] = (s_one[plane, 1].astype(f32) + s_ref[other].astype(f32)).astype(
                s_one.dtype
            )
            two_copy(plane, even).start()
            one_copy(plane, 0, even).wait_recv()
            two_copy(plane, even).wait_recv()
            s_two[plane] = (
                s_two[plane].astype(f32) + s_one[plane, 0].astype(f32) + s_ref[mine].astype(f32)
            ).astype(s_two.dtype)

        by_parity(plane, stage)

    def s_step(plane, way):
        plane_sum(plane)
        behind = at.has_down() if way == 0 else at.has_up()
        held = s_below if way == 0 else s_above

        def add():
            s_line(s_two.at[plane], plane, way).wait_recv()
            held[plane] = (held[plane].astype(f32) + s_two[plane].astype(f32)).astype(held.dtype)
            s_line(held.at[plane], plane, way).start()

        at.when(behind, add)
        at.when(jnp.logical_not(behind), lambda: s_line(s_two.at[plane], plane, way).start())

    def both_ways(action, k):
        at.when(at.has_up(k), lambda: action(at.z + k, 0))
        at.when(at.has_down(k), lambda: action(at.z - k, 1))

    def start_one(plane, way):
        def go(even):
            one_copy(plane, 1, even).start()
            one_copy(plane, 0, even).start()

        by_parity(plane, go)

    for k in range(planes - 1, 0, -1):
        both_ways(start_one, k)
    start_one(at.z, 0)
    for k in range(planes - 1, 0, -1):
        both_ways(e_step, k)
        both_ways(s_step, k)

    for j in range(GROUP):
        block = at.z * GROUP + at.member[j]
        at.when(at.has_down(), lambda: e_line(e_ref.at[block], block, 0).wait_recv())
        at.when(at.has_up(), lambda: e_line(e_ref.at[block], block, 1).wait_recv())
        low = jnp.where(at.has_down(), e_below[block].astype(f32), 0.0)
        high = jnp.where(at.has_up(), e_above[block].astype(f32), 0.0)
        total = e_ref[block].astype(f32) + low + high
        if j == 0:
            e_out[at.p] = total
        else:
            e_below[block] = total.astype(e_below.dtype)
            send(
                e_below.at[block],
                e_last.at[j],
                last_send.at[j],
                last_recv.at[j],
                at.near(j),
            ).start()
    plane_sum(at.z)
    at.when(at.has_down(), lambda: s_line(s_two.at[at.z], at.z, 0).wait_recv())
    at.when(at.has_up(), lambda: s_line(s_two.at[at.z], at.z, 1).wait_recv())
    low = jnp.where(at.has_down(), s_below[at.z].astype(f32), 0.0)
    high = jnp.where(at.has_up(), s_above[at.z].astype(f32), 0.0)
    s_out[...] = s_two[at.z].astype(f32) + low + high
    for j in range(1, GROUP):
        last_copy(j).wait_recv()
        e_out[at.member[j]] = e_last[j].astype(f32)

    for j in range(1, GROUP):
        last_copy(j).wait_send()
    for plane in range(planes):
        even = plane % 2 == 0
        one_copy(plane, 0, even).wait_send()
        one_copy(plane, 1, even).wait_send()
        two_copy(plane, even).wait_send()

        def sent(way):
            s_line(s_two.at[plane], plane, way).wait_send()
            for q in range(GROUP):
                block = plane * GROUP + q
                e_line(e_ref.at[block], block, way).wait_send()

        at.when(at.z < plane, lambda: sent(0))
        at.when(at.z > plane, lambda: sent(1))


def reduce_grads(planes, shared, expert):
    n, rows, s_width = shared.shape
    e_width = expert.shape[2]
    vmem = pl.BlockSpec(memory_space=pltpu.VMEM)
    bf16, dma = jnp.bfloat16, pltpu.SemaphoreType.DMA
    return pl.pallas_call(
        functools.partial(reduce_kernel, planes),
        out_shape=(
            jax.ShapeDtypeStruct((rows, s_width), jnp.float32),
            jax.ShapeDtypeStruct((GROUP, rows, e_width), jnp.float32),
        ),
        in_specs=[vmem, vmem],
        out_specs=(vmem, vmem),
        scratch_shapes=[
            pltpu.VMEM((planes, 2, rows, s_width), bf16),
            pltpu.VMEM((planes, rows, s_width), bf16),
            pltpu.VMEM((planes, rows, s_width), bf16),
            pltpu.VMEM((planes, rows, s_width), bf16),
            pltpu.VMEM((n, rows, e_width), bf16),
            pltpu.VMEM((n, rows, e_width), bf16),
            pltpu.VMEM((GROUP, rows, e_width), bf16),
            dma((planes, 2)),
            dma((planes, 2)),
            dma((planes,)),
            dma((planes,)),
            dma((2, planes)),
            dma((2, planes)),
            dma((2, n)),
            dma((2, n)),
            dma((GROUP,)),
            dma((GROUP,)),
        ],
        compiler_params=pltpu.CompilerParams(
            collective_id=1, has_side_effects=True, vmem_limit_bytes=60 << 20
        ),
    )(shared, expert)


def other_core(values):
    return lax.ppermute(values, "tensor", [(0, 1), (1, 0)])


def add_cores(values):
    return values + other_core(values)


def to_members(planes, blocks):
    out = [blocks[0]]
    for j in range(1, GROUP):
        order = [(d, (d // GROUP) * GROUP + ((d % GROUP) ^ j)) for d in range(planes * GROUP)]
        out.append(lax.ppermute(blocks[j], "dp", order))
    return out


def local_grouped(
    planes,
    tokens,
    segment_ids,
    expert_ids,
    slot_order,
    gain_attn,
    qkv_weight,
    out_weight,
    gain_ffn,
    router_weight,
    gate_up,
    down_weight,
    shared_gate_up,
    shared_down,
    cotangent,
):
    bf16, f32 = jnp.bfloat16, jnp.float32
    rows, heads_width = qkv_weight.shape[0], qkv_weight.shape[2]
    experts, hidden = down_weight.shape[0], down_weight.shape[1]
    s_hidden = shared_down.shape[0]
    length, width = tokens.shape
    top = expert_ids.shape[1]
    capacity = length * top // experts
    heads = heads_width // HD
    scale = HD ** (-0.5)
    n = planes * GROUP
    member = lax.rem(lax.axis_index("dp"), GROUP)
    core = lax.axis_index("tensor")
    cuts = [3 * heads_width, heads_width, 128, 2 * s_hidden, s_hidden]
    edges = [sum(cuts[:i]) for i in range(len(cuts) + 1)]

    def part(array, i):
        return array[..., edges[i] : edges[i + 1]]

    expert_packed = jnp.concatenate(
        [gate_up.reshape(experts, rows, 2 * hidden), down_weight.transpose(0, 2, 1)], axis=2
    )
    small = jnp.concatenate([gain_attn[:, None], gain_ffn[:, None], router_weight], axis=1)
    small = jnp.pad(small, ((0, 0), (0, 128 - small.shape[1])))
    attn_packed = jnp.concatenate(
        [qkv_weight.reshape(rows, 3 * heads_width), out_weight.T, small], axis=1
    )
    shared_packed = jnp.concatenate(
        [shared_gate_up.reshape(rows, 2 * s_hidden), shared_down.T], axis=1
    )
    cosine, sine = rotary(length, HD)
    cosine = jnp.tile(cosine[:, 0], (1, 4))
    sine = jnp.tile(sine[:, 0], (1, 4))
    orders = slot_order.reshape(length, top)
    inputs = (
        tokens,
        cotangent,
        segment_ids.reshape(length, 1),
        segment_ids,
        expert_ids,
        orders,
        expert_ids.T,
        orders.T,
        cosine,
        sine,
    )
    (
        all_attn,
        all_shared,
        all_expert,
        queries,
        keys_all,
        values_all,
        mixed,
        log_totals,
        hidden_state,
        xn_one,
        xn_two,
        probs,
        pair_facts,
        _,
        arrived,
    ) = forward_pass(
        planes, experts, inputs, (attn_packed, shared_packed, expert_packed), heads_width
    )
    all_attn = all_attn.reshape(width, -1)
    all_shared = all_shared.reshape(width, -1)
    all_expert = all_expert.reshape(width, -1)
    w_qkv, w_out_t, small_all = (part(all_attn, i) for i in range(3))
    s_gate_up, s_down_t = all_shared[:, : 2 * s_hidden], all_shared[:, 2 * s_hidden :]
    g_one, g_two = small_all[:, 0].astype(f32), small_all[:, 1].astype(f32)
    w_router = small_all[:, 2 : 2 + experts]
    w_gate_up, w_down_t = all_expert[:, : 2 * hidden], all_expert[:, 2 * hidden :]
    cosine, sine = rotary(length, HD)
    half = capacity // 2
    gates = pair_facts[:, :top]
    slot = pair_facts[:, top : 2 * top].astype(jnp.int32)
    kept_float = (slot >= 0).astype(f32)
    probs = probs[:, 2 : 2 + experts]
    match = (expert_ids[:, :, None] == jnp.arange(experts, dtype=jnp.int32)).astype(f32)
    slots = jnp.arange(experts * capacity, dtype=jnp.int32)
    pick = [(slot[:, r : r + 1] == slots[None, :]).astype(bf16) for r in range(top)]
    pick_any = sum(pick[1:], pick[0])
    segment = segment_ids[0]
    xfull = tokens.astype(f32)
    rms_one, rms_two = rms_scale(xfull), rms_scale(hidden_state)
    queries, keys_all, values_all = (
        a.reshape(length, heads, HD) for a in (queries, keys_all, values_all)
    )
    log_totals = log_totals[:, :heads].T[None]
    arrived = arrived.reshape(experts * capacity, 2 * width)
    xin, dye = arrived[:, :width], arrived[:, width:]

    def mm(spec, a, b):
        return jnp.einsum(spec, a, b, preferred_element_type=f32)

    shared_both = mm("td,df->tf", xn_two, s_gate_up).reshape(length, 2, s_hidden)
    shared_hidden = silu_forward(shared_both)
    shared_out = mm("tf,df->td", shared_hidden, s_down_t)
    grad_shared_hidden = mm("td,df->tf", cotangent, s_down_t)
    grad_s_down_t = mm("td,tf->df", cotangent, shared_hidden)
    grad_shared_both = silu_back(shared_both, grad_shared_hidden).reshape(length, -1)
    grad_s_gate_up = mm("td,tf->df", xn_two, grad_shared_both)
    grad_xn_shared = mm("tf,df->td", grad_shared_both, s_gate_up)

    both_parts = mm("sd,df->sf", xin, w_gate_up).reshape(-1, 2, hidden)
    expert_hidden = silu_forward(both_parts)
    expert_out = mm("sf,df->sd", expert_hidden, w_down_t).astype(bf16)
    grad_hidden_expert = mm("sd,df->sf", dye, w_down_t)
    grad_both = silu_back(both_parts, grad_hidden_expert).reshape(-1, 2 * hidden)
    grad_in = mm("sf,df->sd", grad_both, w_gate_up).astype(bf16)
    grad_down_t = mm("sd,sf->df", dye, expert_hidden)
    grad_gate_up = mm("sd,sf->df", xin, grad_both)
    expert_grads = jnp.concatenate([grad_gate_up.astype(bf16), grad_down_t.astype(bf16)], axis=1)
    def home(values):
        blocks = values.reshape(2, experts, half, width)
        blocks = to_members(planes, [blocks[:, j] for j in range(GROUP)])
        return jnp.stack(blocks, axis=1).reshape(experts * capacity, width)

    expert_out, grad_in = home(expert_out), home(grad_in)
    picked = [mm("ts,sd->td", pick[r], expert_out) for r in range(top)]
    moe = sum(gates[:, r : r + 1] * picked[r] for r in range(top))
    grad_xn_moe = mm("ts,sd->td", pick_any, grad_in)
    grad_y = cotangent.astype(f32)
    grad_gates_part = kept_float * jnp.stack(
        [jnp.sum(grad_y * picked[r], axis=-1) for r in range(top)], axis=1
    )
    ffn_part = (moe + shared_out).astype(bf16)
    output = (
        hidden_state + (ffn_part.astype(f32) + other_core(ffn_part).astype(f32))
    ).astype(bf16)
    grad_xn_sum = add_cores(grad_xn_shared + grad_xn_moe)
    grad_gates = add_cores(grad_gates_part)

    grad_probs = jnp.sum(match * grad_gates[:, :, None], axis=1)
    grad_logits = (
        probs * (grad_probs - jnp.sum(probs * grad_probs, axis=-1, keepdims=True))
    ).astype(bf16)
    grad_w_router = mm("td,te->de", xn_two, grad_logits)
    grad_xn_two = grad_xn_sum + mm("te,de->td", grad_logits, w_router)
    grad_norm_two, grad_g_two = norm_back(grad_xn_two, hidden_state, rms_two, g_two)
    grad_hidden = grad_y + grad_norm_two
    grad_attn = grad_hidden.astype(bf16)
    grad_out_t = mm("td,th->dh", grad_attn, mixed)
    grad_mixed = mm("td,dh->th", grad_attn, w_out_t).astype(bf16)
    grad_queries, grad_keys, grad_values = attend_backward(
        queries, keys_all, values_all, segment, scale, grad_mixed, log_totals
    )
    grad_projected = (
        jnp.stack(
            [rotate(grad_queries, cosine, -sine), rotate(grad_keys, cosine, -sine), grad_values],
            axis=1,
        )
        .astype(bf16)
        .reshape(length, 3 * heads_width)
    )
    grad_w_qkv = mm("td,tc->dc", xn_one, grad_projected)
    xn_part = mm("tc,dc->td", grad_projected, w_qkv).astype(bf16)
    grad_xn_one = xn_part.astype(f32) + other_core(xn_part).astype(f32)
    grad_norm_one, grad_g_one = norm_back(grad_xn_one, xfull, rms_one, g_one)
    grad_tokens = grad_hidden + grad_norm_one

    small_grad = jnp.concatenate(
        [grad_g_one[:, None], grad_g_two[:, None], grad_w_router], axis=1
    )
    small_grad = jnp.pad(small_grad, ((0, 0), (0, 128 - small_grad.shape[1])))
    shared_grads = jnp.concatenate(
        [
            g.astype(bf16)
            for g in (grad_w_qkv, grad_out_t, small_grad, grad_s_gate_up, grad_s_down_t)
        ],
        axis=1,
    ).reshape(n, rows, -1)
    mine, mine_expert = reduce_grads(planes, shared_grads, expert_grads.reshape(n, rows, -1))
    small_mine = part(mine, 2)
    return (
        output,
        grad_tokens,
        small_mine[:, 0],
        part(mine, 0).reshape(rows, 3, heads_width),
        part(mine, 1).T,
        small_mine[:, 1],
        small_mine[:, 2 : 2 + experts],
        mine_expert[:, :, : 2 * hidden].reshape(experts, rows, 2, hidden),
        mine_expert[:, :, 2 * hidden :].transpose(0, 2, 1),
        part(mine, 3).reshape(rows, 2, s_hidden),
        part(mine, 4).T,
    )


def solution(mesh):
    def pick(*args):
        experts, rows = args[9].shape[0], args[5].shape[0]
        if experts == GROUP and mesh.shape["dp"] % GROUP == 0 and rows % 16 == 0:
            return local_grouped(mesh.shape["dp"] // GROUP, *args)
        return local_plain(*args)

    return jax.shard_map(
        pick,
        mesh=mesh,
        in_specs=(
            P("dp", None),
            P("dp", None),
            P("dp", None),
            P("dp", None),
            P("dp"),
            P("dp", None, "tensor"),
            P("tensor", "dp"),
            P("dp"),
            P("dp", None),
            P(None, "dp", None, "tensor"),
            P(None, "tensor", "dp"),
            P("dp", None, "tensor"),
            P("tensor", "dp"),
            P("dp", None),
        ),
        out_specs=(
            P("dp", None),
            P("dp", None),
            P("dp"),
            P("dp", None, "tensor"),
            P("tensor", "dp"),
            P("dp"),
            P("dp", None),
            P(None, "dp", None, "tensor"),
            P(None, "tensor", "dp"),
            P("dp", None, "tensor"),
            P("tensor", "dp"),
        ),
        check_vma=False,
    )
```

```python
import functools
import math

import jax
import jax.numpy as jnp
from jax import lax
from jax.experimental import pallas as pl
from jax.experimental.pallas import tpu as pltpu
from jax.sharding import PartitionSpec as P

HD = 64
GROUP = 4
MESH = pl.DeviceIdType.MESH


epsilon = 1e-06


def rms_scale(values):
    return lax.rsqrt(jnp.mean(values * values, axis=-1, keepdims=True) + epsilon)


def rotary(length, head_dim):
    half_dim = head_dim // 2
    position = jnp.arange(length).astype(jnp.float32)[:, None]
    inverse = jnp.exp(
        jnp.arange(half_dim).astype(jnp.float32) * (-2.0 * math.log(10000.0) / head_dim)
    )
    angles = position * inverse[None, :]
    return (jnp.cos(angles)[:, None, :], jnp.sin(angles)[:, None, :])


def rotate(values, cosine, sine):
    half_dim = values.shape[-1] // 2
    first_half = values[..., :half_dim]
    second_half = values[..., half_dim:]
    return jnp.concatenate(
        [first_half * cosine - second_half * sine, second_half * cosine + first_half * sine],
        axis=-1,
    )


def route_slots(pair_ids, rank_order, capacity, experts):
    length = pair_ids.shape[0]
    top_count = pair_ids.shape[1]
    pair_expert = pair_ids.reshape(-1)
    pair_count = pair_expert.shape[0]
    ordered = jnp.zeros((pair_count,), jnp.int32).at[rank_order].set(pair_expert)
    onehot = (ordered[:, None] == jnp.arange(experts, dtype=jnp.int32)[None, :]).astype(jnp.int32)
    running = jnp.cumsum(onehot, axis=0)
    ranked_slot = jnp.sum(running * onehot, axis=1) - 1
    position = ranked_slot[rank_order]
    kept_pair = position < capacity
    slot_index = jnp.where(kept_pair, pair_expert * capacity + position, experts * capacity)
    token_of_pair = jnp.arange(pair_count, dtype=jnp.int32) // top_count
    slot_token = (
        jnp.full((experts * capacity,), length, jnp.int32)
        .at[slot_index]
        .set(token_of_pair, mode="drop")
    )
    return (slot_token, slot_index.reshape(length, top_count), kept_pair.reshape(length, top_count))


def silu_back(both_parts, grad_hidden):
    gate_part = both_parts[..., 0, :]
    up_part = both_parts[..., 1, :]
    sigma = jax.nn.sigmoid(gate_part)
    slope = sigma * (1.0 + gate_part * (1.0 - sigma))
    return jnp.stack(
        [grad_hidden * up_part * slope, grad_hidden * gate_part * sigma], axis=-2
    ).astype(jnp.bfloat16)


def silu_forward(both_parts):
    return (jax.nn.silu(both_parts[..., 0, :]) * both_parts[..., 1, :]).astype(jnp.bfloat16)


def norm_back(grad_norm, values, scale_rows, gain):
    grad_gain = jnp.sum(grad_norm * values * scale_rows, axis=0)
    inner = grad_norm * gain
    grad_values = scale_rows * inner - values * scale_rows**3 * jnp.mean(
        inner * values, axis=-1, keepdims=True
    )
    return (grad_values, grad_gain)


def split_blocks(length):
    block = min(512, length)
    return (block, length // block)


def masked_scores(query_block, keys_all, query_pos, query_seg, segment, scale):
    positions = jnp.arange(keys_all.shape[0])
    scores = (
        jnp.einsum("qhd,khd->hqk", query_block, keys_all, preferred_element_type=jnp.float32)
        * scale
    )
    allowed = (positions[None, :] <= query_pos[:, None]) & (segment[None, :] == query_seg[:, None])
    return jnp.where(allowed[None], scores, -1e30)


def attend_forward(queries, keys_all, values_all, segment, scale):
    length, head_count, head_dim = queries.shape
    block, count_blocks = split_blocks(length)
    positions = jnp.arange(length)

    def one_block(inputs):
        query_block, query_pos, query_seg = inputs
        scores = masked_scores(query_block, keys_all, query_pos, query_seg, segment, scale)
        largest = jnp.max(scores, axis=-1, keepdims=True)
        expo = jnp.exp(scores - largest)
        total = jnp.sum(expo, axis=-1, keepdims=True)
        probs = (expo / total).astype(jnp.bfloat16)
        mixed = jnp.einsum("hqk,khd->qhd", probs, values_all, preferred_element_type=jnp.float32)
        return (mixed.astype(jnp.bfloat16), (largest + jnp.log(total))[..., 0])

    blocks = (
        queries.reshape(count_blocks, block, head_count, head_dim),
        positions.reshape(count_blocks, block),
        segment.reshape(count_blocks, block),
    )
    mixed_all, log_totals = lax.map(one_block, blocks)
    return (mixed_all.reshape(length, head_count * head_dim), log_totals)


def attend_backward(queries, keys_all, values_all, segment, scale, grad_mixed, log_totals):
    length, head_count, head_dim = queries.shape
    block, count_blocks = split_blocks(length)
    positions = jnp.arange(length)

    def one_block(carry, inputs):
        grad_keys, grad_values = carry
        query_block, query_pos, query_seg, grad_block, log_block = inputs
        scores = masked_scores(query_block, keys_all, query_pos, query_seg, segment, scale)
        probs = jnp.exp(scores - log_block[:, :, None])
        grad_probs = jnp.einsum(
            "qhd,khd->hqk", grad_block, values_all, preferred_element_type=jnp.float32
        )
        inner = jnp.sum(probs * grad_probs, axis=-1, keepdims=True)
        grad_scores = (probs * (grad_probs - inner)).astype(jnp.bfloat16)
        grad_query = (
            jnp.einsum("hqk,khd->qhd", grad_scores, keys_all, preferred_element_type=jnp.float32)
            * scale
        )
        grad_keys = (
            grad_keys
            + jnp.einsum(
                "hqk,qhd->khd", grad_scores, query_block, preferred_element_type=jnp.float32
            )
            * scale
        )
        grad_values = grad_values + jnp.einsum(
            "hqk,qhd->khd",
            probs.astype(jnp.bfloat16),
            grad_block,
            preferred_element_type=jnp.float32,
        )
        return ((grad_keys, grad_values), grad_query)

    zeros_kv = jnp.zeros((length, head_count, head_dim), jnp.float32)
    blocks = (
        queries.reshape(count_blocks, block, head_count, head_dim),
        positions.reshape(count_blocks, block),
        segment.reshape(count_blocks, block),
        grad_mixed.reshape(count_blocks, block, head_count, head_dim),
        log_totals,
    )
    (grad_keys, grad_values), grad_queries = lax.scan(one_block, (zeros_kv, zeros_kv), blocks)
    return (grad_queries.reshape(length, head_count, head_dim), grad_keys, grad_values)


def sum_rows(grad, axis, scatter_dimension, tiled):
    part = lax.psum_scatter(
        grad.astype(jnp.bfloat16), axis, scatter_dimension=scatter_dimension, tiled=tiled
    )
    return part.astype(jnp.float32)


def local_plain(
    tokens,
    segment_ids,
    expert_ids,
    slot_order,
    gain_attn,
    qkv_weight,
    out_weight,
    gain_ffn,
    router_weight,
    gate_up,
    down_weight,
    shared_gate_up,
    shared_down,
    cotangent,
):
    g_one, w_qkv, w_out, g_two, w_router, w_gate_up, w_down, s_gate_up, s_down = (
        lax.all_gather(gain_attn, "dp", axis=0, tiled=True),
        lax.all_gather(qkv_weight, "dp", axis=0, tiled=True),
        lax.all_gather(out_weight, "dp", axis=1, tiled=True),
        lax.all_gather(gain_ffn, "dp", axis=0, tiled=True),
        lax.all_gather(router_weight, "dp", axis=0, tiled=True),
        lax.all_gather(gate_up, "dp", axis=1, tiled=True),
        lax.all_gather(down_weight, "dp", axis=2, tiled=True),
        lax.all_gather(shared_gate_up, "dp", axis=0, tiled=True),
        lax.all_gather(shared_down, "dp", axis=1, tiled=True),
    )
    length = tokens.shape[0]
    width = tokens.shape[1]
    experts_count = w_router.shape[1]
    top_count = expert_ids.shape[1]
    capacity = length * top_count // experts_count
    head_dim = HD
    local_heads = w_qkv.shape[2] // head_dim
    scale = head_dim ** (-0.5)
    segment = segment_ids[0]
    slot_token, slot_index, kept_pair = route_slots(
        expert_ids, slot_order[0], capacity, experts_count
    )
    kept_float = kept_pair.astype(jnp.float32)
    slot_valid = slot_token < length
    slot_rows = jnp.minimum(slot_token, length - 1)
    pair_slots = jnp.minimum(slot_index, experts_count * capacity - 1)
    xfull = tokens.astype(jnp.float32)
    rms_one = rms_scale(xfull)
    xn_one = (xfull * rms_one * g_one.astype(jnp.float32)).astype(jnp.bfloat16)
    projected = jnp.einsum("td,dch->tch", xn_one, w_qkv, preferred_element_type=jnp.float32)
    cosine, sine = rotary(length, head_dim)
    queries = rotate(projected[:, 0].reshape(length, local_heads, head_dim), cosine, sine).astype(
        jnp.bfloat16
    )
    keys_all = rotate(projected[:, 1].reshape(length, local_heads, head_dim), cosine, sine).astype(
        jnp.bfloat16
    )
    values_all = projected[:, 2].reshape(length, local_heads, head_dim).astype(jnp.bfloat16)
    mixed, log_totals = attend_forward(queries, keys_all, values_all, segment, scale)
    attn_share = lax.psum_scatter(
        jnp.dot(mixed, w_out, preferred_element_type=jnp.float32),
        "tensor",
        scatter_dimension=1,
        tiled=True,
    )
    attn = lax.all_gather(attn_share, "tensor", axis=1, tiled=True)
    hidden_state = xfull + attn
    rms_two = rms_scale(hidden_state)
    xn_two = (hidden_state * rms_two * g_two.astype(jnp.float32)).astype(jnp.bfloat16)
    logits = jnp.dot(xn_two, w_router, preferred_element_type=jnp.float32)
    probs = jax.nn.softmax(logits, axis=-1)
    gates = jnp.take_along_axis(probs, expert_ids, axis=1) * kept_float
    dispatched = (xn_two[slot_rows] * slot_valid[:, None].astype(jnp.bfloat16)).reshape(
        experts_count, capacity, width
    )
    both_parts = jnp.einsum(
        "ecd,edjf->ecjf", dispatched, w_gate_up, preferred_element_type=jnp.float32
    )
    expert_hidden = silu_forward(both_parts)
    expert_out = jnp.einsum(
        "ecf,efd->ecd", expert_hidden, w_down, preferred_element_type=jnp.float32
    ).reshape(experts_count * capacity, width)
    picked = expert_out[pair_slots]
    moe = jnp.sum(gates[:, :, None] * picked, axis=1)
    shared_both = jnp.einsum("td,djf->tjf", xn_two, s_gate_up, preferred_element_type=jnp.float32)
    shared_hidden = silu_forward(shared_both)
    shared_out = jnp.dot(shared_hidden, s_down, preferred_element_type=jnp.float32)
    ffn_share = lax.psum_scatter(
        (moe + shared_out).astype(jnp.bfloat16), "tensor", scatter_dimension=1, tiled=True
    ).astype(jnp.float32)
    ffn = lax.all_gather(ffn_share.astype(jnp.bfloat16), "tensor", axis=1, tiled=True).astype(
        ffn_share.dtype
    )
    output = (hidden_state + ffn).astype(jnp.bfloat16)
    grad_y = cotangent.astype(jnp.float32)
    grad_shared_hidden = jnp.einsum(
        "td,fd->tf", cotangent, s_down, preferred_element_type=jnp.float32
    )
    grad_s_down = jnp.einsum(
        "tf,td->fd", shared_hidden, cotangent, preferred_element_type=jnp.float32
    )
    grad_shared_both = silu_back(shared_both, grad_shared_hidden)
    grad_s_gate_up = jnp.einsum(
        "td,tjf->djf", xn_two, grad_shared_both, preferred_element_type=jnp.float32
    )
    grad_xn_shared = jnp.einsum(
        "tjf,djf->td", grad_shared_both, s_gate_up, preferred_element_type=jnp.float32
    )
    slot_gate = (
        jnp.zeros((experts_count * capacity,), jnp.float32)
        .at[slot_index.reshape(-1)]
        .set(gates.reshape(-1), mode="drop")
    )
    grad_expert_out = (
        (slot_gate[:, None] * grad_y[slot_rows])
        .astype(jnp.bfloat16)
        .reshape(experts_count, capacity, width)
    )
    grad_gates_part = kept_float * jnp.sum(grad_y[:, None, :] * picked, axis=-1)
    grad_expert_hidden = jnp.einsum(
        "ecd,efd->ecf", grad_expert_out, w_down, preferred_element_type=jnp.float32
    )
    grad_w_down = jnp.einsum(
        "ecf,ecd->efd", expert_hidden, grad_expert_out, preferred_element_type=jnp.float32
    )
    grad_both = silu_back(both_parts, grad_expert_hidden)
    grad_w_gate_up = jnp.einsum(
        "ecd,ecjf->edjf", dispatched, grad_both, preferred_element_type=jnp.float32
    )
    grad_dispatched = jnp.einsum(
        "ecjf,edjf->ecd", grad_both, w_gate_up, preferred_element_type=jnp.float32
    ).reshape(experts_count * capacity, width)
    grad_xn_moe = jnp.sum(kept_float[:, :, None] * grad_dispatched[pair_slots], axis=1)
    grad_xn_part, grad_gates_share = (
        lax.psum_scatter(grad_xn_shared + grad_xn_moe, "tensor", scatter_dimension=1, tiled=True),
        lax.psum_scatter(grad_gates_part, "tensor", scatter_dimension=1, tiled=True),
    )
    grad_xn_sum, grad_gates = (
        lax.all_gather(grad_xn_part, "tensor", axis=1, tiled=True),
        lax.all_gather(grad_gates_share, "tensor", axis=1, tiled=True),
    )
    expert_match = (
        expert_ids[:, :, None] == jnp.arange(experts_count, dtype=jnp.int32)[None, None, :]
    ).astype(jnp.float32)
    grad_probs = jnp.sum(expert_match * grad_gates[:, :, None], axis=1)
    grad_logits = (
        probs * (grad_probs - jnp.sum(probs * grad_probs, axis=-1, keepdims=True))
    ).astype(jnp.bfloat16)
    grad_w_router = jnp.einsum("td,te->de", xn_two, grad_logits, preferred_element_type=jnp.float32)
    grad_xn_two = grad_xn_sum + jnp.einsum(
        "te,de->td", grad_logits, w_router, preferred_element_type=jnp.float32
    )
    grad_norm_two, grad_g_two = norm_back(
        grad_xn_two, hidden_state, rms_two, g_two.astype(jnp.float32)
    )
    grad_hidden = grad_y + grad_norm_two
    grad_attn = grad_hidden.astype(jnp.bfloat16)
    grad_w_out = jnp.einsum("th,td->hd", mixed, grad_attn, preferred_element_type=jnp.float32)
    grad_mixed = jnp.einsum(
        "td,hd->th", grad_attn, w_out, preferred_element_type=jnp.float32
    ).astype(jnp.bfloat16)
    grad_queries, grad_keys, grad_values = attend_backward(
        queries, keys_all, values_all, segment, scale, grad_mixed, log_totals
    )
    grad_projected = (
        jnp.stack(
            [rotate(grad_queries, cosine, -sine), rotate(grad_keys, cosine, -sine), grad_values],
            axis=1,
        )
        .astype(jnp.bfloat16)
        .reshape(length, 3, local_heads * head_dim)
    )
    grad_w_qkv = jnp.einsum(
        "td,tch->dch", xn_one, grad_projected, preferred_element_type=jnp.float32
    )
    grad_xn_share = lax.psum_scatter(
        jnp.einsum("tch,dch->td", grad_projected, w_qkv, preferred_element_type=jnp.float32).astype(
            jnp.bfloat16
        ),
        "tensor",
        scatter_dimension=1,
        tiled=True,
    ).astype(jnp.float32)
    grad_xn_one = lax.all_gather(
        grad_xn_share.astype(jnp.bfloat16), "tensor", axis=1, tiled=True
    ).astype(grad_xn_share.dtype)
    grad_norm_one, grad_g_one = norm_back(grad_xn_one, xfull, rms_one, g_one.astype(jnp.float32))
    grad_tokens = grad_hidden + grad_norm_one
    (
        grad_g_one,
        grad_w_qkv,
        grad_w_out,
        grad_g_two,
        grad_w_router,
        grad_w_gate_up,
        grad_w_down,
        grad_s_gate_up,
        grad_s_down,
    ) = (
        lax.psum_scatter(grad_g_one, "dp", scatter_dimension=0, tiled=True),
        sum_rows(grad_w_qkv, "dp", scatter_dimension=0, tiled=True),
        sum_rows(grad_w_out, "dp", scatter_dimension=1, tiled=True),
        lax.psum_scatter(grad_g_two, "dp", scatter_dimension=0, tiled=True),
        lax.psum_scatter(grad_w_router, "dp", scatter_dimension=0, tiled=True),
        sum_rows(grad_w_gate_up, "dp", scatter_dimension=1, tiled=True),
        sum_rows(grad_w_down, "dp", scatter_dimension=2, tiled=True),
        sum_rows(grad_s_gate_up, "dp", scatter_dimension=0, tiled=True),
        sum_rows(grad_s_down, "dp", scatter_dimension=1, tiled=True),
    )
    return (
        output,
        grad_tokens,
        grad_g_one,
        grad_w_qkv,
        grad_w_out,
        grad_g_two,
        grad_w_router,
        grad_w_gate_up,
        grad_w_down,
        grad_s_gate_up,
        grad_s_down,
    )


class Place:
    def __init__(self, planes):
        d = lax.axis_index("dp")
        self.planes = planes
        self.d, self.c = d, lax.axis_index("tensor")
        self.z, self.p = d // GROUP, lax.rem(d, GROUP)
        bit0, bit1 = lax.rem(self.p, 2), self.p // 2
        flip0, flip1 = 1 - bit0, 1 - bit1
        self.member = [
            self.p,
            flip0 + 2 * bit1,
            bit0 + 2 * flip1,
            flip0 + 2 * flip1,
        ]

    def near(self, j):
        return (self.z * GROUP + self.member[j], self.c)

    def up(self):
        return (self.d + GROUP, self.c)

    def down(self):
        return (self.d - GROUP, self.c)

    def twin(self):
        return (self.d, 1 - self.c)

    def when(self, condition, action):
        pl.when(condition)(action)

    def has_up(self, k=1):
        return self.z + k < self.planes

    def has_down(self, k=1):
        return self.z - k >= 0

    def greet(self):
        barrier = pltpu.get_barrier_semaphore()

        def hello(device):
            pl.semaphore_signal(barrier, inc=1, device_id=device, device_id_type=MESH)

        hello(self.twin())
        for j in range(1, GROUP):
            hello(self.near(j))
        self.when(self.has_up(), lambda: hello(self.up()))
        self.when(self.has_down(), lambda: hello(self.down()))
        line = self.has_up().astype(jnp.int32) + self.has_down().astype(jnp.int32)
        pl.semaphore_wait(barrier, GROUP + line)


def send(source, target, send_sem, recv_sem, device):
    return pltpu.make_async_remote_copy(
        src_ref=source,
        dst_ref=target,
        send_sem=send_sem,
        recv_sem=recv_sem,
        device_id=device,
        device_id_type=MESH,
    )


class Everywhere:
    def __init__(self, at, own, all_blocks, local_sem, recvs, sends):
        self.at, self.own, self.all = at, own, all_blocks
        self.local_sem, self.recvs, self.sends = local_sem, recvs, sends

    def copy(self, block, source, way, device):
        return send(source, self.all.at[block], self.sends.at[way, block], self.recvs.at[block], device)

    def keep(self):
        return pltpu.make_async_copy(self.own, self.all.at[self.at.d], self.local_sem)

    def landed(self, block):
        self.copy(block, self.own, 0, self.at.near(1)).wait_recv()

    def start_line(self):
        at = self.at
        at.when(at.has_up(), lambda: self.copy(at.d, self.own, 0, at.up()).start())
        at.when(at.has_down(), lambda: self.copy(at.d, self.own, 1, at.down()).start())

    def start_plane(self):
        at = self.at
        self.copy(at.d, self.own, 2, at.near(1)).start()
        self.copy(at.d, self.own, 3, at.near(2)).start()
        self.keep().start()

    def spread(self, k):
        at = self.at

        def go(plane, more, way, device_of):
            block = plane * GROUP + at.p
            source = self.all.at[block]
            self.landed(block)
            at.when(more, lambda: self.copy(block, source, way, device_of()).start())
            self.copy(block, source, 2, at.near(1)).start()
            self.copy(block, source, 3, at.near(2)).start()

        at.when(at.has_down(k), lambda: go(at.z - k, at.has_up(), 0, at.up))
        at.when(at.has_up(k), lambda: go(at.z + k, at.has_down(), 1, at.down))

    def cross(self, k):
        at = self.at

        def go(plane):
            first = plane * GROUP + at.member[1]
            second = plane * GROUP + at.member[2]
            even = lax.rem(plane, 2) == 0
            self.landed(first)
            at.when(even, lambda: self.copy(first, self.all.at[first], 3, at.near(2)).start())
            self.landed(second)
            at.when(
                jnp.logical_not(even),
                lambda: self.copy(second, self.all.at[second], 2, at.near(1)).start(),
            )

        if k == 0:
            go(at.z)
        else:
            at.when(at.has_down(k), lambda: go(at.z - k))
            at.when(at.has_up(k), lambda: go(at.z + k))

    def diagonal(self):
        for plane in range(self.at.planes):
            self.landed(plane * GROUP + self.at.member[3])
        self.keep().wait()

    def sent(self):
        at = self.at
        for plane in range(at.planes):
            block = plane * GROUP + at.p
            self.copy(block, self.own, 2, at.near(1)).wait_send()
            self.copy(block, self.own, 3, at.near(2)).wait_send()
            if plane % 2 == 0:
                self.copy(plane * GROUP + at.member[1], self.own, 3, at.near(2)).wait_send()
            else:
                self.copy(plane * GROUP + at.member[2], self.own, 2, at.near(1)).wait_send()

            def gone(way, device_of):
                self.copy(block, self.own, way, device_of()).wait_send()

            at.when((at.z >= plane) & at.has_up(), lambda: gone(0, at.up))
            at.when((at.z <= plane) & at.has_down(), lambda: gone(1, at.down))


class Experts:
    def __init__(self, at, own, all_blocks, local_sem, recvs, sends):
        self.at, self.own, self.all = at, own, all_blocks
        self.local_sem, self.recvs, self.sends = local_sem, recvs, sends

    def line(self, block, source, way, device):
        return send(source, self.all.at[block], self.sends.at[way, block], self.recvs.at[block], device)

    def across(self, j):
        at = self.at
        return send(
            self.own.at[at.member[j]],
            self.all.at[at.d],
            self.sends.at[1 + j, at.d],
            self.recvs.at[at.d],
            at.near(j),
        )

    def keep(self):
        return pltpu.make_async_copy(self.own.at[self.at.p], self.all.at[self.at.d], self.local_sem)

    def start_plane(self):
        for j in range(1, GROUP):
            self.across(j).start()
        self.keep().start()

    def start_line(self):
        at = self.at
        source = self.own.at[at.p]
        at.when(at.has_up(), lambda: self.line(at.d, source, 0, at.up()).start())
        at.when(at.has_down(), lambda: self.line(at.d, source, 1, at.down()).start())

    def landed(self, block):
        self.line(block, self.own.at[0], 0, self.at.near(1)).wait_recv()

    def plane_step(self, j):
        at = self.at
        block = at.z * GROUP + at.member[j]
        source = self.all.at[block]
        self.landed(block)
        at.when(at.has_up(), lambda: self.line(block, source, 0, at.up()).start())
        at.when(at.has_down(), lambda: self.line(block, source, 1, at.down()).start())

    def line_step(self, k, j):
        at = self.at

        def go(plane, more, way, device_of):
            block = plane * GROUP + at.member[j]
            self.landed(block)
            at.when(more, lambda: self.line(block, self.all.at[block], way, device_of()).start())

        at.when(at.has_down(k), lambda: go(at.z - k, at.has_up(), 0, at.up))
        at.when(at.has_up(k), lambda: go(at.z + k, at.has_down(), 1, at.down))

    def sent(self):
        at = self.at
        self.keep().wait()
        for j in range(1, GROUP):
            self.across(j).wait_send()
        for plane in range(at.planes):

            def gone(way, device_of):
                for q in range(GROUP):
                    self.line(plane * GROUP + q, self.own.at[0], way, device_of()).wait_send()

            at.when((at.z >= plane) & at.has_up(), lambda: gone(0, at.up))
            at.when((at.z <= plane) & at.has_down(), lambda: gone(1, at.down))


def dot_nn(a, b):
    return jnp.dot(a, b, preferred_element_type=jnp.float32)


def dot_nt(a, b):
    return lax.dot_general(a, b, (((1,), (1,)), ((), ())), preferred_element_type=jnp.float32)


def dot_tn(a, b):
    return lax.dot_general(a, b, (((0,), (0,)), ((), ())), preferred_element_type=jnp.float32)


def lanes(count=128):
    return lax.broadcasted_iota(jnp.int32, (1, count), 1)


def turn(values, cosine, sine):
    half = HD // 2
    other = jnp.where(
        lax.rem(lanes(), HD) < half,
        -pltpu.roll(values, 2 * HD - half, 1),
        pltpu.roll(values, half, 1),
    )
    return values * cosine + other * sine


def blocks_of(ref, start, stop):
    block = ref[:, :, start:stop]
    return block.reshape(block.shape[0] * block.shape[1], stop - start)


def attention_blocks(length):
    size = length // 2
    return [(i * size, (i + 1) * size) for i in range(2)]


def forward_kernel(
    planes,
    experts,
    x_ref,
    cot_ref,
    seg_col,
    seg_row,
    ids_ref,
    order_ref,
    ids_t_ref,
    order_t_ref,
    cos_ref,
    sin_ref,
    a_own,
    s_own,
    e_own,
    a_all,
    s_all,
    e_all,
    q_ref,
    k_ref,
    v_ref,
    o_ref,
    lse_ref,
    h_ref,
    xa_ref,
    xf_ref,
    probs_ref,
    pair_ref,
    placed_ref,
    arrived_ref,
    bias_ref,
    mine_ref,
    theirs_ref,
    local_sem,
    a_recv,
    a_send,
    s_recv,
    s_send,
    e_recv,
    e_send,
    twin_sem,
    token_recv,
    token_send,
):
    f32, bf16 = jnp.float32, jnp.bfloat16
    at = Place(planes)
    length, width = x_ref.shape
    heads_width = q_ref.shape[1]
    capacity = length * ids_ref.shape[1] // experts
    half = capacity // 2
    attn = Everywhere(at, a_own, a_all, local_sem.at[0], a_recv, a_send)
    shared = Everywhere(at, s_own, s_all, local_sem.at[1], s_recv, s_send)
    expert = Experts(at, e_own, e_all, local_sem.at[2], e_recv, e_send)

    at.greet()
    attn.start_line()
    attn.start_plane()
    expert.start_plane()
    shared.start_line()
    expert.start_line()

    todo = []
    for j in range(1, GROUP):
        todo.append(functools.partial(expert.plane_step, j))
    todo.append(shared.start_plane)
    for k in range(1, planes):
        todo.append(functools.partial(shared.spread, k))
        for j in range(GROUP):
            todo.append(functools.partial(expert.line_step, k, j))
        todo.append(functools.partial(shared.cross, k - 1))
    todo.append(functools.partial(shared.cross, planes - 1))
    todo.reverse()

    def tick(count=1):
        for _ in range(count):
            if todo:
                todo.pop()()

    for start, stop in attention_blocks(length):
        rows = lax.broadcasted_iota(jnp.int32, (stop - start, stop), 0) + start
        columns = lax.broadcasted_iota(jnp.int32, (stop - start, stop), 1)
        allowed = (columns <= rows) & (seg_col[start:stop, :] == seg_row[:, :stop])
        bias_ref[start:stop, :stop] = jnp.where(allowed, 0.0, -1e30)

    def slot_of(expert_id, position):
        which = position // half
        apart = which + at.c - 2 * which * at.c
        bit0, bit1 = lax.rem(expert_id, 2), expert_id // 2
        p0, p1 = lax.rem(at.p, 2), at.p // 2
        distance = (bit0 + p0 - 2 * bit0 * p0) + 2 * (bit1 + p1 - 2 * bit1 * p1)
        slot = apart * (experts * half) + distance * half + lax.rem(position, half)
        return jnp.where(position < capacity, slot, -1)

    slot_cols, slot_rows = [], []
    top = ids_ref.shape[1]
    for r in range(top):
        count_col = jnp.zeros((length, 1), jnp.int32)
        count_row = jnp.zeros((1, length), jnp.int32)
        for other in range(top):
            first = (ids_t_ref[other : other + 1, :] == ids_ref[:, r : r + 1]) & (
                order_t_ref[other : other + 1, :] < order_ref[:, r : r + 1]
            )
            count_col += jnp.sum(first.astype(jnp.int32), axis=1, keepdims=True)
            first = (ids_ref[:, other : other + 1] == ids_t_ref[r : r + 1, :]) & (
                order_ref[:, other : other + 1] < order_t_ref[r : r + 1, :]
            )
            count_row += jnp.sum(first.astype(jnp.int32), axis=0, keepdims=True)
        slot_cols.append(slot_of(ids_ref[:, r : r + 1], count_col))
        slot_rows.append(slot_of(ids_t_ref[r : r + 1, :], count_row))

    attn.spread(1)
    attn.cross(0)
    for k in range(2, planes):
        attn.spread(k)
        attn.cross(k - 1)
        tick()
    attn.cross(planes - 1)
    attn.diagonal()

    small = blocks_of(a_all, 4 * heads_width, 4 * heads_width + 128)
    small_rows = small.astype(f32).T
    g_one, g_two = small_rows[0:1, :], small_rows[1:2, :]
    x = x_ref[...].astype(f32)
    rms = lax.rsqrt(jnp.mean(x * x, axis=-1, keepdims=True) + epsilon)
    xa_ref[...] = (x * rms * g_one).astype(bf16)
    tick()
    cosine, sine = cos_ref[...], sin_ref[...]
    pairs = heads_width // 128
    for i, ref in enumerate((q_ref, k_ref)):
        part = dot_nn(xa_ref[...], blocks_of(a_all, i * heads_width, (i + 1) * heads_width))
        for g in range(pairs):
            columns = slice(128 * g, 128 * (g + 1))
            ref[:, columns] = turn(part[:, columns], cosine, sine).astype(bf16)
        tick()
    v_ref[...] = dot_nn(
        xa_ref[...], blocks_of(a_all, 2 * heads_width, 3 * heads_width)
    ).astype(bf16)
    tick()

    scale = HD ** (-0.5)
    for start, stop in attention_blocks(length):
        logs = jnp.zeros((stop - start, 128), f32)
        for g in range(pairs):
            columns = slice(128 * g, 128 * (g + 1))
            queries = q_ref[start:stop, columns]
            keys, values = k_ref[:stop, columns], v_ref[:stop, columns]
            mixed = []
            for i in range(2):
                one = jnp.where(lanes() // HD == i, queries, jnp.zeros_like(queries))
                scores = dot_nt(one, keys) * scale + bias_ref[start:stop, :stop]
                largest = jnp.max(scores, axis=-1, keepdims=True)
                expo = jnp.exp(scores - largest)
                total = jnp.sum(expo, axis=-1, keepdims=True)
                weights = (expo * (1.0 / total)).astype(bf16)
                mixed.append(dot_nn(weights, values))
                logs = jnp.where(lanes() == 2 * g + i, largest + jnp.log(total), logs)
            o_ref[start:stop, columns] = jnp.where(lanes() < HD, mixed[0], mixed[1]).astype(bf16)
            tick(2)
        lse_ref[start:stop, :] = logs

    mine_ref[...] = dot_nt(o_ref[...], blocks_of(a_all, 3 * heads_width, 4 * heads_width))
    swap = send(mine_ref, theirs_ref, twin_sem.at[0], twin_sem.at[1], at.twin())
    swap.start()
    tick(2)
    swap.wait_recv()
    h = x_ref[...].astype(f32) + (mine_ref[...] + theirs_ref[...])
    h_ref[...] = h
    rms = lax.rsqrt(jnp.mean(h * h, axis=-1, keepdims=True) + epsilon)
    xf_ref[...] = (h * rms * g_two).astype(bf16)

    is_expert = (lanes() >= 2) & (lanes() < 2 + experts)
    logits = jnp.where(is_expert, dot_nn(xf_ref[...], small), -1e30)
    expo = jnp.exp(logits - jnp.max(logits, axis=-1, keepdims=True))
    probs = expo / jnp.sum(expo, axis=-1, keepdims=True)
    probs_ref[...] = probs
    packed = jnp.zeros((length, 128), f32)
    for r in range(top):
        chosen = lanes() == ids_ref[:, r : r + 1] + 2
        gate = jnp.sum(jnp.where(chosen, probs, 0.0), axis=-1, keepdims=True)
        gate = jnp.where(slot_cols[r] >= 0, gate, 0.0)
        packed = jnp.where(lanes() == r, gate, packed)
        packed = jnp.where(lanes() == top + r, slot_cols[r].astype(f32), packed)
    pair_ref[...] = packed
    gate_rows = packed.T
    tick(2)

    def outgoing(j):
        return send(
            placed_ref.at[j], arrived_ref.at[0, j], token_send.at[j], token_recv.at[j], at.near(j)
        )

    for j in range(experts):
        index = lax.broadcasted_iota(jnp.int32, (half, 1), 0) + j * half
        pick = [slot_rows[r] == index for r in range(top)]
        slot_gate = sum(
            jnp.sum(jnp.where(pick[r], gate_rows[r : r + 1, :], 0.0), axis=1, keepdims=True)
            for r in range(top)
        )
        pick = sum(p.astype(f32) for p in pick).astype(bf16)
        target = arrived_ref.at[0, 0] if j == 0 else placed_ref.at[j]
        target[:, :width] = dot_nn(pick, xf_ref[...]).astype(bf16)
        target[:, width:] = (dot_nn(pick, cot_ref[...]) * slot_gate).astype(bf16)
        if j:
            outgoing(j).start()
        tick()
    for j in range(1, experts):
        outgoing(j).wait_recv()
        tick()
    across = send(arrived_ref.at[0], arrived_ref.at[1], twin_sem.at[2], twin_sem.at[3], at.twin())
    across.start()

    tick(len(todo))
    shared.diagonal()
    across.wait_recv()
    across.wait_send()
    swap.wait_send()
    for j in range(1, experts):
        outgoing(j).wait_send()
    attn.sent()
    shared.sent()
    expert.sent()


def forward_pass(planes, experts, inputs, own, heads_width):
    n = planes * GROUP
    bf16, f32, dma = jnp.bfloat16, jnp.float32, pltpu.SemaphoreType.DMA
    length, width = inputs[0].shape
    half = length * inputs[4].shape[1] // experts // 2
    vmem, anywhere = pl.BlockSpec(memory_space=pltpu.VMEM), pl.BlockSpec(memory_space=pl.ANY)
    shape = jax.ShapeDtypeStruct
    return pl.pallas_call(
        functools.partial(forward_kernel, planes, experts),
        out_shape=(
            shape((n,) + own[0].shape, bf16),
            shape((n,) + own[1].shape, bf16),
            shape((n,) + own[2].shape[1:], bf16),
            shape((length, heads_width), bf16),
            shape((length, heads_width), bf16),
            shape((length, heads_width), bf16),
            shape((length, heads_width), bf16),
            shape((length, 128), f32),
            shape((length, width), f32),
            shape((length, width), bf16),
            shape((length, width), bf16),
            shape((length, 128), f32),
            shape((length, 128), f32),
            shape((experts, half, 2 * width), bf16),
            shape((2, experts, half, 2 * width), bf16),
        ),
        in_specs=[vmem] * len(inputs) + [anywhere] * 3,
        out_specs=(vmem, anywhere, anywhere) + (vmem,) * 12,
        scratch_shapes=[
            pltpu.VMEM((length, length), f32),
            pltpu.VMEM((length, width), f32),
            pltpu.VMEM((length, width), f32),
            dma((3,)),
            dma((n,)),
            dma((4, n)),
            dma((n,)),
            dma((4, n)),
            dma((n,)),
            dma((1 + GROUP, n)),
            dma((4,)),
            dma((GROUP,)),
            dma((GROUP,)),
        ],
        compiler_params=pltpu.CompilerParams(
            collective_id=0, has_side_effects=True, vmem_limit_bytes=48 << 20
        ),
    )(*inputs, *own)


class PlaneSum:
    def __init__(self, at, own, one, two, came, one_sems, two_sems, line_sems):
        self.at, self.own, self.one, self.two, self.came = at, own, one, two, came
        self.one_sems, self.two_sems, self.line_sems = one_sems, two_sems, line_sems

    def one_copy(self, plane, i, even):
        at = self.at
        j = 1 if even else 2
        target = at.member[3] if i else at.member[j]
        return send(
            self.own.at[plane * GROUP + target],
            self.one.at[plane, i],
            self.one_sems.at[0, plane, i],
            self.one_sems.at[1, plane, i],
            at.near(j),
        )

    def two_copy(self, plane, even):
        return send(
            self.one.at[plane, 1],
            self.two.at[plane],
            self.two_sems.at[0, plane],
            self.two_sems.at[1, plane],
            self.at.near(2 if even else 1),
        )

    def by_parity(self, plane, action):
        even = lax.rem(plane, 2) == 0
        self.at.when(even, lambda: action(True))
        self.at.when(jnp.logical_not(even), lambda: action(False))

    def line(self, source, plane, way, here=False):
        at, sems = self.at, self.line_sems
        slot, device = plane, at.up()
        if way:
            slot = jnp.where(plane == (at.z if here else at.z - 1), at.planes, plane)
            device = at.down()
        return send(
            source, self.came.at[slot], sems.at[0, way, plane], sems.at[1, way, plane], device
        )

    def both_ways(self, action, k):
        at = self.at
        if k == 0:
            action(at.z, 0)
            return
        at.when(at.has_up(k), lambda: action(at.z + k, 0))
        at.when(at.has_down(k), lambda: action(at.z - k, 1))

    def start(self, k):
        def go(plane, way):
            def pair(even):
                self.one_copy(plane, 1, even).start()
                self.one_copy(plane, 0, even).start()

            self.by_parity(plane, pair)

        self.both_ways(go, k)

    def middle(self, k):
        f32 = jnp.float32

        def go(plane, way):
            def stage(even):
                at, one = self.at, self.one
                other = plane * GROUP + (at.member[2] if even else at.member[1])
                self.one_copy(plane, 1, even).wait_recv()
                one[plane, 1] = (one[plane, 1].astype(f32) + self.own[other].astype(f32)).astype(
                    one.dtype
                )
                self.two_copy(plane, even).start()

            self.by_parity(plane, stage)

        self.both_ways(go, k)

    def finish_plane(self, plane):
        f32 = jnp.float32

        def stage(even):
            mine = plane * GROUP + self.at.p
            self.one_copy(plane, 0, even).wait_recv()
            self.two_copy(plane, even).wait_recv()
            self.two[plane] = (
                self.two[plane].astype(f32)
                + self.one[plane, 0].astype(f32)
                + self.own[mine].astype(f32)
            ).astype(self.two.dtype)

        self.by_parity(plane, stage)

    def step(self, k):
        f32 = jnp.float32

        def go(plane, way):
            at = self.at
            self.finish_plane(plane)
            behind = at.has_down() if way == 0 else at.has_up()
            held = self.came

            def add():
                self.line(self.two.at[plane], plane, way, True).wait_recv()
                held[plane] = (held[plane].astype(f32) + self.two[plane].astype(f32)).astype(
                    held.dtype
                )
                self.line(held.at[plane], plane, way).start()

            at.when(behind, add)
            at.when(
                jnp.logical_not(behind), lambda: self.line(self.two.at[plane], plane, way).start()
            )

        self.both_ways(go, k)

    def total(self, out):
        at, f32 = self.at, jnp.float32
        z = at.z
        self.finish_plane(z)
        at.when(at.has_down(), lambda: self.line(self.two.at[z], z, 0, True).wait_recv())
        at.when(at.has_up(), lambda: self.line(self.two.at[z], z, 1, True).wait_recv())
        low = jnp.where(at.has_down(), self.came[z].astype(f32), 0.0)
        high = jnp.where(at.has_up(), self.came[at.planes].astype(f32), 0.0)
        out[...] = (self.two[z].astype(f32) + low + high).astype(out.dtype)

    def sent(self):
        at = self.at
        for plane in range(at.planes):
            even = plane % 2 == 0
            self.one_copy(plane, 0, even).wait_send()
            self.one_copy(plane, 1, even).wait_send()
            self.two_copy(plane, even).wait_send()
            at.when(at.z < plane, lambda: self.line(self.two.at[plane], plane, 0).wait_send())
            at.when(at.z > plane, lambda: self.line(self.two.at[plane], plane, 1).wait_send())


class LineSum:
    def __init__(self, at, own, came, out, line_sems, last_sems):
        self.at, self.own, self.came, self.out = at, own, came, out
        self.line_sems, self.last_sems = line_sems, last_sems

    def hop(self, source, plane, j, way, here=False):
        at = self.at
        block = plane * GROUP + at.member[j]
        if way == 0:
            slot, device = block, at.up()
        else:
            end = at.z if here else at.z - 1
            slot = jnp.where(plane == end, at.planes, plane) * GROUP + at.member[j]
            device = at.down()
        sems = self.line_sems
        return send(
            source, self.came.at[slot], sems.at[0, way, block], sems.at[1, way, block], device
        )

    def start_plane(self, plane):
        at = self.at

        def go(way):
            for j in range(GROUP):
                self.hop(self.own.at[plane * GROUP + at.member[j]], plane, j, way).start()

        at.when(jnp.logical_not(at.has_down()) & (plane != at.z), lambda: go(0))
        at.when(jnp.logical_not(at.has_up()) & (plane != at.z), lambda: go(1))

    def step(self, k, j):
        at, f32 = self.at, jnp.float32

        def go(plane, way):
            block = plane * GROUP + at.member[j]
            self.hop(self.own.at[block], plane, j, way, True).wait_recv()
            self.came[block] = (
                self.came[block].astype(f32) + self.own[block].astype(f32)
            ).astype(self.came.dtype)
            self.hop(self.came.at[block], plane, j, way).start()

        at.when(at.has_up(k) & at.has_down(), lambda: go(at.z + k, 0))
        at.when(at.has_down(k) & at.has_up(), lambda: go(at.z - k, 1))

    def last_copy(self, source, j, here=False):
        at = self.at
        return send(
            source,
            self.out.at[at.member[j] if here else at.p],
            self.last_sems.at[0, j],
            self.last_sems.at[1, j],
            at.near(j),
        )

    def total(self, j):
        at, f32, out = self.at, jnp.float32, self.out
        block = at.z * GROUP + at.member[j]
        spare = at.planes * GROUP + at.member[j]
        at.when(at.has_down(), lambda: self.hop(self.own.at[block], at.z, j, 0, True).wait_recv())
        at.when(at.has_up(), lambda: self.hop(self.own.at[block], at.z, j, 1, True).wait_recv())
        low = jnp.where(at.has_down(), self.came[block].astype(f32), 0.0)
        high = jnp.where(at.has_up(), self.came[spare].astype(f32), 0.0)
        total = (self.own[block].astype(f32) + low + high).astype(out.dtype)
        if j == 0:
            out[at.p] = total
        else:
            self.came[block] = total
            self.last_copy(self.came.at[block], j).start()

    def arrive(self, j):
        self.last_copy(self.own.at[0], j, True).wait_recv()

    def sent(self):
        at = self.at
        for j in range(1, GROUP):
            self.last_copy(self.own.at[0], j).wait_send()
        for plane in range(at.planes):

            def gone(way):
                for j in range(GROUP):
                    self.hop(self.own.at[0], plane, j, way).wait_send()

            at.when(at.z < plane, lambda: gone(0))
            at.when(at.z > plane, lambda: gone(1))


def branch(x_of, dy_of, rows, weights, act, y_acc, dx_acc):
    f32, bf16 = jnp.float32, jnp.bfloat16
    hidden = weights.shape[2] // 3
    size, count = 256, rows.stop - rows.start
    step = min(count, 256)

    def body(i, carry):
        offset = pl.multiple_of(i * size, size)

        def weight(part):
            block = weights[:, :, pl.ds(pl.multiple_of(part * hidden + offset, size), size)]
            return block.reshape(block.shape[0] * block.shape[1], size)

        for start in range(0, count, step):
            some = slice(start, start + step)

            def keep(part, values):
                columns = pl.ds(pl.multiple_of(part * hidden + offset, size), size)
                act[rows.start + start : rows.start + start + step, columns] = values

            g, u = dot_nn(x_of(some), weight(0)), dot_nn(x_of(some), weight(1))
            grad = dot_nn(dy_of(some), weight(2))
            sigma = 1.0 / (1.0 + jnp.exp(-g))
            silu = g * sigma
            eh = (silu * u).astype(bf16)
            dg = (grad * u * (sigma * (1.0 + g * (1.0 - sigma)))).astype(bf16)
            du = (grad * silu).astype(bf16)
            keep(0, dg)
            keep(1, du)
            keep(2, eh)
            y_acc[some, :] += dot_nt(eh, weight(2))
            dx_acc[some, :] += dot_nt(dg, weight(0)) + dot_nt(du, weight(1))
        return carry

    y_acc[...] = jnp.zeros(y_acc.shape, f32)
    dx_acc[...] = jnp.zeros(dx_acc.shape, f32)
    lax.fori_loop(0, hidden // size, body, 0)


def weight_grads(plane, planes, count, x_t, dy_t, act, grads):
    width, bf16 = x_t.shape[0], jnp.bfloat16
    rows = width // planes
    hidden = act.shape[1] // 3
    size = 512
    features = pl.ds(pl.multiple_of(plane * rows, 16), rows)
    for part in range(3 * hidden // size):
        columns = slice(part * size, (part + 1) * size)
        left = x_t if part * size < 2 * hidden else dy_t
        block = dot_nn(left[features, :count], act[:count, columns]).astype(bf16)
        grads[pl.ds(plane * GROUP, GROUP), :, columns] = block.reshape(
            GROUP, rows // GROUP, size
        )


def norm_back_rows(grad, values, gain):
    rms = lax.rsqrt(jnp.mean(values * values, axis=-1, keepdims=True) + epsilon)
    grad_gain = jnp.sum(grad * values * rms, axis=0, keepdims=True)
    inner = grad * gain
    grad_values = rms * inner - values * (rms * rms * rms) * jnp.mean(
        inner * values, axis=-1, keepdims=True
    )
    return grad_values, grad_gain


def backward_kernel(
    planes,
    experts,
    x_ref,
    cot_ref,
    seg_col,
    seg_row,
    ids_ref,
    cos_ref,
    sin_ref,
    q_ref,
    k_ref,
    v_ref,
    o_ref,
    lse_ref,
    xf_ref,
    probs_ref,
    pair_ref,
    a_all,
    s_all,
    e_all,
    arrived_ref,
    h_ref,
    out_ref,
    gx_ref,
    a_out,
    s_out,
    e_out,
    aw,
    sw,
    ew,
    tok,
    home,
    act,
    x_t,
    dy_t,
    y_acc,
    dx_acc,
    ffn_theirs,
    dx_theirs,
    gate_mine,
    gate_theirs,
    part_theirs,
    dk_acc,
    dv_acc,
    a_one,
    a_two,
    a_came,
    s_one,
    s_two,
    s_came,
    e_came,
    load_sem,
    a_one_sems,
    a_two_sems,
    a_line_sems,
    s_one_sems,
    s_two_sems,
    s_line_sems,
    e_line_sems,
    e_last_sems,
    home_sems,
    twin_sems,
):
    f32, bf16 = jnp.float32, jnp.bfloat16
    at = Place(planes)
    length, width = x_ref.shape
    heads_width = q_ref.shape[1]
    half = tok.shape[2]
    top = ids_ref.shape[1]
    expert = LineSum(at, ew, e_came, e_out, e_line_sems, e_last_sems)
    shared = PlaneSum(
        at, sw, s_one, s_two, s_came, s_one_sems, s_two_sems, s_line_sems
    )
    attn = PlaneSum(at, aw, a_one, a_two, a_came, a_one_sems, a_two_sems, a_line_sems)
    loads = [
        pltpu.make_async_copy(e_all, ew, load_sem.at[0]),
        pltpu.make_async_copy(arrived_ref, tok, load_sem.at[1]),
        pltpu.make_async_copy(s_all, sw, load_sem.at[2]),
        pltpu.make_async_copy(a_all, aw, load_sem.at[3]),
        pltpu.make_async_copy(h_ref, gx_ref, load_sem.at[4]),
    ]
    ffn_mine = act.at[length:, :width]
    part_mine = act.at[length:, width : 2 * width]
    dx_mine = act.at[length:, 2 * width : 3 * width]
    dproj = act.at[:length, 2 * width : 2 * width + 3 * heads_width]
    step = min(length, 256)
    chunks = [slice(i, i + step) for i in range(0, length, step)]
    for load in loads:
        load.start()
    at.greet()
    loads[0].wait()
    loads[1].wait()

    def home_copy(t, j):
        return send(
            tok.at[t, j], home.at[t, j], home_sems.at[0, t, j], home_sems.at[1, t, j], at.near(j)
        )

    count = experts * half
    for t in range(2):
        rows = slice(t * count, (t + 1) * count)

        def x_of(some):
            some = slice(some.start // half, some.stop // half)
            return tok[t, some, :, :width].reshape(-1, width)

        def dy_of(some):
            some = slice(some.start // half, some.stop // half)
            return tok[t, some, :, width:].reshape(-1, width)

        for some in chunks:
            x_t[:, rows.start + some.start : rows.start + some.stop] = x_of(some).T
            dy_t[:, rows.start + some.start : rows.start + some.stop] = dy_of(some).T
        branch(x_of, dy_of, rows, ew, act, y_acc, dx_acc)
        for j in range(experts):
            some = slice(j * half, (j + 1) * half)
            tok[t, j, :, :width] = y_acc[some, :].astype(bf16)
            tok[t, j, :, width:] = dx_acc[some, :].astype(bf16)
        home[t, 0] = tok[t, 0]
        for j in range(1, experts):
            home_copy(t, j).start()

    def grads_of(i, carry):
        plane = jnp.where(at.z * 2 < planes, planes - 1 - i, i)
        weight_grads(plane, planes, 2 * count, x_t, dy_t, act, ew)
        expert.start_plane(plane)
        return carry

    lax.fori_loop(0, planes, grads_of, 0)

    todo = []
    extra = [functools.partial(shared.middle, k) for k in range(planes - 3, -1, -1)]
    extra += [functools.partial(shared.step, k) for k in range(planes - 1, 0, -1)]
    for k in range(planes - 2, 0, -1):
        for j in range(GROUP):
            todo.append(functools.partial(expert.step, k, j))
            if k == 1 and extra:
                todo.append(extra.pop(0))
    todo += extra
    for j in range(GROUP):
        todo.append(functools.partial(expert.total, j))
    todo.reverse()

    def tick(count=1):
        for _ in range(count):
            if todo:
                todo.pop()()

    loads[2].wait()
    rows = slice(0, length)
    for some in chunks:
        x_t[:, some] = xf_ref[some, :].T
        dy_t[:, some] = cot_ref[some, :].T
    branch(lambda some: xf_ref[some, :], lambda some: cot_ref[some, :], rows, sw, act, y_acc, dx_acc)
    tick()

    def shared_grads(i, carry):
        weight_grads(i, planes, length, x_t, dy_t, act, sw)
        return carry

    lax.fori_loop(0, planes, shared_grads, 0)
    for k in range(planes - 1, -1, -1):
        shared.start(k)
    tick()

    for t in range(2):
        for j in range(1, experts):
            home_copy(t, j).wait_recv()
    for rows in chunks:
        y, dx = y_acc[rows, :], dx_acc[rows, :]
        gate = jnp.zeros((step, 128), f32)
        dy = cot_ref[rows, :].astype(f32)
        for t in range(2):
            index = lax.broadcasted_iota(jnp.int32, (1, count), 1) + t * count
            slot = [
                (pair_ref[rows, top + r : top + r + 1].astype(jnp.int32) == index).astype(f32)
                for r in range(top)
            ]
            for r in range(top):
                part = dot_nn(slot[r].astype(bf16), home[t, :, :, :width].reshape(count, width))
                y += pair_ref[rows, r : r + 1] * part
                grad = jnp.sum(dy * part, axis=-1, keepdims=True)
                gate += jnp.where(lanes() == ids_ref[rows, r : r + 1] + 2, grad, 0.0)
            dx += dot_nn(sum(slot).astype(bf16), home[t, :, :, width:].reshape(count, width))
        ffn_mine[rows, :] = y.astype(bf16)
        dx_mine[rows, :] = dx.astype(bf16)
        gate_mine[rows, :] = gate
    swaps = [
        send(mine, theirs, twin_sems.at[0, i], twin_sems.at[1, i], at.twin())
        for i, (mine, theirs) in enumerate(
            ((dx_mine, dx_theirs), (gate_mine, gate_theirs), (ffn_mine, ffn_theirs))
        )
    ]
    for swap in swaps:
        swap.start()
    shared.middle(planes - 1)
    tick()
    swaps[0].wait_recv()
    swaps[1].wait_recv()

    loads[3].wait()
    loads[4].wait()
    small = blocks_of(aw, 4 * heads_width, 4 * heads_width + 128)
    small_rows = small.astype(f32).T
    g_one, g_two = small_rows[0:1, :], small_rows[1:2, :]
    swaps[2].wait_recv()
    grad_g_two = jnp.zeros((1, width), f32)
    grad_small = jnp.zeros((width, 128), f32)
    for rows in chunks:
        probs = probs_ref[rows, :]
        grad_probs = gate_mine[rows, :] + gate_theirs[rows, :]
        grad_logits = (
            probs * (grad_probs - jnp.sum(probs * grad_probs, axis=-1, keepdims=True))
        ).astype(bf16)
        grad_small += dot_nn(x_t[:, rows], grad_logits)
        grad_xf = dx_mine[rows, :].astype(f32) + dx_theirs[rows, :].astype(f32)
        grad_xf += dot_nt(grad_logits, small)
        h = gx_ref[rows, :]
        out_ref[rows, :] = (
            h + (ffn_mine[rows, :].astype(f32) + ffn_theirs[rows, :].astype(f32))
        ).astype(bf16)
        grad_h, grad_gain = norm_back_rows(grad_xf, h, g_two)
        grad_g_two += grad_gain
        grad_h = cot_ref[rows, :].astype(f32) + grad_h
        gx_ref[rows, :] = grad_h
        dy_t[:, rows] = grad_h.astype(bf16).T
        act[rows, :heads_width] = dot_nn(
            grad_h.astype(bf16), blocks_of(aw, 3 * heads_width, 4 * heads_width)
        ).astype(bf16)
    for rows in chunks:
        x = x_ref[rows, :].astype(f32)
        rms = lax.rsqrt(jnp.mean(x * x, axis=-1, keepdims=True) + epsilon)
        x_t[:, rows] = (x * rms * g_one).astype(bf16).T
    tick()

    def to_grads(start, columns, left, right):
        blocks = aw.shape[0]
        for i in range(0, blocks, blocks // 4):
            some = slice(i, i + blocks // 4)
            features = slice(i * aw.shape[1], (i + blocks // 4) * aw.shape[1])
            block = dot_nn(left[features, :length], right())
            aw[some, :, start : start + columns] = block.astype(bf16).reshape(
                blocks // 4, aw.shape[1], columns
            )

    to_grads(3 * heads_width, heads_width, dy_t, lambda: o_ref[...])
    shared.middle(planes - 2)
    cosine, sine = cos_ref[...], sin_ref[...]
    scale = HD ** (-0.5)
    pairs = heads_width // 128
    spans = attention_blocks(length)[::-1]
    for start, stop in spans:
        row = lax.broadcasted_iota(jnp.int32, (stop - start, stop), 0) + start
        column = lax.broadcasted_iota(jnp.int32, (stop - start, stop), 1)
        allowed = (column <= row) & (seg_col[start:stop, :] == seg_row[:, :stop])
        y_acc[start:stop, :stop] = jnp.where(allowed, 0.0, -1e30)
    for g in range(pairs):
        columns = slice(128 * g, 128 * (g + 1))
        for start, stop in spans:
            queries = q_ref[start:stop, columns]
            grads = act[start:stop, columns]
            keys, values = k_ref[:stop, columns], v_ref[:stop, columns]
            grad_q = jnp.zeros((stop - start, 128), f32)
            grad_k = jnp.zeros((stop, 128), f32)
            grad_v = jnp.zeros((stop, 128), f32)
            for i in range(2):
                mask = lanes() // HD == i
                one_q = jnp.where(mask, queries, jnp.zeros_like(queries))
                one_do = jnp.where(mask, grads, jnp.zeros_like(grads))
                one_k = jnp.where(mask, keys, jnp.zeros_like(keys))
                scores = dot_nt(one_q, keys) * scale + y_acc[start:stop, :stop]
                h = 2 * g + i
                weights = jnp.exp(scores - lse_ref[start:stop, h : h + 1])
                grad_w = dot_nt(one_do, values)
                inner = jnp.sum(weights * grad_w, axis=-1, keepdims=True)
                grad_s = (weights * (grad_w - inner)).astype(bf16)
                grad_q += dot_nn(grad_s, one_k)
                grad_k += dot_tn(grad_s, one_q)
                grad_v += dot_tn(weights.astype(bf16), one_do)
            dproj[start:stop, columns] = turn(
                grad_q * scale, cosine[start:stop, :], -sine[start:stop, :]
            ).astype(bf16)
            if stop == length:
                dk_acc[...] = grad_k * scale
                dv_acc[...] = grad_v
            else:
                dk_acc[:stop, :] += grad_k * scale
                dv_acc[:stop, :] += grad_v
            tick()
        dproj[:, heads_width + 128 * g : heads_width + 128 * (g + 1)] = turn(
            dk_acc[...], cosine, -sine
        ).astype(bf16)
        dproj[:, 2 * heads_width + 128 * g : 2 * heads_width + 128 * (g + 1)] = dv_acc[
            ...
        ].astype(bf16)
    for i, rows in enumerate(chunks):
        part = dot_nt(dproj[rows, :], blocks_of(aw, 0, 3 * heads_width))
        part_mine[rows, :] = part.astype(bf16)
    swap = send(part_mine, part_theirs, twin_sems.at[0, 3], twin_sems.at[1, 3], at.twin())
    swap.start()
    for i in range(3):
        columns = slice(i * heads_width, (i + 1) * heads_width)
        to_grads(i * heads_width, heads_width, x_t, lambda: dproj[:, columns])
    swap.wait_recv()
    grad_g_one = jnp.zeros((1, width), f32)
    for rows in chunks:
        grad_xa = part_mine[rows, :].astype(f32) + part_theirs[rows, :].astype(f32)
        grad_x, grad_gain = norm_back_rows(grad_xa, x_ref[rows, :].astype(f32), g_one)
        gx_ref[rows, :] += grad_x
        grad_g_one += grad_gain
    index = lax.broadcasted_iota(jnp.int32, (128, 1), 0)
    gains = jnp.where(index == 0, grad_g_one, 0.0) + jnp.where(index == 1, grad_g_two, 0.0)
    small_grads = (gains.T + grad_small).astype(bf16)
    aw[:, :, 4 * heads_width :] = small_grads.reshape(aw.shape[0], aw.shape[1], 128)
    for k in range(planes - 1, -1, -1):
        attn.start(k)
    tick(3)
    for k in range(planes - 1, -1, -1):
        attn.middle(k)
        tick()
    for k in range(planes - 1, 0, -1):
        attn.step(k)
        tick()
    tick(len(todo))
    shared.total(s_out)
    attn.total(a_out)
    for j in range(1, GROUP):
        expert.arrive(j)

    for i in range(3):
        swaps[i].wait_send()
    swap.wait_send()
    for t in range(2):
        for j in range(1, experts):
            home_copy(t, j).wait_send()
    expert.sent()
    shared.sent()
    attn.sent()


def backward_pass(planes, experts, inputs, far):
    bf16, f32, dma = jnp.bfloat16, jnp.float32, pltpu.SemaphoreType.DMA
    a_all, s_all, e_all, arrived, _ = far
    length, width = inputs[0].shape
    _, rows, a_width = a_all.shape
    n = planes * GROUP
    s_width, e_width = s_all.shape[2], e_all.shape[2]
    slots = 2 * experts * arrived.shape[2]
    vmem, anywhere = pl.BlockSpec(memory_space=pltpu.VMEM), pl.BlockSpec(memory_space=pl.ANY)
    shape = jax.ShapeDtypeStruct

    def plane_buffers(columns):
        return [
            pltpu.VMEM((planes, 2, rows, columns), bf16),
            pltpu.VMEM((planes, rows, columns), bf16),
            pltpu.VMEM((planes + 1, rows, columns), bf16),
        ]

    plane_sems = [dma((2, planes, 2)), dma((2, planes)), dma((2, 2, planes))]
    return pl.pallas_call(
        functools.partial(backward_kernel, planes, experts),
        out_shape=(
            shape((length, width), bf16),
            shape((length, width), f32),
            shape((rows, a_width), f32),
            shape((rows, s_width), bf16),
            shape((GROUP, rows, e_width), bf16),
        ),
        in_specs=[vmem] * len(inputs) + [anywhere] * len(far),
        out_specs=(vmem,) * 5,
        scratch_shapes=[
            pltpu.VMEM(a_all.shape, bf16),
            pltpu.VMEM(s_all.shape, bf16),
            pltpu.VMEM(e_all.shape, bf16),
            pltpu.VMEM(arrived.shape, bf16),
            pltpu.VMEM(arrived.shape, bf16),
            pltpu.VMEM((slots, max(s_width, e_width)), bf16),
            pltpu.VMEM((width, slots), bf16),
            pltpu.VMEM((width, slots), bf16),
            pltpu.VMEM((length, width), f32),
            pltpu.VMEM((length, width), f32),
            pltpu.VMEM((length, width), bf16),
            pltpu.VMEM((length, width), bf16),
            pltpu.VMEM((length, 128), f32),
            pltpu.VMEM((length, 128), f32),
            pltpu.VMEM((length, width), bf16),
            pltpu.VMEM((length, 128), f32),
            pltpu.VMEM((length, 128), f32),
            *plane_buffers(a_width),
            *plane_buffers(s_width),
            pltpu.VMEM(((planes + 1) * GROUP, rows, e_width), bf16),
            dma((5,)),
            *plane_sems,
            *plane_sems,
            dma((2, 2, n)),
            dma((2, GROUP)),
            dma((2, 2, GROUP)),
            dma((2, 4)),
        ],
        compiler_params=pltpu.CompilerParams(
            collective_id=1, has_side_effects=True, vmem_limit_bytes=62 << 20
        ),
    )(*inputs, *far)


def local_grouped(
    planes,
    tokens,
    segment_ids,
    expert_ids,
    slot_order,
    gain_attn,
    qkv_weight,
    out_weight,
    gain_ffn,
    router_weight,
    gate_up,
    down_weight,
    shared_gate_up,
    shared_down,
    cotangent,
):
    bf16, f32 = jnp.bfloat16, jnp.float32
    rows, heads_width = qkv_weight.shape[0], qkv_weight.shape[2]
    experts, hidden = down_weight.shape[0], down_weight.shape[1]
    s_hidden = shared_down.shape[0]
    length, width = tokens.shape
    top = expert_ids.shape[1]
    member = lax.rem(lax.axis_index("dp"), GROUP)
    core = lax.axis_index("tensor")
    cuts = [3 * heads_width, heads_width, 128]
    edges = [sum(cuts[:i]) for i in range(len(cuts) + 1)]

    def part(array, i):
        return array[..., edges[i] : edges[i + 1]]

    expert_packed = jnp.concatenate(
        [gate_up.reshape(experts, rows, 2 * hidden), down_weight.transpose(0, 2, 1)], axis=2
    )
    small = jnp.concatenate([gain_attn[:, None], gain_ffn[:, None], router_weight], axis=1)
    small = jnp.pad(small, ((0, 0), (0, 128 - small.shape[1])))
    attn_packed = jnp.concatenate(
        [qkv_weight.reshape(rows, 3 * heads_width), out_weight.T, small], axis=1
    )
    shared_packed = jnp.concatenate(
        [shared_gate_up.reshape(rows, 2 * s_hidden), shared_down.T], axis=1
    )
    cosine, sine = rotary(length, HD)
    cosine = jnp.tile(cosine[:, 0], (1, 4))
    sine = jnp.tile(sine[:, 0], (1, 4))
    orders = slot_order.reshape(length, top)
    inputs = (
        tokens,
        cotangent,
        segment_ids.reshape(length, 1),
        segment_ids,
        expert_ids,
        orders,
        expert_ids.T,
        orders.T,
        cosine,
        sine,
    )
    (
        all_attn,
        all_shared,
        all_expert,
        queries,
        keys_all,
        values_all,
        mixed,
        log_totals,
        hidden_state,
        xn_one,
        xn_two,
        probs,
        pair_facts,
        _,
        arrived,
    ) = forward_pass(
        planes, experts, inputs, (attn_packed, shared_packed, expert_packed), heads_width
    )
    output, grad_tokens, mine, mine_shared, mine_expert = backward_pass(
        planes,
        experts,
        (
            tokens,
            cotangent,
            segment_ids.reshape(length, 1),
            segment_ids,
            expert_ids,
            cosine,
            sine,
            queries,
            keys_all,
            values_all,
            mixed,
            log_totals,
            xn_two,
            probs,
            pair_facts,
        ),
        (all_attn, all_shared, all_expert, arrived, hidden_state),
    )
    mine_shared, mine_expert = mine_shared.astype(f32), mine_expert.astype(f32)
    small_mine = part(mine, 2)
    return (
        output,
        grad_tokens,
        small_mine[:, 0],
        part(mine, 0).reshape(rows, 3, heads_width),
        part(mine, 1).T,
        small_mine[:, 1],
        small_mine[:, 2 : 2 + experts],
        mine_expert[:, :, : 2 * hidden].reshape(experts, rows, 2, hidden),
        mine_expert[:, :, 2 * hidden :].transpose(0, 2, 1),
        mine_shared[:, : 2 * s_hidden].reshape(rows, 2, s_hidden),
        mine_shared[:, 2 * s_hidden :].T,
    )


def solution(mesh):
    def pick(*args):
        experts, rows = args[9].shape[0], args[5].shape[0]
        if experts == GROUP and mesh.shape["dp"] % GROUP == 0 and rows % 16 == 0:
            return local_grouped(mesh.shape["dp"] // GROUP, *args)
        return local_plain(*args)

    return jax.shard_map(
        pick,
        mesh=mesh,
        in_specs=(
            P("dp", None),
            P("dp", None),
            P("dp", None),
            P("dp", None),
            P("dp"),
            P("dp", None, "tensor"),
            P("tensor", "dp"),
            P("dp"),
            P("dp", None),
            P(None, "dp", None, "tensor"),
            P(None, "tensor", "dp"),
            P("dp", None, "tensor"),
            P("tensor", "dp"),
            P("dp", None),
        ),
        out_specs=(
            P("dp", None),
            P("dp", None),
            P("dp"),
            P("dp", None, "tensor"),
            P("tensor", "dp"),
            P("dp"),
            P("dp", None),
            P(None, "dp", None, "tensor"),
            P(None, "tensor", "dp"),
            P("dp", None, "tensor"),
            P("tensor", "dp"),
        ),
        check_vma=False,
    )
```

```python
import functools
import math

import jax
import jax.numpy as jnp
from jax import lax
from jax.experimental import pallas as pl
from jax.experimental.pallas import tpu as pltpu
from jax.sharding import PartitionSpec as P

HD = 64
GROUP = 4
MESH = pl.DeviceIdType.MESH


epsilon = 1e-06


def rms_scale(values):
    return lax.rsqrt(jnp.mean(values * values, axis=-1, keepdims=True) + epsilon)


def rotary(length, head_dim):
    half_dim = head_dim // 2
    position = jnp.arange(length).astype(jnp.float32)[:, None]
    inverse = jnp.exp(
        jnp.arange(half_dim).astype(jnp.float32) * (-2.0 * math.log(10000.0) / head_dim)
    )
    angles = position * inverse[None, :]
    return (jnp.cos(angles)[:, None, :], jnp.sin(angles)[:, None, :])


def rotate(values, cosine, sine):
    half_dim = values.shape[-1] // 2
    first_half = values[..., :half_dim]
    second_half = values[..., half_dim:]
    return jnp.concatenate(
        [first_half * cosine - second_half * sine, second_half * cosine + first_half * sine],
        axis=-1,
    )


def route_slots(pair_ids, rank_order, capacity, experts):
    length = pair_ids.shape[0]
    top_count = pair_ids.shape[1]
    pair_expert = pair_ids.reshape(-1)
    pair_count = pair_expert.shape[0]
    ordered = jnp.zeros((pair_count,), jnp.int32).at[rank_order].set(pair_expert)
    onehot = (ordered[:, None] == jnp.arange(experts, dtype=jnp.int32)[None, :]).astype(jnp.int32)
    running = jnp.cumsum(onehot, axis=0)
    ranked_slot = jnp.sum(running * onehot, axis=1) - 1
    position = ranked_slot[rank_order]
    kept_pair = position < capacity
    slot_index = jnp.where(kept_pair, pair_expert * capacity + position, experts * capacity)
    token_of_pair = jnp.arange(pair_count, dtype=jnp.int32) // top_count
    slot_token = (
        jnp.full((experts * capacity,), length, jnp.int32)
        .at[slot_index]
        .set(token_of_pair, mode="drop")
    )
    return (slot_token, slot_index.reshape(length, top_count), kept_pair.reshape(length, top_count))


def silu_back(both_parts, grad_hidden):
    gate_part = both_parts[..., 0, :]
    up_part = both_parts[..., 1, :]
    sigma = jax.nn.sigmoid(gate_part)
    slope = sigma * (1.0 + gate_part * (1.0 - sigma))
    return jnp.stack(
        [grad_hidden * up_part * slope, grad_hidden * gate_part * sigma], axis=-2
    ).astype(jnp.bfloat16)


def silu_forward(both_parts):
    return (jax.nn.silu(both_parts[..., 0, :]) * both_parts[..., 1, :]).astype(jnp.bfloat16)


def norm_back(grad_norm, values, scale_rows, gain):
    grad_gain = jnp.sum(grad_norm * values * scale_rows, axis=0)
    inner = grad_norm * gain
    grad_values = scale_rows * inner - values * scale_rows**3 * jnp.mean(
        inner * values, axis=-1, keepdims=True
    )
    return (grad_values, grad_gain)


def split_blocks(length):
    block = min(512, length)
    return (block, length // block)


def masked_scores(query_block, keys_all, query_pos, query_seg, segment, scale):
    positions = jnp.arange(keys_all.shape[0])
    scores = (
        jnp.einsum("qhd,khd->hqk", query_block, keys_all, preferred_element_type=jnp.float32)
        * scale
    )
    allowed = (positions[None, :] <= query_pos[:, None]) & (segment[None, :] == query_seg[:, None])
    return jnp.where(allowed[None], scores, -1e30)


def attend_forward(queries, keys_all, values_all, segment, scale):
    length, head_count, head_dim = queries.shape
    block, count_blocks = split_blocks(length)
    positions = jnp.arange(length)

    def one_block(inputs):
        query_block, query_pos, query_seg = inputs
        scores = masked_scores(query_block, keys_all, query_pos, query_seg, segment, scale)
        largest = jnp.max(scores, axis=-1, keepdims=True)
        expo = jnp.exp(scores - largest)
        total = jnp.sum(expo, axis=-1, keepdims=True)
        probs = (expo / total).astype(jnp.bfloat16)
        mixed = jnp.einsum("hqk,khd->qhd", probs, values_all, preferred_element_type=jnp.float32)
        return (mixed.astype(jnp.bfloat16), (largest + jnp.log(total))[..., 0])

    blocks = (
        queries.reshape(count_blocks, block, head_count, head_dim),
        positions.reshape(count_blocks, block),
        segment.reshape(count_blocks, block),
    )
    mixed_all, log_totals = lax.map(one_block, blocks)
    return (mixed_all.reshape(length, head_count * head_dim), log_totals)


def attend_backward(queries, keys_all, values_all, segment, scale, grad_mixed, log_totals):
    length, head_count, head_dim = queries.shape
    block, count_blocks = split_blocks(length)
    positions = jnp.arange(length)

    def one_block(carry, inputs):
        grad_keys, grad_values = carry
        query_block, query_pos, query_seg, grad_block, log_block = inputs
        scores = masked_scores(query_block, keys_all, query_pos, query_seg, segment, scale)
        probs = jnp.exp(scores - log_block[:, :, None])
        grad_probs = jnp.einsum(
            "qhd,khd->hqk", grad_block, values_all, preferred_element_type=jnp.float32
        )
        inner = jnp.sum(probs * grad_probs, axis=-1, keepdims=True)
        grad_scores = (probs * (grad_probs - inner)).astype(jnp.bfloat16)
        grad_query = (
            jnp.einsum("hqk,khd->qhd", grad_scores, keys_all, preferred_element_type=jnp.float32)
            * scale
        )
        grad_keys = (
            grad_keys
            + jnp.einsum(
                "hqk,qhd->khd", grad_scores, query_block, preferred_element_type=jnp.float32
            )
            * scale
        )
        grad_values = grad_values + jnp.einsum(
            "hqk,qhd->khd",
            probs.astype(jnp.bfloat16),
            grad_block,
            preferred_element_type=jnp.float32,
        )
        return ((grad_keys, grad_values), grad_query)

    zeros_kv = jnp.zeros((length, head_count, head_dim), jnp.float32)
    blocks = (
        queries.reshape(count_blocks, block, head_count, head_dim),
        positions.reshape(count_blocks, block),
        segment.reshape(count_blocks, block),
        grad_mixed.reshape(count_blocks, block, head_count, head_dim),
        log_totals,
    )
    (grad_keys, grad_values), grad_queries = lax.scan(one_block, (zeros_kv, zeros_kv), blocks)
    return (grad_queries.reshape(length, head_count, head_dim), grad_keys, grad_values)


def sum_rows(grad, axis, scatter_dimension, tiled):
    part = lax.psum_scatter(
        grad.astype(jnp.bfloat16), axis, scatter_dimension=scatter_dimension, tiled=tiled
    )
    return part.astype(jnp.float32)


def local_plain(
    tokens,
    segment_ids,
    expert_ids,
    slot_order,
    gain_attn,
    qkv_weight,
    out_weight,
    gain_ffn,
    router_weight,
    gate_up,
    down_weight,
    shared_gate_up,
    shared_down,
    cotangent,
):
    g_one, w_qkv, w_out, g_two, w_router, w_gate_up, w_down, s_gate_up, s_down = (
        lax.all_gather(gain_attn, "dp", axis=0, tiled=True),
        lax.all_gather(qkv_weight, "dp", axis=0, tiled=True),
        lax.all_gather(out_weight, "dp", axis=1, tiled=True),
        lax.all_gather(gain_ffn, "dp", axis=0, tiled=True),
        lax.all_gather(router_weight, "dp", axis=0, tiled=True),
        lax.all_gather(gate_up, "dp", axis=1, tiled=True),
        lax.all_gather(down_weight, "dp", axis=2, tiled=True),
        lax.all_gather(shared_gate_up, "dp", axis=0, tiled=True),
        lax.all_gather(shared_down, "dp", axis=1, tiled=True),
    )
    length = tokens.shape[0]
    width = tokens.shape[1]
    experts_count = w_router.shape[1]
    top_count = expert_ids.shape[1]
    capacity = length * top_count // experts_count
    head_dim = HD
    local_heads = w_qkv.shape[2] // head_dim
    scale = head_dim ** (-0.5)
    segment = segment_ids[0]
    slot_token, slot_index, kept_pair = route_slots(
        expert_ids, slot_order[0], capacity, experts_count
    )
    kept_float = kept_pair.astype(jnp.float32)
    slot_valid = slot_token < length
    slot_rows = jnp.minimum(slot_token, length - 1)
    pair_slots = jnp.minimum(slot_index, experts_count * capacity - 1)
    xfull = tokens.astype(jnp.float32)
    rms_one = rms_scale(xfull)
    xn_one = (xfull * rms_one * g_one.astype(jnp.float32)).astype(jnp.bfloat16)
    projected = jnp.einsum("td,dch->tch", xn_one, w_qkv, preferred_element_type=jnp.float32)
    cosine, sine = rotary(length, head_dim)
    queries = rotate(projected[:, 0].reshape(length, local_heads, head_dim), cosine, sine).astype(
        jnp.bfloat16
    )
    keys_all = rotate(projected[:, 1].reshape(length, local_heads, head_dim), cosine, sine).astype(
        jnp.bfloat16
    )
    values_all = projected[:, 2].reshape(length, local_heads, head_dim).astype(jnp.bfloat16)
    mixed, log_totals = attend_forward(queries, keys_all, values_all, segment, scale)
    attn_share = lax.psum_scatter(
        jnp.dot(mixed, w_out, preferred_element_type=jnp.float32),
        "tensor",
        scatter_dimension=1,
        tiled=True,
    )
    attn = lax.all_gather(attn_share, "tensor", axis=1, tiled=True)
    hidden_state = xfull + attn
    rms_two = rms_scale(hidden_state)
    xn_two = (hidden_state * rms_two * g_two.astype(jnp.float32)).astype(jnp.bfloat16)
    logits = jnp.dot(xn_two, w_router, preferred_element_type=jnp.float32)
    probs = jax.nn.softmax(logits, axis=-1)
    gates = jnp.take_along_axis(probs, expert_ids, axis=1) * kept_float
    dispatched = (xn_two[slot_rows] * slot_valid[:, None].astype(jnp.bfloat16)).reshape(
        experts_count, capacity, width
    )
    both_parts = jnp.einsum(
        "ecd,edjf->ecjf", dispatched, w_gate_up, preferred_element_type=jnp.float32
    )
    expert_hidden = silu_forward(both_parts)
    expert_out = jnp.einsum(
        "ecf,efd->ecd", expert_hidden, w_down, preferred_element_type=jnp.float32
    ).reshape(experts_count * capacity, width)
    picked = expert_out[pair_slots]
    moe = jnp.sum(gates[:, :, None] * picked, axis=1)
    shared_both = jnp.einsum("td,djf->tjf", xn_two, s_gate_up, preferred_element_type=jnp.float32)
    shared_hidden = silu_forward(shared_both)
    shared_out = jnp.dot(shared_hidden, s_down, preferred_element_type=jnp.float32)
    ffn_share = lax.psum_scatter(
        (moe + shared_out).astype(jnp.bfloat16), "tensor", scatter_dimension=1, tiled=True
    ).astype(jnp.float32)
    ffn = lax.all_gather(ffn_share.astype(jnp.bfloat16), "tensor", axis=1, tiled=True).astype(
        ffn_share.dtype
    )
    output = (hidden_state + ffn).astype(jnp.bfloat16)
    grad_y = cotangent.astype(jnp.float32)
    grad_shared_hidden = jnp.einsum(
        "td,fd->tf", cotangent, s_down, preferred_element_type=jnp.float32
    )
    grad_s_down = jnp.einsum(
        "tf,td->fd", shared_hidden, cotangent, preferred_element_type=jnp.float32
    )
    grad_shared_both = silu_back(shared_both, grad_shared_hidden)
    grad_s_gate_up = jnp.einsum(
        "td,tjf->djf", xn_two, grad_shared_both, preferred_element_type=jnp.float32
    )
    grad_xn_shared = jnp.einsum(
        "tjf,djf->td", grad_shared_both, s_gate_up, preferred_element_type=jnp.float32
    )
    slot_gate = (
        jnp.zeros((experts_count * capacity,), jnp.float32)
        .at[slot_index.reshape(-1)]
        .set(gates.reshape(-1), mode="drop")
    )
    grad_expert_out = (
        (slot_gate[:, None] * grad_y[slot_rows])
        .astype(jnp.bfloat16)
        .reshape(experts_count, capacity, width)
    )
    grad_gates_part = kept_float * jnp.sum(grad_y[:, None, :] * picked, axis=-1)
    grad_expert_hidden = jnp.einsum(
        "ecd,efd->ecf", grad_expert_out, w_down, preferred_element_type=jnp.float32
    )
    grad_w_down = jnp.einsum(
        "ecf,ecd->efd", expert_hidden, grad_expert_out, preferred_element_type=jnp.float32
    )
    grad_both = silu_back(both_parts, grad_expert_hidden)
    grad_w_gate_up = jnp.einsum(
        "ecd,ecjf->edjf", dispatched, grad_both, preferred_element_type=jnp.float32
    )
    grad_dispatched = jnp.einsum(
        "ecjf,edjf->ecd", grad_both, w_gate_up, preferred_element_type=jnp.float32
    ).reshape(experts_count * capacity, width)
    grad_xn_moe = jnp.sum(kept_float[:, :, None] * grad_dispatched[pair_slots], axis=1)
    grad_xn_part, grad_gates_share = (
        lax.psum_scatter(grad_xn_shared + grad_xn_moe, "tensor", scatter_dimension=1, tiled=True),
        lax.psum_scatter(grad_gates_part, "tensor", scatter_dimension=1, tiled=True),
    )
    grad_xn_sum, grad_gates = (
        lax.all_gather(grad_xn_part, "tensor", axis=1, tiled=True),
        lax.all_gather(grad_gates_share, "tensor", axis=1, tiled=True),
    )
    expert_match = (
        expert_ids[:, :, None] == jnp.arange(experts_count, dtype=jnp.int32)[None, None, :]
    ).astype(jnp.float32)
    grad_probs = jnp.sum(expert_match * grad_gates[:, :, None], axis=1)
    grad_logits = (
        probs * (grad_probs - jnp.sum(probs * grad_probs, axis=-1, keepdims=True))
    ).astype(jnp.bfloat16)
    grad_w_router = jnp.einsum("td,te->de", xn_two, grad_logits, preferred_element_type=jnp.float32)
    grad_xn_two = grad_xn_sum + jnp.einsum(
        "te,de->td", grad_logits, w_router, preferred_element_type=jnp.float32
    )
    grad_norm_two, grad_g_two = norm_back(
        grad_xn_two, hidden_state, rms_two, g_two.astype(jnp.float32)
    )
    grad_hidden = grad_y + grad_norm_two
    grad_attn = grad_hidden.astype(jnp.bfloat16)
    grad_w_out = jnp.einsum("th,td->hd", mixed, grad_attn, preferred_element_type=jnp.float32)
    grad_mixed = jnp.einsum(
        "td,hd->th", grad_attn, w_out, preferred_element_type=jnp.float32
    ).astype(jnp.bfloat16)
    grad_queries, grad_keys, grad_values = attend_backward(
        queries, keys_all, values_all, segment, scale, grad_mixed, log_totals
    )
    grad_projected = (
        jnp.stack(
            [rotate(grad_queries, cosine, -sine), rotate(grad_keys, cosine, -sine), grad_values],
            axis=1,
        )
        .astype(jnp.bfloat16)
        .reshape(length, 3, local_heads * head_dim)
    )
    grad_w_qkv = jnp.einsum(
        "td,tch->dch", xn_one, grad_projected, preferred_element_type=jnp.float32
    )
    grad_xn_share = lax.psum_scatter(
        jnp.einsum("tch,dch->td", grad_projected, w_qkv, preferred_element_type=jnp.float32).astype(
            jnp.bfloat16
        ),
        "tensor",
        scatter_dimension=1,
        tiled=True,
    ).astype(jnp.float32)
    grad_xn_one = lax.all_gather(
        grad_xn_share.astype(jnp.bfloat16), "tensor", axis=1, tiled=True
    ).astype(grad_xn_share.dtype)
    grad_norm_one, grad_g_one = norm_back(grad_xn_one, xfull, rms_one, g_one.astype(jnp.float32))
    grad_tokens = grad_hidden + grad_norm_one
    (
        grad_g_one,
        grad_w_qkv,
        grad_w_out,
        grad_g_two,
        grad_w_router,
        grad_w_gate_up,
        grad_w_down,
        grad_s_gate_up,
        grad_s_down,
    ) = (
        lax.psum_scatter(grad_g_one, "dp", scatter_dimension=0, tiled=True),
        sum_rows(grad_w_qkv, "dp", scatter_dimension=0, tiled=True),
        sum_rows(grad_w_out, "dp", scatter_dimension=1, tiled=True),
        lax.psum_scatter(grad_g_two, "dp", scatter_dimension=0, tiled=True),
        lax.psum_scatter(grad_w_router, "dp", scatter_dimension=0, tiled=True),
        sum_rows(grad_w_gate_up, "dp", scatter_dimension=1, tiled=True),
        sum_rows(grad_w_down, "dp", scatter_dimension=2, tiled=True),
        sum_rows(grad_s_gate_up, "dp", scatter_dimension=0, tiled=True),
        sum_rows(grad_s_down, "dp", scatter_dimension=1, tiled=True),
    )
    return (
        output,
        grad_tokens,
        grad_g_one,
        grad_w_qkv,
        grad_w_out,
        grad_g_two,
        grad_w_router,
        grad_w_gate_up,
        grad_w_down,
        grad_s_gate_up,
        grad_s_down,
    )


class Place:
    def __init__(self, planes):
        d = lax.axis_index("dp")
        self.planes = planes
        self.d, self.c = d, lax.axis_index("tensor")
        self.z, self.p = d // GROUP, lax.rem(d, GROUP)
        bit0, bit1 = lax.rem(self.p, 2), self.p // 2
        flip0, flip1 = 1 - bit0, 1 - bit1
        self.member = [
            self.p,
            flip0 + 2 * bit1,
            bit0 + 2 * flip1,
            flip0 + 2 * flip1,
        ]

    def near(self, j):
        return (self.z * GROUP + self.member[j], self.c)

    def up(self):
        return (self.d + GROUP, self.c)

    def down(self):
        return (self.d - GROUP, self.c)

    def twin(self):
        return (self.d, 1 - self.c)

    def when(self, condition, action):
        pl.when(condition)(action)

    def has_up(self, k=1):
        return self.z + k < self.planes

    def has_down(self, k=1):
        return self.z - k >= 0

    def greet(self):
        barrier = pltpu.get_barrier_semaphore()

        def hello(device):
            pl.semaphore_signal(barrier, inc=1, device_id=device, device_id_type=MESH)

        hello(self.twin())
        for j in range(1, GROUP):
            hello(self.near(j))
        self.when(self.has_up(), lambda: hello(self.up()))
        self.when(self.has_down(), lambda: hello(self.down()))
        line = self.has_up().astype(jnp.int32) + self.has_down().astype(jnp.int32)
        pl.semaphore_wait(barrier, GROUP + line)


def send(source, target, send_sem, recv_sem, device):
    return pltpu.make_async_remote_copy(
        src_ref=source,
        dst_ref=target,
        send_sem=send_sem,
        recv_sem=recv_sem,
        device_id=device,
        device_id_type=MESH,
    )


class Everywhere:
    def __init__(self, at, own, all_blocks, local_sem, recvs, sends):
        self.at, self.own, self.all = at, own, all_blocks
        self.local_sem, self.recvs, self.sends = local_sem, recvs, sends

    def copy(self, block, source, way, device):
        return send(source, self.all.at[block], self.sends.at[way, block], self.recvs.at[block], device)

    def keep(self):
        return pltpu.make_async_copy(self.own, self.all.at[self.at.d], self.local_sem)

    def landed(self, block):
        self.copy(block, self.own, 0, self.at.near(1)).wait_recv()

    def start_line(self):
        at = self.at
        at.when(at.has_up(), lambda: self.copy(at.d, self.own, 0, at.up()).start())
        at.when(at.has_down(), lambda: self.copy(at.d, self.own, 1, at.down()).start())

    def start_plane(self):
        at = self.at
        self.copy(at.d, self.own, 2, at.near(1)).start()
        self.copy(at.d, self.own, 3, at.near(2)).start()
        self.keep().start()

    def spread(self, k):
        at = self.at

        def go(plane, more, way, device_of):
            block = plane * GROUP + at.p
            source = self.all.at[block]
            self.landed(block)
            at.when(more, lambda: self.copy(block, source, way, device_of()).start())
            self.copy(block, source, 2, at.near(1)).start()
            self.copy(block, source, 3, at.near(2)).start()

        at.when(at.has_down(k), lambda: go(at.z - k, at.has_up(), 0, at.up))
        at.when(at.has_up(k), lambda: go(at.z + k, at.has_down(), 1, at.down))

    def cross(self, k):
        at = self.at

        def go(plane):
            first = plane * GROUP + at.member[1]
            second = plane * GROUP + at.member[2]
            even = lax.rem(plane, 2) == 0
            self.landed(first)
            at.when(even, lambda: self.copy(first, self.all.at[first], 3, at.near(2)).start())
            self.landed(second)
            at.when(
                jnp.logical_not(even),
                lambda: self.copy(second, self.all.at[second], 2, at.near(1)).start(),
            )

        if k == 0:
            go(at.z)
        else:
            at.when(at.has_down(k), lambda: go(at.z - k))
            at.when(at.has_up(k), lambda: go(at.z + k))

    def diagonal(self):
        for plane in range(self.at.planes):
            self.landed(plane * GROUP + self.at.member[3])
        self.keep().wait()

    def sent(self):
        at = self.at
        for plane in range(at.planes):
            block = plane * GROUP + at.p
            self.copy(block, self.own, 2, at.near(1)).wait_send()
            self.copy(block, self.own, 3, at.near(2)).wait_send()
            if plane % 2 == 0:
                self.copy(plane * GROUP + at.member[1], self.own, 3, at.near(2)).wait_send()
            else:
                self.copy(plane * GROUP + at.member[2], self.own, 2, at.near(1)).wait_send()

            def gone(way, device_of):
                self.copy(block, self.own, way, device_of()).wait_send()

            at.when((at.z >= plane) & at.has_up(), lambda: gone(0, at.up))
            at.when((at.z <= plane) & at.has_down(), lambda: gone(1, at.down))


class Experts:
    def __init__(self, at, own, all_blocks, local_sem, recvs, sends):
        self.at, self.own, self.all = at, own, all_blocks
        self.local_sem, self.recvs, self.sends = local_sem, recvs, sends

    def line(self, block, source, way, device):
        return send(source, self.all.at[block], self.sends.at[way, block], self.recvs.at[block], device)

    def across(self, j):
        at = self.at
        return send(
            self.own.at[at.member[j]],
            self.all.at[at.d],
            self.sends.at[1 + j, at.d],
            self.recvs.at[at.d],
            at.near(j),
        )

    def keep(self):
        return pltpu.make_async_copy(self.own.at[self.at.p], self.all.at[self.at.d], self.local_sem)

    def start_plane(self):
        for j in range(1, GROUP):
            self.across(j).start()
        self.keep().start()

    def start_line(self):
        at = self.at
        source = self.own.at[at.p]
        at.when(at.has_up(), lambda: self.line(at.d, source, 0, at.up()).start())
        at.when(at.has_down(), lambda: self.line(at.d, source, 1, at.down()).start())

    def landed(self, block):
        self.line(block, self.own.at[0], 0, self.at.near(1)).wait_recv()

    def plane_step(self, j):
        at = self.at
        block = at.z * GROUP + at.member[j]
        source = self.all.at[block]
        self.landed(block)
        at.when(at.has_up(), lambda: self.line(block, source, 0, at.up()).start())
        at.when(at.has_down(), lambda: self.line(block, source, 1, at.down()).start())

    def line_step(self, k, j):
        at = self.at

        def go(plane, more, way, device_of):
            block = plane * GROUP + at.member[j]
            self.landed(block)
            at.when(more, lambda: self.line(block, self.all.at[block], way, device_of()).start())

        at.when(at.has_down(k), lambda: go(at.z - k, at.has_up(), 0, at.up))
        at.when(at.has_up(k), lambda: go(at.z + k, at.has_down(), 1, at.down))

    def sent(self):
        at = self.at
        self.keep().wait()
        for j in range(1, GROUP):
            self.across(j).wait_send()
        for plane in range(at.planes):

            def gone(way, device_of):
                for q in range(GROUP):
                    self.line(plane * GROUP + q, self.own.at[0], way, device_of()).wait_send()

            at.when((at.z >= plane) & at.has_up(), lambda: gone(0, at.up))
            at.when((at.z <= plane) & at.has_down(), lambda: gone(1, at.down))


def dot_nn(a, b):
    return jnp.dot(a, b, preferred_element_type=jnp.float32)


def dot_nt(a, b):
    return lax.dot_general(a, b, (((1,), (1,)), ((), ())), preferred_element_type=jnp.float32)


def dot_tn(a, b):
    return lax.dot_general(a, b, (((0,), (0,)), ((), ())), preferred_element_type=jnp.float32)


def lanes(count=128):
    return lax.broadcasted_iota(jnp.int32, (1, count), 1)


def turn(values, cosine, sine):
    half = HD // 2
    other = jnp.where(
        lax.rem(lanes(), HD) < half,
        -pltpu.roll(values, 2 * HD - half, 1),
        pltpu.roll(values, half, 1),
    )
    return values * cosine + other * sine


def blocks_of(ref, start, stop):
    block = ref[:, :, start:stop]
    return block.reshape(block.shape[0] * block.shape[1], stop - start)


def attention_blocks(length):
    size = length // 2
    return [(i * size, (i + 1) * size) for i in range(2)]


def forward_kernel(
    planes,
    experts,
    x_ref,
    cot_ref,
    seg_col,
    seg_row,
    ids_ref,
    order_ref,
    ids_t_ref,
    order_t_ref,
    cos_ref,
    sin_ref,
    a_own,
    s_own,
    e_own,
    a_all,
    s_all,
    e_all,
    q_ref,
    k_ref,
    v_ref,
    o_ref,
    lse_ref,
    h_ref,
    xa_ref,
    xf_ref,
    probs_ref,
    pair_ref,
    placed_ref,
    arrived_ref,
    bias_ref,
    mine_ref,
    theirs_ref,
    local_sem,
    a_recv,
    a_send,
    s_recv,
    s_send,
    e_recv,
    e_send,
    twin_sem,
    token_recv,
    token_send,
):
    f32, bf16 = jnp.float32, jnp.bfloat16
    at = Place(planes)
    length, width = x_ref.shape
    heads_width = q_ref.shape[1]
    capacity = length * ids_ref.shape[1] // experts
    half = capacity // 2
    attn = Everywhere(at, a_own, a_all, local_sem.at[0], a_recv, a_send)
    shared = Everywhere(at, s_own, s_all, local_sem.at[1], s_recv, s_send)
    expert = Experts(at, e_own, e_all, local_sem.at[2], e_recv, e_send)

    at.greet()
    attn.start_line()
    attn.start_plane()
    expert.start_plane()
    shared.start_line()
    expert.start_line()

    todo = [functools.partial(shared.cross, k) for k in range(2)]
    for k in range(1, planes):
        for j in range(GROUP):
            todo.append(functools.partial(expert.line_step, k, j))
        if k == 1:
            todo += [functools.partial(shared.cross, i) for i in range(2, planes)]
    todo.reverse()

    def tick(count=1):
        for _ in range(count):
            if todo:
                todo.pop()()

    for start, stop in attention_blocks(length):
        rows = lax.broadcasted_iota(jnp.int32, (stop - start, stop), 0) + start
        columns = lax.broadcasted_iota(jnp.int32, (stop - start, stop), 1)
        allowed = (columns <= rows) & (seg_col[start:stop, :] == seg_row[:, :stop])
        bias_ref[start:stop, :stop] = jnp.where(allowed, 0.0, -1e30)

    def slot_of(expert_id, position):
        which = position // half
        apart = which + at.c - 2 * which * at.c
        bit0, bit1 = lax.rem(expert_id, 2), expert_id // 2
        p0, p1 = lax.rem(at.p, 2), at.p // 2
        distance = (bit0 + p0 - 2 * bit0 * p0) + 2 * (bit1 + p1 - 2 * bit1 * p1)
        slot = apart * (experts * half) + distance * half + lax.rem(position, half)
        return jnp.where(position < capacity, slot, -1)

    slot_cols, slot_rows = [], []
    top = ids_ref.shape[1]
    for r in range(top):
        count_col = jnp.zeros((length, 1), jnp.int32)
        count_row = jnp.zeros((1, length), jnp.int32)
        for other in range(top):
            first = (ids_t_ref[other : other + 1, :] == ids_ref[:, r : r + 1]) & (
                order_t_ref[other : other + 1, :] < order_ref[:, r : r + 1]
            )
            count_col += jnp.sum(first.astype(jnp.int32), axis=1, keepdims=True)
            first = (ids_ref[:, other : other + 1] == ids_t_ref[r : r + 1, :]) & (
                order_ref[:, other : other + 1] < order_t_ref[r : r + 1, :]
            )
            count_row += jnp.sum(first.astype(jnp.int32), axis=0, keepdims=True)
        slot_cols.append(slot_of(ids_ref[:, r : r + 1], count_col))
        slot_rows.append(slot_of(ids_t_ref[r : r + 1, :], count_row))

    attn.spread(1)
    attn.cross(0)
    for j in range(1, GROUP):
        expert.plane_step(j)
    shared.start_plane()
    for k in range(2, planes):
        attn.spread(k)
        attn.cross(k - 1)
        shared.spread(k - 1)
    attn.cross(planes - 1)
    shared.spread(planes - 1)
    attn.diagonal()

    small = blocks_of(a_all, 4 * heads_width, 4 * heads_width + 128)
    small_rows = small.astype(f32).T
    g_one, g_two = small_rows[0:1, :], small_rows[1:2, :]
    x = x_ref[...].astype(f32)
    rms = lax.rsqrt(jnp.mean(x * x, axis=-1, keepdims=True) + epsilon)
    xa_ref[...] = (x * rms * g_one).astype(bf16)
    cosine, sine = cos_ref[...], sin_ref[...]
    pairs = heads_width // 128
    for i, ref in enumerate((q_ref, k_ref)):
        part = dot_nn(xa_ref[...], blocks_of(a_all, i * heads_width, (i + 1) * heads_width))
        for g in range(pairs):
            columns = slice(128 * g, 128 * (g + 1))
            ref[:, columns] = turn(part[:, columns], cosine, sine).astype(bf16)
    v_ref[...] = dot_nn(
        xa_ref[...], blocks_of(a_all, 2 * heads_width, 3 * heads_width)
    ).astype(bf16)
    tick(2)

    scale = HD ** (-0.5)
    for start, stop in attention_blocks(length):
        logs = jnp.zeros((stop - start, 128), f32)
        for g in range(pairs):
            columns = slice(128 * g, 128 * (g + 1))
            queries = q_ref[start:stop, columns]
            keys, values = k_ref[:stop, columns], v_ref[:stop, columns]
            mixed = []
            for i in range(2):
                one = jnp.where(lanes() // HD == i, queries, jnp.zeros_like(queries))
                scores = dot_nt(one, keys) * scale + bias_ref[start:stop, :stop]
                largest = jnp.max(scores, axis=-1, keepdims=True)
                expo = jnp.exp(scores - largest)
                total = jnp.sum(expo, axis=-1, keepdims=True)
                weights = (expo * (1.0 / total)).astype(bf16)
                mixed.append(dot_nn(weights, values))
                logs = jnp.where(lanes() == 2 * g + i, largest + jnp.log(total), logs)
            o_ref[start:stop, columns] = jnp.where(lanes() < HD, mixed[0], mixed[1]).astype(bf16)
            tick()
        lse_ref[start:stop, :] = logs

    mine_ref[...] = dot_nt(o_ref[...], blocks_of(a_all, 3 * heads_width, 4 * heads_width))
    swap = send(mine_ref, theirs_ref, twin_sem.at[0], twin_sem.at[1], at.twin())
    swap.start()
    swap.wait_recv()
    h = x_ref[...].astype(f32) + (mine_ref[...] + theirs_ref[...])
    h_ref[...] = h
    rms = lax.rsqrt(jnp.mean(h * h, axis=-1, keepdims=True) + epsilon)
    xf_ref[...] = (h * rms * g_two).astype(bf16)

    is_expert = (lanes() >= 2) & (lanes() < 2 + experts)
    logits = jnp.where(is_expert, dot_nn(xf_ref[...], small), -1e30)
    expo = jnp.exp(logits - jnp.max(logits, axis=-1, keepdims=True))
    probs = expo / jnp.sum(expo, axis=-1, keepdims=True)
    probs_ref[...] = probs
    packed = jnp.zeros((length, 128), f32)
    for r in range(top):
        chosen = lanes() == ids_ref[:, r : r + 1] + 2
        gate = jnp.sum(jnp.where(chosen, probs, 0.0), axis=-1, keepdims=True)
        gate = jnp.where(slot_cols[r] >= 0, gate, 0.0)
        packed = jnp.where(lanes() == r, gate, packed)
        packed = jnp.where(lanes() == top + r, slot_cols[r].astype(f32), packed)
    pair_ref[...] = packed
    gate_rows = packed.T

    def outgoing(j):
        return send(
            placed_ref.at[j], arrived_ref.at[0, j], token_send.at[j], token_recv.at[j], at.near(j)
        )

    for j in range(experts):
        index = lax.broadcasted_iota(jnp.int32, (half, 1), 0) + j * half
        pick = [slot_rows[r] == index for r in range(top)]
        slot_gate = sum(
            jnp.sum(jnp.where(pick[r], gate_rows[r : r + 1, :], 0.0), axis=1, keepdims=True)
            for r in range(top)
        )
        pick = sum(p.astype(f32) for p in pick).astype(bf16)
        target = arrived_ref.at[0, 0] if j == 0 else placed_ref.at[j]
        target[:, :width] = dot_nn(pick, xf_ref[...]).astype(bf16)
        target[:, width:] = (dot_nn(pick, cot_ref[...]) * slot_gate).astype(bf16)
        if j:
            outgoing(j).start()
    tick(planes)
    for j in range(1, experts):
        outgoing(j).wait_recv()
    across = send(arrived_ref.at[0], arrived_ref.at[1], twin_sem.at[2], twin_sem.at[3], at.twin())
    across.start()

    tick(len(todo))
    shared.diagonal()
    across.wait_recv()
    across.wait_send()
    swap.wait_send()
    for j in range(1, experts):
        outgoing(j).wait_send()
    attn.sent()
    shared.sent()
    expert.sent()


def forward_pass(planes, experts, inputs, own, heads_width):
    n = planes * GROUP
    bf16, f32, dma = jnp.bfloat16, jnp.float32, pltpu.SemaphoreType.DMA
    length, width = inputs[0].shape
    half = length * inputs[4].shape[1] // experts // 2
    vmem, anywhere = pl.BlockSpec(memory_space=pltpu.VMEM), pl.BlockSpec(memory_space=pl.ANY)
    shape = jax.ShapeDtypeStruct
    return pl.pallas_call(
        functools.partial(forward_kernel, planes, experts),
        out_shape=(
            shape((n,) + own[0].shape, bf16),
            shape((n,) + own[1].shape, bf16),
            shape((n,) + own[2].shape[1:], bf16),
            shape((length, heads_width), bf16),
            shape((length, heads_width), bf16),
            shape((length, heads_width), bf16),
            shape((length, heads_width), bf16),
            shape((length, 128), f32),
            shape((length, width), f32),
            shape((length, width), bf16),
            shape((length, width), bf16),
            shape((length, 128), f32),
            shape((length, 128), f32),
            shape((experts, half, 2 * width), bf16),
            shape((2, experts, half, 2 * width), bf16),
        ),
        in_specs=[vmem] * len(inputs) + [anywhere] * 3,
        out_specs=(vmem, anywhere, anywhere) + (vmem,) * 12,
        scratch_shapes=[
            pltpu.VMEM((length, length), f32),
            pltpu.VMEM((length, width), f32),
            pltpu.VMEM((length, width), f32),
            dma((3,)),
            dma((n,)),
            dma((4, n)),
            dma((n,)),
            dma((4, n)),
            dma((n,)),
            dma((1 + GROUP, n)),
            dma((4,)),
            dma((GROUP,)),
            dma((GROUP,)),
        ],
        compiler_params=pltpu.CompilerParams(
            collective_id=0, has_side_effects=True, vmem_limit_bytes=48 << 20
        ),
    )(*inputs, *own)


class PlaneSum:
    def __init__(self, at, own, one, two, came, one_sems, two_sems, line_sems):
        self.at, self.own, self.one, self.two, self.came = at, own, one, two, came
        self.one_sems, self.two_sems, self.line_sems = one_sems, two_sems, line_sems

    def one_copy(self, plane, i, even):
        at = self.at
        j = 1 if even else 2
        target = at.member[3] if i else at.member[j]
        return send(
            self.own.at[plane * GROUP + target],
            self.one.at[plane, i],
            self.one_sems.at[0, plane, i],
            self.one_sems.at[1, plane, i],
            at.near(j),
        )

    def two_copy(self, plane, even):
        return send(
            self.one.at[plane, 1],
            self.two.at[plane],
            self.two_sems.at[0, plane],
            self.two_sems.at[1, plane],
            self.at.near(2 if even else 1),
        )

    def by_parity(self, plane, action):
        even = lax.rem(plane, 2) == 0
        self.at.when(even, lambda: action(True))
        self.at.when(jnp.logical_not(even), lambda: action(False))

    def line(self, source, plane, way, here=False):
        at, sems = self.at, self.line_sems
        slot, device = plane, at.up()
        if way:
            slot = jnp.where(plane == (at.z if here else at.z - 1), at.planes, plane)
            device = at.down()
        return send(
            source, self.came.at[slot], sems.at[0, way, plane], sems.at[1, way, plane], device
        )

    def both_ways(self, action, k):
        at = self.at
        if k == 0:
            action(at.z, 0)
            return
        at.when(at.has_up(k), lambda: action(at.z + k, 0))
        at.when(at.has_down(k), lambda: action(at.z - k, 1))

    def start(self, k):
        def go(plane, way):
            def pair(even):
                self.one_copy(plane, 1, even).start()
                self.one_copy(plane, 0, even).start()

            self.by_parity(plane, pair)

        self.both_ways(go, k)

    def middle(self, k):
        f32 = jnp.float32

        def go(plane, way):
            def stage(even):
                at, one = self.at, self.one
                other = plane * GROUP + (at.member[2] if even else at.member[1])
                self.one_copy(plane, 1, even).wait_recv()
                one[plane, 1] = (one[plane, 1].astype(f32) + self.own[other].astype(f32)).astype(
                    one.dtype
                )
                self.two_copy(plane, even).start()

            self.by_parity(plane, stage)

        self.both_ways(go, k)

    def finish_plane(self, plane):
        f32 = jnp.float32

        def stage(even):
            mine = plane * GROUP + self.at.p
            self.one_copy(plane, 0, even).wait_recv()
            self.two_copy(plane, even).wait_recv()
            self.two[plane] = (
                self.two[plane].astype(f32)
                + self.one[plane, 0].astype(f32)
                + self.own[mine].astype(f32)
            ).astype(self.two.dtype)

        self.by_parity(plane, stage)

    def step(self, k):
        f32 = jnp.float32

        def go(plane, way):
            at = self.at
            self.finish_plane(plane)
            behind = at.has_down() if way == 0 else at.has_up()
            held = self.came

            def add():
                self.line(self.two.at[plane], plane, way, True).wait_recv()
                held[plane] = (held[plane].astype(f32) + self.two[plane].astype(f32)).astype(
                    held.dtype
                )
                self.line(held.at[plane], plane, way).start()

            at.when(behind, add)
            at.when(
                jnp.logical_not(behind), lambda: self.line(self.two.at[plane], plane, way).start()
            )

        self.both_ways(go, k)

    def total(self, out):
        at, f32 = self.at, jnp.float32
        z = at.z
        self.finish_plane(z)
        at.when(at.has_down(), lambda: self.line(self.two.at[z], z, 0, True).wait_recv())
        at.when(at.has_up(), lambda: self.line(self.two.at[z], z, 1, True).wait_recv())
        low = jnp.where(at.has_down(), self.came[z].astype(f32), 0.0)
        high = jnp.where(at.has_up(), self.came[at.planes].astype(f32), 0.0)
        out[...] = (self.two[z].astype(f32) + low + high).astype(out.dtype)

    def sent(self):
        at = self.at
        for plane in range(at.planes):
            even = plane % 2 == 0
            self.one_copy(plane, 0, even).wait_send()
            self.one_copy(plane, 1, even).wait_send()
            self.two_copy(plane, even).wait_send()
            at.when(at.z < plane, lambda: self.line(self.two.at[plane], plane, 0).wait_send())
            at.when(at.z > plane, lambda: self.line(self.two.at[plane], plane, 1).wait_send())


class LineSum:
    def __init__(self, at, own, came, out, line_sems, last_sems):
        self.at, self.own, self.came, self.out = at, own, came, out
        self.line_sems, self.last_sems = line_sems, last_sems

    def hop(self, source, plane, j, way, here=False):
        at = self.at
        block = plane * GROUP + at.member[j]
        if way == 0:
            slot, device = block, at.up()
        else:
            end = at.z if here else at.z - 1
            slot = jnp.where(plane == end, at.planes, plane) * GROUP + at.member[j]
            device = at.down()
        sems = self.line_sems
        return send(
            source, self.came.at[slot], sems.at[0, way, block], sems.at[1, way, block], device
        )

    def start_plane(self, plane):
        at = self.at

        def go(way):
            for j in range(GROUP):
                self.hop(self.own.at[plane * GROUP + at.member[j]], plane, j, way).start()

        at.when(jnp.logical_not(at.has_down()) & (plane != at.z), lambda: go(0))
        at.when(jnp.logical_not(at.has_up()) & (plane != at.z), lambda: go(1))

    def step(self, k, j):
        at, f32 = self.at, jnp.float32

        def go(plane, way):
            block = plane * GROUP + at.member[j]
            self.hop(self.own.at[block], plane, j, way, True).wait_recv()
            self.came[block] = (
                self.came[block].astype(f32) + self.own[block].astype(f32)
            ).astype(self.came.dtype)
            self.hop(self.came.at[block], plane, j, way).start()

        at.when(at.has_up(k) & at.has_down(), lambda: go(at.z + k, 0))
        at.when(at.has_down(k) & at.has_up(), lambda: go(at.z - k, 1))

    def last_copy(self, source, j, here=False):
        at = self.at
        return send(
            source,
            self.out.at[at.member[j] if here else at.p],
            self.last_sems.at[0, j],
            self.last_sems.at[1, j],
            at.near(j),
        )

    def total(self, j):
        at, f32, out = self.at, jnp.float32, self.out
        block = at.z * GROUP + at.member[j]
        spare = at.planes * GROUP + at.member[j]
        at.when(at.has_down(), lambda: self.hop(self.own.at[block], at.z, j, 0, True).wait_recv())
        at.when(at.has_up(), lambda: self.hop(self.own.at[block], at.z, j, 1, True).wait_recv())
        low = jnp.where(at.has_down(), self.came[block].astype(f32), 0.0)
        high = jnp.where(at.has_up(), self.came[spare].astype(f32), 0.0)
        total = (self.own[block].astype(f32) + low + high).astype(out.dtype)
        if j == 0:
            out[at.p] = total
        else:
            self.came[block] = total
            self.last_copy(self.came.at[block], j).start()

    def arrive(self, j):
        self.last_copy(self.own.at[0], j, True).wait_recv()

    def sent(self):
        at = self.at
        for j in range(1, GROUP):
            self.last_copy(self.own.at[0], j).wait_send()
        for plane in range(at.planes):

            def gone(way):
                for j in range(GROUP):
                    self.hop(self.own.at[0], plane, j, way).wait_send()

            at.when(at.z < plane, lambda: gone(0))
            at.when(at.z > plane, lambda: gone(1))


def branch(x_of, dy_of, rows, weights, act, y_acc, dx_acc):
    f32, bf16 = jnp.float32, jnp.bfloat16
    hidden = weights.shape[2] // 3
    size, count = 256, rows.stop - rows.start
    step = min(count, 256)

    def body(i, carry):
        offset = pl.multiple_of(i * size, size)

        def weight(part):
            block = weights[:, :, pl.ds(pl.multiple_of(part * hidden + offset, size), size)]
            return block.reshape(block.shape[0] * block.shape[1], size)

        for start in range(0, count, step):
            some = slice(start, start + step)

            def keep(part, values):
                columns = pl.ds(pl.multiple_of(part * hidden + offset, size), size)
                act[rows.start + start : rows.start + start + step, columns] = values

            g, u = dot_nn(x_of(some), weight(0)), dot_nn(x_of(some), weight(1))
            grad = dot_nn(dy_of(some), weight(2))
            sigma = 1.0 / (1.0 + jnp.exp(-g))
            silu = g * sigma
            eh = (silu * u).astype(bf16)
            dg = (grad * u * (sigma * (1.0 + g * (1.0 - sigma)))).astype(bf16)
            du = (grad * silu).astype(bf16)
            keep(0, dg)
            keep(1, du)
            keep(2, eh)
            y_acc[some, :] += dot_nt(eh, weight(2))
            dx_acc[some, :] += dot_nt(dg, weight(0)) + dot_nt(du, weight(1))
        return carry

    y_acc[...] = jnp.zeros(y_acc.shape, f32)
    dx_acc[...] = jnp.zeros(dx_acc.shape, f32)
    lax.fori_loop(0, hidden // size, body, 0)


def weight_grads(plane, planes, count, x_t, dy_t, act, grads):
    width, bf16 = x_t.shape[0], jnp.bfloat16
    rows = width // planes
    hidden = act.shape[1] // 3
    size = 512
    features = pl.ds(pl.multiple_of(plane * rows, 16), rows)
    for part in range(3 * hidden // size):
        columns = slice(part * size, (part + 1) * size)
        left = x_t if part * size < 2 * hidden else dy_t
        block = dot_nn(left[features, :count], act[:count, columns]).astype(bf16)
        grads[pl.ds(plane * GROUP, GROUP), :, columns] = block.reshape(
            GROUP, rows // GROUP, size
        )


def norm_back_rows(grad, values, gain):
    rms = lax.rsqrt(jnp.mean(values * values, axis=-1, keepdims=True) + epsilon)
    grad_gain = jnp.sum(grad * values * rms, axis=0, keepdims=True)
    inner = grad * gain
    grad_values = rms * inner - values * (rms * rms * rms) * jnp.mean(
        inner * values, axis=-1, keepdims=True
    )
    return grad_values, grad_gain


def backward_kernel(
    planes,
    experts,
    x_ref,
    cot_ref,
    seg_col,
    seg_row,
    ids_ref,
    cos_ref,
    sin_ref,
    q_ref,
    k_ref,
    v_ref,
    o_ref,
    lse_ref,
    xf_ref,
    probs_ref,
    pair_ref,
    a_all,
    s_all,
    e_all,
    arrived_ref,
    h_ref,
    out_ref,
    gx_ref,
    a_out,
    s_out,
    e_out,
    aw,
    sw,
    ew,
    tok,
    home,
    act,
    x_t,
    dy_t,
    y_acc,
    dx_acc,
    ffn_theirs,
    dx_theirs,
    gate_mine,
    gate_theirs,
    part_theirs,
    dk_acc,
    dv_acc,
    a_one,
    a_two,
    a_came,
    s_one,
    s_two,
    s_came,
    e_came,
    load_sem,
    a_one_sems,
    a_two_sems,
    a_line_sems,
    s_one_sems,
    s_two_sems,
    s_line_sems,
    e_line_sems,
    e_last_sems,
    home_sems,
    twin_sems,
):
    f32, bf16 = jnp.float32, jnp.bfloat16
    at = Place(planes)
    length, width = x_ref.shape
    heads_width = q_ref.shape[1]
    half = tok.shape[2]
    top = ids_ref.shape[1]
    expert = LineSum(at, ew, e_came, e_out, e_line_sems, e_last_sems)
    shared = PlaneSum(
        at, sw, s_one, s_two, s_came, s_one_sems, s_two_sems, s_line_sems
    )
    attn = PlaneSum(at, aw, a_one, a_two, a_came, a_one_sems, a_two_sems, a_line_sems)
    loads = [
        pltpu.make_async_copy(e_all, ew, load_sem.at[0]),
        pltpu.make_async_copy(arrived_ref, tok, load_sem.at[1]),
        pltpu.make_async_copy(s_all, sw, load_sem.at[2]),
        pltpu.make_async_copy(a_all, aw, load_sem.at[3]),
        pltpu.make_async_copy(h_ref, gx_ref, load_sem.at[4]),
    ]
    ffn_mine = act.at[length:, :width]
    part_mine = act.at[length:, width : 2 * width]
    dx_mine = act.at[length:, 2 * width : 3 * width]
    dproj = act.at[:length, 2 * width : 2 * width + 3 * heads_width]
    step = min(length, 256)
    chunks = [slice(i, i + step) for i in range(0, length, step)]
    for load in loads:
        load.start()
    at.greet()
    loads[0].wait()
    loads[1].wait()

    def home_copy(t, j):
        return send(
            tok.at[t, j], home.at[t, j], home_sems.at[0, t, j], home_sems.at[1, t, j], at.near(j)
        )

    count = experts * half
    for t in range(2):
        rows = slice(t * count, (t + 1) * count)

        def x_of(some):
            some = slice(some.start // half, some.stop // half)
            return tok[t, some, :, :width].reshape(-1, width)

        def dy_of(some):
            some = slice(some.start // half, some.stop // half)
            return tok[t, some, :, width:].reshape(-1, width)

        for some in chunks:
            x_t[:, rows.start + some.start : rows.start + some.stop] = x_of(some).T
            dy_t[:, rows.start + some.start : rows.start + some.stop] = dy_of(some).T
        branch(x_of, dy_of, rows, ew, act, y_acc, dx_acc)
        for j in range(experts):
            some = slice(j * half, (j + 1) * half)
            tok[t, j, :, :width] = y_acc[some, :].astype(bf16)
            tok[t, j, :, width:] = dx_acc[some, :].astype(bf16)
        home[t, 0] = tok[t, 0]
        for j in range(1, experts):
            home_copy(t, j).start()

    def grads_of(i, carry):
        plane = jnp.where(at.z * 2 < planes, planes - 1 - i, i)
        weight_grads(plane, planes, 2 * count, x_t, dy_t, act, ew)
        expert.start_plane(plane)
        return carry

    lax.fori_loop(0, planes, grads_of, 0)

    todo = []
    extra = [functools.partial(shared.middle, k) for k in range(planes - 3, -1, -1)]
    extra += [functools.partial(shared.step, k) for k in range(planes - 1, 0, -1)]
    for k in range(planes - 2, 0, -1):
        for j in range(GROUP):
            todo.append(functools.partial(expert.step, k, j))
            if k == 1 and extra:
                todo.append(extra.pop(0))
    todo += extra
    for j in range(GROUP):
        todo.append(functools.partial(expert.total, j))
    todo.reverse()

    def tick(count=1):
        for _ in range(count):
            if todo:
                todo.pop()()

    loads[2].wait()
    rows = slice(0, length)
    for some in chunks:
        x_t[:, some] = xf_ref[some, :].T
        dy_t[:, some] = cot_ref[some, :].T
    branch(lambda some: xf_ref[some, :], lambda some: cot_ref[some, :], rows, sw, act, y_acc, dx_acc)
    tick()

    def shared_grads(i, carry):
        weight_grads(i, planes, length, x_t, dy_t, act, sw)
        return carry

    lax.fori_loop(0, planes, shared_grads, 0)
    for k in range(planes - 1, -1, -1):
        shared.start(k)
    tick()

    for t in range(2):
        for j in range(1, experts):
            home_copy(t, j).wait_recv()
    for rows in chunks:
        y, dx = y_acc[rows, :], dx_acc[rows, :]
        gate = jnp.zeros((step, 128), f32)
        dy = cot_ref[rows, :].astype(f32)
        for t in range(2):
            index = lax.broadcasted_iota(jnp.int32, (1, count), 1) + t * count
            slot = [
                (pair_ref[rows, top + r : top + r + 1].astype(jnp.int32) == index).astype(f32)
                for r in range(top)
            ]
            for r in range(top):
                part = dot_nn(slot[r].astype(bf16), home[t, :, :, :width].reshape(count, width))
                y += pair_ref[rows, r : r + 1] * part
                grad = jnp.sum(dy * part, axis=-1, keepdims=True)
                gate += jnp.where(lanes() == ids_ref[rows, r : r + 1] + 2, grad, 0.0)
            dx += dot_nn(sum(slot).astype(bf16), home[t, :, :, width:].reshape(count, width))
        ffn_mine[rows, :] = y.astype(bf16)
        dx_mine[rows, :] = dx.astype(bf16)
        gate_mine[rows, :] = gate
    swaps = [
        send(mine, theirs, twin_sems.at[0, i], twin_sems.at[1, i], at.twin())
        for i, (mine, theirs) in enumerate(
            ((dx_mine, dx_theirs), (gate_mine, gate_theirs), (ffn_mine, ffn_theirs))
        )
    ]
    for swap in swaps:
        swap.start()
    shared.middle(planes - 1)
    tick()
    swaps[0].wait_recv()
    swaps[1].wait_recv()

    loads[3].wait()
    loads[4].wait()
    small = blocks_of(aw, 4 * heads_width, 4 * heads_width + 128)
    small_rows = small.astype(f32).T
    g_one, g_two = small_rows[0:1, :], small_rows[1:2, :]
    swaps[2].wait_recv()
    grad_g_two = jnp.zeros((1, width), f32)
    grad_small = jnp.zeros((width, 128), f32)
    for rows in chunks:
        probs = probs_ref[rows, :]
        grad_probs = gate_mine[rows, :] + gate_theirs[rows, :]
        grad_logits = (
            probs * (grad_probs - jnp.sum(probs * grad_probs, axis=-1, keepdims=True))
        ).astype(bf16)
        grad_small += dot_nn(x_t[:, rows], grad_logits)
        grad_xf = dx_mine[rows, :].astype(f32) + dx_theirs[rows, :].astype(f32)
        grad_xf += dot_nt(grad_logits, small)
        h = gx_ref[rows, :]
        out_ref[rows, :] = (
            h + (ffn_mine[rows, :].astype(f32) + ffn_theirs[rows, :].astype(f32))
        ).astype(bf16)
        grad_h, grad_gain = norm_back_rows(grad_xf, h, g_two)
        grad_g_two += grad_gain
        grad_h = cot_ref[rows, :].astype(f32) + grad_h
        gx_ref[rows, :] = grad_h
        dy_t[:, rows] = grad_h.astype(bf16).T
        act[rows, :heads_width] = dot_nn(
            grad_h.astype(bf16), blocks_of(aw, 3 * heads_width, 4 * heads_width)
        ).astype(bf16)
    for rows in chunks:
        x = x_ref[rows, :].astype(f32)
        rms = lax.rsqrt(jnp.mean(x * x, axis=-1, keepdims=True) + epsilon)
        x_t[:, rows] = (x * rms * g_one).astype(bf16).T
    tick()

    def to_grads(start, columns, left, right):
        blocks = aw.shape[0]
        for i in range(0, blocks, blocks // 4):
            some = slice(i, i + blocks // 4)
            features = slice(i * aw.shape[1], (i + blocks // 4) * aw.shape[1])
            block = dot_nn(left[features, :length], right())
            aw[some, :, start : start + columns] = block.astype(bf16).reshape(
                blocks // 4, aw.shape[1], columns
            )

    to_grads(3 * heads_width, heads_width, dy_t, lambda: o_ref[...])
    shared.middle(planes - 2)
    cosine, sine = cos_ref[...], sin_ref[...]
    scale = HD ** (-0.5)
    pairs = heads_width // 128
    spans = attention_blocks(length)[::-1]
    for start, stop in spans:
        row = lax.broadcasted_iota(jnp.int32, (stop - start, stop), 0) + start
        column = lax.broadcasted_iota(jnp.int32, (stop - start, stop), 1)
        allowed = (column <= row) & (seg_col[start:stop, :] == seg_row[:, :stop])
        y_acc[start:stop, :stop] = jnp.where(allowed, 0.0, -1e30)
    for g in range(pairs):
        columns = slice(128 * g, 128 * (g + 1))
        for start, stop in spans:
            queries = q_ref[start:stop, columns]
            grads = act[start:stop, columns]
            keys, values = k_ref[:stop, columns], v_ref[:stop, columns]
            grad_q = jnp.zeros((stop - start, 128), f32)
            grad_k = jnp.zeros((stop, 128), f32)
            grad_v = jnp.zeros((stop, 128), f32)
            for i in range(2):
                mask = lanes() // HD == i
                one_q = jnp.where(mask, queries, jnp.zeros_like(queries))
                one_do = jnp.where(mask, grads, jnp.zeros_like(grads))
                one_k = jnp.where(mask, keys, jnp.zeros_like(keys))
                scores = dot_nt(one_q, keys) * scale + y_acc[start:stop, :stop]
                h = 2 * g + i
                weights = jnp.exp(scores - lse_ref[start:stop, h : h + 1])
                grad_w = dot_nt(one_do, values)
                inner = jnp.sum(weights * grad_w, axis=-1, keepdims=True)
                grad_s = (weights * (grad_w - inner)).astype(bf16)
                grad_q += dot_nn(grad_s, one_k)
                grad_k += dot_tn(grad_s, one_q)
                grad_v += dot_tn(weights.astype(bf16), one_do)
            dproj[start:stop, columns] = turn(
                grad_q * scale, cosine[start:stop, :], -sine[start:stop, :]
            ).astype(bf16)
            if stop == length:
                dk_acc[...] = grad_k * scale
                dv_acc[...] = grad_v
            else:
                dk_acc[:stop, :] += grad_k * scale
                dv_acc[:stop, :] += grad_v
            tick()
        dproj[:, heads_width + 128 * g : heads_width + 128 * (g + 1)] = turn(
            dk_acc[...], cosine, -sine
        ).astype(bf16)
        dproj[:, 2 * heads_width + 128 * g : 2 * heads_width + 128 * (g + 1)] = dv_acc[
            ...
        ].astype(bf16)
    for i, rows in enumerate(chunks):
        part = dot_nt(dproj[rows, :], blocks_of(aw, 0, 3 * heads_width))
        part_mine[rows, :] = part.astype(bf16)
    swap = send(part_mine, part_theirs, twin_sems.at[0, 3], twin_sems.at[1, 3], at.twin())
    swap.start()
    for i in range(3):
        columns = slice(i * heads_width, (i + 1) * heads_width)
        to_grads(i * heads_width, heads_width, x_t, lambda: dproj[:, columns])
    swap.wait_recv()
    grad_g_one = jnp.zeros((1, width), f32)
    for rows in chunks:
        grad_xa = part_mine[rows, :].astype(f32) + part_theirs[rows, :].astype(f32)
        grad_x, grad_gain = norm_back_rows(grad_xa, x_ref[rows, :].astype(f32), g_one)
        gx_ref[rows, :] += grad_x
        grad_g_one += grad_gain
    index = lax.broadcasted_iota(jnp.int32, (128, 1), 0)
    gains = jnp.where(index == 0, grad_g_one, 0.0) + jnp.where(index == 1, grad_g_two, 0.0)
    small_grads = (gains.T + grad_small).astype(bf16)
    aw[:, :, 4 * heads_width :] = small_grads.reshape(aw.shape[0], aw.shape[1], 128)
    for k in range(planes - 1, -1, -1):
        attn.start(k)
    tick(3)
    for k in range(planes - 1, -1, -1):
        attn.middle(k)
        tick()
    for k in range(planes - 1, 0, -1):
        attn.step(k)
        tick()
    tick(len(todo))
    shared.total(s_out)
    attn.total(a_out)
    for j in range(1, GROUP):
        expert.arrive(j)

    for i in range(3):
        swaps[i].wait_send()
    swap.wait_send()
    for t in range(2):
        for j in range(1, experts):
            home_copy(t, j).wait_send()
    expert.sent()
    shared.sent()
    attn.sent()


def backward_pass(planes, experts, inputs, far):
    bf16, f32, dma = jnp.bfloat16, jnp.float32, pltpu.SemaphoreType.DMA
    a_all, s_all, e_all, arrived, _ = far
    length, width = inputs[0].shape
    _, rows, a_width = a_all.shape
    n = planes * GROUP
    s_width, e_width = s_all.shape[2], e_all.shape[2]
    slots = 2 * experts * arrived.shape[2]
    vmem, anywhere = pl.BlockSpec(memory_space=pltpu.VMEM), pl.BlockSpec(memory_space=pl.ANY)
    shape = jax.ShapeDtypeStruct

    def plane_buffers(columns):
        return [
            pltpu.VMEM((planes, 2, rows, columns), bf16),
            pltpu.VMEM((planes, rows, columns), bf16),
            pltpu.VMEM((planes + 1, rows, columns), bf16),
        ]

    plane_sems = [dma((2, planes, 2)), dma((2, planes)), dma((2, 2, planes))]
    return pl.pallas_call(
        functools.partial(backward_kernel, planes, experts),
        out_shape=(
            shape((length, width), bf16),
            shape((length, width), f32),
            shape((rows, a_width), f32),
            shape((rows, s_width), bf16),
            shape((GROUP, rows, e_width), bf16),
        ),
        in_specs=[vmem] * len(inputs) + [anywhere] * len(far),
        out_specs=(vmem,) * 5,
        scratch_shapes=[
            pltpu.VMEM(a_all.shape, bf16),
            pltpu.VMEM(s_all.shape, bf16),
            pltpu.VMEM(e_all.shape, bf16),
            pltpu.VMEM(arrived.shape, bf16),
            pltpu.VMEM(arrived.shape, bf16),
            pltpu.VMEM((slots, max(s_width, e_width)), bf16),
            pltpu.VMEM((width, slots), bf16),
            pltpu.VMEM((width, slots), bf16),
            pltpu.VMEM((length, width), f32),
            pltpu.VMEM((length, width), f32),
            pltpu.VMEM((length, width), bf16),
            pltpu.VMEM((length, width), bf16),
            pltpu.VMEM((length, 128), f32),
            pltpu.VMEM((length, 128), f32),
            pltpu.VMEM((length, width), bf16),
            pltpu.VMEM((length, 128), f32),
            pltpu.VMEM((length, 128), f32),
            *plane_buffers(a_width),
            *plane_buffers(s_width),
            pltpu.VMEM(((planes + 1) * GROUP, rows, e_width), bf16),
            dma((5,)),
            *plane_sems,
            *plane_sems,
            dma((2, 2, n)),
            dma((2, GROUP)),
            dma((2, 2, GROUP)),
            dma((2, 4)),
        ],
        compiler_params=pltpu.CompilerParams(
            collective_id=1, has_side_effects=True, vmem_limit_bytes=62 << 20
        ),
    )(*inputs, *far)


def local_grouped(
    planes,
    tokens,
    segment_ids,
    expert_ids,
    slot_order,
    gain_attn,
    qkv_weight,
    out_weight,
    gain_ffn,
    router_weight,
    gate_up,
    down_weight,
    shared_gate_up,
    shared_down,
    cotangent,
):
    bf16, f32 = jnp.bfloat16, jnp.float32
    rows, heads_width = qkv_weight.shape[0], qkv_weight.shape[2]
    experts, hidden = down_weight.shape[0], down_weight.shape[1]
    s_hidden = shared_down.shape[0]
    length, width = tokens.shape
    top = expert_ids.shape[1]
    member = lax.rem(lax.axis_index("dp"), GROUP)
    core = lax.axis_index("tensor")
    cuts = [3 * heads_width, heads_width, 128]
    edges = [sum(cuts[:i]) for i in range(len(cuts) + 1)]

    def part(array, i):
        return array[..., edges[i] : edges[i + 1]]

    expert_packed = jnp.concatenate(
        [gate_up.reshape(experts, rows, 2 * hidden), down_weight.transpose(0, 2, 1)], axis=2
    )
    small = jnp.concatenate([gain_attn[:, None], gain_ffn[:, None], router_weight], axis=1)
    small = jnp.pad(small, ((0, 0), (0, 128 - small.shape[1])))
    attn_packed = jnp.concatenate(
        [qkv_weight.reshape(rows, 3 * heads_width), out_weight.T, small], axis=1
    )
    shared_packed = jnp.concatenate(
        [shared_gate_up.reshape(rows, 2 * s_hidden), shared_down.T], axis=1
    )
    cosine, sine = rotary(length, HD)
    cosine = jnp.tile(cosine[:, 0], (1, 4))
    sine = jnp.tile(sine[:, 0], (1, 4))
    orders = slot_order.reshape(length, top)
    inputs = (
        tokens,
        cotangent,
        segment_ids.reshape(length, 1),
        segment_ids,
        expert_ids,
        orders,
        expert_ids.T,
        orders.T,
        cosine,
        sine,
    )
    (
        all_attn,
        all_shared,
        all_expert,
        queries,
        keys_all,
        values_all,
        mixed,
        log_totals,
        hidden_state,
        xn_one,
        xn_two,
        probs,
        pair_facts,
        _,
        arrived,
    ) = forward_pass(
        planes, experts, inputs, (attn_packed, shared_packed, expert_packed), heads_width
    )
    output, grad_tokens, mine, mine_shared, mine_expert = backward_pass(
        planes,
        experts,
        (
            tokens,
            cotangent,
            segment_ids.reshape(length, 1),
            segment_ids,
            expert_ids,
            cosine,
            sine,
            queries,
            keys_all,
            values_all,
            mixed,
            log_totals,
            xn_two,
            probs,
            pair_facts,
        ),
        (all_attn, all_shared, all_expert, arrived, hidden_state),
    )
    mine_shared, mine_expert = mine_shared.astype(f32), mine_expert.astype(f32)
    small_mine = part(mine, 2)
    return (
        output,
        grad_tokens,
        small_mine[:, 0],
        part(mine, 0).reshape(rows, 3, heads_width),
        part(mine, 1).T,
        small_mine[:, 1],
        small_mine[:, 2 : 2 + experts],
        mine_expert[:, :, : 2 * hidden].reshape(experts, rows, 2, hidden),
        mine_expert[:, :, 2 * hidden :].transpose(0, 2, 1),
        mine_shared[:, : 2 * s_hidden].reshape(rows, 2, s_hidden),
        mine_shared[:, 2 * s_hidden :].T,
    )


def solution(mesh):
    def pick(*args):
        experts, rows = args[9].shape[0], args[5].shape[0]
        if experts == GROUP and mesh.shape["dp"] % GROUP == 0 and rows % 16 == 0:
            return local_grouped(mesh.shape["dp"] // GROUP, *args)
        return local_plain(*args)

    return jax.shard_map(
        pick,
        mesh=mesh,
        in_specs=(
            P("dp", None),
            P("dp", None),
            P("dp", None),
            P("dp", None),
            P("dp"),
            P("dp", None, "tensor"),
            P("tensor", "dp"),
            P("dp"),
            P("dp", None),
            P(None, "dp", None, "tensor"),
            P(None, "tensor", "dp"),
            P("dp", None, "tensor"),
            P("tensor", "dp"),
            P("dp", None),
        ),
        out_specs=(
            P("dp", None),
            P("dp", None),
            P("dp"),
            P("dp", None, "tensor"),
            P("tensor", "dp"),
            P("dp"),
            P("dp", None),
            P(None, "dp", None, "tensor"),
            P(None, "tensor", "dp"),
            P("dp", None, "tensor"),
            P("tensor", "dp"),
        ),
        check_vma=False,
    )
```

```python
import functools
import math

import jax
import jax.numpy as jnp
from jax import lax
from jax.experimental import pallas as pl
from jax.experimental.pallas import tpu as pltpu
from jax.sharding import PartitionSpec as P

HD = 64
GROUP = 4
MESH = pl.DeviceIdType.MESH


epsilon = 1e-06


def rms_scale(values):
    return lax.rsqrt(jnp.mean(values * values, axis=-1, keepdims=True) + epsilon)


def rotary(length, head_dim):
    half_dim = head_dim // 2
    position = jnp.arange(length).astype(jnp.float32)[:, None]
    inverse = jnp.exp(
        jnp.arange(half_dim).astype(jnp.float32) * (-2.0 * math.log(10000.0) / head_dim)
    )
    angles = position * inverse[None, :]
    return (jnp.cos(angles)[:, None, :], jnp.sin(angles)[:, None, :])


def rotate(values, cosine, sine):
    half_dim = values.shape[-1] // 2
    first_half = values[..., :half_dim]
    second_half = values[..., half_dim:]
    return jnp.concatenate(
        [first_half * cosine - second_half * sine, second_half * cosine + first_half * sine],
        axis=-1,
    )


def route_slots(pair_ids, rank_order, capacity, experts):
    length = pair_ids.shape[0]
    top_count = pair_ids.shape[1]
    pair_expert = pair_ids.reshape(-1)
    pair_count = pair_expert.shape[0]
    ordered = jnp.zeros((pair_count,), jnp.int32).at[rank_order].set(pair_expert)
    onehot = (ordered[:, None] == jnp.arange(experts, dtype=jnp.int32)[None, :]).astype(jnp.int32)
    running = jnp.cumsum(onehot, axis=0)
    ranked_slot = jnp.sum(running * onehot, axis=1) - 1
    position = ranked_slot[rank_order]
    kept_pair = position < capacity
    slot_index = jnp.where(kept_pair, pair_expert * capacity + position, experts * capacity)
    token_of_pair = jnp.arange(pair_count, dtype=jnp.int32) // top_count
    slot_token = (
        jnp.full((experts * capacity,), length, jnp.int32)
        .at[slot_index]
        .set(token_of_pair, mode="drop")
    )
    return (slot_token, slot_index.reshape(length, top_count), kept_pair.reshape(length, top_count))


def silu_back(both_parts, grad_hidden):
    gate_part = both_parts[..., 0, :]
    up_part = both_parts[..., 1, :]
    sigma = jax.nn.sigmoid(gate_part)
    slope = sigma * (1.0 + gate_part * (1.0 - sigma))
    return jnp.stack(
        [grad_hidden * up_part * slope, grad_hidden * gate_part * sigma], axis=-2
    ).astype(jnp.bfloat16)


def silu_forward(both_parts):
    return (jax.nn.silu(both_parts[..., 0, :]) * both_parts[..., 1, :]).astype(jnp.bfloat16)


def norm_back(grad_norm, values, scale_rows, gain):
    grad_gain = jnp.sum(grad_norm * values * scale_rows, axis=0)
    inner = grad_norm * gain
    grad_values = scale_rows * inner - values * scale_rows**3 * jnp.mean(
        inner * values, axis=-1, keepdims=True
    )
    return (grad_values, grad_gain)


def split_blocks(length):
    block = min(512, length)
    return (block, length // block)


def masked_scores(query_block, keys_all, query_pos, query_seg, segment, scale):
    positions = jnp.arange(keys_all.shape[0])
    scores = (
        jnp.einsum("qhd,khd->hqk", query_block, keys_all, preferred_element_type=jnp.float32)
        * scale
    )
    allowed = (positions[None, :] <= query_pos[:, None]) & (segment[None, :] == query_seg[:, None])
    return jnp.where(allowed[None], scores, -1e30)


def attend_forward(queries, keys_all, values_all, segment, scale):
    length, head_count, head_dim = queries.shape
    block, count_blocks = split_blocks(length)
    positions = jnp.arange(length)

    def one_block(inputs):
        query_block, query_pos, query_seg = inputs
        scores = masked_scores(query_block, keys_all, query_pos, query_seg, segment, scale)
        largest = jnp.max(scores, axis=-1, keepdims=True)
        expo = jnp.exp(scores - largest)
        total = jnp.sum(expo, axis=-1, keepdims=True)
        probs = (expo / total).astype(jnp.bfloat16)
        mixed = jnp.einsum("hqk,khd->qhd", probs, values_all, preferred_element_type=jnp.float32)
        return (mixed.astype(jnp.bfloat16), (largest + jnp.log(total))[..., 0])

    blocks = (
        queries.reshape(count_blocks, block, head_count, head_dim),
        positions.reshape(count_blocks, block),
        segment.reshape(count_blocks, block),
    )
    mixed_all, log_totals = lax.map(one_block, blocks)
    return (mixed_all.reshape(length, head_count * head_dim), log_totals)


def attend_backward(queries, keys_all, values_all, segment, scale, grad_mixed, log_totals):
    length, head_count, head_dim = queries.shape
    block, count_blocks = split_blocks(length)
    positions = jnp.arange(length)

    def one_block(carry, inputs):
        grad_keys, grad_values = carry
        query_block, query_pos, query_seg, grad_block, log_block = inputs
        scores = masked_scores(query_block, keys_all, query_pos, query_seg, segment, scale)
        probs = jnp.exp(scores - log_block[:, :, None])
        grad_probs = jnp.einsum(
            "qhd,khd->hqk", grad_block, values_all, preferred_element_type=jnp.float32
        )
        inner = jnp.sum(probs * grad_probs, axis=-1, keepdims=True)
        grad_scores = (probs * (grad_probs - inner)).astype(jnp.bfloat16)
        grad_query = (
            jnp.einsum("hqk,khd->qhd", grad_scores, keys_all, preferred_element_type=jnp.float32)
            * scale
        )
        grad_keys = (
            grad_keys
            + jnp.einsum(
                "hqk,qhd->khd", grad_scores, query_block, preferred_element_type=jnp.float32
            )
            * scale
        )
        grad_values = grad_values + jnp.einsum(
            "hqk,qhd->khd",
            probs.astype(jnp.bfloat16),
            grad_block,
            preferred_element_type=jnp.float32,
        )
        return ((grad_keys, grad_values), grad_query)

    zeros_kv = jnp.zeros((length, head_count, head_dim), jnp.float32)
    blocks = (
        queries.reshape(count_blocks, block, head_count, head_dim),
        positions.reshape(count_blocks, block),
        segment.reshape(count_blocks, block),
        grad_mixed.reshape(count_blocks, block, head_count, head_dim),
        log_totals,
    )
    (grad_keys, grad_values), grad_queries = lax.scan(one_block, (zeros_kv, zeros_kv), blocks)
    return (grad_queries.reshape(length, head_count, head_dim), grad_keys, grad_values)


def sum_rows(grad, axis, scatter_dimension, tiled):
    part = lax.psum_scatter(
        grad.astype(jnp.bfloat16), axis, scatter_dimension=scatter_dimension, tiled=tiled
    )
    return part.astype(jnp.float32)


def local_plain(
    tokens,
    segment_ids,
    expert_ids,
    slot_order,
    gain_attn,
    qkv_weight,
    out_weight,
    gain_ffn,
    router_weight,
    gate_up,
    down_weight,
    shared_gate_up,
    shared_down,
    cotangent,
):
    g_one, w_qkv, w_out, g_two, w_router, w_gate_up, w_down, s_gate_up, s_down = (
        lax.all_gather(gain_attn, "dp", axis=0, tiled=True),
        lax.all_gather(qkv_weight, "dp", axis=0, tiled=True),
        lax.all_gather(out_weight, "dp", axis=1, tiled=True),
        lax.all_gather(gain_ffn, "dp", axis=0, tiled=True),
        lax.all_gather(router_weight, "dp", axis=0, tiled=True),
        lax.all_gather(gate_up, "dp", axis=1, tiled=True),
        lax.all_gather(down_weight, "dp", axis=2, tiled=True),
        lax.all_gather(shared_gate_up, "dp", axis=0, tiled=True),
        lax.all_gather(shared_down, "dp", axis=1, tiled=True),
    )
    length = tokens.shape[0]
    width = tokens.shape[1]
    experts_count = w_router.shape[1]
    top_count = expert_ids.shape[1]
    capacity = length * top_count // experts_count
    head_dim = HD
    local_heads = w_qkv.shape[2] // head_dim
    scale = head_dim ** (-0.5)
    segment = segment_ids[0]
    slot_token, slot_index, kept_pair = route_slots(
        expert_ids, slot_order[0], capacity, experts_count
    )
    kept_float = kept_pair.astype(jnp.float32)
    slot_valid = slot_token < length
    slot_rows = jnp.minimum(slot_token, length - 1)
    pair_slots = jnp.minimum(slot_index, experts_count * capacity - 1)
    xfull = tokens.astype(jnp.float32)
    rms_one = rms_scale(xfull)
    xn_one = (xfull * rms_one * g_one.astype(jnp.float32)).astype(jnp.bfloat16)
    projected = jnp.einsum("td,dch->tch", xn_one, w_qkv, preferred_element_type=jnp.float32)
    cosine, sine = rotary(length, head_dim)
    queries = rotate(projected[:, 0].reshape(length, local_heads, head_dim), cosine, sine).astype(
        jnp.bfloat16
    )
    keys_all = rotate(projected[:, 1].reshape(length, local_heads, head_dim), cosine, sine).astype(
        jnp.bfloat16
    )
    values_all = projected[:, 2].reshape(length, local_heads, head_dim).astype(jnp.bfloat16)
    mixed, log_totals = attend_forward(queries, keys_all, values_all, segment, scale)
    attn_share = lax.psum_scatter(
        jnp.dot(mixed, w_out, preferred_element_type=jnp.float32),
        "tensor",
        scatter_dimension=1,
        tiled=True,
    )
    attn = lax.all_gather(attn_share, "tensor", axis=1, tiled=True)
    hidden_state = xfull + attn
    rms_two = rms_scale(hidden_state)
    xn_two = (hidden_state * rms_two * g_two.astype(jnp.float32)).astype(jnp.bfloat16)
    logits = jnp.dot(xn_two, w_router, preferred_element_type=jnp.float32)
    probs = jax.nn.softmax(logits, axis=-1)
    gates = jnp.take_along_axis(probs, expert_ids, axis=1) * kept_float
    dispatched = (xn_two[slot_rows] * slot_valid[:, None].astype(jnp.bfloat16)).reshape(
        experts_count, capacity, width
    )
    both_parts = jnp.einsum(
        "ecd,edjf->ecjf", dispatched, w_gate_up, preferred_element_type=jnp.float32
    )
    expert_hidden = silu_forward(both_parts)
    expert_out = jnp.einsum(
        "ecf,efd->ecd", expert_hidden, w_down, preferred_element_type=jnp.float32
    ).reshape(experts_count * capacity, width)
    picked = expert_out[pair_slots]
    moe = jnp.sum(gates[:, :, None] * picked, axis=1)
    shared_both = jnp.einsum("td,djf->tjf", xn_two, s_gate_up, preferred_element_type=jnp.float32)
    shared_hidden = silu_forward(shared_both)
    shared_out = jnp.dot(shared_hidden, s_down, preferred_element_type=jnp.float32)
    ffn_share = lax.psum_scatter(
        (moe + shared_out).astype(jnp.bfloat16), "tensor", scatter_dimension=1, tiled=True
    ).astype(jnp.float32)
    ffn = lax.all_gather(ffn_share.astype(jnp.bfloat16), "tensor", axis=1, tiled=True).astype(
        ffn_share.dtype
    )
    output = (hidden_state + ffn).astype(jnp.bfloat16)
    grad_y = cotangent.astype(jnp.float32)
    grad_shared_hidden = jnp.einsum(
        "td,fd->tf", cotangent, s_down, preferred_element_type=jnp.float32
    )
    grad_s_down = jnp.einsum(
        "tf,td->fd", shared_hidden, cotangent, preferred_element_type=jnp.float32
    )
    grad_shared_both = silu_back(shared_both, grad_shared_hidden)
    grad_s_gate_up = jnp.einsum(
        "td,tjf->djf", xn_two, grad_shared_both, preferred_element_type=jnp.float32
    )
    grad_xn_shared = jnp.einsum(
        "tjf,djf->td", grad_shared_both, s_gate_up, preferred_element_type=jnp.float32
    )
    slot_gate = (
        jnp.zeros((experts_count * capacity,), jnp.float32)
        .at[slot_index.reshape(-1)]
        .set(gates.reshape(-1), mode="drop")
    )
    grad_expert_out = (
        (slot_gate[:, None] * grad_y[slot_rows])
        .astype(jnp.bfloat16)
        .reshape(experts_count, capacity, width)
    )
    grad_gates_part = kept_float * jnp.sum(grad_y[:, None, :] * picked, axis=-1)
    grad_expert_hidden = jnp.einsum(
        "ecd,efd->ecf", grad_expert_out, w_down, preferred_element_type=jnp.float32
    )
    grad_w_down = jnp.einsum(
        "ecf,ecd->efd", expert_hidden, grad_expert_out, preferred_element_type=jnp.float32
    )
    grad_both = silu_back(both_parts, grad_expert_hidden)
    grad_w_gate_up = jnp.einsum(
        "ecd,ecjf->edjf", dispatched, grad_both, preferred_element_type=jnp.float32
    )
    grad_dispatched = jnp.einsum(
        "ecjf,edjf->ecd", grad_both, w_gate_up, preferred_element_type=jnp.float32
    ).reshape(experts_count * capacity, width)
    grad_xn_moe = jnp.sum(kept_float[:, :, None] * grad_dispatched[pair_slots], axis=1)
    grad_xn_part, grad_gates_share = (
        lax.psum_scatter(grad_xn_shared + grad_xn_moe, "tensor", scatter_dimension=1, tiled=True),
        lax.psum_scatter(grad_gates_part, "tensor", scatter_dimension=1, tiled=True),
    )
    grad_xn_sum, grad_gates = (
        lax.all_gather(grad_xn_part, "tensor", axis=1, tiled=True),
        lax.all_gather(grad_gates_share, "tensor", axis=1, tiled=True),
    )
    expert_match = (
        expert_ids[:, :, None] == jnp.arange(experts_count, dtype=jnp.int32)[None, None, :]
    ).astype(jnp.float32)
    grad_probs = jnp.sum(expert_match * grad_gates[:, :, None], axis=1)
    grad_logits = (
        probs * (grad_probs - jnp.sum(probs * grad_probs, axis=-1, keepdims=True))
    ).astype(jnp.bfloat16)
    grad_w_router = jnp.einsum("td,te->de", xn_two, grad_logits, preferred_element_type=jnp.float32)
    grad_xn_two = grad_xn_sum + jnp.einsum(
        "te,de->td", grad_logits, w_router, preferred_element_type=jnp.float32
    )
    grad_norm_two, grad_g_two = norm_back(
        grad_xn_two, hidden_state, rms_two, g_two.astype(jnp.float32)
    )
    grad_hidden = grad_y + grad_norm_two
    grad_attn = grad_hidden.astype(jnp.bfloat16)
    grad_w_out = jnp.einsum("th,td->hd", mixed, grad_attn, preferred_element_type=jnp.float32)
    grad_mixed = jnp.einsum(
        "td,hd->th", grad_attn, w_out, preferred_element_type=jnp.float32
    ).astype(jnp.bfloat16)
    grad_queries, grad_keys, grad_values = attend_backward(
        queries, keys_all, values_all, segment, scale, grad_mixed, log_totals
    )
    grad_projected = (
        jnp.stack(
            [rotate(grad_queries, cosine, -sine), rotate(grad_keys, cosine, -sine), grad_values],
            axis=1,
        )
        .astype(jnp.bfloat16)
        .reshape(length, 3, local_heads * head_dim)
    )
    grad_w_qkv = jnp.einsum(
        "td,tch->dch", xn_one, grad_projected, preferred_element_type=jnp.float32
    )
    grad_xn_share = lax.psum_scatter(
        jnp.einsum("tch,dch->td", grad_projected, w_qkv, preferred_element_type=jnp.float32).astype(
            jnp.bfloat16
        ),
        "tensor",
        scatter_dimension=1,
        tiled=True,
    ).astype(jnp.float32)
    grad_xn_one = lax.all_gather(
        grad_xn_share.astype(jnp.bfloat16), "tensor", axis=1, tiled=True
    ).astype(grad_xn_share.dtype)
    grad_norm_one, grad_g_one = norm_back(grad_xn_one, xfull, rms_one, g_one.astype(jnp.float32))
    grad_tokens = grad_hidden + grad_norm_one
    (
        grad_g_one,
        grad_w_qkv,
        grad_w_out,
        grad_g_two,
        grad_w_router,
        grad_w_gate_up,
        grad_w_down,
        grad_s_gate_up,
        grad_s_down,
    ) = (
        lax.psum_scatter(grad_g_one, "dp", scatter_dimension=0, tiled=True),
        sum_rows(grad_w_qkv, "dp", scatter_dimension=0, tiled=True),
        sum_rows(grad_w_out, "dp", scatter_dimension=1, tiled=True),
        lax.psum_scatter(grad_g_two, "dp", scatter_dimension=0, tiled=True),
        lax.psum_scatter(grad_w_router, "dp", scatter_dimension=0, tiled=True),
        sum_rows(grad_w_gate_up, "dp", scatter_dimension=1, tiled=True),
        sum_rows(grad_w_down, "dp", scatter_dimension=2, tiled=True),
        sum_rows(grad_s_gate_up, "dp", scatter_dimension=0, tiled=True),
        sum_rows(grad_s_down, "dp", scatter_dimension=1, tiled=True),
    )
    return (
        output,
        grad_tokens,
        grad_g_one,
        grad_w_qkv,
        grad_w_out,
        grad_g_two,
        grad_w_router,
        grad_w_gate_up,
        grad_w_down,
        grad_s_gate_up,
        grad_s_down,
    )


class Place:
    def __init__(self, planes):
        d = lax.axis_index("dp")
        self.planes = planes
        self.d, self.c = d, lax.axis_index("tensor")
        self.z, self.p = d // GROUP, lax.rem(d, GROUP)
        bit0, bit1 = lax.rem(self.p, 2), self.p // 2
        flip0, flip1 = 1 - bit0, 1 - bit1
        self.member = [
            self.p,
            flip0 + 2 * bit1,
            bit0 + 2 * flip1,
            flip0 + 2 * flip1,
        ]

    def near(self, j):
        return (self.z * GROUP + self.member[j], self.c)

    def up(self):
        return (self.d + GROUP, self.c)

    def down(self):
        return (self.d - GROUP, self.c)

    def twin(self):
        return (self.d, 1 - self.c)

    def when(self, condition, action):
        pl.when(condition)(action)

    def has_up(self, k=1):
        return self.z + k < self.planes

    def has_down(self, k=1):
        return self.z - k >= 0

    def greet(self):
        barrier = pltpu.get_barrier_semaphore()

        def hello(device):
            pl.semaphore_signal(barrier, inc=1, device_id=device, device_id_type=MESH)

        hello(self.twin())
        for j in range(1, GROUP):
            hello(self.near(j))
        self.when(self.has_up(), lambda: hello(self.up()))
        self.when(self.has_down(), lambda: hello(self.down()))
        line = self.has_up().astype(jnp.int32) + self.has_down().astype(jnp.int32)
        pl.semaphore_wait(barrier, GROUP + line)


def send(source, target, send_sem, recv_sem, device):
    return pltpu.make_async_remote_copy(
        src_ref=source,
        dst_ref=target,
        send_sem=send_sem,
        recv_sem=recv_sem,
        device_id=device,
        device_id_type=MESH,
    )


class Everywhere:
    def __init__(self, at, own, all_blocks, local_sem, recvs, sends):
        self.at, self.own, self.all = at, own, all_blocks
        self.local_sem, self.recvs, self.sends = local_sem, recvs, sends

    def copy(self, block, source, way, device):
        return send(source, self.all.at[block], self.sends.at[way, block], self.recvs.at[block], device)

    def keep(self):
        return pltpu.make_async_copy(self.own, self.all.at[self.at.d], self.local_sem)

    def landed(self, block):
        self.copy(block, self.own, 0, self.at.near(1)).wait_recv()

    def start_line(self):
        at = self.at
        at.when(at.has_up(), lambda: self.copy(at.d, self.own, 0, at.up()).start())
        at.when(at.has_down(), lambda: self.copy(at.d, self.own, 1, at.down()).start())

    def start_plane(self):
        at = self.at
        self.copy(at.d, self.own, 2, at.near(1)).start()
        self.copy(at.d, self.own, 3, at.near(2)).start()
        self.keep().start()

    def pass_on(self, k):
        at = self.at

        def go(plane, more, way, device_of):
            block = plane * GROUP + at.p
            self.landed(block)
            at.when(more, lambda: self.copy(block, self.all.at[block], way, device_of()).start())

        at.when(at.has_down(k), lambda: go(at.z - k, at.has_up(), 0, at.up))
        at.when(at.has_up(k), lambda: go(at.z + k, at.has_down(), 1, at.down))

    def over_plane(self, k):
        at = self.at

        def go(plane):
            block = plane * GROUP + at.p
            self.copy(block, self.all.at[block], 2, at.near(1)).start()
            self.copy(block, self.all.at[block], 3, at.near(2)).start()

        at.when(at.has_down(k), lambda: go(at.z - k))
        at.when(at.has_up(k), lambda: go(at.z + k))

    def spread(self, k):
        self.pass_on(k)
        self.over_plane(k)

    def cross(self, k):
        at = self.at

        def go(plane):
            first = plane * GROUP + at.member[1]
            second = plane * GROUP + at.member[2]
            even = lax.rem(plane, 2) == 0
            self.landed(first)
            at.when(even, lambda: self.copy(first, self.all.at[first], 3, at.near(2)).start())
            self.landed(second)
            at.when(
                jnp.logical_not(even),
                lambda: self.copy(second, self.all.at[second], 2, at.near(1)).start(),
            )

        if k == 0:
            go(at.z)
        else:
            at.when(at.has_down(k), lambda: go(at.z - k))
            at.when(at.has_up(k), lambda: go(at.z + k))

    def diagonal(self):
        for plane in range(self.at.planes):
            self.landed(plane * GROUP + self.at.member[3])
        self.keep().wait()

    def sent(self):
        at = self.at
        for plane in range(at.planes):
            block = plane * GROUP + at.p
            self.copy(block, self.own, 2, at.near(1)).wait_send()
            self.copy(block, self.own, 3, at.near(2)).wait_send()
            if plane % 2 == 0:
                self.copy(plane * GROUP + at.member[1], self.own, 3, at.near(2)).wait_send()
            else:
                self.copy(plane * GROUP + at.member[2], self.own, 2, at.near(1)).wait_send()

            def gone(way, device_of):
                self.copy(block, self.own, way, device_of()).wait_send()

            at.when((at.z >= plane) & at.has_up(), lambda: gone(0, at.up))
            at.when((at.z <= plane) & at.has_down(), lambda: gone(1, at.down))


class Experts:
    def __init__(self, at, own, all_blocks, local_sem, recvs, sends, across_sends):
        self.at, self.own, self.all = at, own, all_blocks
        self.local_sem, self.recvs, self.sends = local_sem, recvs, sends
        self.across_sends = across_sends

    def line(self, block, source, way, device):
        return send(source, self.all.at[block], self.sends.at[way, block], self.recvs.at[block], device)

    def across(self, j):
        at = self.at
        return send(
            self.own.at[at.member[j]],
            self.all.at[at.d],
            self.across_sends.at[j],
            self.recvs.at[at.d],
            at.near(j),
        )

    def keep(self):
        return pltpu.make_async_copy(self.own.at[self.at.p], self.all.at[self.at.d], self.local_sem)

    def start_plane(self):
        for j in range(1, GROUP):
            self.across(j).start()
        self.keep().start()

    def start_line(self):
        at = self.at
        source = self.own.at[at.p]
        at.when(at.has_up(), lambda: self.line(at.d, source, 0, at.up()).start())
        at.when(at.has_down(), lambda: self.line(at.d, source, 1, at.down()).start())

    def landed(self, block):
        self.line(block, self.own.at[0], 0, self.at.near(1)).wait_recv()

    def plane_step(self, j):
        at = self.at
        block = at.z * GROUP + at.member[j]
        source = self.all.at[block]
        self.landed(block)
        at.when(at.has_up(), lambda: self.line(block, source, 0, at.up()).start())
        at.when(at.has_down(), lambda: self.line(block, source, 1, at.down()).start())

    def line_step(self, k, j):
        at = self.at

        def go(plane, more, way, device_of):
            block = plane * GROUP + at.member[j]
            self.landed(block)
            at.when(more, lambda: self.line(block, self.all.at[block], way, device_of()).start())

        at.when(at.has_down(k), lambda: go(at.z - k, at.has_up(), 0, at.up))
        at.when(at.has_up(k), lambda: go(at.z + k, at.has_down(), 1, at.down))

    def ready(self):
        self.keep().wait()

    def own_sent(self):
        at = self.at
        source = self.own.at[at.p]
        for j in range(1, GROUP):
            self.across(j).wait_send()
        at.when(at.has_up(), lambda: self.line(at.d, source, 0, at.up()).wait_send())
        at.when(at.has_down(), lambda: self.line(at.d, source, 1, at.down()).wait_send())

    def rest_sent(self):
        at = self.at
        for plane in range(at.planes):

            def gone(j, way, device_of):
                block = plane * GROUP + at.member[j]
                self.line(block, self.own.at[0], way, device_of()).wait_send()

            for j in range(GROUP):
                up = at.z >= plane if j else at.z > plane
                down = at.z <= plane if j else at.z < plane
                at.when(up & at.has_up(), lambda: gone(j, 0, at.up))
                at.when(down & at.has_down(), lambda: gone(j, 1, at.down))


def dot_nn(a, b):
    return jnp.dot(a, b, preferred_element_type=jnp.float32)


def dot_nt(a, b):
    return lax.dot_general(a, b, (((1,), (1,)), ((), ())), preferred_element_type=jnp.float32)


def dot_tn(a, b):
    return lax.dot_general(a, b, (((0,), (0,)), ((), ())), preferred_element_type=jnp.float32)


def lanes(count=128):
    return lax.broadcasted_iota(jnp.int32, (1, count), 1)


def turn(values, cosine, sine):
    half = HD // 2
    other = jnp.where(
        lax.rem(lanes(), HD) < half,
        -pltpu.roll(values, 2 * HD - half, 1),
        pltpu.roll(values, half, 1),
    )
    return values * cosine + other * sine


def blocks_of(ref, start, stop):
    block = ref[:, :, start:stop]
    return block.reshape(block.shape[0] * block.shape[1], stop - start)


def attention_blocks(length):
    size = length // 2
    return [(i * size, (i + 1) * size) for i in range(2)]


class PlaneSum:
    def __init__(self, at, own, one, two, came, one_sems, two_sems, line_sems):
        self.at, self.own, self.one, self.two, self.came = at, own, one, two, came
        self.one_sems, self.two_sems, self.line_sems = one_sems, two_sems, line_sems

    def one_copy(self, plane, i, even):
        at = self.at
        j = 1 if even else 2
        target = at.member[3] if i else at.member[j]
        return send(
            self.own.at[plane * GROUP + target],
            self.one.at[plane, i],
            self.one_sems.at[0, plane, i],
            self.one_sems.at[1, plane, i],
            at.near(j),
        )

    def two_copy(self, plane, even):
        return send(
            self.one.at[plane, 1],
            self.two.at[plane],
            self.two_sems.at[0, plane],
            self.two_sems.at[1, plane],
            self.at.near(2 if even else 1),
        )

    def by_parity(self, plane, action):
        even = lax.rem(plane, 2) == 0
        self.at.when(even, lambda: action(True))
        self.at.when(jnp.logical_not(even), lambda: action(False))

    def line(self, source, plane, way, here=False):
        at, sems = self.at, self.line_sems
        slot, device = plane, at.up()
        if way:
            slot = jnp.where(plane == (at.z if here else at.z - 1), at.planes, plane)
            device = at.down()
        return send(
            source, self.came.at[slot], sems.at[0, way, plane], sems.at[1, way, plane], device
        )

    def both_ways(self, action, k):
        at = self.at
        if k == 0:
            action(at.z, 0)
            return
        at.when(at.has_up(k), lambda: action(at.z + k, 0))
        at.when(at.has_down(k), lambda: action(at.z - k, 1))

    def start(self, k):
        def go(plane, way):
            def pair(even):
                self.one_copy(plane, 1, even).start()
                self.one_copy(plane, 0, even).start()

            self.by_parity(plane, pair)

        self.both_ways(go, k)

    def middle(self, k):
        f32 = jnp.float32

        def go(plane, way):
            def stage(even):
                at, one = self.at, self.one
                other = plane * GROUP + (at.member[2] if even else at.member[1])
                self.one_copy(plane, 1, even).wait_recv()
                one[plane, 1] = (one[plane, 1].astype(f32) + self.own[other].astype(f32)).astype(
                    one.dtype
                )
                self.two_copy(plane, even).start()

            self.by_parity(plane, stage)

        self.both_ways(go, k)

    def finish_plane(self, plane):
        f32 = jnp.float32

        def stage(even):
            mine = plane * GROUP + self.at.p
            self.one_copy(plane, 0, even).wait_recv()
            self.two_copy(plane, even).wait_recv()
            self.two[plane] = (
                self.two[plane].astype(f32)
                + self.one[plane, 0].astype(f32)
                + self.own[mine].astype(f32)
            ).astype(self.two.dtype)

        self.by_parity(plane, stage)

    def step(self, k):
        f32 = jnp.float32

        def go(plane, way):
            at = self.at
            self.finish_plane(plane)
            behind = at.has_down() if way == 0 else at.has_up()
            held = self.came

            def add():
                self.line(self.two.at[plane], plane, way, True).wait_recv()
                held[plane] = (held[plane].astype(f32) + self.two[plane].astype(f32)).astype(
                    held.dtype
                )
                self.line(held.at[plane], plane, way).start()

            at.when(behind, add)
            at.when(
                jnp.logical_not(behind), lambda: self.line(self.two.at[plane], plane, way).start()
            )

        self.both_ways(go, k)

    def total(self, out):
        at, f32 = self.at, jnp.float32
        z = at.z
        self.finish_plane(z)
        at.when(at.has_down(), lambda: self.line(self.two.at[z], z, 0, True).wait_recv())
        at.when(at.has_up(), lambda: self.line(self.two.at[z], z, 1, True).wait_recv())
        low = jnp.where(at.has_down(), self.came[z].astype(f32), 0.0)
        high = jnp.where(at.has_up(), self.came[at.planes].astype(f32), 0.0)
        out[...] = (self.two[z].astype(f32) + low + high).astype(out.dtype)

    def sent(self):
        at = self.at
        for plane in range(at.planes):
            even = plane % 2 == 0
            self.one_copy(plane, 0, even).wait_send()
            self.one_copy(plane, 1, even).wait_send()
            self.two_copy(plane, even).wait_send()
            at.when(at.z < plane, lambda: self.line(self.two.at[plane], plane, 0).wait_send())
            at.when(at.z > plane, lambda: self.line(self.two.at[plane], plane, 1).wait_send())


class LineSum:
    def __init__(self, at, own, came, out, columns, line_sems, last_sems):
        self.at, self.own, self.came, self.out = at, own, came, out
        self.line_sems, self.last_sems = line_sems, last_sems
        self.columns, self.size = columns, columns[0].stop - columns[0].start

    def hop(self, source, plane, j, way, here=False):
        at = self.at
        block = plane * GROUP + at.member[j]
        if way == 0:
            slot, device = block, at.up()
        else:
            end = at.z if here else at.z - 1
            slot = jnp.where(plane == end, at.planes, plane) * GROUP + at.member[j]
            device = at.down()
        sems = self.line_sems
        return send(
            source, self.came.at[slot], sems.at[0, way, block], sems.at[1, way, block], device
        )

    def start_plane(self, plane):
        at = self.at

        def go(way):
            for j in range(GROUP):
                self.hop(self.own.at[plane * GROUP + at.member[j]], plane, j, way).start()

        at.when(jnp.logical_not(at.has_down()) & (plane != at.z), lambda: go(0))
        at.when(jnp.logical_not(at.has_up()) & (plane != at.z), lambda: go(1))

    def step(self, k, j):
        at, f32 = self.at, jnp.float32

        def go(plane, way):
            block = plane * GROUP + at.member[j]
            self.hop(self.own.at[block], plane, j, way, True).wait_recv()
            self.came[block] = (
                self.came[block].astype(f32) + self.own[block].astype(f32)
            ).astype(self.came.dtype)
            self.hop(self.came.at[block], plane, j, way).start()

        at.when(at.has_up(k) & at.has_down(), lambda: go(at.z + k, 0))
        at.when(at.has_down(k) & at.has_up(), lambda: go(at.z - k, 1))

    def parts(self, j, here=False):
        at, size = self.at, self.size
        source = self.came.at[at.z * GROUP + at.member[j]]
        target = self.out.at[at.member[j] if here else at.p]
        return [
            send(
                source.at[:, i * size : (i + 1) * size],
                target.at[:, self.columns[i]],
                self.last_sems.at[0, j, i],
                self.last_sems.at[1, j, i],
                at.near(j),
            )
            for i in range(len(self.columns))
        ]

    def total(self, j):
        at, f32, out = self.at, jnp.float32, self.out
        block = at.z * GROUP + at.member[j]
        spare = at.planes * GROUP + at.member[j]
        at.when(at.has_down(), lambda: self.hop(self.own.at[block], at.z, j, 0, True).wait_recv())
        at.when(at.has_up(), lambda: self.hop(self.own.at[block], at.z, j, 1, True).wait_recv())
        low = jnp.where(at.has_down(), self.came[block].astype(f32), 0.0)
        high = jnp.where(at.has_up(), self.came[spare].astype(f32), 0.0)
        total = (self.own[block].astype(f32) + low + high).astype(out.dtype)
        if j == 0:
            for i, columns in enumerate(self.columns):
                out[at.p, :, columns] = total[:, i * self.size : (i + 1) * self.size]
        else:
            self.came[block] = total
            for copy in self.parts(j):
                copy.start()

    def arrive(self, j):
        for copy in self.parts(j, True):
            copy.wait_recv()

    def sent(self):
        at = self.at
        for j in range(1, GROUP):
            for copy in self.parts(j):
                copy.wait_send()
        for plane in range(at.planes):

            def gone(way):
                for j in range(GROUP):
                    self.hop(self.own.at[0], plane, j, way).wait_send()

            at.when(at.z < plane, lambda: gone(0))
            at.when(at.z > plane, lambda: gone(1))


def norm_back_rows(grad, values, gain):
    rms = lax.rsqrt(jnp.mean(values * values, axis=-1, keepdims=True) + epsilon)
    grad_gain = jnp.sum(grad * values * rms, axis=0, keepdims=True)
    inner = grad * gain
    grad_values = rms * inner - values * (rms * rms * rms) * jnp.mean(
        inner * values, axis=-1, keepdims=True
    )
    return grad_values, grad_gain


def branch(x_of, dy_of, rows, weights, start, stride, hidden, act, y_acc, dx_acc):
    f32, bf16 = jnp.float32, jnp.bfloat16
    size, count = 256, rows.stop - rows.start
    step = min(count, 256)

    def body(i, carry):
        offset = pl.multiple_of(i * size, size)

        def weight(part):
            first = pl.multiple_of(start + part * stride + offset, size)
            block = weights[:, :, pl.ds(first, size)]
            return block.reshape(block.shape[0] * block.shape[1], size)

        for first in range(0, count, step):
            some = slice(first, first + step)

            def keep(part, values):
                columns = pl.ds(pl.multiple_of(part * hidden + offset, size), size)
                act[rows.start + first : rows.start + first + step, columns] = values

            g, u = dot_nn(x_of(some), weight(0)), dot_nn(x_of(some), weight(1))
            grad = dot_nn(dy_of(some), weight(2))
            sigma = 1.0 / (1.0 + jnp.exp(-g))
            silu = g * sigma
            eh = (silu * u).astype(bf16)
            dg = (grad * u * (sigma * (1.0 + g * (1.0 - sigma)))).astype(bf16)
            du = (grad * silu).astype(bf16)
            keep(0, dg)
            keep(1, du)
            keep(2, eh)
            y_acc[some, :] += dot_nt(eh, weight(2))
            dx_acc[some, :] += dot_nt(dg, weight(0)) + dot_nt(du, weight(1))
        return carry

    lax.fori_loop(0, hidden // size, body, 0)


def weight_grads(plane, planes, count, x_t, dy_t, act, hidden, grads, start, stride):
    width, bf16 = x_t.shape[0], jnp.bfloat16
    rows = width // planes
    features = pl.ds(pl.multiple_of(plane * rows, 16), rows)
    for part in range(3):
        columns = slice(part * hidden, (part + 1) * hidden)
        left = dy_t if part == 2 else x_t
        block = dot_nn(left[features, :count], act[:count, columns]).astype(bf16)
        target = slice(start + part * stride, start + part * stride + hidden)
        grads[pl.ds(plane * GROUP, GROUP), :, target] = block.reshape(
            GROUP, rows // GROUP, hidden
        )


PROBS, PAIRS, LOGS = 2, 8, 16


def layer_kernel(
    planes,
    experts,
    top,
    heads_width,
    x_ref,
    cot_ref,
    facts,
    facts_t,
    waves,
    a_own,
    s_own,
    e_own,
    out_ref,
    gx_ref,
    a_out,
    s_out,
    e_out,
    aw,
    sw,
    ew,
    tok,
    part_one,
    home,
    act,
    x_t,
    dy_t,
    y_acc,
    dx_acc,
    s_dx,
    q_ref,
    k_ref,
    v_ref,
    o_ref,
    xf_ref,
    row_facts,
    ffn_theirs,
    dx_theirs,
    ret,
    a_one,
    a_two,
    a_came,
    s_one,
    s_two,
    s_came,
    e_came,
    local_sem,
    a_recv,
    a_send,
    s_recv,
    s_send,
    e_recv,
    e_send,
    e_across,
    a_one_sems,
    a_two_sems,
    a_line_sems,
    s_one_sems,
    s_two_sems,
    s_line_sems,
    e_line_sems,
    e_last_sems,
    token_sems,
    home_sems,
    share_sems,
    twin_sems,
):
    f32, bf16 = jnp.float32, jnp.bfloat16
    at = Place(planes)
    length, width = x_ref.shape
    capacity = length * top // experts
    half = capacity // 2
    count = experts * half
    hidden, s_hidden = ew.shape[3] // 3, sw.shape[2] // 6
    step = min(length, 256)
    chunks = [slice(i, i + step) for i in range(0, length, step)]
    seg_col, seg_row = facts[:, 2 * top : 2 * top + 1], facts_t[2 * top : 2 * top + 1, :]

    halves = [
        [slice((2 * k + i) * hidden, (2 * k + i + 1) * hidden) for k in range(3)] for i in range(2)
    ]

    attn_in = Everywhere(at, a_own, aw, local_sem.at[0], a_recv, a_send)
    shared_in = Everywhere(at, s_own, sw, local_sem.at[1], s_recv, s_send)
    expert_in = [
        Experts(
            at,
            part_one.at[i, :, : e_own.shape[1]],
            ew.at[i],
            local_sem.at[2 + i],
            e_recv.at[i],
            e_send.at[i],
            e_across.at[i],
        )
        for i in range(2)
    ]
    expert_out = [
        LineSum(
            at, ew.at[i], e_came.at[i], e_out, halves[i], e_line_sems.at[i], e_last_sems.at[i]
        )
        for i in range(2)
    ]
    shared_out = PlaneSum(at, sw, s_one, s_two, s_came, s_one_sems, s_two_sems, s_line_sems)
    attn_out = PlaneSum(at, aw, a_one, a_two, a_came, a_one_sems, a_two_sems, a_line_sems)

    xa_ref = act.at[:length, :width]
    placed = act.at[:, : 2 * width]
    part_mine = act.at[length:, :width]
    part_theirs = ret.at[:length, :width]
    grad_o = act.at[:length, :heads_width]
    dproj = act.at[:length, heads_width : 4 * heads_width]
    bias = y_acc
    dk_acc, dv_acc = (dx_acc.at[:, 128 * i : 128 * (i + 1)] for i in range(2))

    def halve(i, k):
        return pltpu.make_async_copy(
            e_own.at[:, :, halves[i][k]],
            part_one.at[i, :, : e_own.shape[1], k * hidden : (k + 1) * hidden],
            local_sem.at[4 + 3 * i + k],
        )

    for i in range(2):
        for k in range(3):
            halve(i, k).start()
    at.greet()
    attn_in.start_line()
    attn_in.start_plane()
    for k in range(3):
        halve(0, k).wait()
    expert_in[0].start_plane()
    expert_in[0].start_line()
    shared_in.start_line()
    for k in range(3):
        halve(1, k).wait()

    todo = []

    def tick(amount=1):
        for _ in range(amount):
            if todo:
                todo.pop(0)()

    def lines(i, k, members=range(GROUP)):
        return [functools.partial(expert_in[i].line_step, k, j) for j in members]

    def second_half():
        expert_in[1].start_line()
        for j in range(1, GROUP):
            expert_in[1].plane_step(j)

    todo += lines(0, 1)
    todo.append(second_half)
    todo.append(functools.partial(shared_in.pass_on, planes - 1))
    for k in range(2, planes):
        todo += lines(0, k) + lines(1, k - 1)
    todo += lines(1, planes - 1)
    def masks():
        for start, stop in attention_blocks(length):
            row = lax.broadcasted_iota(jnp.int32, (stop - start, stop), 0) + start
            column = lax.broadcasted_iota(jnp.int32, (stop - start, stop), 1)
            allowed = (column <= row) & (seg_col[start:stop, :] == seg_row[:, :stop])
            bias[start:stop, :stop] = jnp.where(allowed, 0.0, -1e30)

    masks()

    def slot_of(expert_id, position):
        which = position // half
        apart = which + at.c - 2 * which * at.c
        bit0, bit1 = lax.rem(expert_id, 2), expert_id // 2
        p0, p1 = lax.rem(at.p, 2), at.p // 2
        distance = (bit0 + p0 - 2 * bit0 * p0) + 2 * (bit1 + p1 - 2 * bit1 * p1)
        slot = apart * count + distance * half + lax.rem(position, half)
        return jnp.where(position < capacity, slot, -1)

    slot_cols, slot_rows = [], []
    for r in range(top):
        ids_col, order_col = facts[:, r : r + 1], facts[:, top + r : top + r + 1]
        ids_row, order_row = facts_t[r : r + 1, :], facts_t[top + r : top + r + 1, :]
        count_col = jnp.zeros((length, 1), jnp.int32)
        count_row = jnp.zeros((1, length), jnp.int32)
        for other in range(top):
            first = (facts_t[other : other + 1, :] == ids_col) & (
                facts_t[top + other : top + other + 1, :] < order_col
            )
            count_col += jnp.sum(first.astype(jnp.int32), axis=1, keepdims=True)
            first = (facts[:, other : other + 1] == ids_row) & (
                facts[:, top + other : top + other + 1] < order_row
            )
            count_row += jnp.sum(first.astype(jnp.int32), axis=0, keepdims=True)
        slot_cols.append(slot_of(ids_col, count_col))
        slot_rows.append(slot_of(ids_row, count_row))

    attn_in.spread(1)
    attn_in.cross(0)
    for j in range(1, GROUP):
        expert_in[0].plane_step(j)
    for k in range(2, planes):
        attn_in.spread(k)
        attn_in.cross(k - 1)
        shared_in.pass_on(k - 1)
    attn_in.cross(planes - 1)
    expert_in[1].start_plane()
    shared_in.start_plane()
    shared_in.over_plane(1)
    attn_in.diagonal()

    small = blocks_of(aw, 4 * heads_width, 4 * heads_width + 128)
    small_rows = small.astype(f32).T
    g_one, g_two = small_rows[0:1, :], small_rows[1:2, :]
    for rows in chunks:
        x = x_ref[rows, :].astype(f32)
        rms = lax.rsqrt(jnp.mean(x * x, axis=-1, keepdims=True) + epsilon)
        xa_ref[rows, :] = (x * rms * g_one).astype(bf16)
    wave, other = waves[...], pltpu.roll(waves[...], 64, 1)
    cosine = jnp.where(lanes() < 64, wave, other)
    sine = jnp.where(lanes() < 64, other, wave)
    pairs = heads_width // 128
    for i, ref in enumerate((q_ref, k_ref)):
        part = dot_nn(xa_ref[...], blocks_of(aw, i * heads_width, (i + 1) * heads_width))
        for g in range(pairs):
            columns = slice(128 * g, 128 * (g + 1))
            ref[:, columns] = turn(part[:, columns], cosine, sine).astype(bf16)
    v_ref[...] = dot_nn(xa_ref[...], blocks_of(aw, 2 * heads_width, 3 * heads_width)).astype(bf16)

    scale = HD ** (-0.5)
    for start, stop in attention_blocks(length):
        logs = jnp.zeros((stop - start, 128), f32)
        for g in range(pairs):
            columns = slice(128 * g, 128 * (g + 1))
            queries = q_ref[start:stop, columns]
            keys, values = k_ref[:stop, columns], v_ref[:stop, columns]
            mixed = []
            for i in range(2):
                one = jnp.where(lanes() // HD == i, queries, jnp.zeros_like(queries))
                scores = dot_nt(one, keys) * scale + bias[start:stop, :stop]
                largest = jnp.max(scores, axis=-1, keepdims=True)
                expo = jnp.exp(scores - largest)
                total = jnp.sum(expo, axis=-1, keepdims=True)
                weights = (expo * (1.0 / total)).astype(bf16)
                mixed.append(dot_nn(weights, values))
                logs = jnp.where(lanes() == LOGS + 2 * g + i, largest + jnp.log(total), logs)
            o_ref[start:stop, columns] = jnp.where(lanes() < HD, mixed[0], mixed[1]).astype(bf16)
            tick(1)
        row_facts[start:stop, :] = logs

    for rows in chunks:
        dx_acc[rows, :] = dot_nt(
            o_ref[rows, :], blocks_of(aw, 3 * heads_width, 4 * heads_width)
        )
    swap = send(dx_acc, gx_ref, twin_sems.at[0, 0], twin_sems.at[1, 0], at.twin())
    swap.start()
    tick(4)
    swap.wait_recv()

    is_expert = (lanes() >= PROBS) & (lanes() < PROBS + experts)
    for rows in chunks:
        h = x_ref[rows, :].astype(f32) + (dx_acc[rows, :] + gx_ref[rows, :])
        gx_ref[rows, :] = h
        rms = lax.rsqrt(jnp.mean(h * h, axis=-1, keepdims=True) + epsilon)
        xf = (h * rms * g_two).astype(bf16)
        xf_ref[rows, :] = xf
        logits = jnp.where(is_expert, dot_nn(xf, small), -1e30)
        expo = jnp.exp(logits - jnp.max(logits, axis=-1, keepdims=True))
        probs = expo / jnp.sum(expo, axis=-1, keepdims=True)
        packed = jnp.where(is_expert, probs, row_facts[rows, :])
        for r in range(top):
            chosen = lanes() == facts[rows, r : r + 1] + PROBS
            gate = jnp.sum(jnp.where(chosen, probs, 0.0), axis=-1, keepdims=True)
            slot = slot_cols[r][rows, :]
            gate = jnp.where(slot >= 0, gate, 0.0)
            packed = jnp.where(lanes() == PAIRS + r, gate, packed)
            packed = jnp.where(lanes() == PAIRS + top + r, slot.astype(f32), packed)
        row_facts[rows, :] = packed
    gate_rows = row_facts[...].T[PAIRS : PAIRS + 8, :]

    def outgoing(j):
        return send(
            placed.at[j * half : (j + 1) * half, :],
            tok.at[0, j],
            token_sems.at[0, j],
            token_sems.at[1, j],
            at.near(j),
        )

    for j in range(experts):
        index = lax.broadcasted_iota(jnp.int32, (half, 1), 0) + j * half
        pick = [slot_rows[r] == index for r in range(top)]
        slot_gate = sum(
            jnp.sum(jnp.where(pick[r], gate_rows[r : r + 1, :], 0.0), axis=1, keepdims=True)
            for r in range(top)
        )
        pick = sum(p.astype(f32) for p in pick).astype(bf16)
        if j:
            target = placed.at[j * half : (j + 1) * half, :]
        else:
            target = tok.at[0, 0]
        target[:, :width] = dot_nn(pick, xf_ref[...]).astype(bf16)
        target[:, width:] = (dot_nn(pick, cot_ref[...]) * slot_gate).astype(bf16)
        if j:
            outgoing(j).start()

    tick(4)
    for j in range(1, experts):
        outgoing(j).wait_recv()
    for k in range(2, planes):
        shared_in.over_plane(k)
    across = send(tok.at[0], tok.at[1], twin_sems.at[0, 1], twin_sems.at[1, 1], at.twin())
    across.start()
    for j in range(1, experts):
        outgoing(j).wait_send()

    def shared_branch():
        shared_in.diagonal()
        shared_in.sent()
        for some in chunks:
            x_t[:, some] = xf_ref[some, :].T
            dy_t[:, some] = cot_ref[some, :].T
        y_acc[...] = jnp.zeros(y_acc.shape, f32)
        dx_acc[...] = jnp.zeros(dx_acc.shape, f32)
        for i in range(2):
            start = s_hidden * i
            branch(
                lambda some: xf_ref[some, :],
                lambda some: cot_ref[some, :],
                slice(0, length),
                sw,
                start,
                2 * s_hidden,
                s_hidden,
                act,
                y_acc,
                dx_acc,
            )

            def shared_grads(plane, carry):
                weight_grads(
                    plane, planes, length, x_t, dy_t, act, s_hidden, sw, start, 2 * s_hidden
                )
                return carry

            lax.fori_loop(0, planes, shared_grads, 0)
            tick(2)
        out_ref[...] = y_acc[...].astype(bf16)
        s_dx[...] = dx_acc[...].astype(bf16)
        swaps = [
            send(mine, theirs, twin_sems.at[0, 2 + i], twin_sems.at[1, 2 + i], at.twin())
            for i, (mine, theirs) in enumerate(((out_ref, ffn_theirs), (s_dx, dx_theirs)))
        ]
        for swap in swaps:
            swap.start()
        return swaps

    across.wait_recv()
    across.wait_send()
    swap.wait_send()

    def home_copy(j):
        return send(
            tok.at[0, j], home.at[0, j], home_sems.at[0, j], home_sems.at[1, j], at.near(j)
        )

    def share(j):
        return send(
            tok.at[1, j],
            ret.at[j * half : (j + 1) * half],
            share_sems.at[0, j],
            share_sems.at[1, j],
            at.twin(),
        )

    for i in range(2):
        expert_in[i].ready()
        expert_in[i].own_sent()

    def expert_half(i):
        for t in (1, 0):
            rows = slice(t * count, (t + 1) * count)

            def x_of(some):
                some = slice(some.start // half, some.stop // half)
                return tok[t, some, :, :width].reshape(-1, width)

            def dy_of(some):
                some = slice(some.start // half, some.stop // half)
                return tok[t, some, :, width:].reshape(-1, width)

            for some in chunks:
                x_t[:, rows.start + some.start : rows.start + some.stop] = x_of(some).T
                dy_t[:, rows.start + some.start : rows.start + some.stop] = dy_of(some).T
            if i == 0:
                y_acc[...] = jnp.zeros(y_acc.shape, f32)
                dx_acc[...] = jnp.zeros(dx_acc.shape, f32)
            else:
                for j in range(experts):
                    some = slice(j * half, (j + 1) * half)
                    y_acc[some, :] = part_one[t, j, :, :width].astype(f32)
                    dx_acc[some, :] = part_one[t, j, :, width:].astype(f32)
            branch(x_of, dy_of, rows, ew.at[i], 0, hidden, hidden, act, y_acc, dx_acc)
            target = tok if i else part_one
            if i and t == 0:
                for j in range(experts):
                    share(j).wait_recv()
            for j in range(experts):
                some = slice(j * half, (j + 1) * half)
                y, dx = y_acc[some, :], dx_acc[some, :]
                if i and t == 0:
                    y += ret[some, :width].astype(f32)
                    dx += ret[some, width:].astype(f32)
                target[t, j, :, :width] = y.astype(bf16)
                target[t, j, :, width:] = dx.astype(bf16)
                if i and t == 0 and j:
                    home_copy(j).start()
            if i and t:
                for j in range(experts):
                    share(j).start()
            tick(2 if i else 2)
        if i:
            home[0, 0] = tok[0, 0]
        expert_in[i].rest_sent()

        def grads_of(n, carry):
            plane = jnp.where(at.z * 2 < planes, planes - 1 - n, n)
            weight_grads(plane, planes, 2 * count, x_t, dy_t, act, hidden, ew.at[i], 0, hidden)
            expert_out[i].start_plane(plane)
            return carry

        lax.fori_loop(0, planes, grads_of, 0)

    while any(getattr(f, "func", None) == expert_in[0].line_step for f in todo):
        tick()
    expert_half(0)
    for k in range(planes):
        shared_in.cross(k)
    swaps = shared_branch()
    tick(len(todo))
    shared_out.start(planes - 1)
    shared_out.start(planes - 2)
    for k in range(planes - 2, 0, -1):
        for j in range(GROUP):
            todo.append(functools.partial(expert_out[0].step, k, j))
        todo.append(functools.partial(shared_out.middle, k + 1))
    expert_half(1)

    for k in range(planes - 3, -1, -1):
        todo.append(functools.partial(shared_out.start, k))
    for k in range(planes - 2, 0, -1):
        for j in range(GROUP):
            todo.append(functools.partial(expert_out[1].step, k, j))
            if k == planes - 2:
                todo.append(functools.partial(expert_out[0].total, j))
    for k in range(planes - 3, -1, -1):
        todo.append(functools.partial(shared_out.middle, k))
    for k in range(planes - 1, 0, -1):
        todo.append(functools.partial(shared_out.step, k))
    for j in range(GROUP):
        todo.append(functools.partial(expert_out[1].total, j))
    for j in range(1, experts):
        home_copy(j).wait_recv()
    swap = send(home.at[0], home.at[1], twin_sems.at[0, 5], twin_sems.at[1, 5], at.twin())
    swap.start()
    tick(2)
    for other in swaps:
        other.wait_recv()
        other.wait_send()
    swap.wait_recv()
    for rows in chunks:
        y = out_ref[rows, :].astype(f32) + ffn_theirs[rows, :].astype(f32)
        dx = s_dx[rows, :].astype(f32) + dx_theirs[rows, :].astype(f32)
        gate = jnp.zeros((step, 128), f32)
        dy = cot_ref[rows, :].astype(f32)
        for core in range(2):
            t = core + at.c - 2 * core * at.c
            index = lax.broadcasted_iota(jnp.int32, (1, count), 1) + t * count
            slots = [row_facts[rows, PAIRS + top + r : PAIRS + top + r + 1] for r in range(top)]
            slots = [(slot.astype(jnp.int32) == index).astype(f32) for slot in slots]
            for r in range(top):
                part = dot_nn(slots[r].astype(bf16), home[t, :, :, :width].reshape(count, width))
                y += row_facts[rows, PAIRS + r : PAIRS + r + 1] * part
                grad = jnp.sum(dy * part, axis=-1, keepdims=True)
                gate += jnp.where(lanes() == facts[rows, r : r + 1] + PROBS, grad, 0.0)
            dx += dot_nn(sum(slots).astype(bf16), home[t, :, :, width:].reshape(count, width))
        out_ref[rows, :] = (gx_ref[rows, :] + y).astype(bf16)
        dx_acc[rows, :] = dx
        y_acc[rows, :128] = gate
    attn_in.sent()

    grad_g_two = jnp.zeros((1, width), f32)
    grad_small = jnp.zeros((width, 128), f32)
    for rows in chunks:
        probs = jnp.where(is_expert, row_facts[rows, :], 0.0)
        grad_probs = y_acc[rows, :128]
        grad_logits = (
            probs * (grad_probs - jnp.sum(probs * grad_probs, axis=-1, keepdims=True))
        ).astype(bf16)
        grad_small += dot_tn(xf_ref[rows, :], grad_logits)
        grad_xf = dx_acc[rows, :] + dot_nt(grad_logits, small)
        h = gx_ref[rows, :]
        grad_h, grad_gain = norm_back_rows(grad_xf, h, g_two)
        grad_g_two += grad_gain
        grad_h = cot_ref[rows, :].astype(f32) + grad_h
        gx_ref[rows, :] = grad_h
        dy_t[:, rows] = grad_h.astype(bf16).T
        grad_o[rows, :] = dot_nn(
            grad_h.astype(bf16), blocks_of(aw, 3 * heads_width, 4 * heads_width)
        ).astype(bf16)
    for rows in chunks:
        x = x_ref[rows, :].astype(f32)
        rms = lax.rsqrt(jnp.mean(x * x, axis=-1, keepdims=True) + epsilon)
        x_t[:, rows] = (x * rms * g_one).astype(bf16).T
    masks()
    tick(2)

    def to_grads(start, columns, left, right):
        blocks = aw.shape[0]
        for i in range(0, blocks, blocks // 4):
            some = slice(i, i + blocks // 4)
            features = slice(i * aw.shape[1], (i + blocks // 4) * aw.shape[1])
            block = dot_nn(left[features, :length], right())
            aw[some, :, start : start + columns] = block.astype(bf16).reshape(
                blocks // 4, aw.shape[1], columns
            )

    to_grads(3 * heads_width, heads_width, dy_t, lambda: o_ref[...])
    for g in range(pairs):
        columns = slice(128 * g, 128 * (g + 1))
        for start, stop in attention_blocks(length)[::-1]:
            queries = q_ref[start:stop, columns]
            grads = grad_o[start:stop, columns]
            keys, values = k_ref[:stop, columns], v_ref[:stop, columns]
            grad_q = jnp.zeros((stop - start, 128), f32)
            grad_k = jnp.zeros((stop, 128), f32)
            grad_v = jnp.zeros((stop, 128), f32)
            for i in range(2):
                mask = lanes() // HD == i
                one_q = jnp.where(mask, queries, jnp.zeros_like(queries))
                one_do = jnp.where(mask, grads, jnp.zeros_like(grads))
                one_k = jnp.where(mask, keys, jnp.zeros_like(keys))
                scores = dot_nt(one_q, keys) * scale + bias[start:stop, :stop]
                log = LOGS + 2 * g + i
                weights = jnp.exp(scores - row_facts[start:stop, log : log + 1])
                grad_w = dot_nt(one_do, values)
                inner = jnp.sum(weights * grad_w, axis=-1, keepdims=True)
                grad_s = (weights * (grad_w - inner)).astype(bf16)
                grad_q += dot_nn(grad_s, one_k)
                grad_k += dot_tn(grad_s, one_q)
                grad_v += dot_tn(weights.astype(bf16), one_do)
            dproj[start:stop, columns] = turn(
                grad_q * scale, cosine[start:stop, :], -sine[start:stop, :]
            ).astype(bf16)
            if stop == length:
                dk_acc[...] = grad_k * scale
                dv_acc[...] = grad_v
            else:
                dk_acc[:stop, :] += grad_k * scale
                dv_acc[:stop, :] += grad_v
            tick(2)
        dproj[:, heads_width + 128 * g : heads_width + 128 * (g + 1)] = turn(
            dk_acc[...], cosine, -sine
        ).astype(bf16)
        dproj[:, 2 * heads_width + 128 * g : 2 * heads_width + 128 * (g + 1)] = dv_acc[
            ...
        ].astype(bf16)
    for rows in chunks:
        part = dot_nt(dproj[rows, :], blocks_of(aw, 0, 3 * heads_width))
        part_mine[rows, :] = part.astype(bf16)
    last_swap = send(part_mine, part_theirs, twin_sems.at[0, 6], twin_sems.at[1, 6], at.twin())
    last_swap.start()
    for i in range(3):
        columns = slice(i * heads_width, (i + 1) * heads_width)
        to_grads(i * heads_width, heads_width, x_t, lambda: dproj[:, columns])
    last_swap.wait_recv()
    grad_g_one = jnp.zeros((1, width), f32)
    for rows in chunks:
        grad_xa = part_mine[rows, :].astype(f32) + part_theirs[rows, :].astype(f32)
        grad_x, grad_gain = norm_back_rows(grad_xa, x_ref[rows, :].astype(f32), g_one)
        gx_ref[rows, :] += grad_x
        grad_g_one += grad_gain
    index = lax.broadcasted_iota(jnp.int32, (128, 1), 0)
    gains = jnp.where(index == 0, grad_g_one, 0.0) + jnp.where(index == 1, grad_g_two, 0.0)
    small_grads = (gains.T + grad_small).astype(bf16)
    aw[:, :, 4 * heads_width :] = small_grads.reshape(aw.shape[0], aw.shape[1], 128)
    for k in range(planes - 1, -1, -1):
        attn_out.start(k)
    tick(3)
    for k in range(planes - 1, -1, -1):
        attn_out.middle(k)
        tick()
    for k in range(planes - 1, 0, -1):
        attn_out.step(k)
        tick()
    tick(len(todo))
    shared_out.total(s_out)
    attn_out.total(a_out)
    for i in range(2):
        for j in range(1, GROUP):
            expert_out[i].arrive(j)

    swap.wait_send()
    last_swap.wait_send()
    for j in range(experts):
        share(j).wait_send()
    for j in range(1, experts):
        home_copy(j).wait_send()
    for i in range(2):
        expert_out[i].sent()
    shared_out.sent()
    attn_out.sent()


def layer(planes, experts, top, heads_width, inputs, own):
    bf16, f32, dma = jnp.bfloat16, jnp.float32, pltpu.SemaphoreType.DMA
    n = planes * GROUP
    length, width = inputs[0].shape
    rows, a_width = own[0].shape
    s_width, e_width = own[1].shape[1], own[2].shape[2] // 2
    half = length * top // experts // 2
    slots = 2 * experts * half
    vmem, anywhere = pl.BlockSpec(memory_space=pltpu.VMEM), pl.BlockSpec(memory_space=pl.ANY)
    shape = jax.ShapeDtypeStruct
    tokens = pltpu.VMEM((2, experts, half, 2 * width), bf16)
    features = pltpu.VMEM((width, slots), bf16)
    wide = pltpu.VMEM((length, width), f32)
    narrow = pltpu.VMEM((length, width), bf16)
    heads = pltpu.VMEM((length, heads_width), bf16)
    facts = pltpu.VMEM((length, 128), f32)

    def plane_buffers(columns):
        return [
            pltpu.VMEM((planes, 2, rows, columns), bf16),
            pltpu.VMEM((planes, rows, columns), bf16),
            pltpu.VMEM((planes + 1, rows, columns), bf16),
        ]

    plane_sems = [dma((2, planes, 2)), dma((2, planes)), dma((2, 2, planes))]
    return pl.pallas_call(
        functools.partial(layer_kernel, planes, experts, top, heads_width),
        out_shape=(
            shape((length, width), bf16),
            shape((length, width), f32),
            shape((rows, a_width), f32),
            shape((rows, s_width), bf16),
            shape((GROUP, rows, 2 * e_width), bf16),
        ),
        in_specs=[vmem] * len(inputs) + [anywhere] * 3,
        out_specs=(vmem,) * 5,
        scratch_shapes=[
            pltpu.VMEM((n, rows, a_width), bf16),
            pltpu.VMEM((n, rows, s_width), bf16),
            pltpu.VMEM((2, n, rows, e_width), bf16),
            tokens,
            tokens,
            tokens,
            pltpu.VMEM((slots, e_width), bf16),
            features,
            features,
            wide,
            wide,
            narrow,
            heads,
            heads,
            heads,
            heads,
            narrow,
            facts,
            narrow,
            narrow,
            pltpu.VMEM((experts * half, 2 * width), bf16),
            *plane_buffers(a_width),
            *plane_buffers(s_width),
            pltpu.VMEM((2, (planes + 1) * GROUP, rows, e_width), bf16),
            dma((10,)),
            dma((n,)),
            dma((4, n)),
            dma((n,)),
            dma((4, n)),
            dma((2, n)),
            dma((2, 2, n)),
            dma((2, GROUP)),
            *plane_sems,
            *plane_sems,
            dma((2, 2, 2, n)),
            dma((2, 2, GROUP, 3)),
            dma((2, GROUP)),
            dma((2, GROUP)),
            dma((2, GROUP)),
            dma((2, 7)),
        ],
        compiler_params=pltpu.CompilerParams(
            collective_id=0, has_side_effects=True, vmem_limit_bytes=63 << 20
        ),
    )(*inputs, *own)


def local_grouped(
    planes,
    tokens,
    segment_ids,
    expert_ids,
    slot_order,
    gain_attn,
    qkv_weight,
    out_weight,
    gain_ffn,
    router_weight,
    gate_up,
    down_weight,
    shared_gate_up,
    shared_down,
    cotangent,
):
    bf16, f32 = jnp.bfloat16, jnp.float32
    rows, heads_width = qkv_weight.shape[0], qkv_weight.shape[2]
    experts, hidden = down_weight.shape[0], down_weight.shape[1]
    s_hidden = shared_down.shape[0]
    length = tokens.shape[0]
    top = expert_ids.shape[1]
    cuts = [3 * heads_width, heads_width, 128]
    edges = [sum(cuts[:i]) for i in range(len(cuts) + 1)]

    def part(array, i):
        return array[..., edges[i] : edges[i + 1]]

    expert_packed = jnp.concatenate(
        [gate_up.reshape(experts, rows, 2 * hidden), down_weight.transpose(0, 2, 1)], axis=2
    )
    shared_packed = jnp.concatenate(
        [shared_gate_up.reshape(rows, 2 * s_hidden), shared_down.T], axis=1
    )
    small = jnp.concatenate([gain_attn[:, None], gain_ffn[:, None], router_weight], axis=1)
    small = jnp.pad(small, ((0, 0), (0, 128 - small.shape[1])))
    attn_packed = jnp.concatenate(
        [qkv_weight.reshape(rows, 3 * heads_width), out_weight.T, small], axis=1
    )
    cosine, sine = rotary(length, HD)
    waves = jnp.concatenate([cosine[:, 0]] * 2 + [sine[:, 0]] * 2, axis=1)
    facts = jnp.concatenate(
        [expert_ids, slot_order.reshape(length, top), segment_ids.reshape(length, 1)], axis=1
    )
    facts = jnp.pad(facts, ((0, 0), (0, 8 - facts.shape[1])))
    output, grad_tokens, mine, mine_shared, mine_expert = layer(
        planes,
        experts,
        top,
        heads_width,
        (tokens, cotangent, facts, facts.T, waves),
        (attn_packed, shared_packed, expert_packed),
    )
    small_mine = part(mine, 2)
    mine_shared, mine_expert = mine_shared.astype(f32), mine_expert.astype(f32)
    return (
        output,
        grad_tokens,
        small_mine[:, 0],
        part(mine, 0).reshape(rows, 3, heads_width),
        part(mine, 1).T,
        small_mine[:, 1],
        small_mine[:, 2 : 2 + experts],
        mine_expert[:, :, : 2 * hidden].reshape(experts, rows, 2, hidden),
        mine_expert[:, :, 2 * hidden :].transpose(0, 2, 1),
        mine_shared[:, : 2 * s_hidden].reshape(rows, 2, s_hidden),
        mine_shared[:, 2 * s_hidden :].T,
    )


def solution(mesh):
    def pick(*args):
        experts, rows = args[9].shape[0], args[5].shape[0]
        if experts == GROUP and mesh.shape["dp"] % GROUP == 0 and rows % 16 == 0:
            return local_grouped(mesh.shape["dp"] // GROUP, *args)
        return local_plain(*args)

    return jax.shard_map(
        pick,
        mesh=mesh,
        in_specs=(
            P("dp", None),
            P("dp", None),
            P("dp", None),
            P("dp", None),
            P("dp"),
            P("dp", None, "tensor"),
            P("tensor", "dp"),
            P("dp"),
            P("dp", None),
            P(None, "dp", None, "tensor"),
            P(None, "tensor", "dp"),
            P("dp", None, "tensor"),
            P("tensor", "dp"),
            P("dp", None),
        ),
        out_specs=(
            P("dp", None),
            P("dp", None),
            P("dp"),
            P("dp", None, "tensor"),
            P("tensor", "dp"),
            P("dp"),
            P("dp", None),
            P(None, "dp", None, "tensor"),
            P(None, "tensor", "dp"),
            P("dp", None, "tensor"),
            P("tensor", "dp"),
        ),
        check_vma=False,
    )
```

```python
import functools
import math

import jax
import jax.numpy as jnp
from jax import lax
from jax.experimental import pallas as pl
from jax.experimental.pallas import tpu as pltpu
from jax.sharding import PartitionSpec as P

HD = 64
GROUP = 4
MESH = pl.DeviceIdType.MESH


epsilon = 1e-06


def rms_scale(values):
    return lax.rsqrt(jnp.mean(values * values, axis=-1, keepdims=True) + epsilon)


def rotary(length, head_dim):
    half_dim = head_dim // 2
    position = jnp.arange(length).astype(jnp.float32)[:, None]
    inverse = jnp.exp(
        jnp.arange(half_dim).astype(jnp.float32) * (-2.0 * math.log(10000.0) / head_dim)
    )
    angles = position * inverse[None, :]
    return (jnp.cos(angles)[:, None, :], jnp.sin(angles)[:, None, :])


def rotate(values, cosine, sine):
    half_dim = values.shape[-1] // 2
    first_half = values[..., :half_dim]
    second_half = values[..., half_dim:]
    return jnp.concatenate(
        [first_half * cosine - second_half * sine, second_half * cosine + first_half * sine],
        axis=-1,
    )


def route_slots(pair_ids, rank_order, capacity, experts):
    length = pair_ids.shape[0]
    top_count = pair_ids.shape[1]
    pair_expert = pair_ids.reshape(-1)
    pair_count = pair_expert.shape[0]
    ordered = jnp.zeros((pair_count,), jnp.int32).at[rank_order].set(pair_expert)
    onehot = (ordered[:, None] == jnp.arange(experts, dtype=jnp.int32)[None, :]).astype(jnp.int32)
    running = jnp.cumsum(onehot, axis=0)
    ranked_slot = jnp.sum(running * onehot, axis=1) - 1
    position = ranked_slot[rank_order]
    kept_pair = position < capacity
    slot_index = jnp.where(kept_pair, pair_expert * capacity + position, experts * capacity)
    token_of_pair = jnp.arange(pair_count, dtype=jnp.int32) // top_count
    slot_token = (
        jnp.full((experts * capacity,), length, jnp.int32)
        .at[slot_index]
        .set(token_of_pair, mode="drop")
    )
    return (slot_token, slot_index.reshape(length, top_count), kept_pair.reshape(length, top_count))


def silu_back(both_parts, grad_hidden):
    gate_part = both_parts[..., 0, :]
    up_part = both_parts[..., 1, :]
    sigma = jax.nn.sigmoid(gate_part)
    slope = sigma * (1.0 + gate_part * (1.0 - sigma))
    return jnp.stack(
        [grad_hidden * up_part * slope, grad_hidden * gate_part * sigma], axis=-2
    ).astype(jnp.bfloat16)


def silu_forward(both_parts):
    return (jax.nn.silu(both_parts[..., 0, :]) * both_parts[..., 1, :]).astype(jnp.bfloat16)


def norm_back(grad_norm, values, scale_rows, gain):
    grad_gain = jnp.sum(grad_norm * values * scale_rows, axis=0)
    inner = grad_norm * gain
    grad_values = scale_rows * inner - values * scale_rows**3 * jnp.mean(
        inner * values, axis=-1, keepdims=True
    )
    return (grad_values, grad_gain)


def split_blocks(length):
    block = min(512, length)
    return (block, length // block)


def masked_scores(query_block, keys_all, query_pos, query_seg, segment, scale):
    positions = jnp.arange(keys_all.shape[0])
    scores = (
        jnp.einsum("qhd,khd->hqk", query_block, keys_all, preferred_element_type=jnp.float32)
        * scale
    )
    allowed = (positions[None, :] <= query_pos[:, None]) & (segment[None, :] == query_seg[:, None])
    return jnp.where(allowed[None], scores, -1e30)


def attend_forward(queries, keys_all, values_all, segment, scale):
    length, head_count, head_dim = queries.shape
    block, count_blocks = split_blocks(length)
    positions = jnp.arange(length)

    def one_block(inputs):
        query_block, query_pos, query_seg = inputs
        scores = masked_scores(query_block, keys_all, query_pos, query_seg, segment, scale)
        largest = jnp.max(scores, axis=-1, keepdims=True)
        expo = jnp.exp(scores - largest)
        total = jnp.sum(expo, axis=-1, keepdims=True)
        probs = (expo / total).astype(jnp.bfloat16)
        mixed = jnp.einsum("hqk,khd->qhd", probs, values_all, preferred_element_type=jnp.float32)
        return (mixed.astype(jnp.bfloat16), (largest + jnp.log(total))[..., 0])

    blocks = (
        queries.reshape(count_blocks, block, head_count, head_dim),
        positions.reshape(count_blocks, block),
        segment.reshape(count_blocks, block),
    )
    mixed_all, log_totals = lax.map(one_block, blocks)
    return (mixed_all.reshape(length, head_count * head_dim), log_totals)


def attend_backward(queries, keys_all, values_all, segment, scale, grad_mixed, log_totals):
    length, head_count, head_dim = queries.shape
    block, count_blocks = split_blocks(length)
    positions = jnp.arange(length)

    def one_block(carry, inputs):
        grad_keys, grad_values = carry
        query_block, query_pos, query_seg, grad_block, log_block = inputs
        scores = masked_scores(query_block, keys_all, query_pos, query_seg, segment, scale)
        probs = jnp.exp(scores - log_block[:, :, None])
        grad_probs = jnp.einsum(
            "qhd,khd->hqk", grad_block, values_all, preferred_element_type=jnp.float32
        )
        inner = jnp.sum(probs * grad_probs, axis=-1, keepdims=True)
        grad_scores = (probs * (grad_probs - inner)).astype(jnp.bfloat16)
        grad_query = (
            jnp.einsum("hqk,khd->qhd", grad_scores, keys_all, preferred_element_type=jnp.float32)
            * scale
        )
        grad_keys = (
            grad_keys
            + jnp.einsum(
                "hqk,qhd->khd", grad_scores, query_block, preferred_element_type=jnp.float32
            )
            * scale
        )
        grad_values = grad_values + jnp.einsum(
            "hqk,qhd->khd",
            probs.astype(jnp.bfloat16),
            grad_block,
            preferred_element_type=jnp.float32,
        )
        return ((grad_keys, grad_values), grad_query)

    zeros_kv = jnp.zeros((length, head_count, head_dim), jnp.float32)
    blocks = (
        queries.reshape(count_blocks, block, head_count, head_dim),
        positions.reshape(count_blocks, block),
        segment.reshape(count_blocks, block),
        grad_mixed.reshape(count_blocks, block, head_count, head_dim),
        log_totals,
    )
    (grad_keys, grad_values), grad_queries = lax.scan(one_block, (zeros_kv, zeros_kv), blocks)
    return (grad_queries.reshape(length, head_count, head_dim), grad_keys, grad_values)


def sum_rows(grad, axis, scatter_dimension, tiled):
    part = lax.psum_scatter(
        grad.astype(jnp.bfloat16), axis, scatter_dimension=scatter_dimension, tiled=tiled
    )
    return part.astype(jnp.float32)


def local_plain(
    tokens,
    segment_ids,
    expert_ids,
    slot_order,
    gain_attn,
    qkv_weight,
    out_weight,
    gain_ffn,
    router_weight,
    gate_up,
    down_weight,
    shared_gate_up,
    shared_down,
    cotangent,
):
    g_one, w_qkv, w_out, g_two, w_router, w_gate_up, w_down, s_gate_up, s_down = (
        lax.all_gather(gain_attn, "dp", axis=0, tiled=True),
        lax.all_gather(qkv_weight, "dp", axis=0, tiled=True),
        lax.all_gather(out_weight, "dp", axis=1, tiled=True),
        lax.all_gather(gain_ffn, "dp", axis=0, tiled=True),
        lax.all_gather(router_weight, "dp", axis=0, tiled=True),
        lax.all_gather(gate_up, "dp", axis=1, tiled=True),
        lax.all_gather(down_weight, "dp", axis=2, tiled=True),
        lax.all_gather(shared_gate_up, "dp", axis=0, tiled=True),
        lax.all_gather(shared_down, "dp", axis=1, tiled=True),
    )
    length = tokens.shape[0]
    width = tokens.shape[1]
    experts_count = w_router.shape[1]
    top_count = expert_ids.shape[1]
    capacity = length * top_count // experts_count
    head_dim = HD
    local_heads = w_qkv.shape[2] // head_dim
    scale = head_dim ** (-0.5)
    segment = segment_ids[0]
    slot_token, slot_index, kept_pair = route_slots(
        expert_ids, slot_order[0], capacity, experts_count
    )
    kept_float = kept_pair.astype(jnp.float32)
    slot_valid = slot_token < length
    slot_rows = jnp.minimum(slot_token, length - 1)
    pair_slots = jnp.minimum(slot_index, experts_count * capacity - 1)
    xfull = tokens.astype(jnp.float32)
    rms_one = rms_scale(xfull)
    xn_one = (xfull * rms_one * g_one.astype(jnp.float32)).astype(jnp.bfloat16)
    projected = jnp.einsum("td,dch->tch", xn_one, w_qkv, preferred_element_type=jnp.float32)
    cosine, sine = rotary(length, head_dim)
    queries = rotate(projected[:, 0].reshape(length, local_heads, head_dim), cosine, sine).astype(
        jnp.bfloat16
    )
    keys_all = rotate(projected[:, 1].reshape(length, local_heads, head_dim), cosine, sine).astype(
        jnp.bfloat16
    )
    values_all = projected[:, 2].reshape(length, local_heads, head_dim).astype(jnp.bfloat16)
    mixed, log_totals = attend_forward(queries, keys_all, values_all, segment, scale)
    attn_share = lax.psum_scatter(
        jnp.dot(mixed, w_out, preferred_element_type=jnp.float32),
        "tensor",
        scatter_dimension=1,
        tiled=True,
    )
    attn = lax.all_gather(attn_share, "tensor", axis=1, tiled=True)
    hidden_state = xfull + attn
    rms_two = rms_scale(hidden_state)
    xn_two = (hidden_state * rms_two * g_two.astype(jnp.float32)).astype(jnp.bfloat16)
    logits = jnp.dot(xn_two, w_router, preferred_element_type=jnp.float32)
    probs = jax.nn.softmax(logits, axis=-1)
    gates = jnp.take_along_axis(probs, expert_ids, axis=1) * kept_float
    dispatched = (xn_two[slot_rows] * slot_valid[:, None].astype(jnp.bfloat16)).reshape(
        experts_count, capacity, width
    )
    both_parts = jnp.einsum(
        "ecd,edjf->ecjf", dispatched, w_gate_up, preferred_element_type=jnp.float32
    )
    expert_hidden = silu_forward(both_parts)
    expert_out = jnp.einsum(
        "ecf,efd->ecd", expert_hidden, w_down, preferred_element_type=jnp.float32
    ).reshape(experts_count * capacity, width)
    picked = expert_out[pair_slots]
    moe = jnp.sum(gates[:, :, None] * picked, axis=1)
    shared_both = jnp.einsum("td,djf->tjf", xn_two, s_gate_up, preferred_element_type=jnp.float32)
    shared_hidden = silu_forward(shared_both)
    shared_out = jnp.dot(shared_hidden, s_down, preferred_element_type=jnp.float32)
    ffn_share = lax.psum_scatter(
        (moe + shared_out).astype(jnp.bfloat16), "tensor", scatter_dimension=1, tiled=True
    ).astype(jnp.float32)
    ffn = lax.all_gather(ffn_share.astype(jnp.bfloat16), "tensor", axis=1, tiled=True).astype(
        ffn_share.dtype
    )
    output = (hidden_state + ffn).astype(jnp.bfloat16)
    grad_y = cotangent.astype(jnp.float32)
    grad_shared_hidden = jnp.einsum(
        "td,fd->tf", cotangent, s_down, preferred_element_type=jnp.float32
    )
    grad_s_down = jnp.einsum(
        "tf,td->fd", shared_hidden, cotangent, preferred_element_type=jnp.float32
    )
    grad_shared_both = silu_back(shared_both, grad_shared_hidden)
    grad_s_gate_up = jnp.einsum(
        "td,tjf->djf", xn_two, grad_shared_both, preferred_element_type=jnp.float32
    )
    grad_xn_shared = jnp.einsum(
        "tjf,djf->td", grad_shared_both, s_gate_up, preferred_element_type=jnp.float32
    )
    slot_gate = (
        jnp.zeros((experts_count * capacity,), jnp.float32)
        .at[slot_index.reshape(-1)]
        .set(gates.reshape(-1), mode="drop")
    )
    grad_expert_out = (
        (slot_gate[:, None] * grad_y[slot_rows])
        .astype(jnp.bfloat16)
        .reshape(experts_count, capacity, width)
    )
    grad_gates_part = kept_float * jnp.sum(grad_y[:, None, :] * picked, axis=-1)
    grad_expert_hidden = jnp.einsum(
        "ecd,efd->ecf", grad_expert_out, w_down, preferred_element_type=jnp.float32
    )
    grad_w_down = jnp.einsum(
        "ecf,ecd->efd", expert_hidden, grad_expert_out, preferred_element_type=jnp.float32
    )
    grad_both = silu_back(both_parts, grad_expert_hidden)
    grad_w_gate_up = jnp.einsum(
        "ecd,ecjf->edjf", dispatched, grad_both, preferred_element_type=jnp.float32
    )
    grad_dispatched = jnp.einsum(
        "ecjf,edjf->ecd", grad_both, w_gate_up, preferred_element_type=jnp.float32
    ).reshape(experts_count * capacity, width)
    grad_xn_moe = jnp.sum(kept_float[:, :, None] * grad_dispatched[pair_slots], axis=1)
    grad_xn_part, grad_gates_share = (
        lax.psum_scatter(grad_xn_shared + grad_xn_moe, "tensor", scatter_dimension=1, tiled=True),
        lax.psum_scatter(grad_gates_part, "tensor", scatter_dimension=1, tiled=True),
    )
    grad_xn_sum, grad_gates = (
        lax.all_gather(grad_xn_part, "tensor", axis=1, tiled=True),
        lax.all_gather(grad_gates_share, "tensor", axis=1, tiled=True),
    )
    expert_match = (
        expert_ids[:, :, None] == jnp.arange(experts_count, dtype=jnp.int32)[None, None, :]
    ).astype(jnp.float32)
    grad_probs = jnp.sum(expert_match * grad_gates[:, :, None], axis=1)
    grad_logits = (
        probs * (grad_probs - jnp.sum(probs * grad_probs, axis=-1, keepdims=True))
    ).astype(jnp.bfloat16)
    grad_w_router = jnp.einsum("td,te->de", xn_two, grad_logits, preferred_element_type=jnp.float32)
    grad_xn_two = grad_xn_sum + jnp.einsum(
        "te,de->td", grad_logits, w_router, preferred_element_type=jnp.float32
    )
    grad_norm_two, grad_g_two = norm_back(
        grad_xn_two, hidden_state, rms_two, g_two.astype(jnp.float32)
    )
    grad_hidden = grad_y + grad_norm_two
    grad_attn = grad_hidden.astype(jnp.bfloat16)
    grad_w_out = jnp.einsum("th,td->hd", mixed, grad_attn, preferred_element_type=jnp.float32)
    grad_mixed = jnp.einsum(
        "td,hd->th", grad_attn, w_out, preferred_element_type=jnp.float32
    ).astype(jnp.bfloat16)
    grad_queries, grad_keys, grad_values = attend_backward(
        queries, keys_all, values_all, segment, scale, grad_mixed, log_totals
    )
    grad_projected = (
        jnp.stack(
            [rotate(grad_queries, cosine, -sine), rotate(grad_keys, cosine, -sine), grad_values],
            axis=1,
        )
        .astype(jnp.bfloat16)
        .reshape(length, 3, local_heads * head_dim)
    )
    grad_w_qkv = jnp.einsum(
        "td,tch->dch", xn_one, grad_projected, preferred_element_type=jnp.float32
    )
    grad_xn_share = lax.psum_scatter(
        jnp.einsum("tch,dch->td", grad_projected, w_qkv, preferred_element_type=jnp.float32).astype(
            jnp.bfloat16
        ),
        "tensor",
        scatter_dimension=1,
        tiled=True,
    ).astype(jnp.float32)
    grad_xn_one = lax.all_gather(
        grad_xn_share.astype(jnp.bfloat16), "tensor", axis=1, tiled=True
    ).astype(grad_xn_share.dtype)
    grad_norm_one, grad_g_one = norm_back(grad_xn_one, xfull, rms_one, g_one.astype(jnp.float32))
    grad_tokens = grad_hidden + grad_norm_one
    (
        grad_g_one,
        grad_w_qkv,
        grad_w_out,
        grad_g_two,
        grad_w_router,
        grad_w_gate_up,
        grad_w_down,
        grad_s_gate_up,
        grad_s_down,
    ) = (
        lax.psum_scatter(grad_g_one, "dp", scatter_dimension=0, tiled=True),
        sum_rows(grad_w_qkv, "dp", scatter_dimension=0, tiled=True),
        sum_rows(grad_w_out, "dp", scatter_dimension=1, tiled=True),
        lax.psum_scatter(grad_g_two, "dp", scatter_dimension=0, tiled=True),
        lax.psum_scatter(grad_w_router, "dp", scatter_dimension=0, tiled=True),
        sum_rows(grad_w_gate_up, "dp", scatter_dimension=1, tiled=True),
        sum_rows(grad_w_down, "dp", scatter_dimension=2, tiled=True),
        sum_rows(grad_s_gate_up, "dp", scatter_dimension=0, tiled=True),
        sum_rows(grad_s_down, "dp", scatter_dimension=1, tiled=True),
    )
    return (
        output,
        grad_tokens,
        grad_g_one,
        grad_w_qkv,
        grad_w_out,
        grad_g_two,
        grad_w_router,
        grad_w_gate_up,
        grad_w_down,
        grad_s_gate_up,
        grad_s_down,
    )


class Place:
    def __init__(self, planes):
        d = lax.axis_index("dp")
        self.planes = planes
        self.d, self.c = d, lax.axis_index("tensor")
        self.z, self.p = d // GROUP, lax.rem(d, GROUP)
        bit0, bit1 = lax.rem(self.p, 2), self.p // 2
        flip0, flip1 = 1 - bit0, 1 - bit1
        self.member = [
            self.p,
            flip0 + 2 * bit1,
            bit0 + 2 * flip1,
            flip0 + 2 * flip1,
        ]

    def near(self, j):
        return (self.z * GROUP + self.member[j], self.c)

    def up(self):
        return (self.d + GROUP, self.c)

    def down(self):
        return (self.d - GROUP, self.c)

    def twin(self):
        return (self.d, 1 - self.c)

    def when(self, condition, action):
        pl.when(condition)(action)

    def has_up(self, k=1):
        return self.z + k < self.planes

    def has_down(self, k=1):
        return self.z - k >= 0

    def greet(self):
        barrier = pltpu.get_barrier_semaphore()

        def hello(device):
            pl.semaphore_signal(barrier, inc=1, device_id=device, device_id_type=MESH)

        hello(self.twin())
        for j in range(1, GROUP):
            hello(self.near(j))
        self.when(self.has_up(), lambda: hello(self.up()))
        self.when(self.has_down(), lambda: hello(self.down()))
        line = self.has_up().astype(jnp.int32) + self.has_down().astype(jnp.int32)
        pl.semaphore_wait(barrier, GROUP + line)


def send(source, target, send_sem, recv_sem, device):
    return pltpu.make_async_remote_copy(
        src_ref=source,
        dst_ref=target,
        send_sem=send_sem,
        recv_sem=recv_sem,
        device_id=device,
        device_id_type=MESH,
    )


class Everywhere:
    def __init__(self, at, own, all_blocks, local_sem, recvs, sends):
        self.at, self.own, self.all = at, own, all_blocks
        self.local_sem, self.recvs, self.sends = local_sem, recvs, sends

    def copy(self, block, source, way, device):
        return send(source, self.all.at[block], self.sends.at[way, block], self.recvs.at[block], device)

    def keep(self):
        return pltpu.make_async_copy(self.own, self.all.at[self.at.d], self.local_sem)

    def landed(self, block):
        self.copy(block, self.own, 0, self.at.near(1)).wait_recv()

    def start_line(self):
        at = self.at
        at.when(at.has_up(), lambda: self.copy(at.d, self.own, 0, at.up()).start())
        at.when(at.has_down(), lambda: self.copy(at.d, self.own, 1, at.down()).start())

    def start_plane(self):
        at = self.at
        self.copy(at.d, self.own, 2, at.near(1)).start()
        self.copy(at.d, self.own, 3, at.near(2)).start()
        self.keep().start()

    def pass_on(self, k):
        at = self.at

        def go(plane, more, way, device_of):
            block = plane * GROUP + at.p
            self.landed(block)
            at.when(more, lambda: self.copy(block, self.all.at[block], way, device_of()).start())

        at.when(at.has_down(k), lambda: go(at.z - k, at.has_up(), 0, at.up))
        at.when(at.has_up(k), lambda: go(at.z + k, at.has_down(), 1, at.down))

    def over_plane(self, k):
        at = self.at

        def go(plane):
            block = plane * GROUP + at.p
            self.copy(block, self.all.at[block], 2, at.near(1)).start()
            self.copy(block, self.all.at[block], 3, at.near(2)).start()

        at.when(at.has_down(k), lambda: go(at.z - k))
        at.when(at.has_up(k), lambda: go(at.z + k))

    def spread(self, k):
        self.pass_on(k)
        self.over_plane(k)

    def cross(self, k):
        at = self.at

        def go(plane):
            first = plane * GROUP + at.member[1]
            second = plane * GROUP + at.member[2]
            even = lax.rem(plane, 2) == 0
            self.landed(first)
            at.when(even, lambda: self.copy(first, self.all.at[first], 3, at.near(2)).start())
            self.landed(second)
            at.when(
                jnp.logical_not(even),
                lambda: self.copy(second, self.all.at[second], 2, at.near(1)).start(),
            )

        if k == 0:
            go(at.z)
        else:
            at.when(at.has_down(k), lambda: go(at.z - k))
            at.when(at.has_up(k), lambda: go(at.z + k))

    def diagonal(self):
        for plane in range(self.at.planes):
            self.landed(plane * GROUP + self.at.member[3])
        self.keep().wait()

    def sent(self):
        at = self.at
        for plane in range(at.planes):
            block = plane * GROUP + at.p
            self.copy(block, self.own, 2, at.near(1)).wait_send()
            self.copy(block, self.own, 3, at.near(2)).wait_send()
            if plane % 2 == 0:
                self.copy(plane * GROUP + at.member[1], self.own, 3, at.near(2)).wait_send()
            else:
                self.copy(plane * GROUP + at.member[2], self.own, 2, at.near(1)).wait_send()

            def gone(way, device_of):
                self.copy(block, self.own, way, device_of()).wait_send()

            at.when((at.z >= plane) & at.has_up(), lambda: gone(0, at.up))
            at.when((at.z <= plane) & at.has_down(), lambda: gone(1, at.down))


class Experts:
    def __init__(self, at, own, all_blocks, local_sem, recvs, sends, across_sends):
        self.at, self.own, self.all = at, own, all_blocks
        self.local_sem, self.recvs, self.sends = local_sem, recvs, sends
        self.across_sends = across_sends

    def line(self, block, source, way, device):
        return send(source, self.all.at[block], self.sends.at[way, block], self.recvs.at[block], device)

    def across(self, j):
        at = self.at
        return send(
            self.own.at[at.member[j]],
            self.all.at[at.d],
            self.across_sends.at[j],
            self.recvs.at[at.d],
            at.near(j),
        )

    def keep(self):
        return pltpu.make_async_copy(self.own.at[self.at.p], self.all.at[self.at.d], self.local_sem)

    def start_plane(self):
        for j in range(1, GROUP):
            self.across(j).start()
        self.keep().start()

    def start_line(self):
        at = self.at
        source = self.own.at[at.p]
        at.when(at.has_up(), lambda: self.line(at.d, source, 0, at.up()).start())
        at.when(at.has_down(), lambda: self.line(at.d, source, 1, at.down()).start())

    def landed(self, block):
        self.line(block, self.own.at[0], 0, self.at.near(1)).wait_recv()

    def plane_step(self, j):
        at = self.at
        block = at.z * GROUP + at.member[j]
        source = self.all.at[block]
        self.landed(block)
        at.when(at.has_up(), lambda: self.line(block, source, 0, at.up()).start())
        at.when(at.has_down(), lambda: self.line(block, source, 1, at.down()).start())

    def line_step(self, k, j):
        at = self.at

        def go(plane, more, way, device_of):
            block = plane * GROUP + at.member[j]
            self.landed(block)
            at.when(more, lambda: self.line(block, self.all.at[block], way, device_of()).start())

        at.when(at.has_down(k), lambda: go(at.z - k, at.has_up(), 0, at.up))
        at.when(at.has_up(k), lambda: go(at.z + k, at.has_down(), 1, at.down))

    def ready(self):
        self.keep().wait()

    def own_sent(self):
        at = self.at
        source = self.own.at[at.p]
        for j in range(1, GROUP):
            self.across(j).wait_send()
        at.when(at.has_up(), lambda: self.line(at.d, source, 0, at.up()).wait_send())
        at.when(at.has_down(), lambda: self.line(at.d, source, 1, at.down()).wait_send())

    def rest_sent(self):
        at = self.at
        for plane in range(at.planes):

            def gone(j, way, device_of):
                block = plane * GROUP + at.member[j]
                self.line(block, self.own.at[0], way, device_of()).wait_send()

            for j in range(GROUP):
                up = at.z >= plane if j else at.z > plane
                down = at.z <= plane if j else at.z < plane
                at.when(up & at.has_up(), lambda: gone(j, 0, at.up))
                at.when(down & at.has_down(), lambda: gone(j, 1, at.down))


def dot_nn(a, b):
    return jnp.dot(a, b, preferred_element_type=jnp.float32)


def dot_nt(a, b):
    return lax.dot_general(a, b, (((1,), (1,)), ((), ())), preferred_element_type=jnp.float32)


def dot_tn(a, b):
    return lax.dot_general(a, b, (((0,), (0,)), ((), ())), preferred_element_type=jnp.float32)


def lanes(count=128):
    return lax.broadcasted_iota(jnp.int32, (1, count), 1)


def turn(values, cosine, sine):
    half = HD // 2
    other = jnp.where(
        lax.rem(lanes(), HD) < half,
        -pltpu.roll(values, 2 * HD - half, 1),
        pltpu.roll(values, half, 1),
    )
    return values * cosine + other * sine


def blocks_of(ref, start, stop):
    block = ref[:, :, start:stop]
    return block.reshape(block.shape[0] * block.shape[1], stop - start)


def attention_blocks(length):
    size = length // 2
    return [(i * size, (i + 1) * size) for i in range(2)]


class PlaneSum:
    def __init__(self, at, own, one, two, came, one_sems, two_sems, line_sems):
        self.at, self.own, self.one, self.two, self.came = at, own, one, two, came
        self.one_sems, self.two_sems, self.line_sems = one_sems, two_sems, line_sems

    def one_copy(self, plane, i, even):
        at = self.at
        j = 1 if even else 2
        target = at.member[3] if i else at.member[j]
        return send(
            self.own.at[plane * GROUP + target],
            self.one.at[plane, i],
            self.one_sems.at[0, plane, i],
            self.one_sems.at[1, plane, i],
            at.near(j),
        )

    def two_copy(self, plane, even):
        return send(
            self.one.at[plane, 1],
            self.two.at[plane],
            self.two_sems.at[0, plane],
            self.two_sems.at[1, plane],
            self.at.near(2 if even else 1),
        )

    def by_parity(self, plane, action):
        even = lax.rem(plane, 2) == 0
        self.at.when(even, lambda: action(True))
        self.at.when(jnp.logical_not(even), lambda: action(False))

    def line(self, source, plane, way, here=False):
        at, sems = self.at, self.line_sems
        slot, device = plane, at.up()
        if way:
            slot = jnp.where(plane == (at.z if here else at.z - 1), at.planes, plane)
            device = at.down()
        return send(
            source, self.came.at[slot], sems.at[0, way, plane], sems.at[1, way, plane], device
        )

    def both_ways(self, action, k):
        at = self.at
        if k == 0:
            action(at.z, 0)
            return
        at.when(at.has_up(k), lambda: action(at.z + k, 0))
        at.when(at.has_down(k), lambda: action(at.z - k, 1))

    def start(self, k):
        def go(plane, way):
            def pair(even):
                self.one_copy(plane, 1, even).start()
                self.one_copy(plane, 0, even).start()

            self.by_parity(plane, pair)

        self.both_ways(go, k)

    def middle(self, k):
        f32 = jnp.float32

        def go(plane, way):
            def stage(even):
                at, one = self.at, self.one
                other = plane * GROUP + (at.member[2] if even else at.member[1])
                self.one_copy(plane, 1, even).wait_recv()
                one[plane, 1] = (one[plane, 1].astype(f32) + self.own[other].astype(f32)).astype(
                    one.dtype
                )
                self.two_copy(plane, even).start()

            self.by_parity(plane, stage)

        self.both_ways(go, k)

    def finish_plane(self, plane):
        f32 = jnp.float32

        def stage(even):
            mine = plane * GROUP + self.at.p
            self.one_copy(plane, 0, even).wait_recv()
            self.two_copy(plane, even).wait_recv()
            self.two[plane] = (
                self.two[plane].astype(f32)
                + self.one[plane, 0].astype(f32)
                + self.own[mine].astype(f32)
            ).astype(self.two.dtype)

        self.by_parity(plane, stage)

    def step(self, k):
        f32 = jnp.float32

        def go(plane, way):
            at = self.at
            self.finish_plane(plane)
            behind = at.has_down() if way == 0 else at.has_up()
            held = self.came

            def add():
                self.line(self.two.at[plane], plane, way, True).wait_recv()
                held[plane] = (held[plane].astype(f32) + self.two[plane].astype(f32)).astype(
                    held.dtype
                )
                self.line(held.at[plane], plane, way).start()

            at.when(behind, add)
            at.when(
                jnp.logical_not(behind), lambda: self.line(self.two.at[plane], plane, way).start()
            )

        self.both_ways(go, k)

    def total(self, out):
        at, f32 = self.at, jnp.float32
        z = at.z
        self.finish_plane(z)
        at.when(at.has_down(), lambda: self.line(self.two.at[z], z, 0, True).wait_recv())
        at.when(at.has_up(), lambda: self.line(self.two.at[z], z, 1, True).wait_recv())
        low = jnp.where(at.has_down(), self.came[z].astype(f32), 0.0)
        high = jnp.where(at.has_up(), self.came[at.planes].astype(f32), 0.0)
        out[...] = (self.two[z].astype(f32) + low + high).astype(out.dtype)

    def sent(self):
        at = self.at
        for plane in range(at.planes):
            even = plane % 2 == 0
            self.one_copy(plane, 0, even).wait_send()
            self.one_copy(plane, 1, even).wait_send()
            self.two_copy(plane, even).wait_send()
            at.when(at.z < plane, lambda: self.line(self.two.at[plane], plane, 0).wait_send())
            at.when(at.z > plane, lambda: self.line(self.two.at[plane], plane, 1).wait_send())


class LineSum:
    def __init__(self, at, own, came, out, columns, line_sems, last_sems):
        self.at, self.own, self.came, self.out = at, own, came, out
        self.line_sems, self.last_sems = line_sems, last_sems
        self.columns, self.size = columns, columns[0].stop - columns[0].start

    def hop(self, source, plane, j, way, here=False):
        at = self.at
        block = plane * GROUP + at.member[j]
        if way == 0:
            slot, device = block, at.up()
        else:
            end = at.z if here else at.z - 1
            slot = jnp.where(plane == end, at.planes, plane) * GROUP + at.member[j]
            device = at.down()
        sems = self.line_sems
        return send(
            source, self.came.at[slot], sems.at[0, way, block], sems.at[1, way, block], device
        )

    def start_plane(self, plane):
        at = self.at

        def go(way):
            for j in range(GROUP):
                self.hop(self.own.at[plane * GROUP + at.member[j]], plane, j, way).start()

        at.when(jnp.logical_not(at.has_down()) & (plane != at.z), lambda: go(0))
        at.when(jnp.logical_not(at.has_up()) & (plane != at.z), lambda: go(1))

    def step(self, k, j):
        at, f32 = self.at, jnp.float32

        def go(plane, way):
            block = plane * GROUP + at.member[j]
            self.hop(self.own.at[block], plane, j, way, True).wait_recv()
            self.came[block] = (
                self.came[block].astype(f32) + self.own[block].astype(f32)
            ).astype(self.came.dtype)
            self.hop(self.came.at[block], plane, j, way).start()

        at.when(at.has_up(k) & at.has_down(), lambda: go(at.z + k, 0))
        at.when(at.has_down(k) & at.has_up(), lambda: go(at.z - k, 1))

    def parts(self, j, here=False):
        at, size = self.at, self.size
        source = self.came.at[at.z * GROUP + at.member[j]]
        target = self.out.at[at.member[j] if here else at.p]
        return [
            send(
                source.at[:, i * size : (i + 1) * size],
                target.at[:, self.columns[i]],
                self.last_sems.at[0, j, i],
                self.last_sems.at[1, j, i],
                at.near(j),
            )
            for i in range(len(self.columns))
        ]

    def total(self, j):
        at, f32, out = self.at, jnp.float32, self.out
        block = at.z * GROUP + at.member[j]
        spare = at.planes * GROUP + at.member[j]
        at.when(at.has_down(), lambda: self.hop(self.own.at[block], at.z, j, 0, True).wait_recv())
        at.when(at.has_up(), lambda: self.hop(self.own.at[block], at.z, j, 1, True).wait_recv())
        low = jnp.where(at.has_down(), self.came[block].astype(f32), 0.0)
        high = jnp.where(at.has_up(), self.came[spare].astype(f32), 0.0)
        total = (self.own[block].astype(f32) + low + high).astype(out.dtype)
        if j == 0:
            for i, columns in enumerate(self.columns):
                out[at.p, :, columns] = total[:, i * self.size : (i + 1) * self.size]
        else:
            self.came[block] = total
            for copy in self.parts(j):
                copy.start()

    def arrive(self, j):
        for copy in self.parts(j, True):
            copy.wait_recv()

    def sent(self):
        at = self.at
        for j in range(1, GROUP):
            for copy in self.parts(j):
                copy.wait_send()
        for plane in range(at.planes):

            def gone(way):
                for j in range(GROUP):
                    self.hop(self.own.at[0], plane, j, way).wait_send()

            at.when(at.z < plane, lambda: gone(0))
            at.when(at.z > plane, lambda: gone(1))


def norm_back_rows(grad, values, gain):
    rms = lax.rsqrt(jnp.mean(values * values, axis=-1, keepdims=True) + epsilon)
    grad_gain = jnp.sum(grad * values * rms, axis=0, keepdims=True)
    inner = grad * gain
    grad_values = rms * inner - values * (rms * rms * rms) * jnp.mean(
        inner * values, axis=-1, keepdims=True
    )
    return grad_values, grad_gain


def branch(x_of, dy_of, rows, weights, start, stride, hidden, act, y_acc, dx_acc):
    f32, bf16 = jnp.float32, jnp.bfloat16
    size, count = 256, rows.stop - rows.start
    step = min(count, 256)

    def body(i, carry):
        offset = pl.multiple_of(i * size, size)

        def weight(part):
            first = pl.multiple_of(start + part * stride + offset, size)
            block = weights[:, :, pl.ds(first, size)]
            return block.reshape(block.shape[0] * block.shape[1], size)

        for first in range(0, count, step):
            some = slice(first, first + step)

            def keep(part, values):
                columns = pl.ds(pl.multiple_of(part * hidden + offset, size), size)
                act[rows.start + first : rows.start + first + step, columns] = values

            g, u = dot_nn(x_of(some), weight(0)), dot_nn(x_of(some), weight(1))
            grad = dot_nn(dy_of(some), weight(2))
            sigma = 1.0 / (1.0 + jnp.exp(-g))
            silu = g * sigma
            eh = (silu * u).astype(bf16)
            dg = (grad * u * (sigma * (1.0 + g * (1.0 - sigma)))).astype(bf16)
            du = (grad * silu).astype(bf16)
            keep(0, dg)
            keep(1, du)
            keep(2, eh)
            y_acc[some, :] += dot_nt(eh, weight(2))
            dx_acc[some, :] += dot_nt(dg, weight(0)) + dot_nt(du, weight(1))
        return carry

    lax.fori_loop(0, hidden // size, body, 0)


def weight_grads(plane, planes, count, x_t, dy_t, act, hidden, grads, start, stride):
    width, bf16 = x_t.shape[0], jnp.bfloat16
    rows = width // planes
    features = pl.ds(pl.multiple_of(plane * rows, 16), rows)
    for part in range(3):
        columns = slice(part * hidden, (part + 1) * hidden)
        left = dy_t if part == 2 else x_t
        block = dot_nn(left[features, :count], act[:count, columns]).astype(bf16)
        target = slice(start + part * stride, start + part * stride + hidden)
        grads[pl.ds(plane * GROUP, GROUP), :, target] = block.reshape(
            GROUP, rows // GROUP, hidden
        )


PROBS, PAIRS, LOGS = 2, 8, 16


PLAN = {
    "begin": [
        ("E own", 0),
        ("S own",),
    ],
    "gather 1": [
        ("S plane",),
    ],
    "gather 2": [
        ("S line", 1),
        ("E line", 0, 1, 0),
    ],
    "gather 3": [
        ("E across", 1),
        ("E plane", 0, 1),
        ("S line", 2),
        ("E plane", 0, 2),
        ("E plane", 0, 3),
    ],
    "gathered": [
        ("S over", 2),
        ("E line", 0, 2, 0),
        ("S line", 3),
        ("S over", 1),
        ("S over", 3),
        ("E own", 1),
    ],
    "projected": [],
    "attention 0 0": [
        ("E line", 0, 1, 2),
    ],
    "attention 0 1": [],
    "attention 0 2": [
        ("E line", 0, 1, 3),
    ],
    "attention 1 0": [
        ("S cross", 2),
    ],
    "attention 1 1": [
        ("S cross", 1),
    ],
    "attention 1 2": [
        ("E line", 0, 1, 1),
    ],
    "attended": [
        ("E line", 0, 2, 2),
        ("E plane", 1, 1),
        ("E plane", 1, 2),
        ("E plane", 1, 3),
        ("E line", 1, 1, 0),
        ("S cross", 3),
        ("S cross", 0),
    ],
    "dispatched": [
        ("E line", 0, 2, 3),
        ("E line", 0, 3, 2),
    ],
    "shared 0": [
        ("E line", 0, 2, 1),
        ("E line", 1, 1, 2),
        ("E line", 1, 1, 3),
        ("E line", 1, 1, 1),
        ("E line", 0, 3, 0),
    ],
    "shared 1": [],
    "shared": [
        ("S start", 2),
        ("S start", 1),
    ],
    "arrived": [
        ("E line", 0, 3, 1),
        ("E line", 0, 3, 3),
        ("E line", 1, 2, 0),
        ("E line", 1, 2, 1),
        ("E line", 1, 2, 2),
        ("E line", 1, 2, 3),
        ("S start", 3),
    ],
    "expert 0 1": [],
    "expert 0 0": [],
    "expert 0": [
        ("E line", 1, 3, 0),
        ("E line", 1, 3, 1),
        ("E line", 1, 3, 2),
        ("E line", 1, 3, 3),
    ],
    "expert 1 1": [
        ("E step", 0, 2, 0),
    ],
    "expert 1 0": [
        ("E step", 0, 2, 3),
        ("S start", 0),
    ],
    "expert 1": [
        ("E step", 0, 2, 2),
        ("E step", 0, 2, 1),
        ("E step", 0, 1, 0),
        ("E step", 0, 1, 2),
        ("E step", 0, 1, 3),
    ],
    "home": [
        ("E step", 0, 1, 1),
        ("S middle", 3),
        ("S middle", 0),
    ],
    "combined": [],
    "projected out": [
        ("A start", 0, 3),
        ("A start", 0, 2),
        ("A start", 0, 1),
        ("A start", 0, 0),
    ],
    "backward 0 1": [
        ("E total", 0, 1),
        ("E total", 0, 2),
        ("E total", 0, 3),
        ("S middle", 1),
        ("E total", 0, 0),
    ],
    "backward 0 0": [
        ("E step", 1, 2, 0),
        ("E step", 1, 2, 1),
        ("E step", 1, 2, 3),
        ("S step", 3),
    ],
    "backward 1 1": [],
    "backward 1 0": [
        ("E step", 1, 1, 0),
    ],
    "backward 2 1": [],
    "backward 2 0": [
        ("S middle", 2),
    ],
    "projected back": [
        ("E step", 1, 2, 2),
        ("E step", 1, 1, 2),
        ("E step", 1, 1, 1),
    ],
    "last": [
        ("A start", 1, 3),
        ("A start", 1, 0),
        ("A start", 1, 1),
        ("E step", 1, 1, 3),
        ("A middle", 0, 3),
        ("A middle", 1, 3),
        ("A start", 1, 2),
        ("A middle", 0, 2),
        ("A middle", 1, 2),
        ("A step", 0, 3),
        ("A step", 1, 3),
        ("A middle", 0, 1),
        ("A middle", 1, 1),
        ("S step", 2),
        ("E total", 1, 0),
        ("E total", 1, 1),
        ("E total", 1, 2),
        ("E total", 1, 3),
        ("A step", 0, 2),
        ("A step", 1, 2),
        ("A middle", 0, 0),
        ("A middle", 1, 0),
        ("S step", 1),
        ("A step", 0, 1),
        ("A step", 1, 1),
    ],
}


def layer_kernel(
    planes,
    experts,
    top,
    heads_width,
    x_ref,
    cot_ref,
    facts,
    facts_t,
    waves,
    a_own,
    s_own,
    e_own,
    out_ref,
    gx_ref,
    a_out,
    s_out,
    e_out,
    aw,
    sw,
    ew,
    tok,
    part_one,
    home,
    act,
    x_t,
    dy_t,
    y_acc,
    dx_acc,
    s_dx,
    q_ref,
    k_ref,
    v_ref,
    o_ref,
    xf_ref,
    row_facts,
    ffn_theirs,
    dx_theirs,
    ret,
    a_one,
    a_two,
    a_came,
    s_one,
    s_two,
    s_came,
    e_came,
    local_sem,
    a_recv,
    a_send,
    s_recv,
    s_send,
    e_recv,
    e_send,
    e_across,
    a_one_sems,
    a_two_sems,
    a_line_sems,
    s_one_sems,
    s_two_sems,
    s_line_sems,
    e_line_sems,
    e_last_sems,
    token_sems,
    home_sems,
    share_sems,
    twin_sems,
):
    f32, bf16 = jnp.float32, jnp.bfloat16
    at = Place(planes)
    length, width = x_ref.shape
    capacity = length * top // experts
    half = capacity // 2
    count = experts * half
    hidden, s_hidden = ew.shape[3] // 3, sw.shape[2] // 6
    step = min(length, 256)
    chunks = [slice(i, i + step) for i in range(0, length, step)]
    seg_col, seg_row = facts[:, 2 * top : 2 * top + 1], facts_t[2 * top : 2 * top + 1, :]

    halves = [
        [slice((2 * k + i) * hidden, (2 * k + i + 1) * hidden) for k in range(3)] for i in range(2)
    ]

    attn_in = Everywhere(at, a_own, aw, local_sem.at[0], a_recv, a_send)
    shared_in = Everywhere(at, s_own, sw, local_sem.at[1], s_recv, s_send)
    expert_in = [
        Experts(
            at,
            part_one.at[i, :, : e_own.shape[1]],
            ew.at[i],
            local_sem.at[2 + i],
            e_recv.at[i],
            e_send.at[i],
            e_across.at[i],
        )
        for i in range(2)
    ]
    expert_out = [
        LineSum(
            at, ew.at[i], e_came.at[i], e_out, halves[i], e_line_sems.at[i], e_last_sems.at[i]
        )
        for i in range(2)
    ]
    shared_out = PlaneSum(at, sw, s_one, s_two, s_came, s_one_sems, s_two_sems, s_line_sems)
    attn_out = [
        PlaneSum(
            at,
            aw.at[:, :, columns],
            a_one.at[:, :, :, columns],
            a_two.at[:, :, columns],
            a_came.at[:, :, columns],
            a_one_sems.at[i],
            a_two_sems.at[i],
            a_line_sems.at[i],
        )
        for i, columns in enumerate((slice(0, heads_width), slice(heads_width, aw.shape[2])))
    ]

    xa_ref = act.at[:length, :width]
    placed = ret
    part_mine = act.at[length:, :width]
    part_theirs = ret.at[:length, :width]
    grad_o = act.at[:length, :heads_width]
    dproj = act.at[:length, heads_width : 4 * heads_width]
    bias = y_acc
    dk_acc, dv_acc = (dx_acc.at[:, 128 * i : 128 * (i + 1)] for i in range(2))

    def halve(i, k):
        return pltpu.make_async_copy(
            e_own.at[:, :, halves[i][k]],
            part_one.at[i, :, : e_own.shape[1], k * hidden : (k + 1) * hidden],
            local_sem.at[4 + 3 * i + k],
        )

    for i in range(2):
        for k in range(3):
            halve(i, k).start()
    at.greet()
    attn_in.start_line()
    attn_in.start_plane()
    for k in range(3):
        halve(0, k).wait()
    expert_in[0].start_plane()
    for k in range(3):
        halve(1, k).wait()

    def turn_of(name):
        for step in PLAN[name]:
            do(*step)

    def do(kind, *numbers):
        steps[kind](*numbers)

    steps = {
        "E plane": lambda i, j: expert_in[i].plane_step(j),
        "E across": lambda i: expert_in[i].start_plane(),
        "E own": lambda i: expert_in[i].start_line(),
        "E line": lambda i, k, j: expert_in[i].line_step(k, j),
        "S own": lambda: shared_in.start_line(),
        "S plane": lambda: shared_in.start_plane(),
        "S line": lambda k: shared_in.pass_on(k),
        "S over": lambda k: shared_in.over_plane(k),
        "S cross": lambda k: shared_in.cross(k),
        "S start": lambda k: shared_out.start(k),
        "S middle": lambda k: shared_out.middle(k),
        "S step": lambda k: shared_out.step(k),
        "E step": lambda i, k, j: expert_out[i].step(k, j),
        "E total": lambda i, j: expert_out[i].total(j),
        "A start": lambda i, k: attn_out[i].start(k),
        "A middle": lambda i, k: attn_out[i].middle(k),
        "A step": lambda i, k: attn_out[i].step(k),
    }

    turn_of("begin")

    def masks():
        for start, stop in attention_blocks(length):
            row = lax.broadcasted_iota(jnp.int32, (stop - start, stop), 0) + start
            column = lax.broadcasted_iota(jnp.int32, (stop - start, stop), 1)
            allowed = (column <= row) & (seg_col[start:stop, :] == seg_row[:, :stop])
            bias[start:stop, :stop] = jnp.where(allowed, 0.0, -1e30)

    masks()

    def slot_of(expert_id, position):
        which = position // half
        apart = which + at.c - 2 * which * at.c
        bit0, bit1 = lax.rem(expert_id, 2), expert_id // 2
        p0, p1 = lax.rem(at.p, 2), at.p // 2
        distance = (bit0 + p0 - 2 * bit0 * p0) + 2 * (bit1 + p1 - 2 * bit1 * p1)
        slot = apart * count + distance * half + lax.rem(position, half)
        return jnp.where(position < capacity, slot, -1)

    slot_cols, slot_rows = [], []
    for r in range(top):
        ids_col, order_col = facts[:, r : r + 1], facts[:, top + r : top + r + 1]
        ids_row, order_row = facts_t[r : r + 1, :], facts_t[top + r : top + r + 1, :]
        count_col = jnp.zeros((length, 1), jnp.int32)
        count_row = jnp.zeros((1, length), jnp.int32)
        for other in range(top):
            first = (facts_t[other : other + 1, :] == ids_col) & (
                facts_t[top + other : top + other + 1, :] < order_col
            )
            count_col += jnp.sum(first.astype(jnp.int32), axis=1, keepdims=True)
            first = (facts[:, other : other + 1] == ids_row) & (
                facts[:, top + other : top + other + 1] < order_row
            )
            count_row += jnp.sum(first.astype(jnp.int32), axis=0, keepdims=True)
        slot_cols.append(slot_of(ids_col, count_col))
        slot_rows.append(slot_of(ids_row, count_row))

    for k in range(1, planes):
        attn_in.spread(k)
        attn_in.cross(k - 1)
        turn_of(f"gather {k}")
    attn_in.cross(planes - 1)
    turn_of("gathered")
    attn_in.diagonal()

    small = blocks_of(aw, 4 * heads_width, 4 * heads_width + 128)
    small_rows = small.astype(f32).T
    g_one, g_two = small_rows[0:1, :], small_rows[1:2, :]
    for rows in chunks:
        x = x_ref[rows, :].astype(f32)
        rms = lax.rsqrt(jnp.mean(x * x, axis=-1, keepdims=True) + epsilon)
        xa_ref[rows, :] = (x * rms * g_one).astype(bf16)
    wave, other = waves[...], pltpu.roll(waves[...], 64, 1)
    cosine = jnp.where(lanes() < 64, wave, other)
    sine = jnp.where(lanes() < 64, other, wave)
    pairs = heads_width // 128
    for i, ref in enumerate((q_ref, k_ref)):
        part = dot_nn(xa_ref[...], blocks_of(aw, (i + 1) * heads_width, (i + 2) * heads_width))
        for g in range(pairs):
            columns = slice(128 * g, 128 * (g + 1))
            ref[:, columns] = turn(part[:, columns], cosine, sine).astype(bf16)
    v_ref[...] = dot_nn(xa_ref[...], blocks_of(aw, 3 * heads_width, 4 * heads_width)).astype(bf16)
    turn_of("projected")

    scale = HD ** (-0.5)
    for start, stop in attention_blocks(length):
        logs = jnp.zeros((stop - start, 128), f32)
        for g in range(pairs):
            columns = slice(128 * g, 128 * (g + 1))
            queries = q_ref[start:stop, columns]
            keys, values = k_ref[:stop, columns], v_ref[:stop, columns]
            mixed = []
            for i in range(2):
                one = jnp.where(lanes() // HD == i, queries, jnp.zeros_like(queries))
                scores = dot_nt(one, keys) * scale + bias[start:stop, :stop]
                largest = jnp.max(scores, axis=-1, keepdims=True)
                expo = jnp.exp(scores - largest)
                total = jnp.sum(expo, axis=-1, keepdims=True)
                weights = (expo * (1.0 / total)).astype(bf16)
                mixed.append(dot_nn(weights, values))
                logs = jnp.where(lanes() == LOGS + 2 * g + i, largest + jnp.log(total), logs)
            o_ref[start:stop, columns] = jnp.where(lanes() < HD, mixed[0], mixed[1]).astype(bf16)
            turn_of(f"attention {start // (length // 2)} {g}")
        row_facts[start:stop, :] = logs

    for rows in chunks:
        dx_acc[rows, :] = dot_nt(
            o_ref[rows, :], blocks_of(aw, 0, heads_width)
        )
    swap = send(dx_acc, gx_ref, twin_sems.at[0, 0], twin_sems.at[1, 0], at.twin())
    swap.start()
    turn_of("attended")
    swap.wait_recv()

    is_expert = (lanes() >= PROBS) & (lanes() < PROBS + experts)
    for rows in chunks:
        h = x_ref[rows, :].astype(f32) + (dx_acc[rows, :] + gx_ref[rows, :])
        gx_ref[rows, :] = h
        rms = lax.rsqrt(jnp.mean(h * h, axis=-1, keepdims=True) + epsilon)
        xf = (h * rms * g_two).astype(bf16)
        xf_ref[rows, :] = xf
        logits = jnp.where(is_expert, dot_nn(xf, small), -1e30)
        expo = jnp.exp(logits - jnp.max(logits, axis=-1, keepdims=True))
        probs = expo / jnp.sum(expo, axis=-1, keepdims=True)
        packed = jnp.where(is_expert, probs, row_facts[rows, :])
        for r in range(top):
            chosen = lanes() == facts[rows, r : r + 1] + PROBS
            gate = jnp.sum(jnp.where(chosen, probs, 0.0), axis=-1, keepdims=True)
            slot = slot_cols[r][rows, :]
            gate = jnp.where(slot >= 0, gate, 0.0)
            packed = jnp.where(lanes() == PAIRS + r, gate, packed)
            packed = jnp.where(lanes() == PAIRS + top + r, slot.astype(f32), packed)
        row_facts[rows, :] = packed
    gate_rows = row_facts[...].T[PAIRS : PAIRS + 8, :]

    def outgoing(j):
        return send(
            placed.at[j * half : (j + 1) * half, :],
            tok.at[0, j],
            token_sems.at[0, j],
            token_sems.at[1, j],
            at.near(j),
        )

    for j in range(experts):
        index = lax.broadcasted_iota(jnp.int32, (half, 1), 0) + j * half
        pick = [slot_rows[r] == index for r in range(top)]
        slot_gate = sum(
            jnp.sum(jnp.where(pick[r], gate_rows[r : r + 1, :], 0.0), axis=1, keepdims=True)
            for r in range(top)
        )
        pick = sum(p.astype(f32) for p in pick).astype(bf16)
        if j:
            target = placed.at[j * half : (j + 1) * half, :]
        else:
            target = tok.at[0, 0]
        target[:, :width] = dot_nn(pick, xf_ref[...]).astype(bf16)
        target[:, width:] = (dot_nn(pick, cot_ref[...]) * slot_gate).astype(bf16)
        if j:
            outgoing(j).start()

    def shared_branch():
        shared_in.diagonal()
        shared_in.sent()
        for some in chunks:
            x_t[:, some] = xf_ref[some, :].T
            dy_t[:, some] = cot_ref[some, :].T
        y_acc[...] = jnp.zeros(y_acc.shape, f32)
        dx_acc[...] = jnp.zeros(dx_acc.shape, f32)
        for i in range(2):
            start = s_hidden * i
            branch(
                lambda some: xf_ref[some, :],
                lambda some: cot_ref[some, :],
                slice(0, length),
                sw,
                start,
                2 * s_hidden,
                s_hidden,
                act,
                y_acc,
                dx_acc,
            )

            def shared_grads(plane, carry):
                weight_grads(
                    plane, planes, length, x_t, dy_t, act, s_hidden, sw, start, 2 * s_hidden
                )
                return carry

            lax.fori_loop(0, planes, shared_grads, 0)
            turn_of(f"shared {i}")
        out_ref[...] = y_acc[...].astype(bf16)
        s_dx[...] = dx_acc[...].astype(bf16)
        swaps = [
            send(mine, theirs, twin_sems.at[0, 2 + i], twin_sems.at[1, 2 + i], at.twin())
            for i, (mine, theirs) in enumerate(((out_ref, ffn_theirs), (s_dx, dx_theirs)))
        ]
        for swap in swaps:
            swap.start()
        return swaps

    turn_of("dispatched")
    swap.wait_send()
    swaps = shared_branch()
    turn_of("shared")
    for j in range(1, experts):
        outgoing(j).wait_recv()
        outgoing(j).wait_send()
    across = send(tok.at[0], tok.at[1], twin_sems.at[0, 1], twin_sems.at[1, 1], at.twin())
    across.start()
    turn_of("arrived")

    across.wait_recv()
    across.wait_send()

    def home_copy(j):
        return send(
            tok.at[0, j], home.at[0, j], home_sems.at[0, j], home_sems.at[1, j], at.near(j)
        )

    def share(j):
        return send(
            tok.at[1, j],
            ret.at[j * half : (j + 1) * half],
            share_sems.at[0, j],
            share_sems.at[1, j],
            at.twin(),
        )

    for i in range(2):
        expert_in[i].ready()
        expert_in[i].own_sent()

    def expert_half(i):
        for t in (1, 0):
            rows = slice(t * count, (t + 1) * count)

            def x_of(some):
                some = slice(some.start // half, some.stop // half)
                return tok[t, some, :, :width].reshape(-1, width)

            def dy_of(some):
                some = slice(some.start // half, some.stop // half)
                return tok[t, some, :, width:].reshape(-1, width)

            for some in chunks:
                x_t[:, rows.start + some.start : rows.start + some.stop] = x_of(some).T
                dy_t[:, rows.start + some.start : rows.start + some.stop] = dy_of(some).T
            if i == 0:
                y_acc[...] = jnp.zeros(y_acc.shape, f32)
                dx_acc[...] = jnp.zeros(dx_acc.shape, f32)
            else:
                for j in range(experts):
                    some = slice(j * half, (j + 1) * half)
                    y_acc[some, :] = part_one[t, j, :, :width].astype(f32)
                    dx_acc[some, :] = part_one[t, j, :, width:].astype(f32)
            branch(x_of, dy_of, rows, ew.at[i], 0, hidden, hidden, act, y_acc, dx_acc)
            target = tok if i else part_one
            if i and t == 0:
                for j in range(experts):
                    share(j).wait_recv()
            for j in range(experts):
                some = slice(j * half, (j + 1) * half)
                y, dx = y_acc[some, :], dx_acc[some, :]
                if i and t == 0:
                    y += ret[some, :width].astype(f32)
                    dx += ret[some, width:].astype(f32)
                target[t, j, :, :width] = y.astype(bf16)
                target[t, j, :, width:] = dx.astype(bf16)
                if i and t == 0 and j:
                    home_copy(j).start()
            if i and t:
                for j in range(experts):
                    share(j).start()
            turn_of(f"expert {i} {t}")
        if i:
            home[0, 0] = tok[0, 0]
        expert_in[i].rest_sent()

        def grads_of(n, carry):
            plane = jnp.where(at.z * 2 < planes, planes - 1 - n, n)
            weight_grads(plane, planes, 2 * count, x_t, dy_t, act, hidden, ew.at[i], 0, hidden)
            expert_out[i].start_plane(plane)
            return carry

        lax.fori_loop(0, planes, grads_of, 0)

    for i in range(2):
        expert_half(i)
        turn_of(f"expert {i}")

    for j in range(1, experts):
        home_copy(j).wait_recv()
    swap = send(home.at[0], home.at[1], twin_sems.at[0, 5], twin_sems.at[1, 5], at.twin())
    swap.start()
    turn_of("home")
    for other in swaps:
        other.wait_recv()
        other.wait_send()
    swap.wait_recv()
    for rows in chunks:
        y = out_ref[rows, :].astype(f32) + ffn_theirs[rows, :].astype(f32)
        dx = s_dx[rows, :].astype(f32) + dx_theirs[rows, :].astype(f32)
        gate = jnp.zeros((step, 128), f32)
        dy = cot_ref[rows, :].astype(f32)
        for core in range(2):
            t = core + at.c - 2 * core * at.c
            index = lax.broadcasted_iota(jnp.int32, (1, count), 1) + t * count
            slots = [row_facts[rows, PAIRS + top + r : PAIRS + top + r + 1] for r in range(top)]
            slots = [(slot.astype(jnp.int32) == index).astype(f32) for slot in slots]
            for r in range(top):
                part = dot_nn(slots[r].astype(bf16), home[t, :, :, :width].reshape(count, width))
                y += row_facts[rows, PAIRS + r : PAIRS + r + 1] * part
                grad = jnp.sum(dy * part, axis=-1, keepdims=True)
                gate += jnp.where(lanes() == facts[rows, r : r + 1] + PROBS, grad, 0.0)
            dx += dot_nn(sum(slots).astype(bf16), home[t, :, :, width:].reshape(count, width))
        out_ref[rows, :] = (gx_ref[rows, :] + y).astype(bf16)
        dx_acc[rows, :] = dx
        y_acc[rows, :128] = gate
    attn_in.sent()

    grad_g_two = jnp.zeros((1, width), f32)
    grad_small = jnp.zeros((width, 128), f32)
    for rows in chunks:
        probs = jnp.where(is_expert, row_facts[rows, :], 0.0)
        grad_probs = y_acc[rows, :128]
        grad_logits = (
            probs * (grad_probs - jnp.sum(probs * grad_probs, axis=-1, keepdims=True))
        ).astype(bf16)
        grad_small += dot_tn(xf_ref[rows, :], grad_logits)
        grad_xf = dx_acc[rows, :] + dot_nt(grad_logits, small)
        h = gx_ref[rows, :]
        grad_h, grad_gain = norm_back_rows(grad_xf, h, g_two)
        grad_g_two += grad_gain
        grad_h = cot_ref[rows, :].astype(f32) + grad_h
        gx_ref[rows, :] = grad_h
        dy_t[:, rows] = grad_h.astype(bf16).T
        grad_o[rows, :] = dot_nn(
            grad_h.astype(bf16), blocks_of(aw, 0, heads_width)
        ).astype(bf16)
    for rows in chunks:
        x = x_ref[rows, :].astype(f32)
        rms = lax.rsqrt(jnp.mean(x * x, axis=-1, keepdims=True) + epsilon)
        x_t[:, rows] = (x * rms * g_one).astype(bf16).T
    masks()
    turn_of("combined")

    def to_grads(start, columns, left, right):
        blocks = aw.shape[0]
        for i in range(0, blocks, blocks // 4):
            some = slice(i, i + blocks // 4)
            features = slice(i * aw.shape[1], (i + blocks // 4) * aw.shape[1])
            block = dot_nn(left[features, :length], right())
            aw[some, :, start : start + columns] = block.astype(bf16).reshape(
                blocks // 4, aw.shape[1], columns
            )

    to_grads(0, heads_width, dy_t, lambda: o_ref[...])
    turn_of("projected out")
    for g in range(pairs):
        columns = slice(128 * g, 128 * (g + 1))
        for start, stop in attention_blocks(length)[::-1]:
            queries = q_ref[start:stop, columns]
            grads = grad_o[start:stop, columns]
            keys, values = k_ref[:stop, columns], v_ref[:stop, columns]
            grad_q = jnp.zeros((stop - start, 128), f32)
            grad_k = jnp.zeros((stop, 128), f32)
            grad_v = jnp.zeros((stop, 128), f32)
            for i in range(2):
                mask = lanes() // HD == i
                one_q = jnp.where(mask, queries, jnp.zeros_like(queries))
                one_do = jnp.where(mask, grads, jnp.zeros_like(grads))
                one_k = jnp.where(mask, keys, jnp.zeros_like(keys))
                scores = dot_nt(one_q, keys) * scale + bias[start:stop, :stop]
                log = LOGS + 2 * g + i
                weights = jnp.exp(scores - row_facts[start:stop, log : log + 1])
                grad_w = dot_nt(one_do, values)
                inner = jnp.sum(weights * grad_w, axis=-1, keepdims=True)
                grad_s = (weights * (grad_w - inner)).astype(bf16)
                grad_q += dot_nn(grad_s, one_k)
                grad_k += dot_tn(grad_s, one_q)
                grad_v += dot_tn(weights.astype(bf16), one_do)
            dproj[start:stop, columns] = turn(
                grad_q * scale, cosine[start:stop, :], -sine[start:stop, :]
            ).astype(bf16)
            if stop == length:
                dk_acc[...] = grad_k * scale
                dv_acc[...] = grad_v
            else:
                dk_acc[:stop, :] += grad_k * scale
                dv_acc[:stop, :] += grad_v
            turn_of(f"backward {g} {start // (length // 2)}")
        dproj[:, heads_width + 128 * g : heads_width + 128 * (g + 1)] = turn(
            dk_acc[...], cosine, -sine
        ).astype(bf16)
        dproj[:, 2 * heads_width + 128 * g : 2 * heads_width + 128 * (g + 1)] = dv_acc[
            ...
        ].astype(bf16)
    for rows in chunks:
        part = dot_nt(dproj[rows, :], blocks_of(aw, heads_width, 4 * heads_width))
        part_mine[rows, :] = part.astype(bf16)
    last_swap = send(part_mine, part_theirs, twin_sems.at[0, 6], twin_sems.at[1, 6], at.twin())
    last_swap.start()
    for i in range(3):
        columns = slice(i * heads_width, (i + 1) * heads_width)
        to_grads((i + 1) * heads_width, heads_width, x_t, lambda: dproj[:, columns])
    turn_of("projected back")
    last_swap.wait_recv()
    grad_g_one = jnp.zeros((1, width), f32)
    for rows in chunks:
        grad_xa = part_mine[rows, :].astype(f32) + part_theirs[rows, :].astype(f32)
        grad_x, grad_gain = norm_back_rows(grad_xa, x_ref[rows, :].astype(f32), g_one)
        gx_ref[rows, :] += grad_x
        grad_g_one += grad_gain
    index = lax.broadcasted_iota(jnp.int32, (128, 1), 0)
    gains = jnp.where(index == 0, grad_g_one, 0.0) + jnp.where(index == 1, grad_g_two, 0.0)
    small_grads = (gains.T + grad_small).astype(bf16)
    aw[:, :, 4 * heads_width :] = small_grads.reshape(aw.shape[0], aw.shape[1], 128)
    turn_of("last")
    shared_out.total(s_out)
    for i, columns in enumerate((slice(0, heads_width), slice(heads_width, aw.shape[2]))):
        attn_out[i].total(a_out.at[:, columns])
    for i in range(2):
        for j in range(1, GROUP):
            expert_out[i].arrive(j)

    swap.wait_send()
    last_swap.wait_send()
    for j in range(experts):
        share(j).wait_send()
    for j in range(1, experts):
        home_copy(j).wait_send()
    for i in range(2):
        expert_out[i].sent()
    shared_out.sent()
    for i in range(2):
        attn_out[i].sent()


def layer(planes, experts, top, heads_width, inputs, own):
    bf16, f32, dma = jnp.bfloat16, jnp.float32, pltpu.SemaphoreType.DMA
    n = planes * GROUP
    length, width = inputs[0].shape
    rows, a_width = own[0].shape
    s_width, e_width = own[1].shape[1], own[2].shape[2] // 2
    half = length * top // experts // 2
    slots = 2 * experts * half
    vmem, anywhere = pl.BlockSpec(memory_space=pltpu.VMEM), pl.BlockSpec(memory_space=pl.ANY)
    shape = jax.ShapeDtypeStruct
    tokens = pltpu.VMEM((2, experts, half, 2 * width), bf16)
    features = pltpu.VMEM((width, slots), bf16)
    wide = pltpu.VMEM((length, width), f32)
    narrow = pltpu.VMEM((length, width), bf16)
    heads = pltpu.VMEM((length, heads_width), bf16)
    facts = pltpu.VMEM((length, 128), f32)

    def plane_buffers(columns):
        return [
            pltpu.VMEM((planes, 2, rows, columns), bf16),
            pltpu.VMEM((planes, rows, columns), bf16),
            pltpu.VMEM((planes + 1, rows, columns), bf16),
        ]

    plane_sems = [dma((2, planes, 2)), dma((2, planes)), dma((2, 2, planes))]
    return pl.pallas_call(
        functools.partial(layer_kernel, planes, experts, top, heads_width),
        out_shape=(
            shape((length, width), bf16),
            shape((length, width), f32),
            shape((rows, a_width), f32),
            shape((rows, s_width), bf16),
            shape((GROUP, rows, 2 * e_width), bf16),
        ),
        in_specs=[vmem] * len(inputs) + [anywhere] * 3,
        out_specs=(vmem,) * 5,
        scratch_shapes=[
            pltpu.VMEM((n, rows, a_width), bf16),
            pltpu.VMEM((n, rows, s_width), bf16),
            pltpu.VMEM((2, n, rows, e_width), bf16),
            tokens,
            tokens,
            tokens,
            pltpu.VMEM((slots, e_width), bf16),
            features,
            features,
            wide,
            wide,
            narrow,
            heads,
            heads,
            heads,
            heads,
            narrow,
            facts,
            narrow,
            narrow,
            pltpu.VMEM((experts * half, 2 * width), bf16),
            *plane_buffers(a_width),
            *plane_buffers(s_width),
            pltpu.VMEM((2, (planes + 1) * GROUP, rows, e_width), bf16),
            dma((10,)),
            dma((n,)),
            dma((4, n)),
            dma((n,)),
            dma((4, n)),
            dma((2, n)),
            dma((2, 2, n)),
            dma((2, GROUP)),
            *[dma((2,) + s.shape) for s in plane_sems],
            *plane_sems,
            dma((2, 2, 2, n)),
            dma((2, 2, GROUP, 3)),
            dma((2, GROUP)),
            dma((2, GROUP)),
            dma((2, GROUP)),
            dma((2, 7)),
        ],
        compiler_params=pltpu.CompilerParams(
            collective_id=0, has_side_effects=True, vmem_limit_bytes=63 << 20
        ),
    )(*inputs, *own)


def local_grouped(
    planes,
    tokens,
    segment_ids,
    expert_ids,
    slot_order,
    gain_attn,
    qkv_weight,
    out_weight,
    gain_ffn,
    router_weight,
    gate_up,
    down_weight,
    shared_gate_up,
    shared_down,
    cotangent,
):
    bf16, f32 = jnp.bfloat16, jnp.float32
    rows, heads_width = qkv_weight.shape[0], qkv_weight.shape[2]
    experts, hidden = down_weight.shape[0], down_weight.shape[1]
    s_hidden = shared_down.shape[0]
    length = tokens.shape[0]
    top = expert_ids.shape[1]
    cuts = [heads_width, 3 * heads_width, 128]
    edges = [sum(cuts[:i]) for i in range(len(cuts) + 1)]

    def part(array, i):
        return array[..., edges[i] : edges[i + 1]]

    expert_packed = jnp.concatenate(
        [gate_up.reshape(experts, rows, 2 * hidden), down_weight.transpose(0, 2, 1)], axis=2
    )
    shared_packed = jnp.concatenate(
        [shared_gate_up.reshape(rows, 2 * s_hidden), shared_down.T], axis=1
    )
    small = jnp.concatenate([gain_attn[:, None], gain_ffn[:, None], router_weight], axis=1)
    small = jnp.pad(small, ((0, 0), (0, 128 - small.shape[1])))
    attn_packed = jnp.concatenate(
        [out_weight.T, qkv_weight.reshape(rows, 3 * heads_width), small], axis=1
    )
    cosine, sine = rotary(length, HD)
    waves = jnp.concatenate([cosine[:, 0]] * 2 + [sine[:, 0]] * 2, axis=1)
    facts = jnp.concatenate(
        [expert_ids, slot_order.reshape(length, top), segment_ids.reshape(length, 1)], axis=1
    )
    facts = jnp.pad(facts, ((0, 0), (0, 8 - facts.shape[1])))
    output, grad_tokens, mine, mine_shared, mine_expert = layer(
        planes,
        experts,
        top,
        heads_width,
        (tokens, cotangent, facts, facts.T, waves),
        (attn_packed, shared_packed, expert_packed),
    )
    small_mine = part(mine, 2)

    def halves(grads, size):
        both = [grads[..., :size], grads[..., size : 2 * size]]
        return jnp.stack(both, axis=-2).astype(f32)

    return (
        output,
        grad_tokens,
        small_mine[:, 0],
        part(mine, 1).reshape(rows, 3, heads_width),
        part(mine, 0).T,
        small_mine[:, 1],
        small_mine[:, 2 : 2 + experts],
        halves(mine_expert, hidden),
        mine_expert[:, :, 2 * hidden :].transpose(0, 2, 1).astype(f32),
        halves(mine_shared, s_hidden),
        mine_shared[:, 2 * s_hidden :].T.astype(f32),
    )


def solution(mesh):
    def pick(*args):
        experts, rows = args[9].shape[0], args[5].shape[0]
        if experts == GROUP and mesh.shape["dp"] % GROUP == 0 and rows % 16 == 0:
            return local_grouped(mesh.shape["dp"] // GROUP, *args)
        return local_plain(*args)

    return jax.shard_map(
        pick,
        mesh=mesh,
        in_specs=(
            P("dp", None),
            P("dp", None),
            P("dp", None),
            P("dp", None),
            P("dp"),
            P("dp", None, "tensor"),
            P("tensor", "dp"),
            P("dp"),
            P("dp", None),
            P(None, "dp", None, "tensor"),
            P(None, "tensor", "dp"),
            P("dp", None, "tensor"),
            P("tensor", "dp"),
            P("dp", None),
        ),
        out_specs=(
            P("dp", None),
            P("dp", None),
            P("dp"),
            P("dp", None, "tensor"),
            P("tensor", "dp"),
            P("dp"),
            P("dp", None),
            P(None, "dp", None, "tensor"),
            P(None, "tensor", "dp"),
            P("dp", None, "tensor"),
            P("tensor", "dp"),
        ),
        check_vma=False,
    )
```

```python
import functools
import math

import jax
import jax.numpy as jnp
import numpy as np
from jax import lax
from jax.experimental import pallas as pl
from jax.experimental.pallas import tpu as pltpu
from jax.sharding import PartitionSpec as P

HD = 64
GROUP = 4
MESH = pl.DeviceIdType.MESH


epsilon = 1e-06


def rms_scale(values):
    return lax.rsqrt(jnp.mean(values * values, axis=-1, keepdims=True) + epsilon)


def rotary(length, head_dim):
    half_dim = head_dim // 2
    position = jnp.arange(length).astype(jnp.float32)[:, None]
    inverse = jnp.exp(
        jnp.arange(half_dim).astype(jnp.float32) * (-2.0 * math.log(10000.0) / head_dim)
    )
    angles = position * inverse[None, :]
    return (jnp.cos(angles)[:, None, :], jnp.sin(angles)[:, None, :])


def rotate(values, cosine, sine):
    half_dim = values.shape[-1] // 2
    first_half = values[..., :half_dim]
    second_half = values[..., half_dim:]
    return jnp.concatenate(
        [first_half * cosine - second_half * sine, second_half * cosine + first_half * sine],
        axis=-1,
    )


def route_slots(pair_ids, rank_order, capacity, experts):
    length = pair_ids.shape[0]
    top_count = pair_ids.shape[1]
    pair_expert = pair_ids.reshape(-1)
    pair_count = pair_expert.shape[0]
    ordered = jnp.zeros((pair_count,), jnp.int32).at[rank_order].set(pair_expert)
    onehot = (ordered[:, None] == jnp.arange(experts, dtype=jnp.int32)[None, :]).astype(jnp.int32)
    running = jnp.cumsum(onehot, axis=0)
    ranked_slot = jnp.sum(running * onehot, axis=1) - 1
    position = ranked_slot[rank_order]
    kept_pair = position < capacity
    slot_index = jnp.where(kept_pair, pair_expert * capacity + position, experts * capacity)
    token_of_pair = jnp.arange(pair_count, dtype=jnp.int32) // top_count
    slot_token = (
        jnp.full((experts * capacity,), length, jnp.int32)
        .at[slot_index]
        .set(token_of_pair, mode="drop")
    )
    return (slot_token, slot_index.reshape(length, top_count), kept_pair.reshape(length, top_count))


def silu_back(both_parts, grad_hidden):
    gate_part = both_parts[..., 0, :]
    up_part = both_parts[..., 1, :]
    sigma = jax.nn.sigmoid(gate_part)
    slope = sigma * (1.0 + gate_part * (1.0 - sigma))
    return jnp.stack(
        [grad_hidden * up_part * slope, grad_hidden * gate_part * sigma], axis=-2
    ).astype(jnp.bfloat16)


def silu_forward(both_parts):
    return (jax.nn.silu(both_parts[..., 0, :]) * both_parts[..., 1, :]).astype(jnp.bfloat16)


def norm_back(grad_norm, values, scale_rows, gain):
    grad_gain = jnp.sum(grad_norm * values * scale_rows, axis=0)
    inner = grad_norm * gain
    grad_values = scale_rows * inner - values * scale_rows**3 * jnp.mean(
        inner * values, axis=-1, keepdims=True
    )
    return (grad_values, grad_gain)


def split_blocks(length):
    block = min(512, length)
    return (block, length // block)


def masked_scores(query_block, keys_all, query_pos, query_seg, segment, scale):
    positions = jnp.arange(keys_all.shape[0])
    scores = (
        jnp.einsum("qhd,khd->hqk", query_block, keys_all, preferred_element_type=jnp.float32)
        * scale
    )
    allowed = (positions[None, :] <= query_pos[:, None]) & (segment[None, :] == query_seg[:, None])
    return jnp.where(allowed[None], scores, -1e30)


def attend_forward(queries, keys_all, values_all, segment, scale):
    length, head_count, head_dim = queries.shape
    block, count_blocks = split_blocks(length)
    positions = jnp.arange(length)

    def one_block(inputs):
        query_block, query_pos, query_seg = inputs
        scores = masked_scores(query_block, keys_all, query_pos, query_seg, segment, scale)
        largest = jnp.max(scores, axis=-1, keepdims=True)
        expo = jnp.exp(scores - largest)
        total = jnp.sum(expo, axis=-1, keepdims=True)
        probs = (expo / total).astype(jnp.bfloat16)
        mixed = jnp.einsum("hqk,khd->qhd", probs, values_all, preferred_element_type=jnp.float32)
        return (mixed.astype(jnp.bfloat16), (largest + jnp.log(total))[..., 0])

    blocks = (
        queries.reshape(count_blocks, block, head_count, head_dim),
        positions.reshape(count_blocks, block),
        segment.reshape(count_blocks, block),
    )
    mixed_all, log_totals = lax.map(one_block, blocks)
    return (mixed_all.reshape(length, head_count * head_dim), log_totals)


def attend_backward(queries, keys_all, values_all, segment, scale, grad_mixed, log_totals):
    length, head_count, head_dim = queries.shape
    block, count_blocks = split_blocks(length)
    positions = jnp.arange(length)

    def one_block(carry, inputs):
        grad_keys, grad_values = carry
        query_block, query_pos, query_seg, grad_block, log_block = inputs
        scores = masked_scores(query_block, keys_all, query_pos, query_seg, segment, scale)
        probs = jnp.exp(scores - log_block[:, :, None])
        grad_probs = jnp.einsum(
            "qhd,khd->hqk", grad_block, values_all, preferred_element_type=jnp.float32
        )
        inner = jnp.sum(probs * grad_probs, axis=-1, keepdims=True)
        grad_scores = (probs * (grad_probs - inner)).astype(jnp.bfloat16)
        grad_query = (
            jnp.einsum("hqk,khd->qhd", grad_scores, keys_all, preferred_element_type=jnp.float32)
            * scale
        )
        grad_keys = (
            grad_keys
            + jnp.einsum(
                "hqk,qhd->khd", grad_scores, query_block, preferred_element_type=jnp.float32
            )
            * scale
        )
        grad_values = grad_values + jnp.einsum(
            "hqk,qhd->khd",
            probs.astype(jnp.bfloat16),
            grad_block,
            preferred_element_type=jnp.float32,
        )
        return ((grad_keys, grad_values), grad_query)

    zeros_kv = jnp.zeros((length, head_count, head_dim), jnp.float32)
    blocks = (
        queries.reshape(count_blocks, block, head_count, head_dim),
        positions.reshape(count_blocks, block),
        segment.reshape(count_blocks, block),
        grad_mixed.reshape(count_blocks, block, head_count, head_dim),
        log_totals,
    )
    (grad_keys, grad_values), grad_queries = lax.scan(one_block, (zeros_kv, zeros_kv), blocks)
    return (grad_queries.reshape(length, head_count, head_dim), grad_keys, grad_values)


def sum_rows(grad, axis, scatter_dimension, tiled):
    part = lax.psum_scatter(
        grad.astype(jnp.bfloat16), axis, scatter_dimension=scatter_dimension, tiled=tiled
    )
    return part.astype(jnp.float32)


def local_plain(
    tokens,
    segment_ids,
    expert_ids,
    slot_order,
    gain_attn,
    qkv_weight,
    out_weight,
    gain_ffn,
    router_weight,
    gate_up,
    down_weight,
    shared_gate_up,
    shared_down,
    cotangent,
):
    g_one, w_qkv, w_out, g_two, w_router, w_gate_up, w_down, s_gate_up, s_down = (
        lax.all_gather(gain_attn, "dp", axis=0, tiled=True),
        lax.all_gather(qkv_weight, "dp", axis=0, tiled=True),
        lax.all_gather(out_weight, "dp", axis=1, tiled=True),
        lax.all_gather(gain_ffn, "dp", axis=0, tiled=True),
        lax.all_gather(router_weight, "dp", axis=0, tiled=True),
        lax.all_gather(gate_up, "dp", axis=1, tiled=True),
        lax.all_gather(down_weight, "dp", axis=2, tiled=True),
        lax.all_gather(shared_gate_up, "dp", axis=0, tiled=True),
        lax.all_gather(shared_down, "dp", axis=1, tiled=True),
    )
    length = tokens.shape[0]
    width = tokens.shape[1]
    experts_count = w_router.shape[1]
    top_count = expert_ids.shape[1]
    capacity = length * top_count // experts_count
    head_dim = HD
    local_heads = w_qkv.shape[2] // head_dim
    scale = head_dim ** (-0.5)
    segment = segment_ids[0]
    slot_token, slot_index, kept_pair = route_slots(
        expert_ids, slot_order[0], capacity, experts_count
    )
    kept_float = kept_pair.astype(jnp.float32)
    slot_valid = slot_token < length
    slot_rows = jnp.minimum(slot_token, length - 1)
    pair_slots = jnp.minimum(slot_index, experts_count * capacity - 1)
    xfull = tokens.astype(jnp.float32)
    rms_one = rms_scale(xfull)
    xn_one = (xfull * rms_one * g_one.astype(jnp.float32)).astype(jnp.bfloat16)
    projected = jnp.einsum("td,dch->tch", xn_one, w_qkv, preferred_element_type=jnp.float32)
    cosine, sine = rotary(length, head_dim)
    queries = rotate(projected[:, 0].reshape(length, local_heads, head_dim), cosine, sine).astype(
        jnp.bfloat16
    )
    keys_all = rotate(projected[:, 1].reshape(length, local_heads, head_dim), cosine, sine).astype(
        jnp.bfloat16
    )
    values_all = projected[:, 2].reshape(length, local_heads, head_dim).astype(jnp.bfloat16)
    mixed, log_totals = attend_forward(queries, keys_all, values_all, segment, scale)
    attn_share = lax.psum_scatter(
        jnp.dot(mixed, w_out, preferred_element_type=jnp.float32),
        "tensor",
        scatter_dimension=1,
        tiled=True,
    )
    attn = lax.all_gather(attn_share, "tensor", axis=1, tiled=True)
    hidden_state = xfull + attn
    rms_two = rms_scale(hidden_state)
    xn_two = (hidden_state * rms_two * g_two.astype(jnp.float32)).astype(jnp.bfloat16)
    logits = jnp.dot(xn_two, w_router, preferred_element_type=jnp.float32)
    probs = jax.nn.softmax(logits, axis=-1)
    gates = jnp.take_along_axis(probs, expert_ids, axis=1) * kept_float
    dispatched = (xn_two[slot_rows] * slot_valid[:, None].astype(jnp.bfloat16)).reshape(
        experts_count, capacity, width
    )
    both_parts = jnp.einsum(
        "ecd,edjf->ecjf", dispatched, w_gate_up, preferred_element_type=jnp.float32
    )
    expert_hidden = silu_forward(both_parts)
    expert_out = jnp.einsum(
        "ecf,efd->ecd", expert_hidden, w_down, preferred_element_type=jnp.float32
    ).reshape(experts_count * capacity, width)
    picked = expert_out[pair_slots]
    moe = jnp.sum(gates[:, :, None] * picked, axis=1)
    shared_both = jnp.einsum("td,djf->tjf", xn_two, s_gate_up, preferred_element_type=jnp.float32)
    shared_hidden = silu_forward(shared_both)
    shared_out = jnp.dot(shared_hidden, s_down, preferred_element_type=jnp.float32)
    ffn_share = lax.psum_scatter(
        (moe + shared_out).astype(jnp.bfloat16), "tensor", scatter_dimension=1, tiled=True
    ).astype(jnp.float32)
    ffn = lax.all_gather(ffn_share.astype(jnp.bfloat16), "tensor", axis=1, tiled=True).astype(
        ffn_share.dtype
    )
    output = (hidden_state + ffn).astype(jnp.bfloat16)
    grad_y = cotangent.astype(jnp.float32)
    grad_shared_hidden = jnp.einsum(
        "td,fd->tf", cotangent, s_down, preferred_element_type=jnp.float32
    )
    grad_s_down = jnp.einsum(
        "tf,td->fd", shared_hidden, cotangent, preferred_element_type=jnp.float32
    )
    grad_shared_both = silu_back(shared_both, grad_shared_hidden)
    grad_s_gate_up = jnp.einsum(
        "td,tjf->djf", xn_two, grad_shared_both, preferred_element_type=jnp.float32
    )
    grad_xn_shared = jnp.einsum(
        "tjf,djf->td", grad_shared_both, s_gate_up, preferred_element_type=jnp.float32
    )
    slot_gate = (
        jnp.zeros((experts_count * capacity,), jnp.float32)
        .at[slot_index.reshape(-1)]
        .set(gates.reshape(-1), mode="drop")
    )
    grad_expert_out = (
        (slot_gate[:, None] * grad_y[slot_rows])
        .astype(jnp.bfloat16)
        .reshape(experts_count, capacity, width)
    )
    grad_gates_part = kept_float * jnp.sum(grad_y[:, None, :] * picked, axis=-1)
    grad_expert_hidden = jnp.einsum(
        "ecd,efd->ecf", grad_expert_out, w_down, preferred_element_type=jnp.float32
    )
    grad_w_down = jnp.einsum(
        "ecf,ecd->efd", expert_hidden, grad_expert_out, preferred_element_type=jnp.float32
    )
    grad_both = silu_back(both_parts, grad_expert_hidden)
    grad_w_gate_up = jnp.einsum(
        "ecd,ecjf->edjf", dispatched, grad_both, preferred_element_type=jnp.float32
    )
    grad_dispatched = jnp.einsum(
        "ecjf,edjf->ecd", grad_both, w_gate_up, preferred_element_type=jnp.float32
    ).reshape(experts_count * capacity, width)
    grad_xn_moe = jnp.sum(kept_float[:, :, None] * grad_dispatched[pair_slots], axis=1)
    grad_xn_part, grad_gates_share = (
        lax.psum_scatter(grad_xn_shared + grad_xn_moe, "tensor", scatter_dimension=1, tiled=True),
        lax.psum_scatter(grad_gates_part, "tensor", scatter_dimension=1, tiled=True),
    )
    grad_xn_sum, grad_gates = (
        lax.all_gather(grad_xn_part, "tensor", axis=1, tiled=True),
        lax.all_gather(grad_gates_share, "tensor", axis=1, tiled=True),
    )
    expert_match = (
        expert_ids[:, :, None] == jnp.arange(experts_count, dtype=jnp.int32)[None, None, :]
    ).astype(jnp.float32)
    grad_probs = jnp.sum(expert_match * grad_gates[:, :, None], axis=1)
    grad_logits = (
        probs * (grad_probs - jnp.sum(probs * grad_probs, axis=-1, keepdims=True))
    ).astype(jnp.bfloat16)
    grad_w_router = jnp.einsum("td,te->de", xn_two, grad_logits, preferred_element_type=jnp.float32)
    grad_xn_two = grad_xn_sum + jnp.einsum(
        "te,de->td", grad_logits, w_router, preferred_element_type=jnp.float32
    )
    grad_norm_two, grad_g_two = norm_back(
        grad_xn_two, hidden_state, rms_two, g_two.astype(jnp.float32)
    )
    grad_hidden = grad_y + grad_norm_two
    grad_attn = grad_hidden.astype(jnp.bfloat16)
    grad_w_out = jnp.einsum("th,td->hd", mixed, grad_attn, preferred_element_type=jnp.float32)
    grad_mixed = jnp.einsum(
        "td,hd->th", grad_attn, w_out, preferred_element_type=jnp.float32
    ).astype(jnp.bfloat16)
    grad_queries, grad_keys, grad_values = attend_backward(
        queries, keys_all, values_all, segment, scale, grad_mixed, log_totals
    )
    grad_projected = (
        jnp.stack(
            [rotate(grad_queries, cosine, -sine), rotate(grad_keys, cosine, -sine), grad_values],
            axis=1,
        )
        .astype(jnp.bfloat16)
        .reshape(length, 3, local_heads * head_dim)
    )
    grad_w_qkv = jnp.einsum(
        "td,tch->dch", xn_one, grad_projected, preferred_element_type=jnp.float32
    )
    grad_xn_share = lax.psum_scatter(
        jnp.einsum("tch,dch->td", grad_projected, w_qkv, preferred_element_type=jnp.float32).astype(
            jnp.bfloat16
        ),
        "tensor",
        scatter_dimension=1,
        tiled=True,
    ).astype(jnp.float32)
    grad_xn_one = lax.all_gather(
        grad_xn_share.astype(jnp.bfloat16), "tensor", axis=1, tiled=True
    ).astype(grad_xn_share.dtype)
    grad_norm_one, grad_g_one = norm_back(grad_xn_one, xfull, rms_one, g_one.astype(jnp.float32))
    grad_tokens = grad_hidden + grad_norm_one
    (
        grad_g_one,
        grad_w_qkv,
        grad_w_out,
        grad_g_two,
        grad_w_router,
        grad_w_gate_up,
        grad_w_down,
        grad_s_gate_up,
        grad_s_down,
    ) = (
        lax.psum_scatter(grad_g_one, "dp", scatter_dimension=0, tiled=True),
        sum_rows(grad_w_qkv, "dp", scatter_dimension=0, tiled=True),
        sum_rows(grad_w_out, "dp", scatter_dimension=1, tiled=True),
        lax.psum_scatter(grad_g_two, "dp", scatter_dimension=0, tiled=True),
        lax.psum_scatter(grad_w_router, "dp", scatter_dimension=0, tiled=True),
        sum_rows(grad_w_gate_up, "dp", scatter_dimension=1, tiled=True),
        sum_rows(grad_w_down, "dp", scatter_dimension=2, tiled=True),
        sum_rows(grad_s_gate_up, "dp", scatter_dimension=0, tiled=True),
        sum_rows(grad_s_down, "dp", scatter_dimension=1, tiled=True),
    )
    return (
        output,
        grad_tokens,
        grad_g_one,
        grad_w_qkv,
        grad_w_out,
        grad_g_two,
        grad_w_router,
        grad_w_gate_up,
        grad_w_down,
        grad_s_gate_up,
        grad_s_down,
    )


class Place:
    def __init__(self, planes):
        d = lax.axis_index("dp")
        self.planes = planes
        self.d, self.c = d, lax.axis_index("tensor")
        self.z, self.p = d // GROUP, lax.rem(d, GROUP)
        bit0, bit1 = lax.rem(self.p, 2), self.p // 2
        flip0, flip1 = 1 - bit0, 1 - bit1
        self.member = [
            self.p,
            flip0 + 2 * bit1,
            bit0 + 2 * flip1,
            flip0 + 2 * flip1,
        ]

    def near(self, j):
        return (self.z * GROUP + self.member[j], self.c)

    def up(self):
        return (self.d + GROUP, self.c)

    def down(self):
        return (self.d - GROUP, self.c)

    def twin(self):
        return (self.d, 1 - self.c)

    def when(self, condition, action):
        pl.when(condition)(action)

    def has_up(self, k=1):
        return self.z + k < self.planes

    def has_down(self, k=1):
        return self.z - k >= 0

    def greet(self):
        barrier = pltpu.get_barrier_semaphore()

        def hello(device):
            pl.semaphore_signal(barrier, inc=1, device_id=device, device_id_type=MESH)

        hello(self.twin())
        for j in range(1, GROUP):
            hello(self.near(j))
        self.when(self.has_up(), lambda: hello(self.up()))
        self.when(self.has_down(), lambda: hello(self.down()))
        line = self.has_up().astype(jnp.int32) + self.has_down().astype(jnp.int32)
        pl.semaphore_wait(barrier, GROUP + line)


def send(source, target, send_sem, recv_sem, device):
    return pltpu.make_async_remote_copy(
        src_ref=source,
        dst_ref=target,
        send_sem=send_sem,
        recv_sem=recv_sem,
        device_id=device,
        device_id_type=MESH,
    )


class Everywhere:
    def __init__(self, at, own, all_blocks, local_sem, recvs, sends):
        self.at, self.own, self.all = at, own, all_blocks
        self.local_sem, self.recvs, self.sends = local_sem, recvs, sends

    def copy(self, block, source, way, device):
        return send(source, self.all.at[block], self.sends.at[way, block], self.recvs.at[block], device)

    def keep(self):
        return pltpu.make_async_copy(self.own, self.all.at[self.at.d], self.local_sem)

    def landed(self, block):
        self.copy(block, self.own, 0, self.at.near(1)).wait_recv()

    def start_line(self):
        at = self.at
        at.when(at.has_up(), lambda: self.copy(at.d, self.own, 0, at.up()).start())
        at.when(at.has_down(), lambda: self.copy(at.d, self.own, 1, at.down()).start())

    def start_plane(self):
        at = self.at
        self.copy(at.d, self.own, 2, at.near(1)).start()
        self.copy(at.d, self.own, 3, at.near(2)).start()
        self.keep().start()

    def pass_on(self, k):
        at = self.at

        def go(plane, more, way, device_of):
            block = plane * GROUP + at.p
            self.landed(block)
            at.when(more, lambda: self.copy(block, self.all.at[block], way, device_of()).start())

        at.when(at.has_down(k), lambda: go(at.z - k, at.has_up(), 0, at.up))
        at.when(at.has_up(k), lambda: go(at.z + k, at.has_down(), 1, at.down))

    def over_plane(self, k):
        at = self.at

        def go(plane):
            block = plane * GROUP + at.p
            self.copy(block, self.all.at[block], 2, at.near(1)).start()
            self.copy(block, self.all.at[block], 3, at.near(2)).start()

        at.when(at.has_down(k), lambda: go(at.z - k))
        at.when(at.has_up(k), lambda: go(at.z + k))

    def spread(self, k):
        self.pass_on(k)
        self.over_plane(k)

    def cross(self, k):
        at = self.at

        def go(plane):
            first = plane * GROUP + at.member[1]
            second = plane * GROUP + at.member[2]
            even = lax.rem(plane, 2) == 0
            self.landed(first)
            at.when(even, lambda: self.copy(first, self.all.at[first], 3, at.near(2)).start())
            self.landed(second)
            at.when(
                jnp.logical_not(even),
                lambda: self.copy(second, self.all.at[second], 2, at.near(1)).start(),
            )

        if k == 0:
            go(at.z)
        else:
            at.when(at.has_down(k), lambda: go(at.z - k))
            at.when(at.has_up(k), lambda: go(at.z + k))

    def diagonal(self):
        for plane in range(self.at.planes):
            self.landed(plane * GROUP + self.at.member[3])
        self.keep().wait()

    def sent(self):
        at = self.at
        for plane in range(at.planes):
            block = plane * GROUP + at.p
            self.copy(block, self.own, 2, at.near(1)).wait_send()
            self.copy(block, self.own, 3, at.near(2)).wait_send()
            if plane % 2 == 0:
                self.copy(plane * GROUP + at.member[1], self.own, 3, at.near(2)).wait_send()
            else:
                self.copy(plane * GROUP + at.member[2], self.own, 2, at.near(1)).wait_send()

            def gone(way, device_of):
                self.copy(block, self.own, way, device_of()).wait_send()

            at.when((at.z >= plane) & at.has_up(), lambda: gone(0, at.up))
            at.when((at.z <= plane) & at.has_down(), lambda: gone(1, at.down))


class Experts:
    def __init__(self, at, own, all_blocks, local_sem, recvs, sends, across_sends):
        self.at, self.own, self.all = at, own, all_blocks
        self.local_sem, self.recvs, self.sends = local_sem, recvs, sends
        self.across_sends = across_sends

    def line(self, block, source, way, device):
        return send(source, self.all.at[block], self.sends.at[way, block], self.recvs.at[block], device)

    def across(self, j):
        at = self.at
        return send(
            self.own.at[at.member[j]],
            self.all.at[at.d],
            self.across_sends.at[j],
            self.recvs.at[at.d],
            at.near(j),
        )

    def keep(self):
        return pltpu.make_async_copy(self.own.at[self.at.p], self.all.at[self.at.d], self.local_sem)

    def start_plane(self):
        for j in range(1, GROUP):
            self.across(j).start()
        self.keep().start()

    def start_line(self):
        at = self.at
        source = self.own.at[at.p]
        at.when(at.has_up(), lambda: self.line(at.d, source, 0, at.up()).start())
        at.when(at.has_down(), lambda: self.line(at.d, source, 1, at.down()).start())

    def landed(self, block):
        self.line(block, self.own.at[0], 0, self.at.near(1)).wait_recv()

    def plane_step(self, j):
        at = self.at
        block = at.z * GROUP + at.member[j]
        source = self.all.at[block]
        self.landed(block)
        at.when(at.has_up(), lambda: self.line(block, source, 0, at.up()).start())
        at.when(at.has_down(), lambda: self.line(block, source, 1, at.down()).start())

    def line_step(self, k, j):
        at = self.at

        def go(plane, more, way, device_of):
            block = plane * GROUP + at.member[j]
            self.landed(block)
            at.when(more, lambda: self.line(block, self.all.at[block], way, device_of()).start())

        at.when(at.has_down(k), lambda: go(at.z - k, at.has_up(), 0, at.up))
        at.when(at.has_up(k), lambda: go(at.z + k, at.has_down(), 1, at.down))

    def ready(self):
        self.keep().wait()

    def own_sent(self):
        at = self.at
        source = self.own.at[at.p]
        for j in range(1, GROUP):
            self.across(j).wait_send()
        at.when(at.has_up(), lambda: self.line(at.d, source, 0, at.up()).wait_send())
        at.when(at.has_down(), lambda: self.line(at.d, source, 1, at.down()).wait_send())

    def rest_sent(self):
        at = self.at
        for plane in range(at.planes):

            def gone(j, way, device_of):
                block = plane * GROUP + at.member[j]
                self.line(block, self.own.at[0], way, device_of()).wait_send()

            for j in range(GROUP):
                up = at.z >= plane if j else at.z > plane
                down = at.z <= plane if j else at.z < plane
                at.when(up & at.has_up(), lambda: gone(j, 0, at.up))
                at.when(down & at.has_down(), lambda: gone(j, 1, at.down))


def dot_nn(a, b):
    return jnp.dot(a, b, preferred_element_type=jnp.float32)


def dot_nt(a, b):
    return lax.dot_general(a, b, (((1,), (1,)), ((), ())), preferred_element_type=jnp.float32)


def dot_tn(a, b):
    return lax.dot_general(a, b, (((0,), (0,)), ((), ())), preferred_element_type=jnp.float32)


def lanes(count=128):
    return lax.broadcasted_iota(jnp.int32, (1, count), 1)


def turn(values, cosine, sine):
    half = HD // 2
    other = jnp.where(
        lax.rem(lanes(), HD) < half,
        -pltpu.roll(values, 2 * HD - half, 1),
        pltpu.roll(values, half, 1),
    )
    return values * cosine + other * sine


def blocks_of(ref, start, stop):
    block = ref[:, :, start:stop]
    return block.reshape(block.shape[0] * block.shape[1], stop - start)


def attention_blocks(length):
    size = length // 2
    return [(i * size, (i + 1) * size) for i in range(2)]


class PlaneSum:
    def __init__(self, at, own, one, two, came, one_sems, two_sems, line_sems):
        self.at, self.own, self.one, self.two, self.came = at, own, one, two, came
        self.one_sems, self.two_sems, self.line_sems = one_sems, two_sems, line_sems

    def one_copy(self, plane, i, even):
        at = self.at
        j = 1 if even else 2
        target = at.member[3] if i else at.member[j]
        return send(
            self.own.at[plane * GROUP + target],
            self.one.at[plane, i],
            self.one_sems.at[0, plane, i],
            self.one_sems.at[1, plane, i],
            at.near(j),
        )

    def two_copy(self, plane, even):
        return send(
            self.one.at[plane, 1],
            self.two.at[plane],
            self.two_sems.at[0, plane],
            self.two_sems.at[1, plane],
            self.at.near(2 if even else 1),
        )

    def by_parity(self, plane, action):
        even = lax.rem(plane, 2) == 0
        self.at.when(even, lambda: action(True))
        self.at.when(jnp.logical_not(even), lambda: action(False))

    def line(self, source, plane, way, here=False):
        at, sems = self.at, self.line_sems
        slot, device = plane, at.up()
        if way:
            slot = jnp.where(plane == (at.z if here else at.z - 1), at.planes, plane)
            device = at.down()
        return send(
            source, self.came.at[slot], sems.at[0, way, plane], sems.at[1, way, plane], device
        )

    def both_ways(self, action, k):
        at = self.at
        if k == 0:
            action(at.z, 0)
            return
        at.when(at.has_up(k), lambda: action(at.z + k, 0))
        at.when(at.has_down(k), lambda: action(at.z - k, 1))

    def start(self, k):
        def go(plane, way):
            def pair(even):
                self.one_copy(plane, 1, even).start()
                self.one_copy(plane, 0, even).start()

            self.by_parity(plane, pair)

        self.both_ways(go, k)

    def middle(self, k):
        f32 = jnp.float32

        def go(plane, way):
            def stage(even):
                at, one = self.at, self.one
                other = plane * GROUP + (at.member[2] if even else at.member[1])
                self.one_copy(plane, 1, even).wait_recv()
                one[plane, 1] = (one[plane, 1].astype(f32) + self.own[other].astype(f32)).astype(
                    one.dtype
                )
                self.two_copy(plane, even).start()

            self.by_parity(plane, stage)

        self.both_ways(go, k)

    def finish_plane(self, plane):
        f32 = jnp.float32

        def stage(even):
            mine = plane * GROUP + self.at.p
            self.one_copy(plane, 0, even).wait_recv()
            self.two_copy(plane, even).wait_recv()
            self.two[plane] = (
                self.two[plane].astype(f32)
                + self.one[plane, 0].astype(f32)
                + self.own[mine].astype(f32)
            ).astype(self.two.dtype)

        self.by_parity(plane, stage)

    def step(self, k):
        f32 = jnp.float32

        def go(plane, way):
            at = self.at
            self.finish_plane(plane)
            behind = at.has_down() if way == 0 else at.has_up()
            held = self.came

            def add():
                self.line(self.two.at[plane], plane, way, True).wait_recv()
                held[plane] = (held[plane].astype(f32) + self.two[plane].astype(f32)).astype(
                    held.dtype
                )
                self.line(held.at[plane], plane, way).start()

            at.when(behind, add)
            at.when(
                jnp.logical_not(behind), lambda: self.line(self.two.at[plane], plane, way).start()
            )

        self.both_ways(go, k)

    def total(self):
        at, f32 = self.at, jnp.float32
        z = at.z
        self.finish_plane(z)
        at.when(at.has_down(), lambda: self.line(self.two.at[z], z, 0, True).wait_recv())
        at.when(at.has_up(), lambda: self.line(self.two.at[z], z, 1, True).wait_recv())
        low = jnp.where(at.has_down(), self.came[z].astype(f32), 0.0)
        high = jnp.where(at.has_up(), self.came[at.planes].astype(f32), 0.0)
        return self.two[z].astype(f32) + low + high

    def sent(self):
        at = self.at
        for plane in range(at.planes):
            even = plane % 2 == 0
            self.one_copy(plane, 0, even).wait_send()
            self.one_copy(plane, 1, even).wait_send()
            self.two_copy(plane, even).wait_send()
            at.when(at.z < plane, lambda: self.line(self.two.at[plane], plane, 0).wait_send())
            at.when(at.z > plane, lambda: self.line(self.two.at[plane], plane, 1).wait_send())


class LineSum:
    def __init__(self, at, own, came, out, columns, line_sems, last_sems):
        self.at, self.own, self.came, self.out = at, own, came, out
        self.line_sems, self.last_sems = line_sems, last_sems
        self.columns, self.size = columns, columns[0].stop - columns[0].start

    def hop(self, source, plane, j, way, here=False):
        at = self.at
        block = plane * GROUP + at.member[j]
        if way == 0:
            slot, device = block, at.up()
        else:
            end = at.z if here else at.z - 1
            slot = jnp.where(plane == end, at.planes, plane) * GROUP + at.member[j]
            device = at.down()
        sems = self.line_sems
        return send(
            source, self.came.at[slot], sems.at[0, way, block], sems.at[1, way, block], device
        )

    def start_plane(self, plane):
        at = self.at

        def go(way):
            for j in range(GROUP):
                self.hop(self.own.at[plane * GROUP + at.member[j]], plane, j, way).start()

        at.when(jnp.logical_not(at.has_down()) & (plane != at.z), lambda: go(0))
        at.when(jnp.logical_not(at.has_up()) & (plane != at.z), lambda: go(1))

    def step(self, k, j):
        at, f32 = self.at, jnp.float32

        def go(plane, way):
            block = plane * GROUP + at.member[j]
            self.hop(self.own.at[block], plane, j, way, True).wait_recv()
            self.came[block] = (
                self.came[block].astype(f32) + self.own[block].astype(f32)
            ).astype(self.came.dtype)
            self.hop(self.came.at[block], plane, j, way).start()

        at.when(at.has_up(k) & at.has_down(), lambda: go(at.z + k, 0))
        at.when(at.has_down(k) & at.has_up(), lambda: go(at.z - k, 1))

    def parts(self, j, here=False):
        at, size = self.at, self.size
        source = self.came.at[at.z * GROUP + at.member[j]]
        target = self.out.at[at.member[j] if here else at.p]
        return [
            send(
                source.at[:, i * size : (i + 1) * size],
                target.at[:, self.columns[i]],
                self.last_sems.at[0, j, i],
                self.last_sems.at[1, j, i],
                at.near(j),
            )
            for i in range(len(self.columns))
        ]

    def total(self, j):
        at, f32, out = self.at, jnp.float32, self.out
        block = at.z * GROUP + at.member[j]
        spare = at.planes * GROUP + at.member[j]
        at.when(at.has_down(), lambda: self.hop(self.own.at[block], at.z, j, 0, True).wait_recv())
        at.when(at.has_up(), lambda: self.hop(self.own.at[block], at.z, j, 1, True).wait_recv())
        low = jnp.where(at.has_down(), self.came[block].astype(f32), 0.0)
        high = jnp.where(at.has_up(), self.came[spare].astype(f32), 0.0)
        total = (self.own[block].astype(f32) + low + high).astype(out.dtype)
        if j == 0:
            for i, columns in enumerate(self.columns):
                out[at.p, :, columns] = total[:, i * self.size : (i + 1) * self.size]
        else:
            self.came[block] = total
            for copy in self.parts(j):
                copy.start()

    def arrive(self, j):
        for copy in self.parts(j, True):
            copy.wait_recv()

    def sent(self):
        at = self.at
        for j in range(1, GROUP):
            for copy in self.parts(j):
                copy.wait_send()
        for plane in range(at.planes):

            def gone(way):
                for j in range(GROUP):
                    self.hop(self.own.at[0], plane, j, way).wait_send()

            at.when(at.z < plane, lambda: gone(0))
            at.when(at.z > plane, lambda: gone(1))


def norm_back_rows(grad, values, gain):
    rms = lax.rsqrt(jnp.mean(values * values, axis=-1, keepdims=True) + epsilon)
    grad_gain = jnp.sum(grad * values * rms, axis=0, keepdims=True)
    inner = grad * gain
    grad_values = rms * inner - values * (rms * rms * rms) * jnp.mean(
        inner * values, axis=-1, keepdims=True
    )
    return grad_values, grad_gain


def branch(x_of, dy_of, rows, weights, start, stride, hidden, act, y_acc, dx_acc):
    f32, bf16 = jnp.float32, jnp.bfloat16
    size, count = 256, rows.stop - rows.start
    step = min(count, 256)

    def body(i, carry):
        offset = pl.multiple_of(i * size, size)

        def weight(part):
            first = pl.multiple_of(start + part * stride + offset, size)
            block = weights[:, :, pl.ds(first, size)]
            return block.reshape(block.shape[0] * block.shape[1], size)

        for first in range(0, count, step):
            some = slice(first, first + step)

            def keep(part, values):
                columns = pl.ds(pl.multiple_of(part * hidden + offset, size), size)
                act[rows.start + first : rows.start + first + step, columns] = values

            g, u = dot_nn(x_of(some), weight(0)), dot_nn(x_of(some), weight(1))
            grad = dot_nn(dy_of(some), weight(2))
            sigma = 1.0 / (1.0 + jnp.exp(-g))
            silu = g * sigma
            eh = (silu * u).astype(bf16)
            dg = (grad * u * (sigma * (1.0 + g * (1.0 - sigma)))).astype(bf16)
            du = (grad * silu).astype(bf16)
            keep(0, dg)
            keep(1, du)
            keep(2, eh)
            y_acc[some, :] += dot_nt(eh, weight(2))
            dx_acc[some, :] += dot_nt(dg, weight(0)) + dot_nt(du, weight(1))
        return carry

    lax.fori_loop(0, hidden // size, body, 0)


def weight_grads(plane, planes, count, x_t, dy_t, act, hidden, grads, start, stride):
    width, bf16 = x_t.shape[0], jnp.bfloat16
    rows = width // planes
    features = pl.ds(pl.multiple_of(plane * rows, 16), rows)
    for part in range(3):
        columns = slice(part * hidden, (part + 1) * hidden)
        left = dy_t if part == 2 else x_t
        block = dot_nn(left[features, :count], act[:count, columns]).astype(bf16)
        target = slice(start + part * stride, start + part * stride + hidden)
        grads[pl.ds(plane * GROUP, GROUP), :, target] = block.reshape(
            GROUP, rows // GROUP, hidden
        )


PROBS, PAIRS, LOGS = 2, 8, 16


(
    E_PLANE,
    E_ACROSS,
    E_OWN,
    E_LINE,
    S_OWN,
    S_PLANE,
    S_LINE,
    S_OVER,
    S_CROSS,
    S_START,
    S_MIDDLE,
    S_STEP,
    E_STEP,
    E_TOTAL,
    A_START,
    A_MIDDLE,
    A_STEP,
) = range(17)
(
    ARRIVED,
    ATTENDED,
    ATTENTION,
    BACKWARD,
    BEGIN,
    COMBINED,
    DISPATCHED,
    EXPERT,
    GATHER,
    GATHERED,
    HOME,
    LAST,
    PROJECTED,
    PROJECTED_BACK,
    PROJECTED_OUT,
    SHARED,
) = range(16)
LINE = 4
PLAN = {
    (BEGIN,): [
        (E_OWN, 0),
        (S_OWN,),
    ],
    (GATHER, 1): [
        (S_PLANE,),
    ],
    (GATHER, 2): [
        (S_LINE, 1),
        (E_LINE, 0, 1, 0),
    ],
    (GATHER, 3): [
        (E_ACROSS, 1),
        (E_PLANE, 0, 1),
        (S_LINE, 2),
        (E_PLANE, 0, 2),
        (E_PLANE, 0, 3),
    ],
    (GATHERED,): [
        (S_OVER, 2),
        (E_LINE, 0, 2, 0),
        (S_LINE, 3),
        (S_OVER, 1),
        (S_OVER, 3),
        (E_OWN, 1),
    ],
    (PROJECTED,): [],
    (ATTENTION, 0, 0): [
        (E_LINE, 0, 1, 2),
    ],
    (ATTENTION, 0, 1): [],
    (ATTENTION, 0, 2): [
        (E_LINE, 0, 1, 3),
    ],
    (ATTENTION, 1, 0): [
        (S_CROSS, 2),
    ],
    (ATTENTION, 1, 1): [
        (S_CROSS, 1),
    ],
    (ATTENTION, 1, 2): [
        (E_LINE, 0, 1, 1),
    ],
    (ATTENDED,): [
        (E_LINE, 0, 2, 2),
        (E_PLANE, 1, 1),
        (E_PLANE, 1, 2),
        (E_PLANE, 1, 3),
        (E_LINE, 1, 1, 0),
        (S_CROSS, 3),
        (S_CROSS, 0),
    ],
    (DISPATCHED,): [
        (E_LINE, 0, 2, 3),
        (E_LINE, 0, 3, 2),
    ],
    (SHARED, 0): [
        (E_LINE, 0, 2, 1),
        (E_LINE, 1, 1, 2),
        (E_LINE, 1, 1, 3),
        (E_LINE, 1, 1, 1),
        (E_LINE, 0, 3, 0),
    ],
    (SHARED, 1): [],
    (SHARED,): [
        (S_START, 2),
        (S_START, 1),
    ],
    (ARRIVED,): [
        (E_LINE, 0, 3, 1),
        (E_LINE, 0, 3, 3),
        (E_LINE, 1, 2, 0),
        (E_LINE, 1, 2, 1),
        (E_LINE, 1, 2, 2),
        (E_LINE, 1, 2, 3),
        (S_START, 3),
    ],
    (EXPERT, 0, 1): [],
    (EXPERT, 0, 0): [],
    (EXPERT, 0): [
        (E_LINE, 1, 3, 0),
        (E_LINE, 1, 3, 1),
        (E_LINE, 1, 3, 2),
        (E_LINE, 1, 3, 3),
    ],
    (EXPERT, 1, 1): [
        (E_STEP, 0, 2, 0),
    ],
    (EXPERT, 1, 0): [
        (E_STEP, 0, 2, 3),
        (S_START, 0),
    ],
    (EXPERT, 1): [
        (E_STEP, 0, 2, 2),
        (E_STEP, 0, 2, 1),
        (E_STEP, 0, 1, 0),
        (E_STEP, 0, 1, 2),
        (E_STEP, 0, 1, 3),
    ],
    (HOME,): [
        (E_STEP, 0, 1, 1),
        (S_MIDDLE, 3),
        (S_MIDDLE, 0),
    ],
    (COMBINED,): [],
    (PROJECTED_OUT,): [
        (A_START, 0, 3),
        (A_START, 0, 2),
        (A_START, 0, 1),
        (A_START, 0, 0),
    ],
    (BACKWARD, 0, 1): [
        (E_TOTAL, 0, 1),
        (E_TOTAL, 0, 2),
        (E_TOTAL, 0, 3),
        (S_MIDDLE, 1),
        (E_TOTAL, 0, 0),
    ],
    (BACKWARD, 0, 0): [
        (E_STEP, 1, 2, 0),
        (E_STEP, 1, 2, 1),
        (E_STEP, 1, 2, 3),
        (S_STEP, 3),
    ],
    (BACKWARD, 1, 1): [],
    (BACKWARD, 1, 0): [
        (E_STEP, 1, 1, 0),
    ],
    (BACKWARD, 2, 1): [],
    (BACKWARD, 2, 0): [
        (S_MIDDLE, 2),
    ],
    (PROJECTED_BACK,): [
        (E_STEP, 1, 2, 2),
        (E_STEP, 1, 1, 2),
        (E_STEP, 1, 1, 1),
    ],
    (LAST,): [
        (A_START, 1, 3),
        (A_START, 1, 0),
        (A_START, 1, 1),
        (E_STEP, 1, 1, 3),
        (A_MIDDLE, 0, 3),
        (A_MIDDLE, 1, 3),
        (A_START, 1, 2),
        (A_MIDDLE, 0, 2),
        (A_MIDDLE, 1, 2),
        (A_STEP, 0, 3),
        (A_STEP, 1, 3),
        (A_MIDDLE, 0, 1),
        (A_MIDDLE, 1, 1),
        (S_STEP, 2),
        (E_TOTAL, 1, 0),
        (E_TOTAL, 1, 1),
        (E_TOTAL, 1, 2),
        (E_TOTAL, 1, 3),
        (A_STEP, 0, 2),
        (A_STEP, 1, 2),
        (A_MIDDLE, 0, 0),
        (A_MIDDLE, 1, 0),
        (S_STEP, 1),
        (A_STEP, 0, 1),
        (A_STEP, 1, 1),
    ],
}


def layer_kernel(
    planes,
    experts,
    top,
    heads_width,
    x_ref,
    cot_ref,
    facts,
    facts_t,
    waves,
    a_own,
    s_own,
    e_own,
    out_ref,
    gx_ref,
    out_t,
    qkv_out,
    small_out,
    s_out,
    e_out,
    aw,
    sw,
    ew,
    tok,
    part_one,
    home,
    act,
    x_t,
    dy_t,
    y_acc,
    dx_acc,
    s_dx,
    q_ref,
    k_ref,
    v_ref,
    o_ref,
    xf_ref,
    row_facts,
    ffn_theirs,
    dx_theirs,
    ret,
    a_one,
    a_two,
    a_came,
    s_one,
    s_two,
    s_came,
    e_came,
    local_sem,
    a_recv,
    a_send,
    s_recv,
    s_send,
    e_recv,
    e_send,
    e_across,
    a_one_sems,
    a_two_sems,
    a_line_sems,
    s_one_sems,
    s_two_sems,
    s_line_sems,
    e_line_sems,
    e_last_sems,
    token_sems,
    home_sems,
    share_sems,
    twin_sems,
):
    f32, bf16 = jnp.float32, jnp.bfloat16
    at = Place(planes)
    length, width = x_ref.shape
    capacity = length * top // experts
    half = capacity // 2
    count = experts * half
    hidden, s_hidden = ew.shape[3] // 3, sw.shape[2] // 6
    step = min(length, 256)
    chunks = [slice(i, i + step) for i in range(0, length, step)]
    seg_col, seg_row = facts[:, 2 * top : 2 * top + 1], facts_t[2 * top : 2 * top + 1, :]

    halves = [
        [slice((2 * k + i) * hidden, (2 * k + i + 1) * hidden) for k in range(3)] for i in range(2)
    ]

    attn_in = Everywhere(at, a_own, aw, local_sem.at[0], a_recv, a_send)
    shared_in = Everywhere(at, s_own, sw, local_sem.at[1], s_recv, s_send)
    expert_in = [
        Experts(
            at,
            part_one.at[i, :, : e_own.shape[1]],
            ew.at[i],
            local_sem.at[2 + i],
            e_recv.at[i],
            e_send.at[i],
            e_across.at[i],
        )
        for i in range(2)
    ]
    expert_out = [
        LineSum(
            at, ew.at[i], e_came.at[i], e_out, halves[i], e_line_sems.at[i], e_last_sems.at[i]
        )
        for i in range(2)
    ]
    shared_out = PlaneSum(at, sw, s_one, s_two, s_came, s_one_sems, s_two_sems, s_line_sems)
    attn_out = [
        PlaneSum(
            at,
            aw.at[:, :, columns],
            a_one.at[:, :, :, columns],
            a_two.at[:, :, columns],
            a_came.at[:, :, columns],
            a_one_sems.at[i],
            a_two_sems.at[i],
            a_line_sems.at[i],
        )
        for i, columns in enumerate((slice(0, heads_width), slice(heads_width, aw.shape[2])))
    ]

    xa_ref = act.at[:length, :width]
    placed = ret
    part_mine = act.at[length:, :width]
    part_theirs = ret.at[:length, :width]
    grad_o = act.at[:length, :heads_width]
    dproj = act.at[:length, heads_width : 4 * heads_width]
    bias = y_acc
    dk_acc, dv_acc = (dx_acc.at[:, 128 * i : 128 * (i + 1)] for i in range(2))

    def halve(i, k):
        return pltpu.make_async_copy(
            e_own.at[:, :, halves[i][k]],
            part_one.at[i, :, : e_own.shape[1], k * hidden : (k + 1) * hidden],
            local_sem.at[4 + 3 * i + k],
        )

    for i in range(2):
        for k in range(3):
            halve(i, k).start()
    at.greet()
    attn_in.start_line()
    attn_in.start_plane()
    for k in range(3):
        halve(0, k).wait()
    expert_in[0].start_plane()
    for k in range(3):
        halve(1, k).wait()

    def turn_of(*place):
        for step in PLAN[place]:
            do(*step)

    def do(kind, *numbers):
        steps[kind](*numbers)

    steps = {
        E_PLANE: lambda i, j: expert_in[i].plane_step(j),
        E_ACROSS: lambda i: expert_in[i].start_plane(),
        E_OWN: lambda i: expert_in[i].start_line(),
        E_LINE: lambda i, k, j: expert_in[i].line_step(k, j),
        S_OWN: lambda: shared_in.start_line(),
        S_PLANE: lambda: shared_in.start_plane(),
        S_LINE: lambda k: shared_in.pass_on(k),
        S_OVER: lambda k: shared_in.over_plane(k),
        S_CROSS: lambda k: shared_in.cross(k),
        S_START: lambda k: shared_out.start(k),
        S_MIDDLE: lambda k: shared_out.middle(k),
        S_STEP: lambda k: shared_out.step(k),
        E_STEP: lambda i, k, j: expert_out[i].step(k, j),
        E_TOTAL: lambda i, j: expert_out[i].total(j),
        A_START: lambda i, k: attn_out[i].start(k),
        A_MIDDLE: lambda i, k: attn_out[i].middle(k),
        A_STEP: lambda i, k: attn_out[i].step(k),
    }

    turn_of(BEGIN)

    def masks():
        for start, stop in attention_blocks(length):
            row = lax.broadcasted_iota(jnp.int32, (stop - start, stop), 0) + start
            column = lax.broadcasted_iota(jnp.int32, (stop - start, stop), 1)
            allowed = (column <= row) & (seg_col[start:stop, :] == seg_row[:, :stop])
            bias[start:stop, :stop] = jnp.where(allowed, 0.0, -1e30)

    masks()

    def slot_of(expert_id, position):
        which = position // half
        apart = which + at.c - 2 * which * at.c
        bit0, bit1 = lax.rem(expert_id, 2), expert_id // 2
        p0, p1 = lax.rem(at.p, 2), at.p // 2
        distance = (bit0 + p0 - 2 * bit0 * p0) + 2 * (bit1 + p1 - 2 * bit1 * p1)
        slot = apart * count + distance * half + lax.rem(position, half)
        return jnp.where(position < capacity, slot, -1)

    slot_cols, slot_rows = [], []
    for r in range(top):
        ids_col, order_col = facts[:, r : r + 1], facts[:, top + r : top + r + 1]
        ids_row, order_row = facts_t[r : r + 1, :], facts_t[top + r : top + r + 1, :]
        count_col = jnp.zeros((length, 1), jnp.int32)
        count_row = jnp.zeros((1, length), jnp.int32)
        for other in range(top):
            first = (facts_t[other : other + 1, :] == ids_col) & (
                facts_t[top + other : top + other + 1, :] < order_col
            )
            count_col += jnp.sum(first.astype(jnp.int32), axis=1, keepdims=True)
            first = (facts[:, other : other + 1] == ids_row) & (
                facts[:, top + other : top + other + 1] < order_row
            )
            count_row += jnp.sum(first.astype(jnp.int32), axis=0, keepdims=True)
        slot_cols.append(slot_of(ids_col, count_col))
        slot_rows.append(slot_of(ids_row, count_row))

    for k in range(1, planes):
        attn_in.spread(k)
        attn_in.cross(k - 1)
        turn_of(GATHER, k)
    attn_in.cross(planes - 1)
    turn_of(GATHERED)
    attn_in.diagonal()

    small = blocks_of(aw, 4 * heads_width, 4 * heads_width + 128)
    small_rows = small.astype(f32).T
    g_one, g_two = small_rows[0:1, :], small_rows[1:2, :]
    for rows in chunks:
        x = x_ref[rows, :].astype(f32)
        rms = lax.rsqrt(jnp.mean(x * x, axis=-1, keepdims=True) + epsilon)
        xa_ref[rows, :] = (x * rms * g_one).astype(bf16)
    wave, other = waves[...], pltpu.roll(waves[...], 64, 1)
    cosine = jnp.where(lanes() < 64, wave, other)
    sine = jnp.where(lanes() < 64, other, wave)
    pairs = heads_width // 128
    for i, ref in enumerate((q_ref, k_ref)):
        part = dot_nn(xa_ref[...], blocks_of(aw, (i + 1) * heads_width, (i + 2) * heads_width))
        for g in range(pairs):
            columns = slice(128 * g, 128 * (g + 1))
            ref[:, columns] = turn(part[:, columns], cosine, sine).astype(bf16)
    v_ref[...] = dot_nn(xa_ref[...], blocks_of(aw, 3 * heads_width, 4 * heads_width)).astype(bf16)
    turn_of(PROJECTED)

    scale = HD ** (-0.5)
    for start, stop in attention_blocks(length):
        logs = jnp.zeros((stop - start, 128), f32)
        for g in range(pairs):
            columns = slice(128 * g, 128 * (g + 1))
            queries = q_ref[start:stop, columns]
            keys, values = k_ref[:stop, columns], v_ref[:stop, columns]
            mixed = []
            for i in range(2):
                one = jnp.where(lanes() // HD == i, queries, jnp.zeros_like(queries))
                scores = dot_nt(one, keys) * scale + bias[start:stop, :stop]
                largest = jnp.max(scores, axis=-1, keepdims=True)
                expo = jnp.exp(scores - largest)
                total = jnp.sum(expo, axis=-1, keepdims=True)
                weights = (expo * (1.0 / total)).astype(bf16)
                mixed.append(dot_nn(weights, values))
                logs = jnp.where(lanes() == LOGS + 2 * g + i, largest + jnp.log(total), logs)
            o_ref[start:stop, columns] = jnp.where(lanes() < HD, mixed[0], mixed[1]).astype(bf16)
            turn_of(ATTENTION, start // (length // 2), g)
        row_facts[start:stop, :] = logs

    for rows in chunks:
        dx_acc[rows, :] = dot_nt(
            o_ref[rows, :], blocks_of(aw, 0, heads_width)
        )
    swap = send(dx_acc, gx_ref, twin_sems.at[0, 0], twin_sems.at[1, 0], at.twin())
    swap.start()
    turn_of(ATTENDED)
    swap.wait_recv()

    is_expert = (lanes() >= PROBS) & (lanes() < PROBS + experts)
    for rows in chunks:
        h = x_ref[rows, :].astype(f32) + (dx_acc[rows, :] + gx_ref[rows, :])
        gx_ref[rows, :] = h
        rms = lax.rsqrt(jnp.mean(h * h, axis=-1, keepdims=True) + epsilon)
        xf = (h * rms * g_two).astype(bf16)
        xf_ref[rows, :] = xf
        logits = jnp.where(is_expert, dot_nn(xf, small), -1e30)
        expo = jnp.exp(logits - jnp.max(logits, axis=-1, keepdims=True))
        probs = expo / jnp.sum(expo, axis=-1, keepdims=True)
        packed = jnp.where(is_expert, probs, row_facts[rows, :])
        for r in range(top):
            chosen = lanes() == facts[rows, r : r + 1] + PROBS
            gate = jnp.sum(jnp.where(chosen, probs, 0.0), axis=-1, keepdims=True)
            slot = slot_cols[r][rows, :]
            gate = jnp.where(slot >= 0, gate, 0.0)
            packed = jnp.where(lanes() == PAIRS + r, gate, packed)
            packed = jnp.where(lanes() == PAIRS + top + r, slot.astype(f32), packed)
        row_facts[rows, :] = packed
    gate_rows = row_facts[...].T[PAIRS : PAIRS + 8, :]

    def outgoing(j):
        return send(
            placed.at[j * half : (j + 1) * half, :],
            tok.at[0, j],
            token_sems.at[0, j],
            token_sems.at[1, j],
            at.near(j),
        )

    for j in range(experts):
        index = lax.broadcasted_iota(jnp.int32, (half, 1), 0) + j * half
        pick = [slot_rows[r] == index for r in range(top)]
        slot_gate = sum(
            jnp.sum(jnp.where(pick[r], gate_rows[r : r + 1, :], 0.0), axis=1, keepdims=True)
            for r in range(top)
        )
        pick = sum(p.astype(f32) for p in pick).astype(bf16)
        if j:
            target = placed.at[j * half : (j + 1) * half, :]
        else:
            target = tok.at[0, 0]
        target[:, :width] = dot_nn(pick, xf_ref[...]).astype(bf16)
        target[:, width:] = (dot_nn(pick, cot_ref[...]) * slot_gate).astype(bf16)
        if j:
            outgoing(j).start()

    def shared_branch():
        shared_in.diagonal()
        shared_in.sent()
        for some in chunks:
            x_t[:, some] = xf_ref[some, :].T
            dy_t[:, some] = cot_ref[some, :].T
        y_acc[...] = jnp.zeros(y_acc.shape, f32)
        dx_acc[...] = jnp.zeros(dx_acc.shape, f32)
        for i in range(2):
            start = s_hidden * i
            branch(
                lambda some: xf_ref[some, :],
                lambda some: cot_ref[some, :],
                slice(0, length),
                sw,
                start,
                2 * s_hidden,
                s_hidden,
                act,
                y_acc,
                dx_acc,
            )

            def shared_grads(plane, carry):
                weight_grads(
                    plane, planes, length, x_t, dy_t, act, s_hidden, sw, start, 2 * s_hidden
                )
                return carry

            lax.fori_loop(0, planes, shared_grads, 0)
            turn_of(SHARED, i)
        out_ref[...] = y_acc[...].astype(bf16)
        s_dx[...] = dx_acc[...].astype(bf16)
        swaps = [
            send(mine, theirs, twin_sems.at[0, 2 + i], twin_sems.at[1, 2 + i], at.twin())
            for i, (mine, theirs) in enumerate(((out_ref, ffn_theirs), (s_dx, dx_theirs)))
        ]
        for swap in swaps:
            swap.start()
        return swaps

    turn_of(DISPATCHED)
    swap.wait_send()
    swaps = shared_branch()
    turn_of(SHARED)
    for j in range(1, experts):
        outgoing(j).wait_recv()
        outgoing(j).wait_send()
    across = send(tok.at[0], tok.at[1], twin_sems.at[0, 1], twin_sems.at[1, 1], at.twin())
    across.start()
    turn_of(ARRIVED)

    across.wait_recv()
    across.wait_send()

    def home_copy(j):
        return send(
            tok.at[0, j], home.at[0, j], home_sems.at[0, j], home_sems.at[1, j], at.near(j)
        )

    def share(j):
        return send(
            tok.at[1, j],
            ret.at[j * half : (j + 1) * half],
            share_sems.at[0, j],
            share_sems.at[1, j],
            at.twin(),
        )

    for i in range(2):
        expert_in[i].ready()
        expert_in[i].own_sent()

    def expert_half(i):
        for t in (1, 0):
            rows = slice(t * count, (t + 1) * count)

            def x_of(some):
                some = slice(some.start // half, some.stop // half)
                return tok[t, some, :, :width].reshape(-1, width)

            def dy_of(some):
                some = slice(some.start // half, some.stop // half)
                return tok[t, some, :, width:].reshape(-1, width)

            for some in chunks:
                x_t[:, rows.start + some.start : rows.start + some.stop] = x_of(some).T
                dy_t[:, rows.start + some.start : rows.start + some.stop] = dy_of(some).T
            if i == 0:
                y_acc[...] = jnp.zeros(y_acc.shape, f32)
                dx_acc[...] = jnp.zeros(dx_acc.shape, f32)
            else:
                for j in range(experts):
                    some = slice(j * half, (j + 1) * half)
                    y_acc[some, :] = part_one[t, j, :, :width].astype(f32)
                    dx_acc[some, :] = part_one[t, j, :, width:].astype(f32)
            branch(x_of, dy_of, rows, ew.at[i], 0, hidden, hidden, act, y_acc, dx_acc)
            target = tok if i else part_one
            if i and t == 0:
                for j in range(experts):
                    share(j).wait_recv()
            for j in range(experts):
                some = slice(j * half, (j + 1) * half)
                y, dx = y_acc[some, :], dx_acc[some, :]
                if i and t == 0:
                    y += ret[some, :width].astype(f32)
                    dx += ret[some, width:].astype(f32)
                target[t, j, :, :width] = y.astype(bf16)
                target[t, j, :, width:] = dx.astype(bf16)
                if i and t == 0 and j:
                    home_copy(j).start()
            if i and t:
                for j in range(experts):
                    share(j).start()
            turn_of(EXPERT, i, t)
        if i:
            home[0, 0] = tok[0, 0]
        expert_in[i].rest_sent()

        def grads_of(n, carry):
            plane = jnp.where(at.z * 2 < planes, planes - 1 - n, n)
            weight_grads(plane, planes, 2 * count, x_t, dy_t, act, hidden, ew.at[i], 0, hidden)
            expert_out[i].start_plane(plane)
            return carry

        lax.fori_loop(0, planes, grads_of, 0)

    for i in range(2):
        expert_half(i)
        turn_of(EXPERT, i)

    for j in range(1, experts):
        home_copy(j).wait_recv()
    swap = send(home.at[0], home.at[1], twin_sems.at[0, 5], twin_sems.at[1, 5], at.twin())
    swap.start()
    turn_of(HOME)
    for other in swaps:
        other.wait_recv()
        other.wait_send()
    swap.wait_recv()
    for rows in chunks:
        y = out_ref[rows, :].astype(f32) + ffn_theirs[rows, :].astype(f32)
        dx = s_dx[rows, :].astype(f32) + dx_theirs[rows, :].astype(f32)
        gate = jnp.zeros((step, 128), f32)
        dy = cot_ref[rows, :].astype(f32)
        for core in range(2):
            t = core + at.c - 2 * core * at.c
            index = lax.broadcasted_iota(jnp.int32, (1, count), 1) + t * count
            slots = [row_facts[rows, PAIRS + top + r : PAIRS + top + r + 1] for r in range(top)]
            slots = [(slot.astype(jnp.int32) == index).astype(f32) for slot in slots]
            for r in range(top):
                part = dot_nn(slots[r].astype(bf16), home[t, :, :, :width].reshape(count, width))
                y += row_facts[rows, PAIRS + r : PAIRS + r + 1] * part
                grad = jnp.sum(dy * part, axis=-1, keepdims=True)
                gate += jnp.where(lanes() == facts[rows, r : r + 1] + PROBS, grad, 0.0)
            dx += dot_nn(sum(slots).astype(bf16), home[t, :, :, width:].reshape(count, width))
        out_ref[rows, :] = (gx_ref[rows, :] + y).astype(bf16)
        dx_acc[rows, :] = dx
        y_acc[rows, :128] = gate
    attn_in.sent()

    grad_g_two = jnp.zeros((1, width), f32)
    grad_small = jnp.zeros((width, 128), f32)
    for rows in chunks:
        probs = jnp.where(is_expert, row_facts[rows, :], 0.0)
        grad_probs = y_acc[rows, :128]
        grad_logits = (
            probs * (grad_probs - jnp.sum(probs * grad_probs, axis=-1, keepdims=True))
        ).astype(bf16)
        grad_small += dot_tn(xf_ref[rows, :], grad_logits)
        grad_xf = dx_acc[rows, :] + dot_nt(grad_logits, small)
        h = gx_ref[rows, :]
        grad_h, grad_gain = norm_back_rows(grad_xf, h, g_two)
        grad_g_two += grad_gain
        grad_h = cot_ref[rows, :].astype(f32) + grad_h
        gx_ref[rows, :] = grad_h
        dy_t[:, rows] = grad_h.astype(bf16).T
        grad_o[rows, :] = dot_nn(
            grad_h.astype(bf16), blocks_of(aw, 0, heads_width)
        ).astype(bf16)
    for rows in chunks:
        x = x_ref[rows, :].astype(f32)
        rms = lax.rsqrt(jnp.mean(x * x, axis=-1, keepdims=True) + epsilon)
        x_t[:, rows] = (x * rms * g_one).astype(bf16).T
    masks()
    turn_of(COMBINED)

    def to_grads(start, columns, left, right):
        blocks = aw.shape[0]
        for i in range(0, blocks, blocks // 4):
            some = slice(i, i + blocks // 4)
            features = slice(i * aw.shape[1], (i + blocks // 4) * aw.shape[1])
            block = dot_nn(left[features, :length], right())
            aw[some, :, start : start + columns] = block.astype(bf16).reshape(
                blocks // 4, aw.shape[1], columns
            )

    to_grads(0, heads_width, dy_t, lambda: o_ref[...])
    turn_of(PROJECTED_OUT)
    for g in range(pairs):
        columns = slice(128 * g, 128 * (g + 1))
        for start, stop in attention_blocks(length)[::-1]:
            queries = q_ref[start:stop, columns]
            grads = grad_o[start:stop, columns]
            keys, values = k_ref[:stop, columns], v_ref[:stop, columns]
            grad_q = jnp.zeros((stop - start, 128), f32)
            grad_k = jnp.zeros((stop, 128), f32)
            grad_v = jnp.zeros((stop, 128), f32)
            for i in range(2):
                mask = lanes() // HD == i
                one_q = jnp.where(mask, queries, jnp.zeros_like(queries))
                one_do = jnp.where(mask, grads, jnp.zeros_like(grads))
                one_k = jnp.where(mask, keys, jnp.zeros_like(keys))
                scores = dot_nt(one_q, keys) * scale + bias[start:stop, :stop]
                log = LOGS + 2 * g + i
                weights = jnp.exp(scores - row_facts[start:stop, log : log + 1])
                grad_w = dot_nt(one_do, values)
                inner = jnp.sum(weights * grad_w, axis=-1, keepdims=True)
                grad_s = (weights * (grad_w - inner)).astype(bf16)
                grad_q += dot_nn(grad_s, one_k)
                grad_k += dot_tn(grad_s, one_q)
                grad_v += dot_tn(weights.astype(bf16), one_do)
            dproj[start:stop, columns] = turn(
                grad_q * scale, cosine[start:stop, :], -sine[start:stop, :]
            ).astype(bf16)
            if stop == length:
                dk_acc[...] = grad_k * scale
                dv_acc[...] = grad_v
            else:
                dk_acc[:stop, :] += grad_k * scale
                dv_acc[:stop, :] += grad_v
            turn_of(BACKWARD, g, start // (length // 2))
        dproj[:, heads_width + 128 * g : heads_width + 128 * (g + 1)] = turn(
            dk_acc[...], cosine, -sine
        ).astype(bf16)
        dproj[:, 2 * heads_width + 128 * g : 2 * heads_width + 128 * (g + 1)] = dv_acc[
            ...
        ].astype(bf16)
    for rows in chunks:
        part = dot_nt(dproj[rows, :], blocks_of(aw, heads_width, 4 * heads_width))
        part_mine[rows, :] = part.astype(bf16)
    last_swap = send(part_mine, part_theirs, twin_sems.at[0, 6], twin_sems.at[1, 6], at.twin())
    last_swap.start()
    for i in range(3):
        columns = slice(i * heads_width, (i + 1) * heads_width)
        to_grads((i + 1) * heads_width, heads_width, x_t, lambda: dproj[:, columns])
    turn_of(PROJECTED_BACK)
    last_swap.wait_recv()
    grad_g_one = jnp.zeros((1, width), f32)
    for rows in chunks:
        grad_xa = part_mine[rows, :].astype(f32) + part_theirs[rows, :].astype(f32)
        grad_x, grad_gain = norm_back_rows(grad_xa, x_ref[rows, :].astype(f32), g_one)
        gx_ref[rows, :] += grad_x
        grad_g_one += grad_gain
    index = lax.broadcasted_iota(jnp.int32, (128, 1), 0)
    gains = jnp.where(index == 0, grad_g_one, 0.0) + jnp.where(index == 1, grad_g_two, 0.0)
    small_grads = (gains.T + grad_small).astype(bf16)
    aw[:, :, 4 * heads_width :] = small_grads.reshape(aw.shape[0], aw.shape[1], 128)
    turn_of(LAST)
    s_out[...] = shared_out.total().astype(s_out.dtype)
    out_t[...] = attn_out[0].total()
    total = attn_out[1].total()
    for i in range(3):
        qkv_out[i] = total[:, i * heads_width : (i + 1) * heads_width]
    row = lax.broadcasted_iota(jnp.int32, small_out.shape[:1] + (128,), 0)
    lane = lax.broadcasted_iota(jnp.int32, small_out.shape[:1] + (128,), 1)
    small_out[...] = lax.dot_general(
        (row == lane).astype(f32),
        total[:, 3 * heads_width :],
        (((1,), (1,)), ((), ())),
        precision=lax.Precision.HIGHEST,
        preferred_element_type=f32,
    )
    for i in range(2):
        for j in range(1, GROUP):
            expert_out[i].arrive(j)

    swap.wait_send()
    last_swap.wait_send()
    for j in range(experts):
        share(j).wait_send()
    for j in range(1, experts):
        home_copy(j).wait_send()
    for i in range(2):
        expert_out[i].sent()
    shared_out.sent()
    for i in range(2):
        attn_out[i].sent()


def layer(planes, experts, top, heads_width, inputs, own):
    bf16, f32, dma = jnp.bfloat16, jnp.float32, pltpu.SemaphoreType.DMA
    n = planes * GROUP
    length, width = inputs[0].shape
    rows, a_width = own[0].shape
    s_width, e_width = own[1].shape[1], own[2].shape[2] // 2
    half = length * top // experts // 2
    slots = 2 * experts * half
    vmem, anywhere = pl.BlockSpec(memory_space=pltpu.VMEM), pl.BlockSpec(memory_space=pl.ANY)
    shape = jax.ShapeDtypeStruct
    tokens = pltpu.VMEM((2, experts, half, 2 * width), bf16)
    features = pltpu.VMEM((width, slots), bf16)
    wide = pltpu.VMEM((length, width), f32)
    narrow = pltpu.VMEM((length, width), bf16)
    heads = pltpu.VMEM((length, heads_width), bf16)
    facts = pltpu.VMEM((length, 128), f32)

    def plane_buffers(columns):
        return [
            pltpu.VMEM((planes, 2, rows, columns), bf16),
            pltpu.VMEM((planes, rows, columns), bf16),
            pltpu.VMEM((planes + 1, rows, columns), bf16),
        ]

    plane_sems = [dma((2, planes, 2)), dma((2, planes)), dma((2, 2, planes))]
    return pl.pallas_call(
        functools.partial(layer_kernel, planes, experts, top, heads_width),
        out_shape=(
            shape((length, width), bf16),
            shape((length, width), f32),
            shape((rows, heads_width), f32),
            shape((3, rows, heads_width), f32),
            shape((8, rows), f32),
            shape((rows, s_width), bf16),
            shape((GROUP, rows, 2 * e_width), bf16),
        ),
        in_specs=[vmem] * len(inputs) + [anywhere] * 3,
        out_specs=(vmem,) * 7,
        scratch_shapes=[
            pltpu.VMEM((n, rows, a_width), bf16),
            pltpu.VMEM((n, rows, s_width), bf16),
            pltpu.VMEM((2, n, rows, e_width), bf16),
            tokens,
            tokens,
            tokens,
            pltpu.VMEM((slots, e_width), bf16),
            features,
            features,
            wide,
            wide,
            narrow,
            heads,
            heads,
            heads,
            heads,
            narrow,
            facts,
            narrow,
            narrow,
            pltpu.VMEM((experts * half, 2 * width), bf16),
            *plane_buffers(a_width),
            *plane_buffers(s_width),
            pltpu.VMEM((2, (planes + 1) * GROUP, rows, e_width), bf16),
            dma((10,)),
            dma((n,)),
            dma((4, n)),
            dma((n,)),
            dma((4, n)),
            dma((2, n)),
            dma((2, 2, n)),
            dma((2, GROUP)),
            *[dma((2,) + s.shape) for s in plane_sems],
            *plane_sems,
            dma((2, 2, 2, n)),
            dma((2, 2, GROUP, 3)),
            dma((2, GROUP)),
            dma((2, GROUP)),
            dma((2, GROUP)),
            dma((2, 7)),
        ],
        compiler_params=pltpu.CompilerParams(
            collective_id=0, has_side_effects=True, vmem_limit_bytes=63 << 20
        ),
    )(*inputs, *own)


def local_grouped(
    planes,
    tokens,
    segment_ids,
    expert_ids,
    slot_order,
    gain_attn,
    qkv_weight,
    out_weight,
    gain_ffn,
    router_weight,
    gate_up,
    down_weight,
    shared_gate_up,
    shared_down,
    cotangent,
):
    bf16, f32 = jnp.bfloat16, jnp.float32
    rows, heads_width = qkv_weight.shape[0], qkv_weight.shape[2]
    experts, hidden = down_weight.shape[0], down_weight.shape[1]
    s_hidden = shared_down.shape[0]
    length = tokens.shape[0]
    top = expert_ids.shape[1]
    expert_packed = jnp.concatenate(
        [gate_up.reshape(experts, rows, 2 * hidden), down_weight.transpose(0, 2, 1)], axis=2
    )
    shared_packed = jnp.concatenate(
        [shared_gate_up.reshape(rows, 2 * s_hidden), shared_down.T], axis=1
    )
    small = jnp.concatenate([gain_attn[:, None], gain_ffn[:, None], router_weight], axis=1)
    small = jnp.pad(small, ((0, 0), (0, 128 - small.shape[1])))
    attn_packed = jnp.concatenate(
        [out_weight.T, qkv_weight.reshape(rows, 3 * heads_width), small], axis=1
    )
    inverse = np.exp(np.arange(HD // 2, dtype=np.float32) * np.float32(-2.0 * math.log(10000.0) / HD))
    angles = np.arange(length, dtype=np.float32)[:, None] * inverse[None, :]
    waves = np.concatenate([np.cos(angles)] * 2 + [np.sin(angles)] * 2, axis=1)
    waves = jnp.asarray(waves, f32)
    facts = jnp.concatenate(
        [expert_ids, slot_order.reshape(length, top), segment_ids.reshape(length, 1)], axis=1
    )
    facts = jnp.pad(facts, ((0, 0), (0, 8 - facts.shape[1])))
    output, grad_tokens, mine_out, mine_qkv, small_mine, mine_shared, mine_expert = layer(
        planes,
        experts,
        top,
        heads_width,
        (tokens, cotangent, facts, facts.T, waves),
        (attn_packed, shared_packed, expert_packed),
    )

    def halves(grads, size):
        both = [grads[..., :size], grads[..., size : 2 * size]]
        return jnp.stack(both, axis=-2).astype(f32)

    return (
        output,
        grad_tokens,
        small_mine[0],
        mine_qkv.transpose(1, 0, 2),
        mine_out.T,
        small_mine[1],
        small_mine[2 : 2 + experts].T,
        halves(mine_expert, hidden),
        mine_expert[:, :, 2 * hidden :].transpose(0, 2, 1).astype(f32),
        halves(mine_shared, s_hidden),
        mine_shared[:, 2 * s_hidden :].T.astype(f32),
    )


def solution(mesh):
    def pick(*args):
        experts, rows = args[9].shape[0], args[5].shape[0]
        if experts == GROUP and mesh.shape["dp"] == LINE * GROUP and rows % 16 == 0:
            return local_grouped(mesh.shape["dp"] // GROUP, *args)
        return local_plain(*args)

    return jax.shard_map(
        pick,
        mesh=mesh,
        in_specs=(
            P("dp", None),
            P("dp", None),
            P("dp", None),
            P("dp", None),
            P("dp"),
            P("dp", None, "tensor"),
            P("tensor", "dp"),
            P("dp"),
            P("dp", None),
            P(None, "dp", None, "tensor"),
            P(None, "tensor", "dp"),
            P("dp", None, "tensor"),
            P("tensor", "dp"),
            P("dp", None),
        ),
        out_specs=(
            P("dp", None),
            P("dp", None),
            P("dp"),
            P("dp", None, "tensor"),
            P("tensor", "dp"),
            P("dp"),
            P("dp", None),
            P(None, "dp", None, "tensor"),
            P(None, "tensor", "dp"),
            P("dp", None, "tensor"),
            P("tensor", "dp"),
        ),
        check_vma=False,
    )
```

```python
import functools
import math

import jax
import jax.numpy as jnp
import numpy as np
from jax import lax
from jax.experimental import pallas as pl
from jax.experimental.pallas import tpu as pltpu
from jax.sharding import PartitionSpec as P

HD = 64
GROUP = 4
MESH = pl.DeviceIdType.MESH


epsilon = 1e-06


def rms_scale(values):
    return lax.rsqrt(jnp.mean(values * values, axis=-1, keepdims=True) + epsilon)


def rotary(length, head_dim):
    half_dim = head_dim // 2
    position = jnp.arange(length).astype(jnp.float32)[:, None]
    inverse = jnp.exp(
        jnp.arange(half_dim).astype(jnp.float32) * (-2.0 * math.log(10000.0) / head_dim)
    )
    angles = position * inverse[None, :]
    return (jnp.cos(angles)[:, None, :], jnp.sin(angles)[:, None, :])


def rotate(values, cosine, sine):
    half_dim = values.shape[-1] // 2
    first_half = values[..., :half_dim]
    second_half = values[..., half_dim:]
    return jnp.concatenate(
        [first_half * cosine - second_half * sine, second_half * cosine + first_half * sine],
        axis=-1,
    )


def route_slots(pair_ids, rank_order, capacity, experts):
    length = pair_ids.shape[0]
    top_count = pair_ids.shape[1]
    pair_expert = pair_ids.reshape(-1)
    pair_count = pair_expert.shape[0]
    ordered = jnp.zeros((pair_count,), jnp.int32).at[rank_order].set(pair_expert)
    onehot = (ordered[:, None] == jnp.arange(experts, dtype=jnp.int32)[None, :]).astype(jnp.int32)
    running = jnp.cumsum(onehot, axis=0)
    ranked_slot = jnp.sum(running * onehot, axis=1) - 1
    position = ranked_slot[rank_order]
    kept_pair = position < capacity
    slot_index = jnp.where(kept_pair, pair_expert * capacity + position, experts * capacity)
    token_of_pair = jnp.arange(pair_count, dtype=jnp.int32) // top_count
    slot_token = (
        jnp.full((experts * capacity,), length, jnp.int32)
        .at[slot_index]
        .set(token_of_pair, mode="drop")
    )
    return (slot_token, slot_index.reshape(length, top_count), kept_pair.reshape(length, top_count))


def silu_back(both_parts, grad_hidden):
    gate_part = both_parts[..., 0, :]
    up_part = both_parts[..., 1, :]
    sigma = jax.nn.sigmoid(gate_part)
    slope = sigma * (1.0 + gate_part * (1.0 - sigma))
    return jnp.stack(
        [grad_hidden * up_part * slope, grad_hidden * gate_part * sigma], axis=-2
    ).astype(jnp.bfloat16)


def silu_forward(both_parts):
    return (jax.nn.silu(both_parts[..., 0, :]) * both_parts[..., 1, :]).astype(jnp.bfloat16)


def norm_back(grad_norm, values, scale_rows, gain):
    grad_gain = jnp.sum(grad_norm * values * scale_rows, axis=0)
    inner = grad_norm * gain
    grad_values = scale_rows * inner - values * scale_rows**3 * jnp.mean(
        inner * values, axis=-1, keepdims=True
    )
    return (grad_values, grad_gain)


def split_blocks(length):
    block = min(512, length)
    return (block, length // block)


def masked_scores(query_block, keys_all, query_pos, query_seg, segment, scale):
    positions = jnp.arange(keys_all.shape[0])
    scores = (
        jnp.einsum("qhd,khd->hqk", query_block, keys_all, preferred_element_type=jnp.float32)
        * scale
    )
    allowed = (positions[None, :] <= query_pos[:, None]) & (segment[None, :] == query_seg[:, None])
    return jnp.where(allowed[None], scores, -1e30)


def attend_forward(queries, keys_all, values_all, segment, scale):
    length, head_count, head_dim = queries.shape
    block, count_blocks = split_blocks(length)
    positions = jnp.arange(length)

    def one_block(inputs):
        query_block, query_pos, query_seg = inputs
        scores = masked_scores(query_block, keys_all, query_pos, query_seg, segment, scale)
        largest = jnp.max(scores, axis=-1, keepdims=True)
        expo = jnp.exp(scores - largest)
        total = jnp.sum(expo, axis=-1, keepdims=True)
        probs = (expo / total).astype(jnp.bfloat16)
        mixed = jnp.einsum("hqk,khd->qhd", probs, values_all, preferred_element_type=jnp.float32)
        return (mixed.astype(jnp.bfloat16), (largest + jnp.log(total))[..., 0])

    blocks = (
        queries.reshape(count_blocks, block, head_count, head_dim),
        positions.reshape(count_blocks, block),
        segment.reshape(count_blocks, block),
    )
    mixed_all, log_totals = lax.map(one_block, blocks)
    return (mixed_all.reshape(length, head_count * head_dim), log_totals)


def attend_backward(queries, keys_all, values_all, segment, scale, grad_mixed, log_totals):
    length, head_count, head_dim = queries.shape
    block, count_blocks = split_blocks(length)
    positions = jnp.arange(length)

    def one_block(carry, inputs):
        grad_keys, grad_values = carry
        query_block, query_pos, query_seg, grad_block, log_block = inputs
        scores = masked_scores(query_block, keys_all, query_pos, query_seg, segment, scale)
        probs = jnp.exp(scores - log_block[:, :, None])
        grad_probs = jnp.einsum(
            "qhd,khd->hqk", grad_block, values_all, preferred_element_type=jnp.float32
        )
        inner = jnp.sum(probs * grad_probs, axis=-1, keepdims=True)
        grad_scores = (probs * (grad_probs - inner)).astype(jnp.bfloat16)
        grad_query = (
            jnp.einsum("hqk,khd->qhd", grad_scores, keys_all, preferred_element_type=jnp.float32)
            * scale
        )
        grad_keys = (
            grad_keys
            + jnp.einsum(
                "hqk,qhd->khd", grad_scores, query_block, preferred_element_type=jnp.float32
            )
            * scale
        )
        grad_values = grad_values + jnp.einsum(
            "hqk,qhd->khd",
            probs.astype(jnp.bfloat16),
            grad_block,
            preferred_element_type=jnp.float32,
        )
        return ((grad_keys, grad_values), grad_query)

    zeros_kv = jnp.zeros((length, head_count, head_dim), jnp.float32)
    blocks = (
        queries.reshape(count_blocks, block, head_count, head_dim),
        positions.reshape(count_blocks, block),
        segment.reshape(count_blocks, block),
        grad_mixed.reshape(count_blocks, block, head_count, head_dim),
        log_totals,
    )
    (grad_keys, grad_values), grad_queries = lax.scan(one_block, (zeros_kv, zeros_kv), blocks)
    return (grad_queries.reshape(length, head_count, head_dim), grad_keys, grad_values)


def sum_rows(grad, axis, scatter_dimension, tiled):
    part = lax.psum_scatter(
        grad.astype(jnp.bfloat16), axis, scatter_dimension=scatter_dimension, tiled=tiled
    )
    return part.astype(jnp.float32)


def local_plain(
    tokens,
    segment_ids,
    expert_ids,
    slot_order,
    gain_attn,
    qkv_weight,
    out_weight,
    gain_ffn,
    router_weight,
    gate_up,
    down_weight,
    shared_gate_up,
    shared_down,
    cotangent,
):
    g_one, w_qkv, w_out, g_two, w_router, w_gate_up, w_down, s_gate_up, s_down = (
        lax.all_gather(gain_attn, "dp", axis=0, tiled=True),
        lax.all_gather(qkv_weight, "dp", axis=0, tiled=True),
        lax.all_gather(out_weight, "dp", axis=1, tiled=True),
        lax.all_gather(gain_ffn, "dp", axis=0, tiled=True),
        lax.all_gather(router_weight, "dp", axis=0, tiled=True),
        lax.all_gather(gate_up, "dp", axis=1, tiled=True),
        lax.all_gather(down_weight, "dp", axis=2, tiled=True),
        lax.all_gather(shared_gate_up, "dp", axis=0, tiled=True),
        lax.all_gather(shared_down, "dp", axis=1, tiled=True),
    )
    length = tokens.shape[0]
    width = tokens.shape[1]
    experts_count = w_router.shape[1]
    top_count = expert_ids.shape[1]
    capacity = length * top_count // experts_count
    head_dim = HD
    local_heads = w_qkv.shape[2] // head_dim
    scale = head_dim ** (-0.5)
    segment = segment_ids[0]
    slot_token, slot_index, kept_pair = route_slots(
        expert_ids, slot_order[0], capacity, experts_count
    )
    kept_float = kept_pair.astype(jnp.float32)
    slot_valid = slot_token < length
    slot_rows = jnp.minimum(slot_token, length - 1)
    pair_slots = jnp.minimum(slot_index, experts_count * capacity - 1)
    xfull = tokens.astype(jnp.float32)
    rms_one = rms_scale(xfull)
    xn_one = (xfull * rms_one * g_one.astype(jnp.float32)).astype(jnp.bfloat16)
    projected = jnp.einsum("td,dch->tch", xn_one, w_qkv, preferred_element_type=jnp.float32)
    cosine, sine = rotary(length, head_dim)
    queries = rotate(projected[:, 0].reshape(length, local_heads, head_dim), cosine, sine).astype(
        jnp.bfloat16
    )
    keys_all = rotate(projected[:, 1].reshape(length, local_heads, head_dim), cosine, sine).astype(
        jnp.bfloat16
    )
    values_all = projected[:, 2].reshape(length, local_heads, head_dim).astype(jnp.bfloat16)
    mixed, log_totals = attend_forward(queries, keys_all, values_all, segment, scale)
    attn_share = lax.psum_scatter(
        jnp.dot(mixed, w_out, preferred_element_type=jnp.float32),
        "tensor",
        scatter_dimension=1,
        tiled=True,
    )
    attn = lax.all_gather(attn_share, "tensor", axis=1, tiled=True)
    hidden_state = xfull + attn
    rms_two = rms_scale(hidden_state)
    xn_two = (hidden_state * rms_two * g_two.astype(jnp.float32)).astype(jnp.bfloat16)
    logits = jnp.dot(xn_two, w_router, preferred_element_type=jnp.float32)
    probs = jax.nn.softmax(logits, axis=-1)
    gates = jnp.take_along_axis(probs, expert_ids, axis=1) * kept_float
    dispatched = (xn_two[slot_rows] * slot_valid[:, None].astype(jnp.bfloat16)).reshape(
        experts_count, capacity, width
    )
    both_parts = jnp.einsum(
        "ecd,edjf->ecjf", dispatched, w_gate_up, preferred_element_type=jnp.float32
    )
    expert_hidden = silu_forward(both_parts)
    expert_out = jnp.einsum(
        "ecf,efd->ecd", expert_hidden, w_down, preferred_element_type=jnp.float32
    ).reshape(experts_count * capacity, width)
    picked = expert_out[pair_slots]
    moe = jnp.sum(gates[:, :, None] * picked, axis=1)
    shared_both = jnp.einsum("td,djf->tjf", xn_two, s_gate_up, preferred_element_type=jnp.float32)
    shared_hidden = silu_forward(shared_both)
    shared_out = jnp.dot(shared_hidden, s_down, preferred_element_type=jnp.float32)
    ffn_share = lax.psum_scatter(
        (moe + shared_out).astype(jnp.bfloat16), "tensor", scatter_dimension=1, tiled=True
    ).astype(jnp.float32)
    ffn = lax.all_gather(ffn_share.astype(jnp.bfloat16), "tensor", axis=1, tiled=True).astype(
        ffn_share.dtype
    )
    output = (hidden_state + ffn).astype(jnp.bfloat16)
    grad_y = cotangent.astype(jnp.float32)
    grad_shared_hidden = jnp.einsum(
        "td,fd->tf", cotangent, s_down, preferred_element_type=jnp.float32
    )
    grad_s_down = jnp.einsum(
        "tf,td->fd", shared_hidden, cotangent, preferred_element_type=jnp.float32
    )
    grad_shared_both = silu_back(shared_both, grad_shared_hidden)
    grad_s_gate_up = jnp.einsum(
        "td,tjf->djf", xn_two, grad_shared_both, preferred_element_type=jnp.float32
    )
    grad_xn_shared = jnp.einsum(
        "tjf,djf->td", grad_shared_both, s_gate_up, preferred_element_type=jnp.float32
    )
    slot_gate = (
        jnp.zeros((experts_count * capacity,), jnp.float32)
        .at[slot_index.reshape(-1)]
        .set(gates.reshape(-1), mode="drop")
    )
    grad_expert_out = (
        (slot_gate[:, None] * grad_y[slot_rows])
        .astype(jnp.bfloat16)
        .reshape(experts_count, capacity, width)
    )
    grad_gates_part = kept_float * jnp.sum(grad_y[:, None, :] * picked, axis=-1)
    grad_expert_hidden = jnp.einsum(
        "ecd,efd->ecf", grad_expert_out, w_down, preferred_element_type=jnp.float32
    )
    grad_w_down = jnp.einsum(
        "ecf,ecd->efd", expert_hidden, grad_expert_out, preferred_element_type=jnp.float32
    )
    grad_both = silu_back(both_parts, grad_expert_hidden)
    grad_w_gate_up = jnp.einsum(
        "ecd,ecjf->edjf", dispatched, grad_both, preferred_element_type=jnp.float32
    )
    grad_dispatched = jnp.einsum(
        "ecjf,edjf->ecd", grad_both, w_gate_up, preferred_element_type=jnp.float32
    ).reshape(experts_count * capacity, width)
    grad_xn_moe = jnp.sum(kept_float[:, :, None] * grad_dispatched[pair_slots], axis=1)
    grad_xn_part, grad_gates_share = (
        lax.psum_scatter(grad_xn_shared + grad_xn_moe, "tensor", scatter_dimension=1, tiled=True),
        lax.psum_scatter(grad_gates_part, "tensor", scatter_dimension=1, tiled=True),
    )
    grad_xn_sum, grad_gates = (
        lax.all_gather(grad_xn_part, "tensor", axis=1, tiled=True),
        lax.all_gather(grad_gates_share, "tensor", axis=1, tiled=True),
    )
    expert_match = (
        expert_ids[:, :, None] == jnp.arange(experts_count, dtype=jnp.int32)[None, None, :]
    ).astype(jnp.float32)
    grad_probs = jnp.sum(expert_match * grad_gates[:, :, None], axis=1)
    grad_logits = (
        probs * (grad_probs - jnp.sum(probs * grad_probs, axis=-1, keepdims=True))
    ).astype(jnp.bfloat16)
    grad_w_router = jnp.einsum("td,te->de", xn_two, grad_logits, preferred_element_type=jnp.float32)
    grad_xn_two = grad_xn_sum + jnp.einsum(
        "te,de->td", grad_logits, w_router, preferred_element_type=jnp.float32
    )
    grad_norm_two, grad_g_two = norm_back(
        grad_xn_two, hidden_state, rms_two, g_two.astype(jnp.float32)
    )
    grad_hidden = grad_y + grad_norm_two
    grad_attn = grad_hidden.astype(jnp.bfloat16)
    grad_w_out = jnp.einsum("th,td->hd", mixed, grad_attn, preferred_element_type=jnp.float32)
    grad_mixed = jnp.einsum(
        "td,hd->th", grad_attn, w_out, preferred_element_type=jnp.float32
    ).astype(jnp.bfloat16)
    grad_queries, grad_keys, grad_values = attend_backward(
        queries, keys_all, values_all, segment, scale, grad_mixed, log_totals
    )
    grad_projected = (
        jnp.stack(
            [rotate(grad_queries, cosine, -sine), rotate(grad_keys, cosine, -sine), grad_values],
            axis=1,
        )
        .astype(jnp.bfloat16)
        .reshape(length, 3, local_heads * head_dim)
    )
    grad_w_qkv = jnp.einsum(
        "td,tch->dch", xn_one, grad_projected, preferred_element_type=jnp.float32
    )
    grad_xn_share = lax.psum_scatter(
        jnp.einsum("tch,dch->td", grad_projected, w_qkv, preferred_element_type=jnp.float32).astype(
            jnp.bfloat16
        ),
        "tensor",
        scatter_dimension=1,
        tiled=True,
    ).astype(jnp.float32)
    grad_xn_one = lax.all_gather(
        grad_xn_share.astype(jnp.bfloat16), "tensor", axis=1, tiled=True
    ).astype(grad_xn_share.dtype)
    grad_norm_one, grad_g_one = norm_back(grad_xn_one, xfull, rms_one, g_one.astype(jnp.float32))
    grad_tokens = grad_hidden + grad_norm_one
    (
        grad_g_one,
        grad_w_qkv,
        grad_w_out,
        grad_g_two,
        grad_w_router,
        grad_w_gate_up,
        grad_w_down,
        grad_s_gate_up,
        grad_s_down,
    ) = (
        lax.psum_scatter(grad_g_one, "dp", scatter_dimension=0, tiled=True),
        sum_rows(grad_w_qkv, "dp", scatter_dimension=0, tiled=True),
        sum_rows(grad_w_out, "dp", scatter_dimension=1, tiled=True),
        lax.psum_scatter(grad_g_two, "dp", scatter_dimension=0, tiled=True),
        lax.psum_scatter(grad_w_router, "dp", scatter_dimension=0, tiled=True),
        sum_rows(grad_w_gate_up, "dp", scatter_dimension=1, tiled=True),
        sum_rows(grad_w_down, "dp", scatter_dimension=2, tiled=True),
        sum_rows(grad_s_gate_up, "dp", scatter_dimension=0, tiled=True),
        sum_rows(grad_s_down, "dp", scatter_dimension=1, tiled=True),
    )
    return (
        output,
        grad_tokens,
        grad_g_one,
        grad_w_qkv,
        grad_w_out,
        grad_g_two,
        grad_w_router,
        grad_w_gate_up,
        grad_w_down,
        grad_s_gate_up,
        grad_s_down,
    )


class Place:
    def __init__(self, planes):
        d = lax.axis_index("dp")
        self.planes = planes
        self.d, self.c = d, lax.axis_index("tensor")
        self.z, self.p = d // GROUP, lax.rem(d, GROUP)
        bit0, bit1 = lax.rem(self.p, 2), self.p // 2
        flip0, flip1 = 1 - bit0, 1 - bit1
        self.member = [
            self.p,
            flip0 + 2 * bit1,
            bit0 + 2 * flip1,
            flip0 + 2 * flip1,
        ]

    def near(self, j):
        return (self.z * GROUP + self.member[j], self.c)

    def up(self):
        return (self.d + GROUP, self.c)

    def down(self):
        return (self.d - GROUP, self.c)

    def twin(self):
        return (self.d, 1 - self.c)

    def when(self, condition, action):
        pl.when(condition)(action)

    def has_up(self, k=1):
        return self.z + k < self.planes

    def has_down(self, k=1):
        return self.z - k >= 0

    def greet(self):
        barrier = pltpu.get_barrier_semaphore()

        def hello(device):
            pl.semaphore_signal(barrier, inc=1, device_id=device, device_id_type=MESH)

        hello(self.twin())
        for j in range(1, GROUP):
            hello(self.near(j))
        self.when(self.has_up(), lambda: hello(self.up()))
        self.when(self.has_down(), lambda: hello(self.down()))
        line = self.has_up().astype(jnp.int32) + self.has_down().astype(jnp.int32)
        pl.semaphore_wait(barrier, GROUP + line)


def send(source, target, send_sem, recv_sem, device):
    return pltpu.make_async_remote_copy(
        src_ref=source,
        dst_ref=target,
        send_sem=send_sem,
        recv_sem=recv_sem,
        device_id=device,
        device_id_type=MESH,
    )


class Everywhere:
    def __init__(self, at, own, all_blocks, local_sem, recvs, sends):
        self.at, self.own, self.all = at, own, all_blocks
        self.local_sem, self.recvs, self.sends = local_sem, recvs, sends

    def copy(self, block, source, way, device):
        return send(source, self.all.at[block], self.sends.at[way, block], self.recvs.at[block], device)

    def keep(self):
        return pltpu.make_async_copy(self.own, self.all.at[self.at.d], self.local_sem)

    def landed(self, block):
        self.copy(block, self.own, 0, self.at.near(1)).wait_recv()

    def start_line(self):
        at = self.at
        at.when(at.has_up(), lambda: self.copy(at.d, self.own, 0, at.up()).start())
        at.when(at.has_down(), lambda: self.copy(at.d, self.own, 1, at.down()).start())

    def start_plane(self):
        at = self.at
        self.copy(at.d, self.own, 2, at.near(1)).start()
        self.copy(at.d, self.own, 3, at.near(2)).start()
        self.keep().start()

    def pass_on(self, k):
        at = self.at

        def go(plane, more, way, device_of):
            block = plane * GROUP + at.p
            self.landed(block)
            at.when(more, lambda: self.copy(block, self.all.at[block], way, device_of()).start())

        at.when(at.has_down(k), lambda: go(at.z - k, at.has_up(), 0, at.up))
        at.when(at.has_up(k), lambda: go(at.z + k, at.has_down(), 1, at.down))

    def over_plane(self, k):
        at = self.at

        def go(plane):
            block = plane * GROUP + at.p
            self.copy(block, self.all.at[block], 2, at.near(1)).start()
            self.copy(block, self.all.at[block], 3, at.near(2)).start()

        at.when(at.has_down(k), lambda: go(at.z - k))
        at.when(at.has_up(k), lambda: go(at.z + k))

    def spread(self, k):
        self.pass_on(k)
        self.over_plane(k)

    def cross(self, k):
        at = self.at

        def go(plane):
            first = plane * GROUP + at.member[1]
            second = plane * GROUP + at.member[2]
            even = lax.rem(plane, 2) == 0
            self.landed(first)
            at.when(even, lambda: self.copy(first, self.all.at[first], 3, at.near(2)).start())
            self.landed(second)
            at.when(
                jnp.logical_not(even),
                lambda: self.copy(second, self.all.at[second], 2, at.near(1)).start(),
            )

        if k == 0:
            go(at.z)
        else:
            at.when(at.has_down(k), lambda: go(at.z - k))
            at.when(at.has_up(k), lambda: go(at.z + k))

    def diagonal(self):
        for plane in range(self.at.planes):
            self.landed(plane * GROUP + self.at.member[3])
        self.keep().wait()

    def sent(self):
        at = self.at
        for plane in range(at.planes):
            block = plane * GROUP + at.p
            self.copy(block, self.own, 2, at.near(1)).wait_send()
            self.copy(block, self.own, 3, at.near(2)).wait_send()
            if plane % 2 == 0:
                self.copy(plane * GROUP + at.member[1], self.own, 3, at.near(2)).wait_send()
            else:
                self.copy(plane * GROUP + at.member[2], self.own, 2, at.near(1)).wait_send()

            def gone(way, device_of):
                self.copy(block, self.own, way, device_of()).wait_send()

            at.when((at.z >= plane) & at.has_up(), lambda: gone(0, at.up))
            at.when((at.z <= plane) & at.has_down(), lambda: gone(1, at.down))


class Experts:
    def __init__(self, at, own, all_blocks, local_sem, recvs, sends, across_sends):
        self.at, self.own, self.all = at, own, all_blocks
        self.local_sem, self.recvs, self.sends = local_sem, recvs, sends
        self.across_sends = across_sends

    def line(self, block, source, way, device):
        return send(source, self.all.at[block], self.sends.at[way, block], self.recvs.at[block], device)

    def across(self, j):
        at = self.at
        return send(
            self.own.at[at.member[j]],
            self.all.at[at.d],
            self.across_sends.at[j],
            self.recvs.at[at.d],
            at.near(j),
        )

    def keep(self):
        return pltpu.make_async_copy(self.own.at[self.at.p], self.all.at[self.at.d], self.local_sem)

    def start_plane(self):
        for j in range(1, GROUP):
            self.across(j).start()
        self.keep().start()

    def start_line(self):
        at = self.at
        source = self.own.at[at.p]
        at.when(at.has_up(), lambda: self.line(at.d, source, 0, at.up()).start())
        at.when(at.has_down(), lambda: self.line(at.d, source, 1, at.down()).start())

    def landed(self, block):
        self.line(block, self.own.at[0], 0, self.at.near(1)).wait_recv()

    def plane_step(self, j):
        at = self.at
        block = at.z * GROUP + at.member[j]
        source = self.all.at[block]
        self.landed(block)
        at.when(at.has_up(), lambda: self.line(block, source, 0, at.up()).start())
        at.when(at.has_down(), lambda: self.line(block, source, 1, at.down()).start())

    def line_step(self, k, j):
        at = self.at

        def go(plane, more, way, device_of):
            block = plane * GROUP + at.member[j]
            self.landed(block)
            at.when(more, lambda: self.line(block, self.all.at[block], way, device_of()).start())

        at.when(at.has_down(k), lambda: go(at.z - k, at.has_up(), 0, at.up))
        at.when(at.has_up(k), lambda: go(at.z + k, at.has_down(), 1, at.down))

    def ready(self):
        self.keep().wait()

    def own_sent(self):
        at = self.at
        source = self.own.at[at.p]
        for j in range(1, GROUP):
            self.across(j).wait_send()
        at.when(at.has_up(), lambda: self.line(at.d, source, 0, at.up()).wait_send())
        at.when(at.has_down(), lambda: self.line(at.d, source, 1, at.down()).wait_send())

    def rest_sent(self):
        at = self.at
        for plane in range(at.planes):

            def gone(j, way, device_of):
                block = plane * GROUP + at.member[j]
                self.line(block, self.own.at[0], way, device_of()).wait_send()

            for j in range(GROUP):
                up = at.z >= plane if j else at.z > plane
                down = at.z <= plane if j else at.z < plane
                at.when(up & at.has_up(), lambda: gone(j, 0, at.up))
                at.when(down & at.has_down(), lambda: gone(j, 1, at.down))


def dot_nn(a, b):
    return jnp.dot(a, b, preferred_element_type=jnp.float32)


def dot_nt(a, b):
    return lax.dot_general(a, b, (((1,), (1,)), ((), ())), preferred_element_type=jnp.float32)


def dot_tn(a, b):
    return lax.dot_general(a, b, (((0,), (0,)), ((), ())), preferred_element_type=jnp.float32)


def lanes(count=128):
    return lax.broadcasted_iota(jnp.int32, (1, count), 1)


def turn(values, cosine, sine):
    half = HD // 2
    other = jnp.where(
        lax.rem(lanes(), HD) < half,
        -pltpu.roll(values, 2 * HD - half, 1),
        pltpu.roll(values, half, 1),
    )
    return values * cosine + other * sine


def blocks_of(ref, start, stop):
    block = ref[:, :, start:stop]
    return block.reshape(block.shape[0] * block.shape[1], stop - start)


def attention_blocks(length):
    size = length // 2
    return [(i * size, (i + 1) * size) for i in range(2)]


class PlaneSum:
    def __init__(self, at, own, one, two, came, one_sems, two_sems, line_sems):
        self.at, self.own, self.one, self.two, self.came = at, own, one, two, came
        self.one_sems, self.two_sems, self.line_sems = one_sems, two_sems, line_sems

    def one_copy(self, plane, i, even):
        at = self.at
        j = 1 if even else 2
        target = at.member[3] if i else at.member[j]
        return send(
            self.own.at[plane * GROUP + target],
            self.one.at[plane, i],
            self.one_sems.at[0, plane, i],
            self.one_sems.at[1, plane, i],
            at.near(j),
        )

    def two_copy(self, plane, even):
        return send(
            self.one.at[plane, 1],
            self.two.at[plane],
            self.two_sems.at[0, plane],
            self.two_sems.at[1, plane],
            self.at.near(2 if even else 1),
        )

    def by_parity(self, plane, action):
        even = lax.rem(plane, 2) == 0
        self.at.when(even, lambda: action(True))
        self.at.when(jnp.logical_not(even), lambda: action(False))

    def line(self, source, plane, way, here=False):
        at, sems = self.at, self.line_sems
        slot, device = plane, at.up()
        if way:
            slot = jnp.where(plane == (at.z if here else at.z - 1), at.planes, plane)
            device = at.down()
        return send(
            source, self.came.at[slot], sems.at[0, way, plane], sems.at[1, way, plane], device
        )

    def both_ways(self, action, k):
        at = self.at
        if k == 0:
            action(at.z, 0)
            return
        at.when(at.has_up(k), lambda: action(at.z + k, 0))
        at.when(at.has_down(k), lambda: action(at.z - k, 1))

    def start(self, k):
        def go(plane, way):
            def pair(even):
                self.one_copy(plane, 1, even).start()
                self.one_copy(plane, 0, even).start()

            self.by_parity(plane, pair)

        self.both_ways(go, k)

    def middle(self, k):
        f32 = jnp.float32

        def go(plane, way):
            def stage(even):
                at, one = self.at, self.one
                other = plane * GROUP + (at.member[2] if even else at.member[1])
                self.one_copy(plane, 1, even).wait_recv()
                one[plane, 1] = (one[plane, 1].astype(f32) + self.own[other].astype(f32)).astype(
                    one.dtype
                )
                self.two_copy(plane, even).start()

            self.by_parity(plane, stage)

        self.both_ways(go, k)

    def finish_plane(self, plane):
        f32 = jnp.float32

        def stage(even):
            mine = plane * GROUP + self.at.p
            self.one_copy(plane, 0, even).wait_recv()
            self.two_copy(plane, even).wait_recv()
            self.two[plane] = (
                self.two[plane].astype(f32)
                + self.one[plane, 0].astype(f32)
                + self.own[mine].astype(f32)
            ).astype(self.two.dtype)

        self.by_parity(plane, stage)

    def step(self, k):
        f32 = jnp.float32

        def go(plane, way):
            at = self.at
            self.finish_plane(plane)
            behind = at.has_down() if way == 0 else at.has_up()
            held = self.came

            def add():
                self.line(self.two.at[plane], plane, way, True).wait_recv()
                held[plane] = (held[plane].astype(f32) + self.two[plane].astype(f32)).astype(
                    held.dtype
                )
                self.line(held.at[plane], plane, way).start()

            at.when(behind, add)
            at.when(
                jnp.logical_not(behind), lambda: self.line(self.two.at[plane], plane, way).start()
            )

        self.both_ways(go, k)

    def total(self):
        at, f32 = self.at, jnp.float32
        z = at.z
        self.finish_plane(z)
        at.when(at.has_down(), lambda: self.line(self.two.at[z], z, 0, True).wait_recv())
        at.when(at.has_up(), lambda: self.line(self.two.at[z], z, 1, True).wait_recv())
        low = jnp.where(at.has_down(), self.came[z].astype(f32), 0.0)
        high = jnp.where(at.has_up(), self.came[at.planes].astype(f32), 0.0)
        return self.two[z].astype(f32) + low + high

    def sent(self):
        at = self.at
        for plane in range(at.planes):
            even = plane % 2 == 0
            self.one_copy(plane, 0, even).wait_send()
            self.one_copy(plane, 1, even).wait_send()
            self.two_copy(plane, even).wait_send()
            at.when(at.z < plane, lambda: self.line(self.two.at[plane], plane, 0).wait_send())
            at.when(at.z > plane, lambda: self.line(self.two.at[plane], plane, 1).wait_send())


class LineSum:
    def __init__(self, at, own, came, out, columns, line_sems, last_sems):
        self.at, self.own, self.came, self.out = at, own, came, out
        self.line_sems, self.last_sems = line_sems, last_sems
        self.columns, self.size = columns, columns[0].stop - columns[0].start

    def hop(self, source, plane, j, way, here=False):
        at = self.at
        block = plane * GROUP + at.member[j]
        if way == 0:
            slot, device = block, at.up()
        else:
            end = at.z if here else at.z - 1
            slot = jnp.where(plane == end, at.planes, plane) * GROUP + at.member[j]
            device = at.down()
        sems = self.line_sems
        return send(
            source, self.came.at[slot], sems.at[0, way, block], sems.at[1, way, block], device
        )

    def start_plane(self, plane):
        at = self.at

        def go(way):
            for j in range(GROUP):
                self.hop(self.own.at[plane * GROUP + at.member[j]], plane, j, way).start()

        at.when(jnp.logical_not(at.has_down()) & (plane != at.z), lambda: go(0))
        at.when(jnp.logical_not(at.has_up()) & (plane != at.z), lambda: go(1))

    def step(self, k, j):
        at, f32 = self.at, jnp.float32

        def go(plane, way):
            block = plane * GROUP + at.member[j]
            self.hop(self.own.at[block], plane, j, way, True).wait_recv()
            self.came[block] = (
                self.came[block].astype(f32) + self.own[block].astype(f32)
            ).astype(self.came.dtype)
            self.hop(self.came.at[block], plane, j, way).start()

        at.when(at.has_up(k) & at.has_down(), lambda: go(at.z + k, 0))
        at.when(at.has_down(k) & at.has_up(), lambda: go(at.z - k, 1))

    def parts(self, j, here=False):
        at, size = self.at, self.size
        source = self.came.at[at.z * GROUP + at.member[j]]
        target = self.out.at[at.member[j] if here else at.p]
        return [
            send(
                source.at[:, i * size : (i + 1) * size],
                target.at[:, self.columns[i]],
                self.last_sems.at[0, j, i],
                self.last_sems.at[1, j, i],
                at.near(j),
            )
            for i in range(len(self.columns))
        ]

    def total(self, j):
        at, f32, out = self.at, jnp.float32, self.out
        block = at.z * GROUP + at.member[j]
        spare = at.planes * GROUP + at.member[j]
        at.when(at.has_down(), lambda: self.hop(self.own.at[block], at.z, j, 0, True).wait_recv())
        at.when(at.has_up(), lambda: self.hop(self.own.at[block], at.z, j, 1, True).wait_recv())
        low = jnp.where(at.has_down(), self.came[block].astype(f32), 0.0)
        high = jnp.where(at.has_up(), self.came[spare].astype(f32), 0.0)
        total = (self.own[block].astype(f32) + low + high).astype(out.dtype)
        if j == 0:
            for i, columns in enumerate(self.columns):
                out[at.p, :, columns] = total[:, i * self.size : (i + 1) * self.size]
        else:
            self.came[block] = total
            for copy in self.parts(j):
                copy.start()

    def arrive(self, j):
        for copy in self.parts(j, True):
            copy.wait_recv()

    def sent(self):
        at = self.at
        for j in range(1, GROUP):
            for copy in self.parts(j):
                copy.wait_send()
        for plane in range(at.planes):

            def gone(way):
                for j in range(GROUP):
                    self.hop(self.own.at[0], plane, j, way).wait_send()

            at.when(at.z < plane, lambda: gone(0))
            at.when(at.z > plane, lambda: gone(1))


def norm_back_rows(grad, values, gain):
    rms = lax.rsqrt(jnp.mean(values * values, axis=-1, keepdims=True) + epsilon)
    grad_gain = jnp.sum(grad * values * rms, axis=0, keepdims=True)
    inner = grad * gain
    grad_values = rms * inner - values * (rms * rms * rms) * jnp.mean(
        inner * values, axis=-1, keepdims=True
    )
    return grad_values, grad_gain


def branch(x_of, dy_of, rows, weights, start, stride, hidden, act, y_acc, dx_acc):
    f32, bf16 = jnp.float32, jnp.bfloat16
    size, count = 256, rows.stop - rows.start
    step = min(count, 256)

    def body(i, carry):
        offset = pl.multiple_of(i * size, size)

        def weight(part):
            first = pl.multiple_of(start + part * stride + offset, size)
            block = weights[:, :, pl.ds(first, size)]
            return block.reshape(block.shape[0] * block.shape[1], size)

        for first in range(0, count, step):
            some = slice(first, first + step)

            def keep(part, values):
                columns = pl.ds(pl.multiple_of(part * hidden + offset, size), size)
                act[rows.start + first : rows.start + first + step, columns] = values

            g, u = dot_nn(x_of(some), weight(0)), dot_nn(x_of(some), weight(1))
            grad = dot_nn(dy_of(some), weight(2))
            sigma = 1.0 / (1.0 + jnp.exp(-g))
            silu = g * sigma
            eh = (silu * u).astype(bf16)
            dg = (grad * u * (sigma * (1.0 + g * (1.0 - sigma)))).astype(bf16)
            du = (grad * silu).astype(bf16)
            keep(0, dg)
            keep(1, du)
            keep(2, eh)
            y_acc[some, :] += dot_nt(eh, weight(2))
            dx_acc[some, :] += dot_nt(dg, weight(0)) + dot_nt(du, weight(1))
        return carry

    lax.fori_loop(0, hidden // size, body, 0)


def weight_grads(plane, planes, count, x_t, dy_t, act, hidden, grads, start, stride):
    width, bf16 = x_t.shape[0], jnp.bfloat16
    rows = width // planes
    features = pl.ds(pl.multiple_of(plane * rows, 16), rows)
    for part in range(3):
        columns = slice(part * hidden, (part + 1) * hidden)
        left = dy_t if part == 2 else x_t
        block = dot_nn(left[features, :count], act[:count, columns]).astype(bf16)
        target = slice(start + part * stride, start + part * stride + hidden)
        grads[pl.ds(plane * GROUP, GROUP), :, target] = block.reshape(
            GROUP, rows // GROUP, hidden
        )


PROBS, PAIRS, LOGS = 2, 8, 16


(
    E_PLANE,
    E_ACROSS,
    E_OWN,
    E_LINE,
    S_OWN,
    S_PLANE,
    S_LINE,
    S_OVER,
    S_CROSS,
    S_START,
    S_MIDDLE,
    S_STEP,
    E_STEP,
    E_TOTAL,
    A_START,
    A_MIDDLE,
    A_STEP,
) = range(17)
(
    ARRIVED,
    ATTENDED,
    ATTENTION,
    BACKWARD,
    BEGIN,
    COMBINED,
    DISPATCHED,
    EXPERT,
    GATHER,
    GATHERED,
    HOME,
    LAST,
    PROJECTED,
    PROJECTED_BACK,
    PROJECTED_OUT,
    SHARED,
) = range(16)
LINE = 4
PLAN = {
    (BEGIN,): [
        (E_OWN, 0),
        (S_OWN,),
    ],
    (GATHER, 1): [
        (S_PLANE,),
    ],
    (GATHER, 2): [
        (S_LINE, 1),
        (E_LINE, 0, 1, 0),
    ],
    (GATHER, 3): [
        (E_ACROSS, 1),
        (E_PLANE, 0, 1),
        (S_LINE, 2),
        (E_PLANE, 0, 2),
        (E_PLANE, 0, 3),
    ],
    (GATHERED,): [
        (S_OVER, 2),
        (E_LINE, 0, 2, 0),
        (S_LINE, 3),
        (S_OVER, 1),
        (S_OVER, 3),
        (E_OWN, 1),
    ],
    (PROJECTED,): [],
    (ATTENTION, 0, 0): [
        (E_LINE, 0, 1, 2),
    ],
    (ATTENTION, 0, 1): [],
    (ATTENTION, 0, 2): [
        (E_LINE, 0, 1, 3),
    ],
    (ATTENTION, 1, 0): [
        (S_CROSS, 2),
    ],
    (ATTENTION, 1, 1): [
        (S_CROSS, 1),
    ],
    (ATTENTION, 1, 2): [
        (E_LINE, 0, 1, 1),
    ],
    (ATTENDED,): [
        (E_LINE, 0, 2, 2),
        (E_PLANE, 1, 1),
        (E_PLANE, 1, 2),
        (E_PLANE, 1, 3),
        (E_LINE, 1, 1, 0),
        (S_CROSS, 3),
        (S_CROSS, 0),
    ],
    (DISPATCHED,): [
        (E_LINE, 0, 2, 3),
        (E_LINE, 0, 3, 2),
    ],
    (SHARED, 0): [
        (E_LINE, 0, 2, 1),
        (E_LINE, 1, 1, 2),
        (E_LINE, 1, 1, 3),
        (E_LINE, 1, 1, 1),
        (E_LINE, 0, 3, 0),
    ],
    (SHARED, 1): [],
    (SHARED,): [
        (S_START, 2),
        (S_START, 1),
    ],
    (ARRIVED,): [
        (E_LINE, 0, 3, 1),
        (E_LINE, 0, 3, 3),
        (E_LINE, 1, 2, 0),
        (E_LINE, 1, 2, 1),
        (E_LINE, 1, 2, 2),
        (E_LINE, 1, 2, 3),
        (S_START, 3),
    ],
    (EXPERT, 0, 1): [],
    (EXPERT, 0, 0): [],
    (EXPERT, 0): [
        (E_LINE, 1, 3, 0),
        (E_LINE, 1, 3, 1),
        (E_LINE, 1, 3, 2),
        (E_LINE, 1, 3, 3),
    ],
    (EXPERT, 1, 1): [
        (E_STEP, 0, 2, 0),
    ],
    (EXPERT, 1, 0): [
        (E_STEP, 0, 2, 3),
        (S_START, 0),
    ],
    (EXPERT, 1): [
        (E_STEP, 0, 2, 2),
        (E_STEP, 0, 2, 1),
        (E_STEP, 0, 1, 0),
        (E_STEP, 0, 1, 2),
        (E_STEP, 0, 1, 3),
    ],
    (HOME,): [
        (E_STEP, 0, 1, 1),
        (S_MIDDLE, 3),
        (S_MIDDLE, 0),
    ],
    (COMBINED,): [],
    (PROJECTED_OUT,): [
        (A_START, 0, 3),
        (A_START, 0, 2),
        (A_START, 0, 1),
        (A_START, 0, 0),
    ],
    (BACKWARD, 0, 1): [
        (E_TOTAL, 0, 1),
        (E_TOTAL, 0, 2),
        (E_TOTAL, 0, 3),
        (S_MIDDLE, 1),
        (E_TOTAL, 0, 0),
    ],
    (BACKWARD, 0, 0): [
        (E_STEP, 1, 2, 0),
        (E_STEP, 1, 2, 1),
        (E_STEP, 1, 2, 3),
        (S_STEP, 3),
    ],
    (BACKWARD, 1, 1): [],
    (BACKWARD, 1, 0): [
        (E_STEP, 1, 1, 0),
    ],
    (BACKWARD, 2, 1): [],
    (BACKWARD, 2, 0): [
        (S_MIDDLE, 2),
    ],
    (PROJECTED_BACK,): [
        (E_STEP, 1, 2, 2),
        (E_STEP, 1, 1, 2),
        (E_STEP, 1, 1, 1),
    ],
    (LAST,): [
        (A_START, 1, 3),
        (A_START, 1, 0),
        (A_START, 1, 1),
        (E_STEP, 1, 1, 3),
        (A_MIDDLE, 0, 3),
        (A_MIDDLE, 1, 3),
        (A_START, 1, 2),
        (A_MIDDLE, 0, 2),
        (A_MIDDLE, 1, 2),
        (A_STEP, 0, 3),
        (A_STEP, 1, 3),
        (A_MIDDLE, 0, 1),
        (A_MIDDLE, 1, 1),
        (S_STEP, 2),
        (E_TOTAL, 1, 0),
        (E_TOTAL, 1, 1),
        (E_TOTAL, 1, 2),
        (E_TOTAL, 1, 3),
        (A_STEP, 0, 2),
        (A_STEP, 1, 2),
        (A_MIDDLE, 0, 0),
        (A_MIDDLE, 1, 0),
        (S_STEP, 1),
        (A_STEP, 0, 1),
        (A_STEP, 1, 1),
    ],
}


def layer_kernel(
    planes,
    experts,
    top,
    heads_width,
    x_ref,
    cot_ref,
    ids_in,
    order_in,
    segment_in,
    waves,
    a_own,
    s_own,
    e_own,
    out_ref,
    gx_ref,
    out_t,
    qkv_out,
    small_out,
    s_out,
    e_out,
    facts,
    facts_t,
    aw,
    sw,
    ew,
    tok,
    part_one,
    home,
    act,
    x_t,
    dy_t,
    y_acc,
    dx_acc,
    s_dx,
    q_ref,
    k_ref,
    v_ref,
    o_ref,
    xf_ref,
    row_facts,
    ffn_theirs,
    dx_theirs,
    ret,
    a_one,
    a_two,
    a_came,
    s_one,
    s_two,
    s_came,
    e_came,
    local_sem,
    a_recv,
    a_send,
    s_recv,
    s_send,
    e_recv,
    e_send,
    e_across,
    a_one_sems,
    a_two_sems,
    a_line_sems,
    s_one_sems,
    s_two_sems,
    s_line_sems,
    e_line_sems,
    e_last_sems,
    token_sems,
    home_sems,
    share_sems,
    twin_sems,
):
    f32, bf16 = jnp.float32, jnp.bfloat16
    at = Place(planes)
    length, width = x_ref.shape
    capacity = length * top // experts
    half = capacity // 2
    count = experts * half
    hidden, s_hidden = ew.shape[3] // 3, sw.shape[2] // 6
    step = min(length, 256)
    chunks = [slice(i, i + step) for i in range(0, length, step)]

    halves = [
        [slice((2 * k + i) * hidden, (2 * k + i + 1) * hidden) for k in range(3)] for i in range(2)
    ]

    attn_in = Everywhere(at, a_own, aw, local_sem.at[0], a_recv, a_send)
    shared_in = Everywhere(at, s_own, sw, local_sem.at[1], s_recv, s_send)
    expert_in = [
        Experts(
            at,
            part_one.at[i, :, : e_own.shape[1]],
            ew.at[i],
            local_sem.at[2 + i],
            e_recv.at[i],
            e_send.at[i],
            e_across.at[i],
        )
        for i in range(2)
    ]
    expert_out = [
        LineSum(
            at, ew.at[i], e_came.at[i], e_out, halves[i], e_line_sems.at[i], e_last_sems.at[i]
        )
        for i in range(2)
    ]
    shared_out = PlaneSum(at, sw, s_one, s_two, s_came, s_one_sems, s_two_sems, s_line_sems)
    attn_out = [
        PlaneSum(
            at,
            aw.at[:, :, columns],
            a_one.at[:, :, :, columns],
            a_two.at[:, :, columns],
            a_came.at[:, :, columns],
            a_one_sems.at[i],
            a_two_sems.at[i],
            a_line_sems.at[i],
        )
        for i, columns in enumerate((slice(0, heads_width), slice(heads_width, aw.shape[2])))
    ]

    xa_ref = act.at[:length, :width]
    placed = ret
    part_mine = act.at[length:, :width]
    part_theirs = ret.at[:length, :width]
    grad_o = act.at[:length, :heads_width]
    dproj = act.at[:length, heads_width : 4 * heads_width]
    bias = y_acc
    dk_acc, dv_acc = (dx_acc.at[:, 128 * i : 128 * (i + 1)] for i in range(2))

    def halve(i, k):
        return pltpu.make_async_copy(
            e_own.at[:, :, halves[i][k]],
            part_one.at[i, :, : e_own.shape[1], k * hidden : (k + 1) * hidden],
            local_sem.at[4 + 3 * i + k],
        )

    for i in range(2):
        for k in range(3):
            halve(i, k).start()
    at.greet()
    attn_in.start_line()
    attn_in.start_plane()
    for k in range(3):
        halve(0, k).wait()
    expert_in[0].start_plane()
    for k in range(3):
        halve(1, k).wait()

    def turn_of(*place):
        for step in PLAN[place]:
            do(*step)

    def do(kind, *numbers):
        steps[kind](*numbers)

    steps = {
        E_PLANE: lambda i, j: expert_in[i].plane_step(j),
        E_ACROSS: lambda i: expert_in[i].start_plane(),
        E_OWN: lambda i: expert_in[i].start_line(),
        E_LINE: lambda i, k, j: expert_in[i].line_step(k, j),
        S_OWN: lambda: shared_in.start_line(),
        S_PLANE: lambda: shared_in.start_plane(),
        S_LINE: lambda k: shared_in.pass_on(k),
        S_OVER: lambda k: shared_in.over_plane(k),
        S_CROSS: lambda k: shared_in.cross(k),
        S_START: lambda k: shared_out.start(k),
        S_MIDDLE: lambda k: shared_out.middle(k),
        S_STEP: lambda k: shared_out.step(k),
        E_STEP: lambda i, k, j: expert_out[i].step(k, j),
        E_TOTAL: lambda i, j: expert_out[i].total(j),
        A_START: lambda i, k: attn_out[i].start(k),
        A_MIDDLE: lambda i, k: attn_out[i].middle(k),
        A_STEP: lambda i, k: attn_out[i].step(k),
    }

    turn_of(BEGIN)

    def ranks(r):
        size = length // 2
        total = jnp.zeros((8, length), f32)
        for first in range(0, top * length, size):
            pair = lax.broadcasted_iota(jnp.int32, (size, length), 0) + first
            token = lax.broadcasted_iota(jnp.int32, (size, length), 1)
            pick = (pair == token * top + r).astype(f32).astype(bf16)
            rank = jnp.broadcast_to(order_in[:, first : first + size], (8, size))
            for value, weight in ((rank // 32, 32.0), (lax.rem(rank, 32), 1.0)):
                total += weight * dot_nn(value.astype(f32).astype(bf16), pick)
        return total[0:1, :]

    found = [ids_in[r : r + 1, :].astype(f32) for r in range(top)]
    found += [ranks(r) for r in range(top)] + [segment_in[...].astype(f32)]
    line = lax.broadcasted_iota(jnp.int32, (128, 1), 0)
    table = jnp.zeros((128, length), f32)
    for i, row in enumerate(found):
        table = jnp.where(line == i, row, table)
    facts_t[...] = table[:8, :].astype(jnp.int32)
    facts[...] = table.T.astype(jnp.int32)
    seg_col, seg_row = facts[:, 2 * top : 2 * top + 1], facts_t[2 * top : 2 * top + 1, :]

    def masks():
        for start, stop in attention_blocks(length):
            row = lax.broadcasted_iota(jnp.int32, (stop - start, stop), 0) + start
            column = lax.broadcasted_iota(jnp.int32, (stop - start, stop), 1)
            allowed = (column <= row) & (seg_col[start:stop, :] == seg_row[:, :stop])
            bias[start:stop, :stop] = jnp.where(allowed, 0.0, -1e30)

    masks()

    def slot_of(expert_id, position):
        which = position // half
        apart = which + at.c - 2 * which * at.c
        bit0, bit1 = lax.rem(expert_id, 2), expert_id // 2
        p0, p1 = lax.rem(at.p, 2), at.p // 2
        distance = (bit0 + p0 - 2 * bit0 * p0) + 2 * (bit1 + p1 - 2 * bit1 * p1)
        slot = apart * count + distance * half + lax.rem(position, half)
        return jnp.where(position < capacity, slot, -1)

    slot_cols, slot_rows = [], []
    for r in range(top):
        ids_col, order_col = facts[:, r : r + 1], facts[:, top + r : top + r + 1]
        ids_row, order_row = facts_t[r : r + 1, :], facts_t[top + r : top + r + 1, :]
        count_col = jnp.zeros((length, 1), jnp.int32)
        count_row = jnp.zeros((1, length), jnp.int32)
        for other in range(top):
            first = (facts_t[other : other + 1, :] == ids_col) & (
                facts_t[top + other : top + other + 1, :] < order_col
            )
            count_col += jnp.sum(first.astype(jnp.int32), axis=1, keepdims=True)
            first = (facts[:, other : other + 1] == ids_row) & (
                facts[:, top + other : top + other + 1] < order_row
            )
            count_row += jnp.sum(first.astype(jnp.int32), axis=0, keepdims=True)
        slot_cols.append(slot_of(ids_col, count_col))
        slot_rows.append(slot_of(ids_row, count_row))

    for k in range(1, planes):
        attn_in.spread(k)
        attn_in.cross(k - 1)
        turn_of(GATHER, k)
    attn_in.cross(planes - 1)
    turn_of(GATHERED)
    attn_in.diagonal()

    small = blocks_of(aw, 4 * heads_width, 4 * heads_width + 128)
    small_rows = small.astype(f32).T
    g_one, g_two = small_rows[0:1, :], small_rows[1:2, :]
    for rows in chunks:
        x = x_ref[rows, :].astype(f32)
        rms = lax.rsqrt(jnp.mean(x * x, axis=-1, keepdims=True) + epsilon)
        xa_ref[rows, :] = (x * rms * g_one).astype(bf16)
    wave, other = waves[...], pltpu.roll(waves[...], 64, 1)
    cosine = jnp.where(lanes() < 64, wave, other)
    sine = jnp.where(lanes() < 64, other, wave)
    pairs = heads_width // 128
    for i, ref in enumerate((q_ref, k_ref)):
        part = dot_nn(xa_ref[...], blocks_of(aw, (i + 1) * heads_width, (i + 2) * heads_width))
        for g in range(pairs):
            columns = slice(128 * g, 128 * (g + 1))
            ref[:, columns] = turn(part[:, columns], cosine, sine).astype(bf16)
    v_ref[...] = dot_nn(xa_ref[...], blocks_of(aw, 3 * heads_width, 4 * heads_width)).astype(bf16)
    turn_of(PROJECTED)

    scale = HD ** (-0.5)
    for start, stop in attention_blocks(length):
        logs = jnp.zeros((stop - start, 128), f32)
        for g in range(pairs):
            columns = slice(128 * g, 128 * (g + 1))
            queries = q_ref[start:stop, columns]
            keys, values = k_ref[:stop, columns], v_ref[:stop, columns]
            mixed = []
            for i in range(2):
                one = jnp.where(lanes() // HD == i, queries, jnp.zeros_like(queries))
                scores = dot_nt(one, keys) * scale + bias[start:stop, :stop]
                largest = jnp.max(scores, axis=-1, keepdims=True)
                expo = jnp.exp(scores - largest)
                total = jnp.sum(expo, axis=-1, keepdims=True)
                weights = (expo * (1.0 / total)).astype(bf16)
                mixed.append(dot_nn(weights, values))
                logs = jnp.where(lanes() == LOGS + 2 * g + i, largest + jnp.log(total), logs)
            o_ref[start:stop, columns] = jnp.where(lanes() < HD, mixed[0], mixed[1]).astype(bf16)
            turn_of(ATTENTION, start // (length // 2), g)
        row_facts[start:stop, :] = logs

    for rows in chunks:
        dx_acc[rows, :] = dot_nt(
            o_ref[rows, :], blocks_of(aw, 0, heads_width)
        )
    swap = send(dx_acc, gx_ref, twin_sems.at[0, 0], twin_sems.at[1, 0], at.twin())
    swap.start()
    turn_of(ATTENDED)
    swap.wait_recv()

    is_expert = (lanes() >= PROBS) & (lanes() < PROBS + experts)
    for rows in chunks:
        h = x_ref[rows, :].astype(f32) + (dx_acc[rows, :] + gx_ref[rows, :])
        gx_ref[rows, :] = h
        rms = lax.rsqrt(jnp.mean(h * h, axis=-1, keepdims=True) + epsilon)
        xf = (h * rms * g_two).astype(bf16)
        xf_ref[rows, :] = xf
        logits = jnp.where(is_expert, dot_nn(xf, small), -1e30)
        expo = jnp.exp(logits - jnp.max(logits, axis=-1, keepdims=True))
        probs = expo / jnp.sum(expo, axis=-1, keepdims=True)
        packed = jnp.where(is_expert, probs, row_facts[rows, :])
        for r in range(top):
            chosen = lanes() == facts[rows, r : r + 1] + PROBS
            gate = jnp.sum(jnp.where(chosen, probs, 0.0), axis=-1, keepdims=True)
            slot = slot_cols[r][rows, :]
            gate = jnp.where(slot >= 0, gate, 0.0)
            packed = jnp.where(lanes() == PAIRS + r, gate, packed)
            packed = jnp.where(lanes() == PAIRS + top + r, slot.astype(f32), packed)
        row_facts[rows, :] = packed
    gate_rows = row_facts[...].T[PAIRS : PAIRS + 8, :]

    def outgoing(j):
        return send(
            placed.at[j * half : (j + 1) * half, :],
            tok.at[0, j],
            token_sems.at[0, j],
            token_sems.at[1, j],
            at.near(j),
        )

    for j in range(experts):
        index = lax.broadcasted_iota(jnp.int32, (half, 1), 0) + j * half
        pick = [slot_rows[r] == index for r in range(top)]
        slot_gate = sum(
            jnp.sum(jnp.where(pick[r], gate_rows[r : r + 1, :], 0.0), axis=1, keepdims=True)
            for r in range(top)
        )
        pick = sum(p.astype(f32) for p in pick).astype(bf16)
        if j:
            target = placed.at[j * half : (j + 1) * half, :]
        else:
            target = tok.at[0, 0]
        target[:, :width] = dot_nn(pick, xf_ref[...]).astype(bf16)
        target[:, width:] = (dot_nn(pick, cot_ref[...]) * slot_gate).astype(bf16)
        if j:
            outgoing(j).start()

    def shared_branch():
        shared_in.diagonal()
        shared_in.sent()
        for some in chunks:
            x_t[:, some] = xf_ref[some, :].T
            dy_t[:, some] = cot_ref[some, :].T
        y_acc[...] = jnp.zeros(y_acc.shape, f32)
        dx_acc[...] = jnp.zeros(dx_acc.shape, f32)
        for i in range(2):
            start = s_hidden * i
            branch(
                lambda some: xf_ref[some, :],
                lambda some: cot_ref[some, :],
                slice(0, length),
                sw,
                start,
                2 * s_hidden,
                s_hidden,
                act,
                y_acc,
                dx_acc,
            )

            def shared_grads(plane, carry):
                weight_grads(
                    plane, planes, length, x_t, dy_t, act, s_hidden, sw, start, 2 * s_hidden
                )
                return carry

            lax.fori_loop(0, planes, shared_grads, 0)
            turn_of(SHARED, i)
        out_ref[...] = y_acc[...].astype(bf16)
        s_dx[...] = dx_acc[...].astype(bf16)
        swaps = [
            send(mine, theirs, twin_sems.at[0, 2 + i], twin_sems.at[1, 2 + i], at.twin())
            for i, (mine, theirs) in enumerate(((out_ref, ffn_theirs), (s_dx, dx_theirs)))
        ]
        for swap in swaps:
            swap.start()
        return swaps

    turn_of(DISPATCHED)
    swap.wait_send()
    swaps = shared_branch()
    turn_of(SHARED)
    for j in range(1, experts):
        outgoing(j).wait_recv()
        outgoing(j).wait_send()
    across = send(tok.at[0], tok.at[1], twin_sems.at[0, 1], twin_sems.at[1, 1], at.twin())
    across.start()
    turn_of(ARRIVED)

    across.wait_recv()
    across.wait_send()

    def home_copy(j):
        return send(
            tok.at[0, j], home.at[0, j], home_sems.at[0, j], home_sems.at[1, j], at.near(j)
        )

    def share(j):
        return send(
            tok.at[1, j],
            ret.at[j * half : (j + 1) * half],
            share_sems.at[0, j],
            share_sems.at[1, j],
            at.twin(),
        )

    for i in range(2):
        expert_in[i].ready()
        expert_in[i].own_sent()

    def expert_half(i):
        for t in (1, 0):
            rows = slice(t * count, (t + 1) * count)

            def x_of(some):
                some = slice(some.start // half, some.stop // half)
                return tok[t, some, :, :width].reshape(-1, width)

            def dy_of(some):
                some = slice(some.start // half, some.stop // half)
                return tok[t, some, :, width:].reshape(-1, width)

            for some in chunks:
                x_t[:, rows.start + some.start : rows.start + some.stop] = x_of(some).T
                dy_t[:, rows.start + some.start : rows.start + some.stop] = dy_of(some).T
            if i == 0:
                y_acc[...] = jnp.zeros(y_acc.shape, f32)
                dx_acc[...] = jnp.zeros(dx_acc.shape, f32)
            else:
                for j in range(experts):
                    some = slice(j * half, (j + 1) * half)
                    y_acc[some, :] = part_one[t, j, :, :width].astype(f32)
                    dx_acc[some, :] = part_one[t, j, :, width:].astype(f32)
            branch(x_of, dy_of, rows, ew.at[i], 0, hidden, hidden, act, y_acc, dx_acc)
            target = tok if i else part_one
            if i and t == 0:
                for j in range(experts):
                    share(j).wait_recv()
            for j in range(experts):
                some = slice(j * half, (j + 1) * half)
                y, dx = y_acc[some, :], dx_acc[some, :]
                if i and t == 0:
                    y += ret[some, :width].astype(f32)
                    dx += ret[some, width:].astype(f32)
                target[t, j, :, :width] = y.astype(bf16)
                target[t, j, :, width:] = dx.astype(bf16)
                if i and t == 0 and j:
                    home_copy(j).start()
            if i and t:
                for j in range(experts):
                    share(j).start()
            turn_of(EXPERT, i, t)
        if i:
            home[0, 0] = tok[0, 0]
        expert_in[i].rest_sent()

        def grads_of(n, carry):
            plane = jnp.where(at.z * 2 < planes, planes - 1 - n, n)
            weight_grads(plane, planes, 2 * count, x_t, dy_t, act, hidden, ew.at[i], 0, hidden)
            expert_out[i].start_plane(plane)
            return carry

        lax.fori_loop(0, planes, grads_of, 0)

    for i in range(2):
        expert_half(i)
        turn_of(EXPERT, i)

    for j in range(1, experts):
        home_copy(j).wait_recv()
    swap = send(home.at[0], home.at[1], twin_sems.at[0, 5], twin_sems.at[1, 5], at.twin())
    swap.start()
    turn_of(HOME)
    for other in swaps:
        other.wait_recv()
        other.wait_send()
    swap.wait_recv()
    for rows in chunks:
        y = out_ref[rows, :].astype(f32) + ffn_theirs[rows, :].astype(f32)
        dx = s_dx[rows, :].astype(f32) + dx_theirs[rows, :].astype(f32)
        gate = jnp.zeros((step, 128), f32)
        dy = cot_ref[rows, :].astype(f32)
        for core in range(2):
            t = core + at.c - 2 * core * at.c
            index = lax.broadcasted_iota(jnp.int32, (1, count), 1) + t * count
            slots = [row_facts[rows, PAIRS + top + r : PAIRS + top + r + 1] for r in range(top)]
            slots = [(slot.astype(jnp.int32) == index).astype(f32) for slot in slots]
            for r in range(top):
                part = dot_nn(slots[r].astype(bf16), home[t, :, :, :width].reshape(count, width))
                y += row_facts[rows, PAIRS + r : PAIRS + r + 1] * part
                grad = jnp.sum(dy * part, axis=-1, keepdims=True)
                gate += jnp.where(lanes() == facts[rows, r : r + 1] + PROBS, grad, 0.0)
            dx += dot_nn(sum(slots).astype(bf16), home[t, :, :, width:].reshape(count, width))
        out_ref[rows, :] = (gx_ref[rows, :] + y).astype(bf16)
        dx_acc[rows, :] = dx
        y_acc[rows, :128] = gate
    attn_in.sent()

    grad_g_two = jnp.zeros((1, width), f32)
    grad_small = jnp.zeros((width, 128), f32)
    for rows in chunks:
        probs = jnp.where(is_expert, row_facts[rows, :], 0.0)
        grad_probs = y_acc[rows, :128]
        grad_logits = (
            probs * (grad_probs - jnp.sum(probs * grad_probs, axis=-1, keepdims=True))
        ).astype(bf16)
        grad_small += dot_tn(xf_ref[rows, :], grad_logits)
        grad_xf = dx_acc[rows, :] + dot_nt(grad_logits, small)
        h = gx_ref[rows, :]
        grad_h, grad_gain = norm_back_rows(grad_xf, h, g_two)
        grad_g_two += grad_gain
        grad_h = cot_ref[rows, :].astype(f32) + grad_h
        gx_ref[rows, :] = grad_h
        dy_t[:, rows] = grad_h.astype(bf16).T
        grad_o[rows, :] = dot_nn(
            grad_h.astype(bf16), blocks_of(aw, 0, heads_width)
        ).astype(bf16)
    for rows in chunks:
        x = x_ref[rows, :].astype(f32)
        rms = lax.rsqrt(jnp.mean(x * x, axis=-1, keepdims=True) + epsilon)
        x_t[:, rows] = (x * rms * g_one).astype(bf16).T
    masks()
    turn_of(COMBINED)

    def to_grads(start, columns, left, right):
        blocks = aw.shape[0]
        for i in range(0, blocks, blocks // 4):
            some = slice(i, i + blocks // 4)
            features = slice(i * aw.shape[1], (i + blocks // 4) * aw.shape[1])
            block = dot_nn(left[features, :length], right())
            aw[some, :, start : start + columns] = block.astype(bf16).reshape(
                blocks // 4, aw.shape[1], columns
            )

    to_grads(0, heads_width, dy_t, lambda: o_ref[...])
    turn_of(PROJECTED_OUT)
    for g in range(pairs):
        columns = slice(128 * g, 128 * (g + 1))
        for start, stop in attention_blocks(length)[::-1]:
            queries = q_ref[start:stop, columns]
            grads = grad_o[start:stop, columns]
            keys, values = k_ref[:stop, columns], v_ref[:stop, columns]
            grad_q = jnp.zeros((stop - start, 128), f32)
            grad_k = jnp.zeros((stop, 128), f32)
            grad_v = jnp.zeros((stop, 128), f32)
            for i in range(2):
                mask = lanes() // HD == i
                one_q = jnp.where(mask, queries, jnp.zeros_like(queries))
                one_do = jnp.where(mask, grads, jnp.zeros_like(grads))
                one_k = jnp.where(mask, keys, jnp.zeros_like(keys))
                scores = dot_nt(one_q, keys) * scale + bias[start:stop, :stop]
                log = LOGS + 2 * g + i
                weights = jnp.exp(scores - row_facts[start:stop, log : log + 1])
                grad_w = dot_nt(one_do, values)
                inner = jnp.sum(weights * grad_w, axis=-1, keepdims=True)
                grad_s = (weights * (grad_w - inner)).astype(bf16)
                grad_q += dot_nn(grad_s, one_k)
                grad_k += dot_tn(grad_s, one_q)
                grad_v += dot_tn(weights.astype(bf16), one_do)
            dproj[start:stop, columns] = turn(
                grad_q * scale, cosine[start:stop, :], -sine[start:stop, :]
            ).astype(bf16)
            if stop == length:
                dk_acc[...] = grad_k * scale
                dv_acc[...] = grad_v
            else:
                dk_acc[:stop, :] += grad_k * scale
                dv_acc[:stop, :] += grad_v
            turn_of(BACKWARD, g, start // (length // 2))
        dproj[:, heads_width + 128 * g : heads_width + 128 * (g + 1)] = turn(
            dk_acc[...], cosine, -sine
        ).astype(bf16)
        dproj[:, 2 * heads_width + 128 * g : 2 * heads_width + 128 * (g + 1)] = dv_acc[
            ...
        ].astype(bf16)
    for rows in chunks:
        part = dot_nt(dproj[rows, :], blocks_of(aw, heads_width, 4 * heads_width))
        part_mine[rows, :] = part.astype(bf16)
    last_swap = send(part_mine, part_theirs, twin_sems.at[0, 6], twin_sems.at[1, 6], at.twin())
    last_swap.start()
    for i in range(3):
        columns = slice(i * heads_width, (i + 1) * heads_width)
        to_grads((i + 1) * heads_width, heads_width, x_t, lambda: dproj[:, columns])
    turn_of(PROJECTED_BACK)
    last_swap.wait_recv()
    grad_g_one = jnp.zeros((1, width), f32)
    for rows in chunks:
        grad_xa = part_mine[rows, :].astype(f32) + part_theirs[rows, :].astype(f32)
        grad_x, grad_gain = norm_back_rows(grad_xa, x_ref[rows, :].astype(f32), g_one)
        gx_ref[rows, :] += grad_x
        grad_g_one += grad_gain
    index = lax.broadcasted_iota(jnp.int32, (128, 1), 0)
    gains = jnp.where(index == 0, grad_g_one, 0.0) + jnp.where(index == 1, grad_g_two, 0.0)
    small_grads = (gains.T + grad_small).astype(bf16)
    aw[:, :, 4 * heads_width :] = small_grads.reshape(aw.shape[0], aw.shape[1], 128)
    turn_of(LAST)
    s_out[...] = shared_out.total().astype(s_out.dtype)
    out_t[...] = attn_out[0].total()
    total = attn_out[1].total()
    for i in range(3):
        qkv_out[i] = total[:, i * heads_width : (i + 1) * heads_width]
    row = lax.broadcasted_iota(jnp.int32, small_out.shape[:1] + (128,), 0)
    lane = lax.broadcasted_iota(jnp.int32, small_out.shape[:1] + (128,), 1)
    small_out[...] = lax.dot_general(
        (row == lane).astype(f32),
        total[:, 3 * heads_width :],
        (((1,), (1,)), ((), ())),
        precision=lax.Precision.HIGHEST,
        preferred_element_type=f32,
    )
    for i in range(2):
        for j in range(1, GROUP):
            expert_out[i].arrive(j)

    swap.wait_send()
    last_swap.wait_send()
    for j in range(experts):
        share(j).wait_send()
    for j in range(1, experts):
        home_copy(j).wait_send()
    for i in range(2):
        expert_out[i].sent()
    shared_out.sent()
    for i in range(2):
        attn_out[i].sent()


def layer(planes, experts, top, heads_width, inputs, own):
    bf16, f32, dma = jnp.bfloat16, jnp.float32, pltpu.SemaphoreType.DMA
    n = planes * GROUP
    length, width = inputs[0].shape
    rows, a_width = own[0].shape
    s_width, e_width = own[1].shape[1], own[2].shape[2] // 2
    half = length * top // experts // 2
    slots = 2 * experts * half
    vmem, anywhere = pl.BlockSpec(memory_space=pltpu.VMEM), pl.BlockSpec(memory_space=pl.ANY)
    shape = jax.ShapeDtypeStruct
    tokens = pltpu.VMEM((2, experts, half, 2 * width), bf16)
    features = pltpu.VMEM((width, slots), bf16)
    wide = pltpu.VMEM((length, width), f32)
    narrow = pltpu.VMEM((length, width), bf16)
    heads = pltpu.VMEM((length, heads_width), bf16)
    row_facts = pltpu.VMEM((length, 128), f32)

    def plane_buffers(columns):
        return [
            pltpu.VMEM((planes, 2, rows, columns), bf16),
            pltpu.VMEM((planes, rows, columns), bf16),
            pltpu.VMEM((planes + 1, rows, columns), bf16),
        ]

    plane_sems = [dma((2, planes, 2)), dma((2, planes)), dma((2, 2, planes))]
    return pl.pallas_call(
        functools.partial(layer_kernel, planes, experts, top, heads_width),
        out_shape=(
            shape((length, width), bf16),
            shape((length, width), f32),
            shape((rows, heads_width), f32),
            shape((3, rows, heads_width), f32),
            shape((8, rows), f32),
            shape((rows, s_width), bf16),
            shape((GROUP, rows, 2 * e_width), bf16),
        ),
        in_specs=[vmem] * len(inputs) + [anywhere] * 3,
        out_specs=(vmem,) * 7,
        scratch_shapes=[
            pltpu.VMEM((length, 128), jnp.int32),
            pltpu.VMEM((8, length), jnp.int32),
            pltpu.VMEM((n, rows, a_width), bf16),
            pltpu.VMEM((n, rows, s_width), bf16),
            pltpu.VMEM((2, n, rows, e_width), bf16),
            tokens,
            tokens,
            tokens,
            pltpu.VMEM((slots, e_width), bf16),
            features,
            features,
            wide,
            wide,
            narrow,
            heads,
            heads,
            heads,
            heads,
            narrow,
            row_facts,
            narrow,
            narrow,
            pltpu.VMEM((experts * half, 2 * width), bf16),
            *plane_buffers(a_width),
            *plane_buffers(s_width),
            pltpu.VMEM((2, (planes + 1) * GROUP, rows, e_width), bf16),
            dma((10,)),
            dma((n,)),
            dma((4, n)),
            dma((n,)),
            dma((4, n)),
            dma((2, n)),
            dma((2, 2, n)),
            dma((2, GROUP)),
            *[dma((2,) + s.shape) for s in plane_sems],
            *plane_sems,
            dma((2, 2, 2, n)),
            dma((2, 2, GROUP, 3)),
            dma((2, GROUP)),
            dma((2, GROUP)),
            dma((2, GROUP)),
            dma((2, 7)),
        ],
        compiler_params=pltpu.CompilerParams(
            collective_id=0, has_side_effects=True, vmem_limit_bytes=63 << 20
        ),
    )(*inputs, *own)


def local_grouped(
    planes,
    tokens,
    segment_ids,
    expert_ids,
    slot_order,
    gain_attn,
    qkv_weight,
    out_weight,
    gain_ffn,
    router_weight,
    gate_up,
    down_weight,
    shared_gate_up,
    shared_down,
    cotangent,
):
    bf16, f32 = jnp.bfloat16, jnp.float32
    rows, heads_width = qkv_weight.shape[0], qkv_weight.shape[2]
    experts, hidden = down_weight.shape[0], down_weight.shape[1]
    s_hidden = shared_down.shape[0]
    length = tokens.shape[0]
    top = expert_ids.shape[1]
    expert_packed = jnp.concatenate(
        [gate_up.reshape(experts, rows, 2 * hidden), down_weight.transpose(0, 2, 1)], axis=2
    )
    shared_packed = jnp.concatenate(
        [shared_gate_up.reshape(rows, 2 * s_hidden), shared_down.T], axis=1
    )
    small = jnp.concatenate([gain_attn[:, None], gain_ffn[:, None], router_weight], axis=1)
    small = jnp.pad(small, ((0, 0), (0, 128 - small.shape[1])))
    attn_packed = jnp.concatenate(
        [out_weight.T, qkv_weight.reshape(rows, 3 * heads_width), small], axis=1
    )
    inverse = np.exp(np.arange(HD // 2, dtype=np.float32) * np.float32(-2.0 * math.log(10000.0) / HD))
    angles = np.arange(length, dtype=np.float32)[:, None] * inverse[None, :]
    waves = np.concatenate([np.cos(angles)] * 2 + [np.sin(angles)] * 2, axis=1)
    waves = jnp.asarray(waves, f32)
    output, grad_tokens, mine_out, mine_qkv, small_mine, mine_shared, mine_expert = layer(
        planes,
        experts,
        top,
        heads_width,
        (tokens, cotangent, expert_ids.T, slot_order, segment_ids, waves),
        (attn_packed, shared_packed, expert_packed),
    )

    def halves(grads, size):
        both = [grads[..., :size], grads[..., size : 2 * size]]
        return jnp.stack(both, axis=-2).astype(f32)

    return (
        output,
        grad_tokens,
        small_mine[0],
        mine_qkv.transpose(1, 0, 2),
        mine_out.T,
        small_mine[1],
        small_mine[2 : 2 + experts].T,
        halves(mine_expert, hidden),
        mine_expert[:, :, 2 * hidden :].transpose(0, 2, 1).astype(f32),
        halves(mine_shared, s_hidden),
        mine_shared[:, 2 * s_hidden :].T.astype(f32),
    )


def solution(mesh):
    def pick(*args):
        experts, rows = args[9].shape[0], args[5].shape[0]
        if experts == GROUP and mesh.shape["dp"] == LINE * GROUP and rows % 16 == 0:
            return local_grouped(mesh.shape["dp"] // GROUP, *args)
        return local_plain(*args)

    return jax.shard_map(
        pick,
        mesh=mesh,
        in_specs=(
            P("dp", None),
            P("dp", None),
            P("dp", None),
            P("dp", None),
            P("dp"),
            P("dp", None, "tensor"),
            P("tensor", "dp"),
            P("dp"),
            P("dp", None),
            P(None, "dp", None, "tensor"),
            P(None, "tensor", "dp"),
            P("dp", None, "tensor"),
            P("tensor", "dp"),
            P("dp", None),
        ),
        out_specs=(
            P("dp", None),
            P("dp", None),
            P("dp"),
            P("dp", None, "tensor"),
            P("tensor", "dp"),
            P("dp"),
            P("dp", None),
            P(None, "dp", None, "tensor"),
            P(None, "tensor", "dp"),
            P("dp", None, "tensor"),
            P("tensor", "dp"),
        ),
        check_vma=False,
    )
```
